32 devices in a mesh: group: 2 (over x), expert: 16 (over z, y, core).
Axes of the slice: x: 2, y: 2, z: 4, core: 2. Of those that a mesh axis runs over, the one named last changes fastest.
Arguments:
- hidden: bfloat16 [3, 512, 2048], P(None, ('group', 'expert')), parts along dimension 1, may hold values from -6 to 6
- route_ids: int32 [3, 512, 8], P(None, ('group', 'expert')), parts along dimension 1, may hold values from 0 to 15, all different within a row; in each aligned block of 16 rows (0 to 15, 16 to 31, ..., all dimensions but the last counted through in order) at most 16 rows name the same one
- route_logits: float32 [3, 512, 8], P(None, ('group', 'expert')), parts along dimension 1, may hold values from -4 to 368
- placement: int32 [16], replicated, may hold values from 0 to 15, each once
- factors: bfloat16 [16, 540672], P(None, 'expert'), may hold values from -0.375 to 0.375
- w_gate: bfloat16 [16, 2048, 768], P('expert'), may hold values from -0.125 to 0.125
- w_up: bfloat16 [16, 2048, 768], P('expert'), may hold values from -0.125 to 0.125
- down_weight: bfloat16 [16, 768, 2048], P('expert'), may hold values from -0.21875 to 0.21875
Outputs:
- decoded: bfloat16 [3, 512, 2048], P(None, ('group', 'expert')), parts along dimension 1
The draws below stay inside these ranges and needn't reach their ends.
There are 2 independent parts, one for each index of `group`. The reference program is written for one: setup_inputs(seed, part) draws one part's arguments, and reference() takes and returns one part's arrays. A program takes and returns all parts, laid end to end along the dimension named above; an argument that names none is the same for every part. Nothing has to cross between parts.
Inputs may be any that keep to these rules, and one draw needn't show every extreme that they name: `route_ids`: in every decode step the 16 rows of one device name each expert at most 16 times, and in every draw some device names some expert exactly 16 times; the 8 ids of a row differ. `placement`: each expert stands in exactly one slot.
All inputs are finite; a program needn't handle non-finite values.
Results may differ from the reference program's by a relative error of at most 0.0083.
Values may be sent and summed in bfloat16 or wider, within the bound.
No kernel may reach another device: no remote copies, remote signals or barrier semaphores. Data moves between devices by JAX's collectives and lax.ppermute only.
A program may use at most 128 MiB of HBM per device.

```python
import math
import jax
import jax.numpy as jnp
import numpy as np
from jax import lax

D = 2048
FF = 768
RANK = 64
TOP = 8
STEPS = 3
ROWS_DEV = 16
EXPERTS = 16
ROWS = 256
CAP = 16
FLAT = 540672
N_EXPERT = 16


def draw_route_logits(key, part):
    key = jax.random.fold_in(key, 11)
    first_key, second_key = jax.random.split(key, 2)
    shape_all = (STEPS, ROWS, TOP)
    center = jax.random.uniform(second_key, (STEPS, ROWS, 1), jnp.float32, -2.5, 2.5)
    values = center + jax.random.uniform(first_key, shape_all, jnp.float32, -1.0, 1.0)
    return values


def steps_of(rng, dims, pieces, smallest, largest):
    loudness, own = 1.0, jax.random.fold_in(rng, 6)
    for dim, parts in pieces:
        draws = jnp.exp(jax.random.uniform(jax.random.fold_in(own, dim), (parts,), jnp.float32, smallest / len(pieces), largest / len(pieces)))
        loudness = loudness * jnp.repeat(draws, dims[dim] // parts).reshape([-1 if axis == dim else 1 for axis in range(len(dims))])
    return loudness


def routed_block(stream_key, own, number, rows, amount, top, bound, skew):
    ranking = jax.random.permutation(stream_key, amount)
    packed, usual = load_shares(amount, rows * top, bound, skew, True), load_shares(amount, rows * top, bound, skew, False)
    places = jnp.arange(amount)

    def named(tallies, turn):
        used = int((tallies > 0).sum())
        fixed = max(1, used // 4)
        passed = fixed + (places - fixed + turn * (used - fixed)) % max(1, amount - fixed)
        return jnp.zeros((amount,), jnp.int32).at[ranking[jnp.where(places < fixed, places, passed)]].set(jnp.asarray(tallies, jnp.int32))

    tallies = jnp.where(number % 4 == 0, named(packed, number // 4), named(usual, number - number // 4 - 1))
    mixed = jax.random.permutation(jax.random.fold_in(own, 3), amount)
    giver, taker = mixed[0:amount // 2 * 2:2], mixed[1:amount // 2 * 2:2]
    room = jnp.minimum(tallies[giver] - 1, bound - tallies[taker]) // 2
    room = jnp.where((giver == ranking[0]) | (taker == ranking[0]) | (tallies[taker] == 0), 0, jnp.maximum(room, 0))
    passed = jax.random.randint(jax.random.fold_in(own, 4), (amount // 2,), 0, 1 << 20) % (room + 1)
    tallies = tallies.at[giver].add(-passed).at[taker].add(passed)
    labels = jnp.searchsorted(jnp.cumsum(tallies), jnp.arange(rows * top), side="right").astype(jnp.int32)
    listing = labels.reshape(top, rows).T
    listing = listing[jax.random.permutation(jax.random.fold_in(own, 1), rows)]
    turn = jax.random.randint(jax.random.fold_in(own, 2), (rows, 1), 0, top)
    return jnp.take_along_axis(listing, (jnp.arange(top)[None, :] + turn) % top, axis=1)


def load_shares(count, total, limit, skew, full):
    weights = [(1 << 20) // math.isqrt(rank ** skew) + 1 for rank in range(1, count + 1)]
    largest = limit if full else min(limit, max(-(-total // count), total * weights[0] // sum(weights)))
    least = 1 if total - largest >= count - 1 else 0
    holding, rest = [largest] + [least] * (count - 1), total - largest - least * (count - 1)
    while rest > 0:
        free = [i for i in range(1, count) if holding[i] < largest] or [i for i in range(1, count) if holding[i] < limit]
        whole, remaining = sum([weights[i] for i in free]), rest
        for i in free:
            extra = min(limit - holding[i], max(1, remaining * weights[i] // whole), rest)
            holding[i] = holding[i] + extra
            rest = rest - extra
    return np.array(holding)


def normal_values(key, extent, spread, reach, cuts=(), held_as=jnp.bfloat16):
    values = spread * jax.random.normal(key, extent, jnp.float32)
    if cuts:
        values = values * steps_of(key, extent, cuts, -0.22, 0.18)
    return jnp.clip(values, -reach, reach).astype(held_as)


def setup_inputs(seed: int = 0, part: int = 0) -> dict:
    key_list = jax.random.split(jax.random.key(seed), 9)
    part_splits = jax.random.split(jax.random.fold_in(key_list[8], part), 9)
    hidden = normal_values(part_splits[0], (STEPS, ROWS, D), 1.0, 6.0, ((1, 16),))
    route_ids_keys = jax.random.split(jax.random.fold_in(part_splits[1], 1), STEPS * ROWS // ROWS_DEV)
    route_ids_turns = jax.random.permutation(jax.random.fold_in(part_splits[1], 3), STEPS * ROWS // ROWS_DEV)
    route_ids = jax.vmap(lambda own, number: routed_block(jax.random.fold_in(part_splits[1], 2), own, number, ROWS_DEV, EXPERTS, TOP, CAP, 2))(route_ids_keys, route_ids_turns).reshape((STEPS, ROWS, TOP))
    route_logits = draw_route_logits(jax.random.fold_in(jax.random.fold_in(key_list[8], part), 71), part)
    placement = jax.random.permutation(key_list[3], EXPERTS).astype(jnp.int32)
    factors = normal_values(key_list[4], (EXPERTS, FLAT), (0.45 / (RANK * D) ** 0.25), 0.375, ((1, 16),))
    w_gate = normal_values(key_list[5], (EXPERTS, D, FF), D ** -0.5, 0.125, ((0, 16),))
    w_up = normal_values(key_list[6], (EXPERTS, D, FF), D ** -0.5, 0.125, ((0, 16),))
    down_weight = normal_values(key_list[7], (EXPERTS, FF, D), FF ** -0.5, 0.21875, ((0, 16),))
    return dict(hidden=hidden, route_ids=route_ids, route_logits=route_logits, placement=placement, factors=factors, w_gate=w_gate, w_up=w_up, down_weight=down_weight)


adapter_scale = 2.0


def unpack_factors(flat_factors, width, hidden_units, rank_size):
    layouts = [(width, rank_size), (rank_size, hidden_units), (width, rank_size), (rank_size, hidden_units), (hidden_units, rank_size), (rank_size, width)]
    offset = 0
    segments = []
    for leading, trailing in layouts:
        segments.append(flat_factors[offset:offset + leading * trailing].reshape(leading, trailing))
        offset = offset + leading * trailing
    return segments


def merge_weight(loaded_weights, factor_a, factor_b):
    adapter_delta = jnp.dot(factor_a, factor_b, preferred_element_type=jnp.float32)
    return (loaded_weights.astype(jnp.float32) + adapter_scale * adapter_delta).astype(jnp.bfloat16)


def apply_expert_block(inputs, merged_gate, merged_up, combined_down_weight):
    gate_part = jnp.dot(inputs, merged_gate, preferred_element_type=jnp.float32)
    up_part = jnp.dot(inputs, merged_up, preferred_element_type=jnp.float32)
    inner = (jax.nn.silu(gate_part) * up_part).astype(jnp.bfloat16)
    return jnp.dot(inner, combined_down_weight, preferred_element_type=jnp.float32).astype(jnp.bfloat16)


def route_gates(logits):
    highest = jnp.max(logits, axis=-1, keepdims=True)
    router_scores = jnp.exp(logits - highest)
    return (router_scores / jnp.sum(router_scores, axis=-1, keepdims=True)).astype(jnp.bfloat16)


def reference(hidden, route_ids, route_logits, placement, factors, w_gate, w_up, down_weight):
    slot_of = jnp.zeros((EXPERTS,), jnp.int32).at[placement].set(jnp.arange(EXPERTS, dtype=jnp.int32))
    gates = route_gates(route_logits)
    buffer_size = N_EXPERT * CAP
    pair_total = ROWS * TOP

    def expert_grouped(running, expert_id):
        flat_factors = lax.dynamic_index_in_dim(factors, slot_of[expert_id], 0, keepdims=False)
        segments = unpack_factors(flat_factors, D, FF, RANK)
        resident_gate = lax.dynamic_index_in_dim(w_gate, expert_id, 0, keepdims=False)
        resident_up = lax.dynamic_index_in_dim(w_up, expert_id, 0, keepdims=False)
        resident_down = lax.dynamic_index_in_dim(down_weight, expert_id, 0, keepdims=False)
        merged_gate = merge_weight(resident_gate, segments[0], segments[1])
        merged_up = merge_weight(resident_up, segments[2], segments[3])
        combined_down_weight = merge_weight(resident_down, segments[4], segments[5])
        for step_index in range(STEPS):
            ids_flat = route_ids[step_index].reshape(-1)
            chosen = ids_flat == expert_id
            position = jnp.cumsum(chosen.astype(jnp.int32)) - 1
            target = jnp.where(chosen, position, buffer_size).astype(jnp.int32)
            index_buffer = jnp.full((buffer_size,), pair_total, jnp.int32).at[target].set(jnp.arange(pair_total, dtype=jnp.int32), mode="drop")
            valid = index_buffer < pair_total
            safe_pairs = jnp.minimum(index_buffer, pair_total - 1)
            row_ids = (safe_pairs // TOP).astype(jnp.int32)
            inputs = hidden[step_index][row_ids]
            outputs = apply_expert_block(inputs, merged_gate, merged_up, combined_down_weight)
            weights = jnp.where(valid, gates[step_index].reshape(-1)[safe_pairs].astype(jnp.float32), jnp.float32(0.0))
            running = running.at[step_index, row_ids].add(outputs.astype(jnp.float32) * weights[:, None])
        return running, None

    running = jnp.zeros((STEPS, ROWS, D), jnp.float32)
    running, unused = lax.scan(expert_grouped, running, jnp.arange(EXPERTS, dtype=jnp.int32))
    return running.astype(jnp.bfloat16)
```

```python
import jax
import jax.numpy as jnp
from jax import lax
from jax.sharding import PartitionSpec as P

adapter_scale = 2.0
LANES = 128


def route_gates(logits):
    highest = jnp.max(logits, axis=-1, keepdims=True)
    router_scores = jnp.exp(logits - highest)
    return (router_scores / jnp.sum(router_scores, axis=-1, keepdims=True)).astype(jnp.bfloat16)


def dot(a, b):
    return jnp.dot(a, b, preferred_element_type=jnp.float32)


def shards(hidden, route_ids, route_logits, placement, factors, w_gate, w_up, down_weight):
    owners = lax.axis_size("expert")
    experts = placement.shape[0]
    steps, rows, width = hidden.shape
    units = w_gate.shape[2]
    rank = factors.shape[1] * owners // (3 * (width + units))
    total = rows * owners

    gates = route_gates(route_logits)
    chosen = route_ids[..., None] == jnp.arange(experts, dtype=jnp.int32)
    dense = jnp.sum(jnp.where(chosen, gates[..., None], 0), axis=2, dtype=jnp.float32)
    dense = dense.astype(jnp.bfloat16)
    padded = -(-experts // LANES) * LANES
    dense = jnp.pad(dense, ((0, 0), (0, 0), (0, padded - experts)))
    payload = jnp.concatenate([hidden, dense], axis=-1)
    gathered = lax.all_gather(payload, "expert", axis=1, tiled=True)

    slot_of = (
        jnp.zeros((experts,), jnp.int32).at[placement].set(jnp.arange(experts, dtype=jnp.int32))
    )
    ordered = jnp.take(factors, slot_of, axis=0).reshape(experts, -1, LANES)
    received = lax.all_to_all(ordered, "expert", split_axis=0, concat_axis=0, tiled=True)
    flat = received.reshape(-1, LANES)
    shapes = [(width, rank), (rank, units)] * 2 + [(units, rank), (rank, width)]
    segments, at = [], 0
    for lead, trail in shapes:
        n = lead * trail // LANES
        segments.append(flat[at : at + n].reshape(lead, trail))
        at += n
    gate_a, gate_b, up_a, up_b, down_a, down_b = segments

    x = gathered[..., :width].reshape(steps * total, width)
    me = lax.axis_index("expert")
    mine = lax.dynamic_index_in_dim(gathered[..., width:], me, 2, keepdims=True)
    gate_part = dot(x, w_gate[0])
    up_part = dot(x, w_up[0])

    results = []
    for s in range(steps):
        cut = slice(s * total, (s + 1) * total)
        low_g = (adapter_scale * dot(x[cut], gate_a)).astype(jnp.bfloat16)
        low_u = (adapter_scale * dot(x[cut], up_a)).astype(jnp.bfloat16)
        g = gate_part[cut] + dot(low_g, gate_b)
        u = up_part[cut] + dot(low_u, up_b)
        inner = (jax.nn.silu(g) * u).astype(jnp.bfloat16)
        low_d = (adapter_scale * dot(inner, down_a)).astype(jnp.bfloat16)
        out = dot(inner, down_weight[0]) + dot(low_d, down_b)
        weighted = (out * mine[s].astype(jnp.float32)).astype(jnp.bfloat16)
        results.append(lax.psum_scatter(weighted, "expert", scatter_dimension=0, tiled=True))
    return jnp.stack(results, axis=0)


def solution(mesh):
    placed = (
        P(None, ("group", "expert"), None),
        P(None, ("group", "expert"), None),
        P(None, ("group", "expert"), None),
        P(),
        P(None, "expert"),
        P("expert", None, None),
        P("expert", None, None),
        P("expert", None, None),
    )
    return jax.shard_map(
        shards,
        mesh=mesh,
        in_specs=placed,
        out_specs=P(None, ("group", "expert"), None),
        check_vma=False,
    )
```

```python
import jax
import jax.numpy as jnp
from jax import lax
from jax.sharding import PartitionSpec as P

adapter_scale = 2.0
LANES = 128


def route_gates(logits):
    highest = jnp.max(logits, axis=-1, keepdims=True)
    router_scores = jnp.exp(logits - highest)
    return (router_scores / jnp.sum(router_scores, axis=-1, keepdims=True)).astype(jnp.bfloat16)


def split_axis(n):
    cores = 2 if n % 2 == 0 else 1
    chips = n // cores
    middle = 1
    while chips % (2 * middle) == 0 and 4 * middle * middle <= chips:
        middle *= 2
    return chips // middle, middle, cores


def shift(x, n, stride, size, k):
    pairs = []
    for i in range(n):
        place = i // stride % size
        pairs.append((i, i + ((place + k) % size - place) * stride))
    return lax.ppermute(x, "expert", pairs)


def gather_rows(x, n):
    outer, middle, cores = split_axis(n)
    for stride, size in ((middle * cores, outer), (cores, middle), (1, cores)):
        x = jnp.stack([x] + [shift(x, n, stride, size, k) for k in range(1, size)])
    return x


def scatter_rows(x, n):
    outer, middle, cores = split_axis(n)
    for stride, size in ((1, cores), (cores, middle), (middle * cores, outer)):
        kept = x[0]
        for k in range(1, size):
            sent = shift(x[k].astype(jnp.bfloat16), n, stride, size, size - k)
            kept = kept + sent.astype(jnp.float32)
        x = kept
    return x.astype(jnp.bfloat16)


def dot(a, b):
    return jnp.dot(a, b, preferred_element_type=jnp.float32)


def dense_shards(hidden, route_ids, route_logits, placement, factors, w_gate, w_up, down_weight):
    owners = lax.axis_size("expert")
    experts = placement.shape[0]
    steps, rows, width = hidden.shape
    units = w_gate.shape[2]
    rank = factors.shape[1] * owners // (3 * (width + units))
    total = rows * owners

    gates = route_gates(route_logits)
    chosen = route_ids[..., None] == jnp.arange(experts, dtype=jnp.int32)
    dense = jnp.sum(jnp.where(chosen, gates[..., None], 0), axis=2, dtype=jnp.float32)
    dense = dense.astype(jnp.bfloat16)
    padded = -(-experts // LANES) * LANES
    dense = jnp.pad(dense, ((0, 0), (0, 0), (0, padded - experts)))
    payload = jnp.concatenate([hidden, dense], axis=-1)
    gathered = [
        gather_rows(payload[s], owners).reshape(total, width + padded) for s in range(steps)
    ]

    slot_of = (
        jnp.zeros((experts,), jnp.int32).at[placement].set(jnp.arange(experts, dtype=jnp.int32))
    )
    ordered = jnp.take(factors, slot_of, axis=0).reshape(experts, -1, LANES)
    received = lax.all_to_all(ordered, "expert", split_axis=0, concat_axis=0, tiled=True)
    flat = received.reshape(-1, LANES)
    shapes = [(width, rank), (rank, units)] * 2 + [(units, rank), (rank, width)]
    segments, at = [], 0
    for lead, trail in shapes:
        n = lead * trail // LANES
        segments.append(flat[at : at + n].reshape(lead, trail))
        at += n
    gate_a, gate_b, up_a, up_b, down_a, down_b = segments

    me = lax.axis_index("expert")
    results = []
    for s in range(steps):
        x = gathered[s][:, :width]
        mine = lax.dynamic_index_in_dim(gathered[s][:, width:], me, 1, keepdims=True)
        low_g = (adapter_scale * dot(x, gate_a)).astype(jnp.bfloat16)
        low_u = (adapter_scale * dot(x, up_a)).astype(jnp.bfloat16)
        g = dot(x, w_gate[0]) + dot(low_g, gate_b)
        u = dot(x, w_up[0]) + dot(low_u, up_b)
        inner = (jax.nn.silu(g) * u).astype(jnp.bfloat16)
        low_d = (adapter_scale * dot(inner, down_a)).astype(jnp.bfloat16)
        out = dot(inner, down_weight[0]) + dot(low_d, down_b)
        weighted = out * mine.astype(jnp.float32)
        outer, middle, cores = split_axis(owners)
        weighted = weighted.reshape(cores, middle, outer, rows, width)
        results.append(scatter_rows(weighted, owners))
    return jnp.stack(results, axis=0)


def row_capacity(rows, top, experts):
    return min(rows, 3 * max(1, rows * top // experts))


def unpack_factors(flat_factors, width, hidden_units, rank_size):
    layouts = [
        (width, rank_size),
        (rank_size, hidden_units),
        (width, rank_size),
        (rank_size, hidden_units),
        (hidden_units, rank_size),
        (rank_size, width),
    ]
    offset = 0
    segments = []
    for leading, trailing in layouts:
        segments.append(
            flat_factors[offset : offset + leading * trailing].reshape(leading, trailing)
        )
        offset = offset + leading * trailing
    return segments


def merge_weight(loaded_weights, factor_a, factor_b):
    adapter_delta = jnp.dot(factor_a, factor_b, preferred_element_type=jnp.float32)
    return (loaded_weights.astype(jnp.float32) + adapter_scale * adapter_delta).astype(jnp.bfloat16)


def apply_expert_block(inputs, merged_gate, merged_up, combined_down_weight):
    gate_part = jnp.dot(inputs, merged_gate, preferred_element_type=jnp.float32)
    up_part = jnp.dot(inputs, merged_up, preferred_element_type=jnp.float32)
    inner = (jax.nn.silu(gate_part) * up_part).astype(jnp.bfloat16)
    return jnp.dot(inner, combined_down_weight, preferred_element_type=jnp.float32).astype(
        jnp.bfloat16
    )


def sparse_shards(hidden, route_ids, route_logits, placement, factors, w_gate, w_up, down_weight):
    owners = lax.axis_size("expert")
    experts = placement.shape[0]
    steps_count, row_count, width = hidden.shape
    top_count = route_ids.shape[2]
    hidden_units = w_gate.shape[2]
    rank_size = factors.shape[1] * owners // (3 * (width + hidden_units))
    capacity = row_capacity(row_count, top_count, experts)
    slot_of = (
        jnp.zeros((experts,), jnp.int32).at[placement].set(jnp.arange(experts, dtype=jnp.int32))
    )
    ordered = jnp.take(factors, slot_of, axis=0)
    received = lax.all_to_all(ordered, "expert", split_axis=0, concat_axis=1, tiled=True)
    segments = unpack_factors(received[0], width, hidden_units, rank_size)
    merged_gate = merge_weight(w_gate[0], segments[0], segments[1])
    merged_up = merge_weight(w_up[0], segments[2], segments[3])
    combined_down_weight = merge_weight(down_weight[0], segments[4], segments[5])

    def layout(step_index):
        ids_flat = route_ids[step_index].reshape(-1)
        onehot = (ids_flat[:, None] == jnp.arange(experts, dtype=jnp.int32)[None, :]).astype(
            jnp.int32
        )
        position = jnp.sum((jnp.cumsum(onehot, axis=0) - 1) * onehot, axis=1)
        target = ids_flat * capacity + position
        placed = (
            jnp.arange(experts * capacity, dtype=jnp.int32)[:, None] == target[None, :]
        ).astype(jnp.bfloat16)
        pair_rows = jnp.repeat(hidden[step_index], top_count, axis=0)
        outgoing = jnp.dot(placed, pair_rows, preferred_element_type=jnp.float32).astype(
            jnp.bfloat16
        )
        outgoing = outgoing.reshape(experts, 1, capacity, width)
        gates = route_gates(route_logits[step_index]).reshape(-1)
        weighted = placed * gates[None, :]
        return (outgoing, weighted)

    layouts_all = [layout(step_index) for step_index in range(steps_count)]
    results = []
    for step_index in range(steps_count):
        outgoing, weighted = layouts_all[step_index]
        arrived = lax.all_to_all(outgoing, "expert", split_axis=0, concat_axis=1, tiled=True)
        outputs = apply_expert_block(
            arrived.reshape(-1, width), merged_gate, merged_up, combined_down_weight
        )
        outputs = outputs.reshape(arrived.shape)
        returned = lax.all_to_all(outputs, "expert", split_axis=1, concat_axis=0, tiled=True)
        flat_back = returned.reshape(experts * capacity, width)
        pair_out = jnp.einsum("cp,cd->pd", weighted, flat_back, preferred_element_type=jnp.float32)
        results.append(
            pair_out.reshape(row_count, top_count, width).sum(axis=1).astype(jnp.bfloat16)
        )
    return jnp.stack(results, axis=0)


def shards(hidden, route_ids, *rest):
    rows, top = route_ids.shape[1:]
    experts = rest[1].shape[0]
    every = row_capacity(rows, top, experts) == rows
    return (dense_shards if every else sparse_shards)(hidden, route_ids, *rest)


def solution(mesh):
    placed = (
        P(None, ("group", "expert"), None),
        P(None, ("group", "expert"), None),
        P(None, ("group", "expert"), None),
        P(),
        P(None, "expert"),
        P("expert", None, None),
        P("expert", None, None),
        P("expert", None, None),
    )
    return jax.shard_map(
        shards,
        mesh=mesh,
        in_specs=placed,
        out_specs=P(None, ("group", "expert"), None),
        check_vma=False,
    )
```

```python
import functools

import jax
import jax.numpy as jnp
from jax import lax
from jax.experimental import pallas as pl
from jax.experimental.pallas import tpu as pltpu
from jax.sharding import PartitionSpec as P

adapter_scale = 2.0
LANES = 128


def route_gates(logits):
    highest = jnp.max(logits, axis=-1, keepdims=True)
    router_scores = jnp.exp(logits - highest)
    return (router_scores / jnp.sum(router_scores, axis=-1, keepdims=True)).astype(jnp.bfloat16)


def split_axis(n):
    cores = 2 if n % 2 == 0 else 1
    chips = n // cores
    middle = 1
    while chips % (2 * middle) == 0 and 4 * middle * middle <= chips:
        middle *= 2
    return chips // middle, middle, cores


def shift(x, n, stride, size, k):
    pairs = []
    for i in range(n):
        place = i // stride % size
        pairs.append((i, i + ((place + k) % size - place) * stride))
    return lax.ppermute(x, "expert", pairs)


def gather_rows(x, n):
    outer, middle, cores = split_axis(n)
    column = [x] + [shift(x, n, middle * cores, outer, k) for k in range(1, outer)]
    column = jnp.concatenate(column, axis=0)
    sheet = [column] + [shift(column, n, cores, middle, k) for k in range(1, middle)]
    return sheet + [shift(p, n, 1, cores, k) for k in range(1, cores) for p in sheet]


def scatter_rows(kept, sent, n):
    outer, middle, cores = split_axis(n)
    count, width = kept.shape
    if cores > 1:
        kept = kept + shift(sent, n, 1, cores, 1).astype(jnp.float32)
    for stride, size in ((cores, middle), (middle * cores, outer)):
        count //= size
        total = kept[:count]
        for k in range(1, size):
            part = kept[k * count : (k + 1) * count].astype(jnp.bfloat16)
            total = total + shift(part, n, stride, size, size - k).astype(jnp.float32)
        kept = total
    return kept.astype(jnp.bfloat16)


def dot(a, b):
    return jnp.dot(a, b, preferred_element_type=jnp.float32)


def payload_kernel(hidden_ref, ids_ref, logits_ref, *out_refs):
    rows, width = out_refs[0].shape[0], hidden_ref.shape[1]
    padded = out_refs[0].shape[1] - width
    gates = route_gates(logits_ref[...]).astype(jnp.float32)
    ids = ids_ref[...]
    lane = lax.broadcasted_iota(jnp.int32, (ids.shape[0], padded), 1)
    dense = jnp.zeros(lane.shape, jnp.float32)
    for k in range(ids.shape[1]):
        dense += jnp.where(ids[:, k : k + 1] == lane, gates[:, k : k + 1], 0.0)
    dense = dense.astype(jnp.bfloat16)
    for s, out_ref in enumerate(out_refs):
        out_ref[:, :width] = hidden_ref[s * rows : (s + 1) * rows, :]
        out_ref[:, width:] = dense[s * rows : (s + 1) * rows, :]


def make_payload(hidden, route_ids, route_logits, experts):
    steps, rows, width = hidden.shape
    padded = -(-experts // LANES) * LANES
    shape = jax.ShapeDtypeStruct((rows, width + padded), jnp.bfloat16)
    return pl.pallas_call(
        payload_kernel,
        out_shape=[shape] * steps,
        name="payload",
    )(
        hidden.reshape(steps * rows, width),
        route_ids.reshape(steps * rows, -1),
        route_logits.reshape(steps * rows, -1),
    )


def order_kernel(placement_ref, factors_ref, out_ref, wide_ref):
    slots, length, lanes = out_ref.shape

    def cut(t, carry):
        start = pl.multiple_of(t * lanes, lanes)
        tile = factors_ref[:, pl.ds(start, lanes)].astype(jnp.float32)
        wide_ref[pl.ds(t, slots, stride=length), :] = tile
        return carry

    lax.fori_loop(0, length, cut, 0, unroll=8)
    for s in range(slots):
        out_ref[placement_ref[s]] = wide_ref[s * length : (s + 1) * length, :].astype(jnp.bfloat16)


def order_factors(placement, factors):
    slots, entries = factors.shape
    length = entries // LANES
    return pl.pallas_call(
        order_kernel,
        out_shape=jax.ShapeDtypeStruct((slots, length, LANES), jnp.bfloat16),
        in_specs=[
            pl.BlockSpec(memory_space=pltpu.SMEM),
            pl.BlockSpec(memory_space=pltpu.VMEM),
        ],
        scratch_shapes=[pltpu.VMEM((slots * length, LANES), jnp.float32)],
        compiler_params=pltpu.CompilerParams(vmem_limit_bytes=12 << 20),
        name="order_factors",
    )(placement, factors)


def relayout_kernel(flat_ref, a_gu_ref, gate_b_ref, up_b_ref, down_a_ref, down_b_ref, wide_ref):
    width, units = a_gu_ref.shape[0], gate_b_ref.shape[1]
    rank = gate_b_ref.shape[0]
    n_wide, n_unit = width // 2, units // 2
    at_ub = 2 * n_wide + n_unit
    at_da = 2 * n_wide + 2 * n_unit
    chunk = 128
    left = lax.broadcasted_iota(jnp.int32, (chunk, LANES), 1) < rank

    def load(start):
        return flat_ref[pl.ds(pl.multiple_of(start, 128), chunk), :].astype(jnp.float32)

    def gate_up(i, carry):
        g, u = load(i * chunk), load(n_wide + n_unit + i * chunk)
        at = 2 * i * chunk
        wide_ref[pl.ds(at, chunk, stride=2), :] = jnp.where(left, g, pltpu.roll(u, rank, 1))
        wide_ref[pl.ds(at + 1, chunk, stride=2), :] = jnp.where(left, pltpu.roll(g, rank, 1), u)
        both = wide_ref[pl.ds(pl.multiple_of(at, 128), 2 * chunk), :]
        a_gu_ref[pl.ds(pl.multiple_of(at, 128), 2 * chunk), :] = both.astype(jnp.bfloat16)
        return carry

    lax.fori_loop(0, n_wide // chunk, gate_up, 0, unroll=2)
    for i in range(n_unit // chunk):
        d = load(at_da + i * chunk)
        at = 2 * i * chunk
        wide_ref[pl.ds(at, chunk, stride=2), :] = jnp.where(left, d, 0.0)
        wide_ref[pl.ds(at + 1, chunk, stride=2), :] = jnp.where(left, pltpu.roll(d, rank, 1), 0.0)
        down_a_ref[at : at + 2 * chunk, :] = wide_ref[at : at + 2 * chunk, :].astype(jnp.bfloat16)
    for start, b_ref in (
        (n_wide, gate_b_ref),
        (at_ub, up_b_ref),
        (at_da + n_unit, down_b_ref),
    ):
        tiles = b_ref.shape[1] // LANES
        count = rank * tiles
        wide_ref[:count, :] = flat_ref[start : start + count, :].astype(jnp.float32)
        for j in range(tiles):
            row = wide_ref[pl.ds(j, rank, stride=tiles), :]
            b_ref[:, j * LANES : (j + 1) * LANES] = row.astype(jnp.bfloat16)


def relayout_factors(flat, width, units, rank):
    shapes = [(width, 2 * rank), (rank, units), (rank, units), (units, 2 * rank), (rank, width)]
    return pl.pallas_call(
        relayout_kernel,
        out_shape=[jax.ShapeDtypeStruct(shape, jnp.bfloat16) for shape in shapes],
        scratch_shapes=[pltpu.VMEM((max(width, rank * width // LANES), LANES), jnp.float32)],
        compiler_params=pltpu.CompilerParams(vmem_limit_bytes=12 << 20),
        name="relayout_factors",
    )(flat)


def fill_rows(pieces, x_ref):
    rows, width = pieces[0].shape[0], x_ref.shape[1]
    for i, piece in enumerate(pieces):
        x_ref[i * rows : (i + 1) * rows, :] = piece[:, :width]


def base_kernel(count, *refs):
    pieces = refs[:count]
    w_gate_ref, w_up_ref, gate_ref, up_ref, x_ref = refs[count:]

    @pl.when(pl.program_id(0) == 0)
    def _():
        fill_rows(pieces, x_ref)

    gate_ref[...] = dot(x_ref[...], w_gate_ref[...])
    up_ref[...] = dot(x_ref[...], w_up_ref[...])


def base_products(pieces, w_gate, w_up):
    width, units = w_gate.shape
    total = sum(p.shape[0] for p in pieces)
    block = 256 if units % 256 == 0 else units
    out = jax.ShapeDtypeStruct((total, units), jnp.float32)
    return pl.pallas_call(
        functools.partial(base_kernel, len(pieces)),
        grid=(units // block,),
        out_shape=[out, out],
        in_specs=[pl.BlockSpec(p.shape, lambda i: (0, 0)) for p in pieces]
        + [pl.BlockSpec((width, block), lambda i: (0, i))] * 2,
        out_specs=[pl.BlockSpec((total, block), lambda i: (0, i))] * 2,
        scratch_shapes=[pltpu.VMEM((total, width), jnp.bfloat16)],
        compiler_params=pltpu.CompilerParams(vmem_limit_bytes=24 << 20),
        cost_estimate=pl.CostEstimate(
            flops=4 * total * width * units,
            bytes_accessed=4 * width * units + 2 * total * width + 8 * total * units,
            transcendentals=0,
        ),
        name="base_products",
    )(*pieces, w_gate, w_up)


def finish_kernel(count, me_ref, *refs):
    pieces = refs[:count]
    (gate_ref, up_ref, a_gu_ref, gate_b_ref, up_b_ref, down_a_ref, down_b_ref, w_down_ref) = refs[
        count : count + 8
    ]
    out_refs = refs[count + 8 : -4]
    x_ref, inner_ref, low_ref, mine_ref = refs[-4:]
    rank = gate_b_ref.shape[0]
    rows, width = pieces[0].shape[0], x_ref.shape[1]

    @pl.when(pl.program_id(0) == 0)
    def _():
        fill_rows(pieces, x_ref)
        for i, piece in enumerate(pieces):
            gates = piece[:, width:].astype(jnp.float32)
            lane = lax.broadcasted_iota(jnp.int32, gates.shape, 1)
            own = jnp.sum(jnp.where(lane == me_ref[0], gates, 0.0), axis=1, keepdims=True)
            mine_ref[i * rows : (i + 1) * rows, :] = jnp.broadcast_to(own, (rows, LANES))
        low = (adapter_scale * dot(x_ref[...], a_gu_ref[...])).astype(jnp.bfloat16)
        g = gate_ref[...] + dot(low[:, :rank], gate_b_ref[...])
        u = up_ref[...] + dot(low[:, rank:], up_b_ref[...])
        inner = (g / (1.0 + jnp.exp(-g)) * u).astype(jnp.bfloat16)
        inner_ref[...] = inner
        low_ref[...] = (adapter_scale * dot(inner, down_a_ref[...])).astype(jnp.bfloat16)

    out = dot(inner_ref[...], w_down_ref[...]) + dot(low_ref[:, :rank], down_b_ref[...])
    out = out * mine_ref[:, :1]
    at = 0
    for out_ref in out_refs:
        n = out_ref.shape[0]
        out_ref[...] = out[at : at + n].astype(out_ref.dtype)
        at += n


def finish_step(me, pieces, gate, up, low_rank, w_down, cores):
    units, width = w_down.shape
    total = gate.shape[0]
    block = 512 if width % 512 == 0 else width
    own = total // cores
    outs = [jax.ShapeDtypeStruct((own, width), jnp.float32)]
    if cores > 1:
        outs.append(jax.ShapeDtypeStruct((total - own, width), jnp.bfloat16))
    a_gu, gate_b, up_b, down_a, down_b = low_rank
    rank = down_b.shape[0]
    whole = [*pieces, gate, up, a_gu, gate_b, up_b, down_a]
    return pl.pallas_call(
        functools.partial(finish_kernel, len(pieces)),
        grid=(width // block,),
        out_shape=outs,
        in_specs=[pl.BlockSpec(memory_space=pltpu.SMEM)]
        + [pl.BlockSpec(a.shape, lambda i: (0, 0)) for a in whole]
        + [
            pl.BlockSpec((rank, block), lambda i: (0, i)),
            pl.BlockSpec((units, block), lambda i: (0, i)),
        ],
        out_specs=[pl.BlockSpec((o.shape[0], block), lambda i: (0, i)) for o in outs],
        scratch_shapes=[
            pltpu.VMEM((total, width), jnp.bfloat16),
            pltpu.VMEM((total, units), jnp.bfloat16),
            pltpu.VMEM((total, down_a.shape[1]), jnp.bfloat16),
            pltpu.VMEM((total, LANES), jnp.float32),
        ],
        compiler_params=pltpu.CompilerParams(vmem_limit_bytes=28 << 20),
        cost_estimate=pl.CostEstimate(
            flops=2 * total * units * (width + 4 * rank) + 4 * total * width * rank,
            bytes_accessed=2 * units * width + 8 * total * width + 8 * total * units,
            transcendentals=total * units,
        ),
        name="finish_step",
    )(me, *whole, down_b, w_down)


def dense_shards(
    hidden, route_ids, route_logits, placement, factors, w_gate, w_up, down_weight
):
    owners = lax.axis_size("expert")
    experts = placement.shape[0]
    steps, rows, width = hidden.shape
    units = w_gate.shape[2]
    rank = factors.shape[1] * owners // (3 * (width + units))
    cores = split_axis(owners)[2]

    payload = make_payload(hidden, route_ids, route_logits, experts)
    gathered = [gather_rows(payload[s], owners) for s in range(steps)]
    ordered = order_factors(placement, factors)
    received = lax.all_to_all(ordered, "expert", split_axis=0, concat_axis=0, tiled=True)
    base = [base_products(pieces, w_gate[0], w_up[0]) for pieces in gathered]
    low_rank = relayout_factors(received.reshape(-1, LANES), width, units, rank)
    me = lax.axis_index("expert").reshape(1)
    results = []
    for pieces, (gate, up) in zip(gathered, base):
        parts = finish_step(me, pieces, gate, up, low_rank, down_weight[0], cores)
        results.append(scatter_rows(parts[0], parts[-1], owners))
    return jnp.stack(results, axis=0)


def row_capacity(rows, top, experts):
    return min(rows, 3 * max(1, rows * top // experts))


def unpack_factors(flat_factors, width, hidden_units, rank_size):
    layouts = [
        (width, rank_size),
        (rank_size, hidden_units),
        (width, rank_size),
        (rank_size, hidden_units),
        (hidden_units, rank_size),
        (rank_size, width),
    ]
    offset = 0
    segments = []
    for leading, trailing in layouts:
        segments.append(
            flat_factors[offset : offset + leading * trailing].reshape(leading, trailing)
        )
        offset = offset + leading * trailing
    return segments


def merge_weight(loaded_weights, factor_a, factor_b):
    adapter_delta = jnp.dot(factor_a, factor_b, preferred_element_type=jnp.float32)
    return (loaded_weights.astype(jnp.float32) + adapter_scale * adapter_delta).astype(jnp.bfloat16)


def apply_expert_block(inputs, merged_gate, merged_up, combined_down_weight):
    gate_part = jnp.dot(inputs, merged_gate, preferred_element_type=jnp.float32)
    up_part = jnp.dot(inputs, merged_up, preferred_element_type=jnp.float32)
    inner = (jax.nn.silu(gate_part) * up_part).astype(jnp.bfloat16)
    return jnp.dot(inner, combined_down_weight, preferred_element_type=jnp.float32).astype(
        jnp.bfloat16
    )


def sparse_shards(hidden, route_ids, route_logits, placement, factors, w_gate, w_up, down_weight):
    owners = lax.axis_size("expert")
    experts = placement.shape[0]
    steps_count, row_count, width = hidden.shape
    top_count = route_ids.shape[2]
    hidden_units = w_gate.shape[2]
    rank_size = factors.shape[1] * owners // (3 * (width + hidden_units))
    capacity = row_capacity(row_count, top_count, experts)
    slot_of = (
        jnp.zeros((experts,), jnp.int32).at[placement].set(jnp.arange(experts, dtype=jnp.int32))
    )
    ordered = jnp.take(factors, slot_of, axis=0)
    received = lax.all_to_all(ordered, "expert", split_axis=0, concat_axis=1, tiled=True)
    segments = unpack_factors(received[0], width, hidden_units, rank_size)
    merged_gate = merge_weight(w_gate[0], segments[0], segments[1])
    merged_up = merge_weight(w_up[0], segments[2], segments[3])
    combined_down_weight = merge_weight(down_weight[0], segments[4], segments[5])

    def layout(step_index):
        ids_flat = route_ids[step_index].reshape(-1)
        onehot = (ids_flat[:, None] == jnp.arange(experts, dtype=jnp.int32)[None, :]).astype(
            jnp.int32
        )
        position = jnp.sum((jnp.cumsum(onehot, axis=0) - 1) * onehot, axis=1)
        target = ids_flat * capacity + position
        placed = (
            jnp.arange(experts * capacity, dtype=jnp.int32)[:, None] == target[None, :]
        ).astype(jnp.bfloat16)
        pair_rows = jnp.repeat(hidden[step_index], top_count, axis=0)
        outgoing = jnp.dot(placed, pair_rows, preferred_element_type=jnp.float32).astype(
            jnp.bfloat16
        )
        outgoing = outgoing.reshape(experts, 1, capacity, width)
        gates = route_gates(route_logits[step_index]).reshape(-1)
        weighted = placed * gates[None, :]
        return (outgoing, weighted)

    layouts_all = [layout(step_index) for step_index in range(steps_count)]
    results = []
    for step_index in range(steps_count):
        outgoing, weighted = layouts_all[step_index]
        arrived = lax.all_to_all(outgoing, "expert", split_axis=0, concat_axis=1, tiled=True)
        outputs = apply_expert_block(
            arrived.reshape(-1, width), merged_gate, merged_up, combined_down_weight
        )
        outputs = outputs.reshape(arrived.shape)
        returned = lax.all_to_all(outputs, "expert", split_axis=1, concat_axis=0, tiled=True)
        flat_back = returned.reshape(experts * capacity, width)
        pair_out = jnp.einsum("cp,cd->pd", weighted, flat_back, preferred_element_type=jnp.float32)
        results.append(
            pair_out.reshape(row_count, top_count, width).sum(axis=1).astype(jnp.bfloat16)
        )
    return jnp.stack(results, axis=0)


def shards(hidden, route_ids, *rest):
    rows, top = route_ids.shape[1:]
    experts = rest[1].shape[0]
    every = row_capacity(rows, top, experts) == rows
    return (dense_shards if every else sparse_shards)(hidden, route_ids, *rest)


def solution(mesh):
    placed = (
        P(None, ("group", "expert"), None),
        P(None, ("group", "expert"), None),
        P(None, ("group", "expert"), None),
        P(),
        P(None, "expert"),
        P("expert", None, None),
        P("expert", None, None),
        P("expert", None, None),
    )
    return jax.shard_map(
        shards,
        mesh=mesh,
        in_specs=placed,
        out_specs=P(None, ("group", "expert"), None),
        check_vma=False,
    )
```

```python
import functools

import jax
import jax.numpy as jnp
from jax import lax
from jax.experimental import pallas as pl
from jax.experimental.pallas import tpu as pltpu
from jax.sharding import PartitionSpec as P

adapter_scale = 2.0
LANES = 128
GRANT = 60 << 20


def route_gates(logits):
    highest = jnp.max(logits, axis=-1, keepdims=True)
    router_scores = jnp.exp(logits - highest)
    return (router_scores / jnp.sum(router_scores, axis=-1, keepdims=True)).astype(jnp.bfloat16)


def split_axis(n):
    cores = 2 if n % 2 == 0 else 1
    chips = n // cores
    middle = 1
    while chips % (2 * middle) == 0 and 4 * middle * middle <= chips:
        middle *= 2
    return chips // middle, middle, cores


def shift(x, n, stride, size, k):
    pairs = []
    for i in range(n):
        place = i // stride % size
        pairs.append((i, i + ((place + k) % size - place) * stride))
    return lax.ppermute(x, "expert", pairs)


def gather_rows(x, n):
    outer, middle, cores = split_axis(n)
    column = [x] + [shift(x, n, middle * cores, outer, k) for k in range(1, outer)]
    column = jnp.stack(column).reshape(-1, x.shape[1])
    sheet = [column] + [shift(column, n, cores, middle, k) for k in range(1, middle)]
    return sheet + [shift(p, n, 1, cores, k) for k in range(1, cores) for p in sheet]


def scatter_rows(parts, n):
    outer, middle, cores = split_axis(n)
    results, before = [], None
    for kept, sent in parts:
        count = kept.shape[0] // middle
        kept = kept + shift(sent, n, 1, cores, 1).astype(jnp.float32)
        away = kept[count:].astype(jnp.bfloat16)
        if before is not None:
            away, before = lax.optimization_barrier((away, before))
            results[-1] = before
        total = kept[:count]
        for k in range(1, middle):
            part = away[(k - 1) * count : k * count]
            total = total + shift(part, n, cores, middle, middle - k).astype(jnp.float32)
        results.append(total)
        before = total
    finals = []
    for kept in results:
        count = kept.shape[0] // outer
        total = kept[:count]
        for k in range(1, outer):
            part = kept[k * count : (k + 1) * count].astype(jnp.bfloat16)
            total = total + shift(part, n, middle * cores, outer, outer - k).astype(jnp.float32)
        finals.append(total.astype(jnp.bfloat16))
    return finals


def exchange_factors(blocks, n):
    outer, middle, cores = split_axis(n)
    stride = middle * cores
    turned = [blocks[0]] + [shift(blocks[r], n, cores, middle, r) for r in range(1, middle)]
    here, there = [], []
    for q in range(outer):
        pairs = []
        for g in range(2):
            for i in range(n):
                place = i // stride
                to = (i + ((place + q) % outer - place) * stride) ^ g
                pairs.append((g * n + i, g * n + to))
        part = jnp.stack([t[q] for t in turned])
        part = lax.ppermute(part, ("group", "expert"), pairs)
        here.append(part)
        there.append(lax.ppermute(part, "group", [(0, 1), (1, 0)]))
    return here, there


def dot(a, b):
    return jnp.dot(a, b, preferred_element_type=jnp.float32)


def payload_kernel(hidden_ref, ids_ref, logits_ref, *refs):
    out_refs, turned_ref = refs[:-1], refs[-1]
    steps, top, rows = ids_ref.shape
    width = hidden_ref.shape[2]
    turned_ref[...] = jnp.zeros_like(turned_ref)
    for s in range(steps):
        logits, ids = logits_ref[s], ids_ref[s]
        scores = jnp.exp(logits - jnp.max(logits, axis=0, keepdims=True))
        gates = scores / jnp.sum(scores, axis=0, keepdims=True)
        expert = lax.broadcasted_iota(jnp.int32, (turned_ref.shape[0], rows), 0)
        dense = jnp.zeros(expert.shape, jnp.float32)
        for k in range(top):
            dense += jnp.where(ids[k : k + 1, :] == expert, gates[k : k + 1, :], 0.0)
        turned_ref[:, s * rows : (s + 1) * rows] = dense
    dense = turned_ref[...].T.astype(jnp.bfloat16)
    for s, out_ref in enumerate(out_refs):
        out_ref[:, :width] = hidden_ref[s]
        out_ref[:, width:] = dense[s * rows : (s + 1) * rows, :]


def make_payload(hidden, route_ids, route_logits, experts):
    steps, rows, width = hidden.shape
    padded = -(-experts // LANES) * LANES
    shape = jax.ShapeDtypeStruct((rows, width + padded), jnp.bfloat16)
    return pl.pallas_call(
        payload_kernel,
        out_shape=[shape] * steps,
        scratch_shapes=[pltpu.VMEM((padded, -(-steps * rows // LANES) * LANES), jnp.float32)],
        compiler_params=pltpu.CompilerParams(vmem_limit_bytes=GRANT),
        name="payload",
    )(hidden, jnp.swapaxes(route_ids, 1, 2), jnp.swapaxes(route_logits, 1, 2))


def order_kernel(outer, middle, place_ref, placement_ref, factors_ref, *refs):
    out_refs, wide_ref = refs[:-1], refs[-1]
    slots = factors_ref.shape[0]
    length, lanes = out_refs[0].shape[1:]
    group, me = place_ref[0], place_ref[1]

    def cut(t, carry):
        start = pl.multiple_of(t * lanes, lanes)
        tile = factors_ref[:, pl.ds(start, lanes)].astype(jnp.float32)
        wide_ref[pl.ds(t, slots, stride=length), :] = tile
        return carry

    lax.fori_loop(0, length, cut, 0, unroll=8)

    def put(s, carry):
        to = placement_ref[s]
        aside = lax.rem(to // 2 + middle - lax.rem(me // 2, middle), middle)
        ahead = lax.rem(to // (2 * middle) + outer - me // (2 * middle), outer)
        ours = lax.rem(to + me + group, 2) == 0
        rows = wide_ref[pl.ds(pl.multiple_of(s * length, 8), length), :].astype(jnp.bfloat16)
        for r, out_ref in enumerate(out_refs):

            @pl.when(jnp.logical_and(ours, aside == r))
            def _():
                out_ref[ahead] = rows

        return carry

    lax.fori_loop(0, slots, put, 0)


def order_factors(place, placement, factors, n):
    outer, middle, _ = split_axis(n)
    slots, entries = factors.shape
    length = entries // LANES
    return pl.pallas_call(
        functools.partial(order_kernel, outer, middle),
        out_shape=[jax.ShapeDtypeStruct((outer, length, LANES), jnp.bfloat16)] * middle,
        in_specs=[
            pl.BlockSpec(memory_space=pltpu.SMEM),
            pl.BlockSpec(memory_space=pltpu.SMEM),
            pl.BlockSpec(memory_space=pltpu.VMEM),
        ],
        scratch_shapes=[pltpu.VMEM((slots * length, LANES), jnp.float32)],
        compiler_params=pltpu.CompilerParams(vmem_limit_bytes=GRANT),
        name="order_factors",
    )(place, placement, factors)


def relayout_kernel(outer, middle, place_ref, *refs):
    pieces = refs[: 2 * outer]
    a_gu_ref, gate_b_ref, up_b_ref, down_a_ref, down_b_ref, flat_ref, wide_ref = refs[2 * outer :]
    width, units = a_gu_ref.shape[0], gate_b_ref.shape[1]
    rank = gate_b_ref.shape[0]
    length = pieces[0].shape[1]
    group, me = place_ref[0], place_ref[1]
    for i, piece in enumerate(pieces):
        swapped, q = i // outer, i % outer
        core = lax.rem(me + group + swapped, 2)
        for r in range(middle):
            row = lax.rem(me // 2 + middle - r, middle)
            column = lax.rem(me // (2 * middle) + outer - q, outer)
            source = (column * middle + row) * 2 + core
            start = pl.multiple_of(source * length, 8)
            flat_ref[pl.ds(start, length), :] = piece[r].astype(jnp.float32)

    n_wide, n_unit = width // 2, units // 2
    at_ub = 2 * n_wide + n_unit
    at_da = 2 * n_wide + 2 * n_unit
    chunk = 128
    left = lax.broadcasted_iota(jnp.int32, (chunk, LANES), 1) < rank

    def load(start):
        return flat_ref[pl.ds(pl.multiple_of(start, 128), chunk), :]

    def gate_up(i, carry):
        g, u = load(i * chunk), load(n_wide + n_unit + i * chunk)
        at = 2 * i * chunk
        wide_ref[pl.ds(at, chunk, stride=2), :] = jnp.where(left, g, pltpu.roll(u, rank, 1))
        wide_ref[pl.ds(at + 1, chunk, stride=2), :] = jnp.where(left, pltpu.roll(g, rank, 1), u)
        both = wide_ref[pl.ds(pl.multiple_of(at, 128), 2 * chunk), :]
        a_gu_ref[pl.ds(pl.multiple_of(at, 128), 2 * chunk), :] = both.astype(jnp.bfloat16)
        return carry

    lax.fori_loop(0, n_wide // chunk, gate_up, 0, unroll=2)
    for i in range(n_unit // chunk):
        d = load(at_da + i * chunk)
        at = 2 * i * chunk
        wide_ref[pl.ds(at, chunk, stride=2), :] = jnp.where(left, d, 0.0)
        wide_ref[pl.ds(at + 1, chunk, stride=2), :] = jnp.where(left, pltpu.roll(d, rank, 1), 0.0)
        down_a_ref[at : at + 2 * chunk, :] = wide_ref[at : at + 2 * chunk, :].astype(jnp.bfloat16)
    for start, b_ref in (
        (n_wide, gate_b_ref),
        (at_ub, up_b_ref),
        (at_da + n_unit, down_b_ref),
    ):
        tiles = b_ref.shape[1] // LANES
        for j in range(tiles):
            row = flat_ref[pl.ds(start + j, rank, stride=tiles), :]
            b_ref[:, j * LANES : (j + 1) * LANES] = row.astype(jnp.bfloat16)


def relayout_factors(place, here, there, width, units, rank, n):
    outer, middle, _ = split_axis(n)
    shapes = [(width, 2 * rank), (rank, units), (rank, units), (units, 2 * rank), (rank, width)]
    length = here[0].shape[1]
    return pl.pallas_call(
        functools.partial(relayout_kernel, outer, middle),
        out_shape=[jax.ShapeDtypeStruct(shape, jnp.bfloat16) for shape in shapes],
        in_specs=[pl.BlockSpec(memory_space=pltpu.SMEM)]
        + [pl.BlockSpec(memory_space=pltpu.VMEM)] * (2 * outer),
        scratch_shapes=[
            pltpu.VMEM((n * length, LANES), jnp.float32),
            pltpu.VMEM((width, LANES), jnp.float32),
        ],
        compiler_params=pltpu.CompilerParams(vmem_limit_bytes=GRANT),
        name="relayout_factors",
    )(place, *here, *there)


def fill_rows(pieces, x_ref):
    rows, width = pieces[0].shape[0], x_ref.shape[1]
    for i, piece in enumerate(pieces):
        x_ref[i * rows : (i + 1) * rows, :] = piece[:, :width]


def base_kernel(count, *refs):
    pieces = refs[:count]
    w_gate_ref, w_up_ref, gate_ref, up_ref, x_ref = refs[count:]

    @pl.when(pl.program_id(0) == 0)
    def _():
        fill_rows(pieces, x_ref)

    gate_ref[...] = dot(x_ref[...], w_gate_ref[...])
    up_ref[...] = dot(x_ref[...], w_up_ref[...])


def base_products(pieces, w_gate, w_up):
    width, units = w_gate.shape
    total = sum(p.shape[0] for p in pieces)
    block = 256 if units % 256 == 0 else units
    out = jax.ShapeDtypeStruct((total, units), jnp.float32)
    return pl.pallas_call(
        functools.partial(base_kernel, len(pieces)),
        grid=(units // block,),
        out_shape=[out, out],
        in_specs=[pl.BlockSpec(p.shape, lambda i: (0, 0)) for p in pieces]
        + [pl.BlockSpec((width, block), lambda i: (0, i))] * 2,
        out_specs=[pl.BlockSpec((total, block), lambda i: (0, i))] * 2,
        scratch_shapes=[pltpu.VMEM((total, width), jnp.bfloat16)],
        compiler_params=pltpu.CompilerParams(vmem_limit_bytes=GRANT),
        cost_estimate=pl.CostEstimate(
            flops=4 * total * width * units,
            bytes_accessed=4 * width * units + 2 * total * width + 8 * total * units,
            transcendentals=0,
        ),
        name="base_products",
    )(*pieces, w_gate, w_up)


def finish_kernel(count, place_ref, *refs):
    pieces = refs[:count]
    (gate_ref, up_ref, a_gu_ref, gate_b_ref, up_b_ref, down_a_ref, down_b_ref, w_down_ref) = refs[
        count : count + 8
    ]
    out_refs = refs[count + 8 : -4]
    x_ref, inner_ref, low_ref, mine_ref = refs[-4:]
    rank = gate_b_ref.shape[0]
    rows, width = pieces[0].shape[0], x_ref.shape[1]

    @pl.when(pl.program_id(0) == 0)
    def _():
        fill_rows(pieces, x_ref)
        for i, piece in enumerate(pieces):
            gates = piece[:, width:].astype(jnp.float32)
            lane = lax.broadcasted_iota(jnp.int32, gates.shape, 1)
            own = jnp.sum(jnp.where(lane == place_ref[1], gates, 0.0), axis=1, keepdims=True)
            mine_ref[i * rows : (i + 1) * rows, :] = jnp.broadcast_to(own, (rows, LANES))
        low = (adapter_scale * dot(x_ref[...], a_gu_ref[...])).astype(jnp.bfloat16)
        g = gate_ref[...] + dot(low[:, :rank], gate_b_ref[...])
        u = up_ref[...] + dot(low[:, rank:], up_b_ref[...])
        inner = (g / (1.0 + jnp.exp(-g)) * u).astype(jnp.bfloat16)
        inner_ref[...] = inner
        low_ref[...] = (adapter_scale * dot(inner, down_a_ref[...])).astype(jnp.bfloat16)

    out = dot(inner_ref[...], w_down_ref[...]) + dot(low_ref[:, :rank], down_b_ref[...])
    out = out * mine_ref[:, :1]
    at = 0
    for out_ref in out_refs:
        n = out_ref.shape[0]
        out_ref[...] = out[at : at + n].astype(out_ref.dtype)
        at += n


def finish_step(place, pieces, gate, up, low_rank, w_down, cores):
    units, width = w_down.shape
    total = gate.shape[0]
    block = 512 if width % 512 == 0 else width
    own = total // cores
    outs = [jax.ShapeDtypeStruct((own, width), jnp.float32)]
    if cores > 1:
        outs.append(jax.ShapeDtypeStruct((total - own, width), jnp.bfloat16))
    a_gu, gate_b, up_b, down_a, down_b = low_rank
    rank = down_b.shape[0]
    whole = [*pieces, gate, up, a_gu, gate_b, up_b, down_a]
    return pl.pallas_call(
        functools.partial(finish_kernel, len(pieces)),
        grid=(width // block,),
        out_shape=outs,
        in_specs=[pl.BlockSpec(memory_space=pltpu.SMEM)]
        + [pl.BlockSpec(a.shape, lambda i: (0, 0)) for a in whole]
        + [
            pl.BlockSpec((rank, block), lambda i: (0, i)),
            pl.BlockSpec((units, block), lambda i: (0, i)),
        ],
        out_specs=[pl.BlockSpec((o.shape[0], block), lambda i: (0, i)) for o in outs],
        scratch_shapes=[
            pltpu.VMEM((total, width), jnp.bfloat16),
            pltpu.VMEM((total, units), jnp.bfloat16),
            pltpu.VMEM((total, down_a.shape[1]), jnp.bfloat16),
            pltpu.VMEM((total, LANES), jnp.float32),
        ],
        compiler_params=pltpu.CompilerParams(vmem_limit_bytes=GRANT),
        cost_estimate=pl.CostEstimate(
            flops=2 * total * units * (width + 4 * rank) + 4 * total * width * rank,
            bytes_accessed=2 * units * width + 8 * total * width + 8 * total * units,
            transcendentals=total * units,
        ),
        name="finish_step",
    )(place, *whole, down_b, w_down)


def dense_shards(
    hidden, route_ids, route_logits, placement, factors, w_gate, w_up, down_weight
):
    owners = lax.axis_size("expert")
    experts = placement.shape[0]
    steps, rows, width = hidden.shape
    units = w_gate.shape[2]
    rank = factors.shape[1] * owners // (3 * (width + units))
    cores = split_axis(owners)[2]
    place = jnp.stack([lax.axis_index("group"), lax.axis_index("expert")]).astype(jnp.int32)

    payload = make_payload(hidden, route_ids, route_logits, experts)
    blocks = order_factors(place, placement, factors, owners)
    gathered = [gather_rows(payload[s], owners) for s in range(steps)]
    here, there = exchange_factors(blocks, owners)
    base = [base_products(pieces, w_gate[0], w_up[0]) for pieces in gathered]
    here, there, base = lax.optimization_barrier((here, there, base))
    low_rank = relayout_factors(place, here, there, width, units, rank, owners)
    parts = [
        finish_step(place, pieces, gate, up, low_rank, down_weight[0], cores)
        for pieces, (gate, up) in zip(gathered, base)
    ]
    return jnp.stack(scatter_rows(parts, owners), axis=0)


def row_capacity(rows, top, experts):
    return min(rows, 3 * max(1, rows * top // experts))


def unpack_factors(flat_factors, width, hidden_units, rank_size):
    layouts = [
        (width, rank_size),
        (rank_size, hidden_units),
        (width, rank_size),
        (rank_size, hidden_units),
        (hidden_units, rank_size),
        (rank_size, width),
    ]
    offset = 0
    segments = []
    for leading, trailing in layouts:
        segments.append(
            flat_factors[offset : offset + leading * trailing].reshape(leading, trailing)
        )
        offset = offset + leading * trailing
    return segments


def merge_weight(loaded_weights, factor_a, factor_b):
    adapter_delta = jnp.dot(factor_a, factor_b, preferred_element_type=jnp.float32)
    return (loaded_weights.astype(jnp.float32) + adapter_scale * adapter_delta).astype(jnp.bfloat16)


def apply_expert_block(inputs, merged_gate, merged_up, combined_down_weight):
    gate_part = jnp.dot(inputs, merged_gate, preferred_element_type=jnp.float32)
    up_part = jnp.dot(inputs, merged_up, preferred_element_type=jnp.float32)
    inner = (jax.nn.silu(gate_part) * up_part).astype(jnp.bfloat16)
    return jnp.dot(inner, combined_down_weight, preferred_element_type=jnp.float32).astype(
        jnp.bfloat16
    )


def sparse_shards(hidden, route_ids, route_logits, placement, factors, w_gate, w_up, down_weight):
    owners = lax.axis_size("expert")
    experts = placement.shape[0]
    steps_count, row_count, width = hidden.shape
    top_count = route_ids.shape[2]
    hidden_units = w_gate.shape[2]
    rank_size = factors.shape[1] * owners // (3 * (width + hidden_units))
    capacity = row_capacity(row_count, top_count, experts)
    slot_of = (
        jnp.zeros((experts,), jnp.int32).at[placement].set(jnp.arange(experts, dtype=jnp.int32))
    )
    ordered = jnp.take(factors, slot_of, axis=0)
    received = lax.all_to_all(ordered, "expert", split_axis=0, concat_axis=1, tiled=True)
    segments = unpack_factors(received[0], width, hidden_units, rank_size)
    merged_gate = merge_weight(w_gate[0], segments[0], segments[1])
    merged_up = merge_weight(w_up[0], segments[2], segments[3])
    combined_down_weight = merge_weight(down_weight[0], segments[4], segments[5])

    def layout(step_index):
        ids_flat = route_ids[step_index].reshape(-1)
        onehot = (ids_flat[:, None] == jnp.arange(experts, dtype=jnp.int32)[None, :]).astype(
            jnp.int32
        )
        position = jnp.sum((jnp.cumsum(onehot, axis=0) - 1) * onehot, axis=1)
        target = ids_flat * capacity + position
        placed = (
            jnp.arange(experts * capacity, dtype=jnp.int32)[:, None] == target[None, :]
        ).astype(jnp.bfloat16)
        pair_rows = jnp.repeat(hidden[step_index], top_count, axis=0)
        outgoing = jnp.dot(placed, pair_rows, preferred_element_type=jnp.float32).astype(
            jnp.bfloat16
        )
        outgoing = outgoing.reshape(experts, 1, capacity, width)
        gates = route_gates(route_logits[step_index]).reshape(-1)
        weighted = placed * gates[None, :]
        return (outgoing, weighted)

    layouts_all = [layout(step_index) for step_index in range(steps_count)]
    results = []
    for step_index in range(steps_count):
        outgoing, weighted = layouts_all[step_index]
        arrived = lax.all_to_all(outgoing, "expert", split_axis=0, concat_axis=1, tiled=True)
        outputs = apply_expert_block(
            arrived.reshape(-1, width), merged_gate, merged_up, combined_down_weight
        )
        outputs = outputs.reshape(arrived.shape)
        returned = lax.all_to_all(outputs, "expert", split_axis=1, concat_axis=0, tiled=True)
        flat_back = returned.reshape(experts * capacity, width)
        pair_out = jnp.einsum("cp,cd->pd", weighted, flat_back, preferred_element_type=jnp.float32)
        results.append(
            pair_out.reshape(row_count, top_count, width).sum(axis=1).astype(jnp.bfloat16)
        )
    return jnp.stack(results, axis=0)


def shards(hidden, route_ids, route_logits, placement, factors, w_gate, w_up, down_weight):
    rows, top = route_ids.shape[1:]
    width, units = w_gate.shape[1:]
    owners = lax.axis_size("expert")
    rank = factors.shape[1] * owners // (3 * (width + units))
    dense = row_capacity(rows, top, placement.shape[0]) == rows
    dense = dense and lax.axis_size("group") == 2 and split_axis(owners)[2] == 2
    dense = dense and 2 * rank == LANES and width % 256 == 0 and units % 256 == 0
    dense = dense and factors.shape[1] % (8 * LANES) == 0
    return (dense_shards if dense else sparse_shards)(
        hidden, route_ids, route_logits, placement, factors, w_gate, w_up, down_weight
    )


def solution(mesh):
    placed = (
        P(None, ("group", "expert"), None),
        P(None, ("group", "expert"), None),
        P(None, ("group", "expert"), None),
        P(),
        P(None, "expert"),
        P("expert", None, None),
        P("expert", None, None),
        P("expert", None, None),
    )
    return jax.shard_map(
        shards,
        mesh=mesh,
        in_specs=placed,
        out_specs=P(None, ("group", "expert"), None),
        check_vma=False,
    )
```

```python
import functools

import jax
import jax.numpy as jnp
from jax import lax
from jax.experimental import pallas as pl
from jax.experimental.pallas import tpu as pltpu
from jax.sharding import PartitionSpec as P

adapter_scale = 2.0
LANES = 128
GRANT = 60 << 20


def route_gates(logits):
    highest = jnp.max(logits, axis=-1, keepdims=True)
    router_scores = jnp.exp(logits - highest)
    return (router_scores / jnp.sum(router_scores, axis=-1, keepdims=True)).astype(jnp.bfloat16)


def split_axis(n):
    cores = 2 if n % 2 == 0 else 1
    chips = n // cores
    middle = 1
    while chips % (2 * middle) == 0 and 4 * middle * middle <= chips:
        middle *= 2
    return chips // middle, middle, cores


def shift(x, n, stride, size, k):
    pairs = []
    for i in range(n):
        place = i // stride % size
        pairs.append((i, i + ((place + k) % size - place) * stride))
    return lax.ppermute(x, "expert", pairs)


def stack_rows(pieces):
    return jnp.stack(pieces).reshape(-1, pieces[0].shape[1])


def gather_along(x, n, stride, size):
    return stack_rows([x] + [shift(x, n, stride, size, k) for k in range(1, size)])


def scatter_along(total, n, stride, size):
    count = total.shape[0] // size
    result = total[:count]
    for k in range(1, size):
        part = total[k * count : (k + 1) * count].astype(jnp.bfloat16)
        result = result + shift(part, n, stride, size, size - k).astype(jnp.float32)
    return result


def exchange_factors(blocks, n):
    outer, middle, cores = split_axis(n)
    stride = middle * cores
    turned = [blocks[0]] + [shift(blocks[r], n, cores, middle, r) for r in range(1, middle)]
    here, there = [], []
    for q in range(outer):
        pairs = []
        for g in range(2):
            for i in range(n):
                place = i // stride
                to = (i + ((place + q) % outer - place) * stride) ^ g
                pairs.append((g * n + i, g * n + to))
        part = jnp.stack([t[q] for t in turned])
        part = lax.ppermute(part, ("group", "expert"), pairs)
        here.append(part)
        there.append(lax.ppermute(part, "group", [(0, 1), (1, 0)]))
    return here, there


def dot(a, b):
    return jnp.dot(a, b, preferred_element_type=jnp.float32)


def payload_kernel(hidden_ref, ids_ref, logits_ref, *refs):
    out_refs, turned_ref = refs[:-1], refs[-1]
    steps, top, rows = ids_ref.shape
    width = hidden_ref.shape[2]
    turned_ref[...] = jnp.zeros_like(turned_ref)
    for s in range(steps):
        logits, ids = logits_ref[s], ids_ref[s]
        scores = jnp.exp(logits - jnp.max(logits, axis=0, keepdims=True))
        gates = scores / jnp.sum(scores, axis=0, keepdims=True)
        expert = lax.broadcasted_iota(jnp.int32, (turned_ref.shape[0], rows), 0)
        dense = jnp.zeros(expert.shape, jnp.float32)
        for k in range(top):
            dense += jnp.where(ids[k : k + 1, :] == expert, gates[k : k + 1, :], 0.0)
        turned_ref[:, s * rows : (s + 1) * rows] = dense
    dense = turned_ref[...].T.astype(jnp.bfloat16)
    s = 0
    for out_ref in out_refs:
        for at in range(0, out_ref.shape[0], rows):
            out_ref[at : at + rows, :width] = hidden_ref[s]
            out_ref[at : at + rows, width:] = dense[s * rows : (s + 1) * rows, :]
            s += 1


def make_payload(hidden, route_ids, route_logits, experts, first):
    steps, rows, width = hidden.shape
    padded = -(-experts // LANES) * LANES
    return pl.pallas_call(
        payload_kernel,
        out_shape=[
            jax.ShapeDtypeStruct((count * rows, width + padded), jnp.bfloat16)
            for count in (first, steps - first)
        ],
        scratch_shapes=[pltpu.VMEM((padded, -(-steps * rows // LANES) * LANES), jnp.float32)],
        compiler_params=pltpu.CompilerParams(vmem_limit_bytes=GRANT),
        name="payload",
    )(hidden, jnp.swapaxes(route_ids, 1, 2), jnp.swapaxes(route_logits, 1, 2))


def order_kernel(outer, middle, place_ref, placement_ref, factors_ref, *refs):
    out_refs, wide_ref = refs[:-1], refs[-1]
    slots = factors_ref.shape[0]
    length, lanes = out_refs[0].shape[1:]
    group, me = place_ref[0], place_ref[1]

    def cut(t, carry):
        start = pl.multiple_of(t * lanes, lanes)
        tile = factors_ref[:, pl.ds(start, lanes)].astype(jnp.float32)
        wide_ref[pl.ds(t, slots, stride=length), :] = tile
        return carry

    lax.fori_loop(0, length, cut, 0, unroll=8)

    def put(s, carry):
        to = placement_ref[s]
        aside = lax.rem(to // 2 + middle - lax.rem(me // 2, middle), middle)
        ahead = lax.rem(to // (2 * middle) + outer - me // (2 * middle), outer)
        ours = lax.rem(to + me + group, 2) == 0
        rows = wide_ref[pl.ds(pl.multiple_of(s * length, 8), length), :].astype(jnp.bfloat16)
        for r, out_ref in enumerate(out_refs):

            @pl.when(jnp.logical_and(ours, aside == r))
            def _():
                out_ref[ahead] = rows

        return carry

    lax.fori_loop(0, slots, put, 0)


def order_factors(place, placement, factors, n):
    outer, middle, _ = split_axis(n)
    slots, entries = factors.shape
    length = entries // LANES
    return pl.pallas_call(
        functools.partial(order_kernel, outer, middle),
        out_shape=[jax.ShapeDtypeStruct((outer, length, LANES), jnp.bfloat16)] * middle,
        in_specs=[
            pl.BlockSpec(memory_space=pltpu.SMEM),
            pl.BlockSpec(memory_space=pltpu.SMEM),
            pl.BlockSpec(memory_space=pltpu.VMEM),
        ],
        scratch_shapes=[pltpu.VMEM((slots * length, LANES), jnp.float32)],
        compiler_params=pltpu.CompilerParams(vmem_limit_bytes=GRANT),
        name="order_factors",
    )(place, placement, factors)


def relayout_kernel(outer, middle, place_ref, *refs):
    pieces = refs[: 2 * outer]
    a_gu_ref, gate_b_ref, up_b_ref, down_a_ref, down_b_ref, flat_ref, wide_ref = refs[2 * outer :]
    width, units = a_gu_ref.shape[0], gate_b_ref.shape[1]
    rank = gate_b_ref.shape[0]
    length = pieces[0].shape[1]
    group, me = place_ref[0], place_ref[1]
    for i, piece in enumerate(pieces):
        swapped, q = i // outer, i % outer
        core = lax.rem(me + group + swapped, 2)
        for r in range(middle):
            row = lax.rem(me // 2 + middle - r, middle)
            column = lax.rem(me // (2 * middle) + outer - q, outer)
            source = (column * middle + row) * 2 + core
            start = pl.multiple_of(source * length, 8)
            flat_ref[pl.ds(start, length), :] = piece[r].astype(jnp.float32)

    n_wide, n_unit = width // 2, units // 2
    at_ub = 2 * n_wide + n_unit
    at_da = 2 * n_wide + 2 * n_unit
    chunk = 128
    left = lax.broadcasted_iota(jnp.int32, (chunk, LANES), 1) < rank

    def load(start):
        return flat_ref[pl.ds(pl.multiple_of(start, 128), chunk), :]

    def gate_up(i, carry):
        g, u = load(i * chunk), load(n_wide + n_unit + i * chunk)
        at = 2 * i * chunk
        wide_ref[pl.ds(at, chunk, stride=2), :] = jnp.where(left, g, pltpu.roll(u, rank, 1))
        wide_ref[pl.ds(at + 1, chunk, stride=2), :] = jnp.where(left, pltpu.roll(g, rank, 1), u)
        both = wide_ref[pl.ds(pl.multiple_of(at, 128), 2 * chunk), :]
        a_gu_ref[pl.ds(pl.multiple_of(at, 128), 2 * chunk), :] = both.astype(jnp.bfloat16)
        return carry

    lax.fori_loop(0, n_wide // chunk, gate_up, 0, unroll=2)
    for i in range(n_unit // chunk):
        d = load(at_da + i * chunk)
        at = 2 * i * chunk
        wide_ref[pl.ds(at, chunk, stride=2), :] = jnp.where(left, d, 0.0)
        wide_ref[pl.ds(at + 1, chunk, stride=2), :] = jnp.where(left, pltpu.roll(d, rank, 1), 0.0)
        down_a_ref[at : at + 2 * chunk, :] = wide_ref[at : at + 2 * chunk, :].astype(jnp.bfloat16)
    for start, b_ref in (
        (n_wide, gate_b_ref),
        (at_ub, up_b_ref),
        (at_da + n_unit, down_b_ref),
    ):
        tiles = b_ref.shape[1] // LANES
        for j in range(tiles):
            row = flat_ref[pl.ds(start + j, rank, stride=tiles), :]
            b_ref[:, j * LANES : (j + 1) * LANES] = row.astype(jnp.bfloat16)


def relayout_factors(place, here, there, width, units, rank, n):
    outer, middle, _ = split_axis(n)
    shapes = [(width, 2 * rank), (rank, units), (rank, units), (units, 2 * rank), (rank, width)]
    length = here[0].shape[1]
    return pl.pallas_call(
        functools.partial(relayout_kernel, outer, middle),
        out_shape=[jax.ShapeDtypeStruct(shape, jnp.bfloat16) for shape in shapes],
        in_specs=[pl.BlockSpec(memory_space=pltpu.SMEM)]
        + [pl.BlockSpec(memory_space=pltpu.VMEM)] * (2 * outer),
        scratch_shapes=[
            pltpu.VMEM((n * length, LANES), jnp.float32),
            pltpu.VMEM((width, LANES), jnp.float32),
        ],
        compiler_params=pltpu.CompilerParams(vmem_limit_bytes=GRANT),
        name="relayout_factors",
    )(place, *here, *there)


def expert_kernel(count, place_ref, *refs):
    pieces, refs = refs[:count], refs[count:]
    a_gu_hbm, gate_b_hbm, up_b_hbm, down_a_hbm, down_b_hbm = refs[:5]
    w_gate_hbm, w_up_hbm, w_down_hbm, kept_hbm, sent_hbm = refs[5:10]
    x_ref, a_gu_ref, gate_b_ref, up_b_ref, down_a_ref, down_b_ref = refs[10:16]
    w_gate_ref, w_up_ref, w_down_ref, inner_ref, kept_ref, sent_ref, sem, out_sem = refs[16:]
    rows = pieces[0].shape[0]
    units, width = w_down_ref.shape
    rank = gate_b_ref.shape[0]
    own = kept_ref.shape[0]
    begun = []

    def begin(src, dst):
        copy = pltpu.make_async_copy(src, dst, sem.at[len(begun)])
        copy.start()
        begun.append(copy)
        return copy

    def blocks(length, block):
        return [slice(at, at + block) for at in range(0, length, block)]

    x_in = [begin(p, x_ref.at[pl.ds(i * rows, rows)]) for i, p in enumerate(pieces)]
    x_in.append(begin(a_gu_hbm, a_gu_ref))
    b_in = [begin(gate_b_hbm, gate_b_ref), begin(up_b_hbm, up_b_ref)]
    unit_cuts, width_cuts = blocks(units, 256), blocks(width, 512 if width % 512 == 0 else 256)
    gu_in = [
        (
            begin(w_gate_hbm.at[:, cut], w_gate_ref.at[:, cut]),
            begin(w_up_hbm.at[:, cut], w_up_ref.at[:, cut]),
        )
        for cut in unit_cuts
    ]
    d_in = [begin(down_a_hbm, down_a_ref), begin(down_b_hbm, down_b_ref)]
    down_in = [begin(w_down_hbm.at[:, cut], w_down_ref.at[:, cut]) for cut in width_cuts]

    for copy in x_in:
        copy.wait()
    gates = x_ref[:, width:].astype(jnp.float32)
    lane = lax.broadcasted_iota(jnp.int32, gates.shape, 1)
    mine = jnp.sum(jnp.where(lane == place_ref[1], gates, 0.0), axis=1, keepdims=True)
    x = x_ref[:, :width]
    low = (adapter_scale * dot(x, a_gu_ref[...])).astype(jnp.bfloat16)
    for copy in b_in:
        copy.wait()
    for cut, (gate_in, up_in) in zip(unit_cuts, gu_in):
        gate_in.wait()
        g = dot(x, w_gate_ref[:, cut]) + dot(low[:, :rank], gate_b_ref[:, cut])
        up_in.wait()
        u = dot(x, w_up_ref[:, cut]) + dot(low[:, rank:], up_b_ref[:, cut])
        inner_ref[:, cut] = (g / (1.0 + jnp.exp(-g)) * u).astype(jnp.bfloat16)
    for copy in d_in:
        copy.wait()
    inner = inner_ref[...]
    low = (adapter_scale * dot(inner, down_a_ref[...])).astype(jnp.bfloat16)[:, :rank]
    out_copies = []
    for i, (cut, copy) in enumerate(zip(width_cuts, down_in)):
        copy.wait()
        out = dot(inner, w_down_ref[:, cut]) + dot(low, down_b_ref[:, cut])
        out = out * mine
        sent_ref[:, cut] = out[own:].astype(jnp.bfloat16)
        kept_ref[:, cut] = out[:own]
        for j, (src, dst) in enumerate(((sent_ref, sent_hbm), (kept_ref, kept_hbm))):
            copy = pltpu.make_async_copy(src.at[:, cut], dst.at[:, cut], out_sem.at[2 * i + j])
            copy.start()
            out_copies.append(copy)
    for copy in out_copies:
        copy.wait()


def run_expert(place, pieces, low_rank, w_gate, w_up, w_down):
    units, width = w_down.shape
    total = sum(p.shape[0] for p in pieces)
    own = total // 2
    a_gu, gate_b, up_b, down_a, down_b = low_rank
    rank = down_b.shape[0]
    outs = [
        jax.ShapeDtypeStruct((own, width), jnp.float32),
        jax.ShapeDtypeStruct((total - own, width), jnp.bfloat16),
    ]
    kept = [a_gu, gate_b, up_b, down_a, down_b, w_gate, w_up, w_down]
    width_block = 512 if width % 512 == 0 else 256
    copies = len(pieces) + 5 + 2 * (units // 256) + width // width_block
    return pl.pallas_call(
        functools.partial(expert_kernel, len(pieces)),
        out_shape=outs,
        in_specs=[pl.BlockSpec(memory_space=pltpu.SMEM)]
        + [pl.BlockSpec(memory_space=pl.ANY)] * (len(pieces) + len(kept)),
        out_specs=[pl.BlockSpec(memory_space=pl.ANY)] * 2,
        scratch_shapes=[pltpu.VMEM((total, pieces[0].shape[1]), jnp.bfloat16)]
        + [pltpu.VMEM(a.shape, a.dtype) for a in kept]
        + [
            pltpu.VMEM((total, units), jnp.bfloat16),
            pltpu.VMEM(outs[0].shape, outs[0].dtype),
            pltpu.VMEM(outs[1].shape, outs[1].dtype),
            pltpu.SemaphoreType.DMA((copies,)),
            pltpu.SemaphoreType.DMA((2 * (width // width_block),)),
        ],
        compiler_params=pltpu.CompilerParams(vmem_limit_bytes=GRANT),
        cost_estimate=pl.CostEstimate(
            flops=2 * total * units * (3 * width + 4 * rank) + 8 * total * width * rank,
            bytes_accessed=6 * units * width + 5 * total * width,
            transcendentals=total * units,
        ),
        name="run_expert",
    )(place, *pieces, *kept)


def dense_shards(
    hidden, route_ids, route_logits, placement, factors, w_gate, w_up, down_weight
):
    owners = lax.axis_size("expert")
    experts = placement.shape[0]
    steps, rows, width = hidden.shape
    units = w_gate.shape[2]
    rank = factors.shape[1] * owners // (3 * (width + units))
    outer, middle, cores = split_axis(owners)
    along_outer, along_middle = (middle * cores, outer), (cores, middle)
    place = jnp.stack([lax.axis_index("group"), lax.axis_index("expert")]).astype(jnp.int32)

    first = max(1, steps * 2 // 3)
    head, tail = make_payload(hidden, route_ids, route_logits, experts, first)
    tail = gather_along(tail, owners, *along_middle)
    head = gather_along(head, owners, *along_outer)
    blocks = order_factors(place, placement, factors, owners)
    here, there = exchange_factors(blocks, owners)
    heads = [head] + [shift(head, owners, *along_middle, k) for k in range(1, middle)]
    heads += [shift(p, owners, 1, cores, 1) for p in heads]
    tail = gather_along(tail, owners, *along_outer)
    tails = [tail, shift(tail, owners, 1, cores, 1)]

    low_rank = relayout_factors(place, here, there, width, units, rank, owners)
    weights = (w_gate[0], w_up[0], down_weight[0])
    head, head_sent = run_expert(place, heads, low_rank, *weights)
    tail, tail_sent = run_expert(place, tails, low_rank, *weights)
    head = head + shift(head_sent, owners, 1, cores, 1).astype(jnp.float32)
    tail = tail + shift(tail_sent, owners, 1, cores, 1).astype(jnp.float32)
    head = scatter_along(head, owners, *along_middle)
    tail = scatter_along(tail, owners, *along_outer)
    head = scatter_along(head, owners, *along_outer)
    tail = scatter_along(tail, owners, *along_middle)
    return jnp.concatenate([head, tail]).astype(jnp.bfloat16).reshape(steps, rows, width)


def row_capacity(rows, top, experts):
    return min(rows, 3 * max(1, rows * top // experts))


def unpack_factors(flat_factors, width, hidden_units, rank_size):
    layouts = [
        (width, rank_size),
        (rank_size, hidden_units),
        (width, rank_size),
        (rank_size, hidden_units),
        (hidden_units, rank_size),
        (rank_size, width),
    ]
    offset = 0
    segments = []
    for leading, trailing in layouts:
        segments.append(
            flat_factors[offset : offset + leading * trailing].reshape(leading, trailing)
        )
        offset = offset + leading * trailing
    return segments


def merge_weight(loaded_weights, factor_a, factor_b):
    adapter_delta = jnp.dot(factor_a, factor_b, preferred_element_type=jnp.float32)
    return (loaded_weights.astype(jnp.float32) + adapter_scale * adapter_delta).astype(jnp.bfloat16)


def apply_expert_block(inputs, merged_gate, merged_up, combined_down_weight):
    gate_part = jnp.dot(inputs, merged_gate, preferred_element_type=jnp.float32)
    up_part = jnp.dot(inputs, merged_up, preferred_element_type=jnp.float32)
    inner = (jax.nn.silu(gate_part) * up_part).astype(jnp.bfloat16)
    return jnp.dot(inner, combined_down_weight, preferred_element_type=jnp.float32).astype(
        jnp.bfloat16
    )


def sparse_shards(hidden, route_ids, route_logits, placement, factors, w_gate, w_up, down_weight):
    owners = lax.axis_size("expert")
    experts = placement.shape[0]
    steps_count, row_count, width = hidden.shape
    top_count = route_ids.shape[2]
    hidden_units = w_gate.shape[2]
    rank_size = factors.shape[1] * owners // (3 * (width + hidden_units))
    capacity = row_capacity(row_count, top_count, experts)
    slot_of = (
        jnp.zeros((experts,), jnp.int32).at[placement].set(jnp.arange(experts, dtype=jnp.int32))
    )
    ordered = jnp.take(factors, slot_of, axis=0)
    received = lax.all_to_all(ordered, "expert", split_axis=0, concat_axis=1, tiled=True)
    segments = unpack_factors(received[0], width, hidden_units, rank_size)
    merged_gate = merge_weight(w_gate[0], segments[0], segments[1])
    merged_up = merge_weight(w_up[0], segments[2], segments[3])
    combined_down_weight = merge_weight(down_weight[0], segments[4], segments[5])

    def layout(step_index):
        ids_flat = route_ids[step_index].reshape(-1)
        onehot = (ids_flat[:, None] == jnp.arange(experts, dtype=jnp.int32)[None, :]).astype(
            jnp.int32
        )
        position = jnp.sum((jnp.cumsum(onehot, axis=0) - 1) * onehot, axis=1)
        target = ids_flat * capacity + position
        placed = (
            jnp.arange(experts * capacity, dtype=jnp.int32)[:, None] == target[None, :]
        ).astype(jnp.bfloat16)
        pair_rows = jnp.repeat(hidden[step_index], top_count, axis=0)
        outgoing = jnp.dot(placed, pair_rows, preferred_element_type=jnp.float32).astype(
            jnp.bfloat16
        )
        outgoing = outgoing.reshape(experts, 1, capacity, width)
        gates = route_gates(route_logits[step_index]).reshape(-1)
        weighted = placed * gates[None, :]
        return (outgoing, weighted)

    layouts_all = [layout(step_index) for step_index in range(steps_count)]
    results = []
    for step_index in range(steps_count):
        outgoing, weighted = layouts_all[step_index]
        arrived = lax.all_to_all(outgoing, "expert", split_axis=0, concat_axis=1, tiled=True)
        outputs = apply_expert_block(
            arrived.reshape(-1, width), merged_gate, merged_up, combined_down_weight
        )
        outputs = outputs.reshape(arrived.shape)
        returned = lax.all_to_all(outputs, "expert", split_axis=1, concat_axis=0, tiled=True)
        flat_back = returned.reshape(experts * capacity, width)
        pair_out = jnp.einsum("cp,cd->pd", weighted, flat_back, preferred_element_type=jnp.float32)
        results.append(
            pair_out.reshape(row_count, top_count, width).sum(axis=1).astype(jnp.bfloat16)
        )
    return jnp.stack(results, axis=0)


def shards(hidden, route_ids, route_logits, placement, factors, w_gate, w_up, down_weight):
    rows, top = route_ids.shape[1:]
    width, units = w_gate.shape[1:]
    owners = lax.axis_size("expert")
    rank = factors.shape[1] * owners // (3 * (width + units))
    dense = row_capacity(rows, top, placement.shape[0]) == rows
    dense = dense and lax.axis_size("group") == 2 and split_axis(owners)[2] == 2
    dense = dense and 2 * rank == LANES and width % 256 == 0 and units % 256 == 0
    dense = dense and factors.shape[1] % (8 * LANES) == 0 and hidden.shape[0] > 1
    return (dense_shards if dense else sparse_shards)(
        hidden, route_ids, route_logits, placement, factors, w_gate, w_up, down_weight
    )


def solution(mesh):
    placed = (
        P(None, ("group", "expert"), None),
        P(None, ("group", "expert"), None),
        P(None, ("group", "expert"), None),
        P(),
        P(None, "expert"),
        P("expert", None, None),
        P("expert", None, None),
        P("expert", None, None),
    )
    return jax.shard_map(
        shards,
        mesh=mesh,
        in_specs=placed,
        out_specs=P(None, ("group", "expert"), None),
        check_vma=False,
    )
```

```python
import functools

import jax
import jax.numpy as jnp
from jax import lax
from jax.experimental import pallas as pl
from jax.experimental.pallas import tpu as pltpu
from jax.sharding import PartitionSpec as P

adapter_scale = 2.0
LANES = 128
GRANT = 16 << 20
EXPERT_GRANT = 36 << 20


def route_gates(logits):
    highest = jnp.max(logits, axis=-1, keepdims=True)
    router_scores = jnp.exp(logits - highest)
    return (router_scores / jnp.sum(router_scores, axis=-1, keepdims=True)).astype(jnp.bfloat16)


def split_axis(n):
    cores = 2 if n % 2 == 0 else 1
    chips = n // cores
    middle = 1
    while chips % (2 * middle) == 0 and 4 * middle * middle <= chips:
        middle *= 2
    return chips // middle, middle, cores


def shift(x, n, stride, size, k):
    pairs = []
    for i in range(n):
        place = i // stride % size
        pairs.append((i, i + ((place + k) % size - place) * stride))
    return lax.ppermute(x, "expert", pairs)


def stack_rows(pieces):
    return jnp.stack(pieces).reshape(-1, pieces[0].shape[1])


def gather_along(x, n, stride, size):
    return stack_rows([x] + [shift(x, n, stride, size, k) for k in range(1, size)])


def scatter_along(total, n, stride, size):
    count = total.shape[0] // size
    result = total[:count]
    for k in range(1, size):
        part = total[k * count : (k + 1) * count].astype(jnp.bfloat16)
        result = result + shift(part, n, stride, size, size - k).astype(jnp.float32)
    return result


def exchange_factors(blocks, n):
    outer, middle, cores = split_axis(n)
    stride = middle * cores
    turned = [blocks[0]] + [shift(blocks[r], n, cores, middle, r) for r in range(1, middle)]
    here, there = [], []
    for q in range(outer):
        pairs = []
        for g in range(2):
            for i in range(n):
                place = i // stride
                to = (i + ((place + q) % outer - place) * stride) ^ g
                pairs.append((g * n + i, g * n + to))
        part = jnp.stack([t[q] for t in turned])
        part = lax.ppermute(part, ("group", "expert"), pairs)
        here.append(part)
        there.append(lax.ppermute(part, "group", [(0, 1), (1, 0)]))
    return here, there


def dot(a, b):
    return jnp.dot(a, b, preferred_element_type=jnp.float32)


def payload_kernel(hidden_ref, ids_ref, logits_ref, *refs):
    out_refs, turned_ref = refs[:-1], refs[-1]
    steps, top, rows = ids_ref.shape
    width = hidden_ref.shape[2]
    turned_ref[...] = jnp.zeros_like(turned_ref)
    for s in range(steps):
        logits, ids = logits_ref[s], ids_ref[s]
        scores = jnp.exp(logits - jnp.max(logits, axis=0, keepdims=True))
        gates = scores / jnp.sum(scores, axis=0, keepdims=True)
        expert = lax.broadcasted_iota(jnp.int32, (turned_ref.shape[0], rows), 0)
        dense = jnp.zeros(expert.shape, jnp.float32)
        for k in range(top):
            dense += jnp.where(ids[k : k + 1, :] == expert, gates[k : k + 1, :], 0.0)
        turned_ref[:, s * rows : (s + 1) * rows] = dense
    dense = turned_ref[...].T.astype(jnp.bfloat16)
    s = 0
    for out_ref in out_refs:
        for at in range(0, out_ref.shape[0], rows):
            out_ref[at : at + rows, :width] = hidden_ref[s]
            out_ref[at : at + rows, width:] = dense[s * rows : (s + 1) * rows, :]
            s += 1


def make_payload(hidden, route_ids, route_logits, experts, first):
    steps, rows, width = hidden.shape
    padded = -(-experts // LANES) * LANES
    return pl.pallas_call(
        payload_kernel,
        out_shape=[
            jax.ShapeDtypeStruct((count * rows, width + padded), jnp.bfloat16)
            for count in (first, steps - first)
        ],
        scratch_shapes=[pltpu.VMEM((padded, -(-steps * rows // LANES) * LANES), jnp.float32)],
        compiler_params=pltpu.CompilerParams(vmem_limit_bytes=GRANT),
        name="payload",
    )(hidden, jnp.swapaxes(route_ids, 1, 2), jnp.swapaxes(route_logits, 1, 2))


def order_kernel(outer, middle, place_ref, placement_ref, factors_ref, *refs):
    out_refs, wide_ref = refs[:-1], refs[-1]
    slots = factors_ref.shape[0]
    length, lanes = out_refs[0].shape[1:]
    group, me = place_ref[0], place_ref[1]

    def cut(t, carry):
        start = pl.multiple_of(t * lanes, lanes)
        tile = factors_ref[:, pl.ds(start, lanes)].astype(jnp.float32)
        wide_ref[pl.ds(t, slots, stride=length), :] = tile
        return carry

    lax.fori_loop(0, length, cut, 0, unroll=8)

    def put(s, carry):
        to = placement_ref[s]
        aside = lax.rem(to // 2 + middle - lax.rem(me // 2, middle), middle)
        ahead = lax.rem(to // (2 * middle) + outer - me // (2 * middle), outer)
        ours = lax.rem(to + me + group, 2) == 0
        rows = wide_ref[pl.ds(pl.multiple_of(s * length, 8), length), :].astype(jnp.bfloat16)
        for r, out_ref in enumerate(out_refs):

            @pl.when(jnp.logical_and(ours, aside == r))
            def _():
                out_ref[ahead] = rows

        return carry

    lax.fori_loop(0, slots, put, 0)


def order_factors(place, placement, factors, n):
    outer, middle, _ = split_axis(n)
    slots, entries = factors.shape
    length = entries // LANES
    return pl.pallas_call(
        functools.partial(order_kernel, outer, middle),
        out_shape=[jax.ShapeDtypeStruct((outer, length, LANES), jnp.bfloat16)] * middle,
        in_specs=[
            pl.BlockSpec(memory_space=pltpu.SMEM),
            pl.BlockSpec(memory_space=pltpu.SMEM),
            pl.BlockSpec(memory_space=pltpu.VMEM),
        ],
        scratch_shapes=[pltpu.VMEM((slots * length, LANES), jnp.float32)],
        compiler_params=pltpu.CompilerParams(vmem_limit_bytes=GRANT),
        name="order_factors",
    )(place, placement, factors)


def relayout_kernel(outer, middle, place_ref, *refs):
    pieces = refs[: 2 * outer]
    a_gu_ref, gate_b_ref, up_b_ref, down_a_ref, down_b_ref, flat_ref, wide_ref = refs[2 * outer :]
    width, units = a_gu_ref.shape[0], gate_b_ref.shape[1]
    rank = gate_b_ref.shape[0]
    length = pieces[0].shape[1]
    group, me = place_ref[0], place_ref[1]
    for i, piece in enumerate(pieces):
        swapped, q = i // outer, i % outer
        core = lax.rem(me + group + swapped, 2)
        for r in range(middle):
            row = lax.rem(me // 2 + middle - r, middle)
            column = lax.rem(me // (2 * middle) + outer - q, outer)
            source = (column * middle + row) * 2 + core
            start = pl.multiple_of(source * length, 8)
            flat_ref[pl.ds(start, length), :] = piece[r].astype(jnp.float32)

    n_wide, n_unit = width // 2, units // 2
    at_ub = 2 * n_wide + n_unit
    at_da = 2 * n_wide + 2 * n_unit
    chunk = 128
    left = lax.broadcasted_iota(jnp.int32, (chunk, LANES), 1) < rank

    def load(start):
        return flat_ref[pl.ds(pl.multiple_of(start, 128), chunk), :]

    def gate_up(i, carry):
        g, u = load(i * chunk), load(n_wide + n_unit + i * chunk)
        at = 2 * i * chunk
        wide_ref[pl.ds(at, chunk, stride=2), :] = jnp.where(left, g, pltpu.roll(u, rank, 1))
        wide_ref[pl.ds(at + 1, chunk, stride=2), :] = jnp.where(left, pltpu.roll(g, rank, 1), u)
        both = wide_ref[pl.ds(pl.multiple_of(at, 128), 2 * chunk), :]
        a_gu_ref[pl.ds(pl.multiple_of(at, 128), 2 * chunk), :] = both.astype(jnp.bfloat16)
        return carry

    lax.fori_loop(0, n_wide // chunk, gate_up, 0, unroll=2)
    for i in range(n_unit // chunk):
        d = load(at_da + i * chunk)
        at = 2 * i * chunk
        wide_ref[pl.ds(at, chunk, stride=2), :] = jnp.where(left, d, 0.0)
        wide_ref[pl.ds(at + 1, chunk, stride=2), :] = jnp.where(left, pltpu.roll(d, rank, 1), 0.0)
        down_a_ref[at : at + 2 * chunk, :] = wide_ref[at : at + 2 * chunk, :].astype(jnp.bfloat16)
    for start, b_ref in (
        (n_wide, gate_b_ref),
        (at_ub, up_b_ref),
        (at_da + n_unit, down_b_ref),
    ):
        tiles = b_ref.shape[1] // LANES
        for j in range(tiles):
            row = flat_ref[pl.ds(start + j, rank, stride=tiles), :]
            b_ref[:, j * LANES : (j + 1) * LANES] = row.astype(jnp.bfloat16)


def relayout_factors(place, here, there, width, units, rank, n):
    outer, middle, _ = split_axis(n)
    shapes = [(width, 2 * rank), (rank, units), (rank, units), (units, 2 * rank), (rank, width)]
    length = here[0].shape[1]
    return pl.pallas_call(
        functools.partial(relayout_kernel, outer, middle),
        out_shape=[jax.ShapeDtypeStruct(shape, jnp.bfloat16) for shape in shapes],
        in_specs=[pl.BlockSpec(memory_space=pltpu.SMEM)]
        + [pl.BlockSpec(memory_space=pltpu.VMEM)] * (2 * outer),
        scratch_shapes=[
            pltpu.VMEM((n * length, LANES), jnp.float32),
            pltpu.VMEM((width, LANES), jnp.float32),
        ],
        compiler_params=pltpu.CompilerParams(vmem_limit_bytes=GRANT),
        name="relayout_factors",
    )(place, *here, *there)


def expert_kernel(count, place_ref, *refs):
    pieces, refs = refs[:count], refs[count:]
    a_gu_hbm, gate_b_hbm, up_b_hbm, down_a_hbm, down_b_hbm = refs[:5]
    w_gate_hbm, w_up_hbm, w_down_hbm, kept_hbm, sent_hbm = refs[5:10]
    x_ref, a_gu_ref, gate_b_ref, up_b_ref, down_a_ref, down_b_ref = refs[10:16]
    w_gate_ref, w_up_ref, w_down_ref, inner_ref, kept_ref, sent_ref, sem, out_sem = refs[16:]
    rows = pieces[0].shape[0]
    units, width = w_down_ref.shape
    rank = gate_b_ref.shape[0]
    own = kept_ref.shape[0]
    begun = []

    def begin(src, dst):
        copy = pltpu.make_async_copy(src, dst, sem.at[len(begun)])
        copy.start()
        begun.append(copy)
        return copy

    def begin_rows(src, dst):
        quarter = src.shape[0] // 4
        cuts = [pl.ds(at, quarter) for at in range(0, src.shape[0], quarter)]
        return [begin(src.at[cut], dst.at[cut]) for cut in cuts]

    def wait(copies):
        for copy in copies:
            copy.wait()

    x_in = [begin(p, x_ref.at[pl.ds(i * rows, rows)]) for i, p in enumerate(pieces)]
    x_in.append(begin(a_gu_hbm, a_gu_ref))
    gate_in = begin_rows(w_gate_hbm, w_gate_ref) + [begin(gate_b_hbm, gate_b_ref)]
    up_in = begin_rows(w_up_hbm, w_up_ref) + [begin(up_b_hbm, up_b_ref)]
    down_in = [begin(down_a_hbm, down_a_ref), begin(down_b_hbm, down_b_ref)]
    down_in += begin_rows(w_down_hbm, w_down_ref)

    wait(x_in)
    gates = x_ref[:, width:].astype(jnp.float32)
    lane = lax.broadcasted_iota(jnp.int32, gates.shape, 1)
    mine = jnp.sum(jnp.where(lane == place_ref[1], gates, 0.0), axis=1, keepdims=True)
    low = (adapter_scale * dot(x_ref[:, :width], a_gu_ref[...])).astype(jnp.bfloat16)
    wait(gate_in)
    g = dot(x_ref[:, :width], w_gate_ref[...]) + dot(low[:, :rank], gate_b_ref[...])
    wait(up_in)
    u = dot(x_ref[:, :width], w_up_ref[...]) + dot(low[:, rank:], up_b_ref[...])
    inner_ref[...] = (g / (1.0 + jnp.exp(-g)) * u).astype(jnp.bfloat16)
    wait(down_in)
    low = (adapter_scale * dot(inner_ref[...], down_a_ref[...])).astype(jnp.bfloat16)[:, :rank]
    out_copies = []
    block = width // 2
    for i, cut in enumerate((slice(0, block), slice(block, width))):
        out = dot(inner_ref[...], w_down_ref[:, cut]) + dot(low, down_b_ref[:, cut])
        out = out * mine
        sent_ref[:, cut] = out[own:].astype(jnp.bfloat16)
        kept_ref[:, cut] = out[:own]
        for j, (src, dst) in enumerate(((sent_ref, sent_hbm), (kept_ref, kept_hbm))):
            copy = pltpu.make_async_copy(src.at[:, cut], dst.at[:, cut], out_sem.at[2 * i + j])
            copy.start()
            out_copies.append(copy)
    for copy in out_copies:
        copy.wait()


def run_expert(place, pieces, low_rank, w_gate, w_up, w_down):
    units, width = w_down.shape
    total = sum(p.shape[0] for p in pieces)
    own = total // 2
    a_gu, gate_b, up_b, down_a, down_b = low_rank
    rank = down_b.shape[0]
    outs = [
        jax.ShapeDtypeStruct((own, width), jnp.float32),
        jax.ShapeDtypeStruct((total - own, width), jnp.bfloat16),
    ]
    kept = [a_gu, gate_b, up_b, down_a, down_b, w_gate, w_up, w_down]
    copies = len(pieces) + 5 + 3 * 4
    return pl.pallas_call(
        functools.partial(expert_kernel, len(pieces)),
        out_shape=outs,
        in_specs=[pl.BlockSpec(memory_space=pltpu.SMEM)]
        + [pl.BlockSpec(memory_space=pl.ANY)] * (len(pieces) + len(low_rank))
        + [pl.BlockSpec(memory_space=pltpu.HBM)] * 3,
        out_specs=[pl.BlockSpec(memory_space=pl.ANY)] * 2,
        scratch_shapes=[pltpu.VMEM((total, pieces[0].shape[1]), jnp.bfloat16)]
        + [pltpu.VMEM(a.shape, a.dtype) for a in kept]
        + [
            pltpu.VMEM((total, units), jnp.bfloat16),
            pltpu.VMEM(outs[0].shape, outs[0].dtype),
            pltpu.VMEM(outs[1].shape, outs[1].dtype),
            pltpu.SemaphoreType.DMA((copies,)),
            pltpu.SemaphoreType.DMA((4,)),
        ],
        compiler_params=pltpu.CompilerParams(vmem_limit_bytes=EXPERT_GRANT),
        cost_estimate=pl.CostEstimate(
            flops=2 * total * units * (3 * width + 4 * rank) + 8 * total * width * rank,
            bytes_accessed=6 * units * width + 5 * total * width,
            transcendentals=total * units,
        ),
        name="run_expert",
    )(place, *pieces, *kept)


def dense_shards(
    hidden, route_ids, route_logits, placement, factors, w_gate, w_up, down_weight
):
    owners = lax.axis_size("expert")
    experts = placement.shape[0]
    steps, rows, width = hidden.shape
    units = w_gate.shape[2]
    rank = factors.shape[1] * owners // (3 * (width + units))
    outer, middle, cores = split_axis(owners)
    along_outer, along_middle = (middle * cores, outer), (cores, middle)
    place = jnp.stack([lax.axis_index("group"), lax.axis_index("expert")]).astype(jnp.int32)

    first = max(1, steps * 2 // 3)
    head, tail = make_payload(hidden, route_ids, route_logits, experts, first)
    tail = gather_along(tail, owners, *along_middle)
    head = gather_along(head, owners, *along_outer)
    blocks = order_factors(place, placement, factors, owners)
    here, there = exchange_factors(blocks, owners)
    heads = [head] + [shift(head, owners, *along_middle, k) for k in range(1, middle)]
    heads += [shift(p, owners, 1, cores, 1) for p in heads]
    tail, here = lax.optimization_barrier((tail, here))
    tail = gather_along(tail, owners, *along_outer)
    tails = [tail, shift(tail, owners, 1, cores, 1)]

    low_rank = relayout_factors(place, here, there, width, units, rank, owners)
    weights = (w_gate[0], w_up[0], down_weight[0])
    head, head_sent = run_expert(place, heads, low_rank, *weights)
    tail, tail_sent = run_expert(place, tails, low_rank, *weights)
    head = head + shift(head_sent, owners, 1, cores, 1).astype(jnp.float32)
    tail = tail + shift(tail_sent, owners, 1, cores, 1).astype(jnp.float32)
    head = scatter_along(head, owners, *along_middle)
    tail = scatter_along(tail, owners, *along_outer)
    head = scatter_along(head, owners, *along_outer)
    tail = scatter_along(tail, owners, *along_middle)
    return jnp.concatenate([head, tail]).astype(jnp.bfloat16).reshape(steps, rows, width)


def row_capacity(rows, top, experts):
    return min(rows, 3 * max(1, rows * top // experts))


def unpack_factors(flat_factors, width, hidden_units, rank_size):
    layouts = [
        (width, rank_size),
        (rank_size, hidden_units),
        (width, rank_size),
        (rank_size, hidden_units),
        (hidden_units, rank_size),
        (rank_size, width),
    ]
    offset = 0
    segments = []
    for leading, trailing in layouts:
        segments.append(
            flat_factors[offset : offset + leading * trailing].reshape(leading, trailing)
        )
        offset = offset + leading * trailing
    return segments


def merge_weight(loaded_weights, factor_a, factor_b):
    adapter_delta = jnp.dot(factor_a, factor_b, preferred_element_type=jnp.float32)
    return (loaded_weights.astype(jnp.float32) + adapter_scale * adapter_delta).astype(jnp.bfloat16)


def apply_expert_block(inputs, merged_gate, merged_up, combined_down_weight):
    gate_part = jnp.dot(inputs, merged_gate, preferred_element_type=jnp.float32)
    up_part = jnp.dot(inputs, merged_up, preferred_element_type=jnp.float32)
    inner = (jax.nn.silu(gate_part) * up_part).astype(jnp.bfloat16)
    return jnp.dot(inner, combined_down_weight, preferred_element_type=jnp.float32).astype(
        jnp.bfloat16
    )


def sparse_shards(hidden, route_ids, route_logits, placement, factors, w_gate, w_up, down_weight):
    owners = lax.axis_size("expert")
    experts = placement.shape[0]
    steps_count, row_count, width = hidden.shape
    top_count = route_ids.shape[2]
    hidden_units = w_gate.shape[2]
    rank_size = factors.shape[1] * owners // (3 * (width + hidden_units))
    capacity = row_capacity(row_count, top_count, experts)
    slot_of = (
        jnp.zeros((experts,), jnp.int32).at[placement].set(jnp.arange(experts, dtype=jnp.int32))
    )
    ordered = jnp.take(factors, slot_of, axis=0)
    received = lax.all_to_all(ordered, "expert", split_axis=0, concat_axis=1, tiled=True)
    segments = unpack_factors(received[0], width, hidden_units, rank_size)
    merged_gate = merge_weight(w_gate[0], segments[0], segments[1])
    merged_up = merge_weight(w_up[0], segments[2], segments[3])
    combined_down_weight = merge_weight(down_weight[0], segments[4], segments[5])

    def layout(step_index):
        ids_flat = route_ids[step_index].reshape(-1)
        onehot = (ids_flat[:, None] == jnp.arange(experts, dtype=jnp.int32)[None, :]).astype(
            jnp.int32
        )
        position = jnp.sum((jnp.cumsum(onehot, axis=0) - 1) * onehot, axis=1)
        target = ids_flat * capacity + position
        placed = (
            jnp.arange(experts * capacity, dtype=jnp.int32)[:, None] == target[None, :]
        ).astype(jnp.bfloat16)
        pair_rows = jnp.repeat(hidden[step_index], top_count, axis=0)
        outgoing = jnp.dot(placed, pair_rows, preferred_element_type=jnp.float32).astype(
            jnp.bfloat16
        )
        outgoing = outgoing.reshape(experts, 1, capacity, width)
        gates = route_gates(route_logits[step_index]).reshape(-1)
        weighted = placed * gates[None, :]
        return (outgoing, weighted)

    layouts_all = [layout(step_index) for step_index in range(steps_count)]
    results = []
    for step_index in range(steps_count):
        outgoing, weighted = layouts_all[step_index]
        arrived = lax.all_to_all(outgoing, "expert", split_axis=0, concat_axis=1, tiled=True)
        outputs = apply_expert_block(
            arrived.reshape(-1, width), merged_gate, merged_up, combined_down_weight
        )
        outputs = outputs.reshape(arrived.shape)
        returned = lax.all_to_all(outputs, "expert", split_axis=1, concat_axis=0, tiled=True)
        flat_back = returned.reshape(experts * capacity, width)
        pair_out = jnp.einsum("cp,cd->pd", weighted, flat_back, preferred_element_type=jnp.float32)
        results.append(
            pair_out.reshape(row_count, top_count, width).sum(axis=1).astype(jnp.bfloat16)
        )
    return jnp.stack(results, axis=0)


def shards(hidden, route_ids, route_logits, placement, factors, w_gate, w_up, down_weight):
    rows, top = route_ids.shape[1:]
    width, units = w_gate.shape[1:]
    owners = lax.axis_size("expert")
    rank = factors.shape[1] * owners // (3 * (width + units))
    dense = row_capacity(rows, top, placement.shape[0]) == rows
    dense = dense and lax.axis_size("group") == 2 and split_axis(owners)[2] == 2
    dense = dense and 2 * rank == LANES and width % 256 == 0 and units % 256 == 0
    dense = dense and factors.shape[1] % (8 * LANES) == 0 and hidden.shape[0] > 1
    return (dense_shards if dense else sparse_shards)(
        hidden, route_ids, route_logits, placement, factors, w_gate, w_up, down_weight
    )


def solution(mesh):
    placed = (
        P(None, ("group", "expert"), None),
        P(None, ("group", "expert"), None),
        P(None, ("group", "expert"), None),
        P(),
        P(None, "expert"),
        P("expert", None, None),
        P("expert", None, None),
        P("expert", None, None),
    )
    return jax.shard_map(
        shards,
        mesh=mesh,
        in_specs=placed,
        out_specs=P(None, ("group", "expert"), None),
        check_vma=False,
    )
```

```python
import functools

import jax
import jax.numpy as jnp
from jax import lax
from jax.experimental import pallas as pl
from jax.experimental.pallas import tpu as pltpu
from jax.sharding import PartitionSpec as P

adapter_scale = 2.0
LANES = 128
GRANT = 16 << 20
EXPERT_GRANT = 36 << 20


def route_gates(logits):
    highest = jnp.max(logits, axis=-1, keepdims=True)
    router_scores = jnp.exp(logits - highest)
    return (router_scores / jnp.sum(router_scores, axis=-1, keepdims=True)).astype(jnp.bfloat16)


def split_axis(n):
    cores = 2 if n % 2 == 0 else 1
    chips = n // cores
    middle = 1
    while chips % (2 * middle) == 0 and 4 * middle * middle <= chips:
        middle *= 2
    return chips // middle, middle, cores


def shift(x, n, stride, size, k):
    pairs = []
    for i in range(n):
        place = i // stride % size
        pairs.append((i, i + ((place + k) % size - place) * stride))
    return lax.ppermute(x, "expert", pairs)


def stack_rows(pieces):
    return jnp.stack(pieces).reshape(-1, pieces[0].shape[1])


def gather_along(x, n, stride, size):
    return stack_rows([x] + [shift(x, n, stride, size, k) for k in range(1, size)])


def scatter_along(total, n, stride, size):
    count = total.shape[0] // size
    result = total[:count]
    for k in range(1, size):
        part = total[k * count : (k + 1) * count].astype(jnp.bfloat16)
        result = result + shift(part, n, stride, size, size - k).astype(jnp.float32)
    return result


def exchange_factors(blocks, n):
    outer, middle, cores = split_axis(n)
    stride = middle * cores
    here, there = [], []
    for q in range(outer):
        pairs = []
        for g in range(2):
            for i in range(n):
                place = i // stride
                to = (i + ((place + q) % outer - place) * stride) ^ g
                pairs.append((g * n + i, g * n + to))
        part = jnp.stack([block[q] for block in blocks])
        part = lax.ppermute(part, ("group", "expert"), pairs)
        here.append(part)
        there.append(lax.ppermute(part, "group", [(0, 1), (1, 0)]))
    return here, there


def dot(a, b):
    return jnp.dot(a, b, preferred_element_type=jnp.float32)


def payload_kernel(hidden_ref, ids_ref, logits_ref, *refs):
    out_refs, turned_ref = refs[:-1], refs[-1]
    steps, top, rows = ids_ref.shape
    width = hidden_ref.shape[2]
    turned_ref[...] = jnp.zeros_like(turned_ref)
    for s in range(steps):
        logits, ids = logits_ref[s], ids_ref[s]
        scores = jnp.exp(logits - jnp.max(logits, axis=0, keepdims=True))
        gates = scores / jnp.sum(scores, axis=0, keepdims=True)
        expert = lax.broadcasted_iota(jnp.int32, (turned_ref.shape[0], rows), 0)
        dense = jnp.zeros(expert.shape, jnp.float32)
        for k in range(top):
            dense += jnp.where(ids[k : k + 1, :] == expert, gates[k : k + 1, :], 0.0)
        turned_ref[:, s * rows : (s + 1) * rows] = dense
    dense = turned_ref[...].T.astype(jnp.bfloat16)
    s = 0
    for out_ref in out_refs:
        for at in range(0, out_ref.shape[0], rows):
            out_ref[at : at + rows, :width] = hidden_ref[s]
            out_ref[at : at + rows, width:] = dense[s * rows : (s + 1) * rows, :]
            s += 1


def make_payload(hidden, route_ids, route_logits, experts, first):
    steps, rows, width = hidden.shape
    padded = -(-experts // LANES) * LANES
    return pl.pallas_call(
        payload_kernel,
        out_shape=[
            jax.ShapeDtypeStruct((count * rows, width + padded), jnp.bfloat16)
            for count in (first, steps - first)
        ],
        scratch_shapes=[pltpu.VMEM((padded, -(-steps * rows // LANES) * LANES), jnp.float32)],
        compiler_params=pltpu.CompilerParams(vmem_limit_bytes=GRANT),
        name="payload",
    )(hidden, jnp.swapaxes(route_ids, 1, 2), jnp.swapaxes(route_logits, 1, 2))


def order_kernel(outer, middle, place_ref, placement_ref, factors_ref, *refs):
    out_refs, wide_ref = refs[:-1], refs[-1]
    slots = factors_ref.shape[0]
    length, lanes = out_refs[0].shape[1:]
    group, me = place_ref[0], place_ref[1]

    def cut(t, carry):
        start = pl.multiple_of(t * lanes, lanes)
        tile = factors_ref[:, pl.ds(start, lanes)].astype(jnp.float32)
        wide_ref[pl.ds(t, slots, stride=length), :] = tile
        return carry

    lax.fori_loop(0, length, cut, 0, unroll=8)

    def put(s, carry):
        to = placement_ref[s]
        aside = lax.rem(to // 2 + middle - lax.rem(me // 2, middle), middle)
        ahead = lax.rem(to // (2 * middle) + outer - me // (2 * middle), outer)
        ours = lax.rem(to + me + group, 2) == 0
        rows = wide_ref[pl.ds(pl.multiple_of(s * length, 8), length), :].astype(jnp.bfloat16)
        for r, out_ref in enumerate(out_refs):

            @pl.when(jnp.logical_and(ours, aside == r))
            def _():
                out_ref[ahead] = rows

        return carry

    lax.fori_loop(0, slots, put, 0)


def order_factors(place, placement, factors, n):
    outer, middle, _ = split_axis(n)
    slots, entries = factors.shape
    length = entries // LANES
    return pl.pallas_call(
        functools.partial(order_kernel, outer, middle),
        out_shape=[jax.ShapeDtypeStruct((outer, length, LANES), jnp.bfloat16)] * middle,
        in_specs=[
            pl.BlockSpec(memory_space=pltpu.SMEM),
            pl.BlockSpec(memory_space=pltpu.SMEM),
            pl.BlockSpec(memory_space=pltpu.VMEM),
        ],
        scratch_shapes=[pltpu.VMEM((slots * length, LANES), jnp.float32)],
        compiler_params=pltpu.CompilerParams(vmem_limit_bytes=GRANT),
        name="order_factors",
    )(place, placement, factors)


def relayout_kernel(outer, middle, place_ref, *refs):
    pieces = refs[: 2 * outer]
    a_gu_ref, gate_b_ref, up_b_ref, down_a_ref, down_b_ref, flat_ref, wide_ref = refs[2 * outer :]
    width, units = a_gu_ref.shape[0], gate_b_ref.shape[1]
    rank = gate_b_ref.shape[0]
    length = pieces[0].shape[1]
    group, me = place_ref[0], place_ref[1]
    for i, piece in enumerate(pieces):
        swapped, q = i // outer, i % outer
        core = lax.rem(me + group + swapped, 2)
        for r in range(middle):
            row = lax.rem(me // 2 + middle - r, middle)
            column = lax.rem(me // (2 * middle) + outer - q, outer)
            source = (column * middle + row) * 2 + core
            start = pl.multiple_of(source * length, 8)
            flat_ref[pl.ds(start, length), :] = piece[r].astype(jnp.float32)

    n_wide, n_unit = width // 2, units // 2
    at_ub = 2 * n_wide + n_unit
    at_da = 2 * n_wide + 2 * n_unit
    chunk = 128
    left = lax.broadcasted_iota(jnp.int32, (chunk, LANES), 1) < rank

    def load(start):
        return flat_ref[pl.ds(pl.multiple_of(start, 128), chunk), :]

    def gate_up(i, carry):
        g, u = load(i * chunk), load(n_wide + n_unit + i * chunk)
        at = 2 * i * chunk
        wide_ref[pl.ds(at, chunk, stride=2), :] = jnp.where(left, g, pltpu.roll(u, rank, 1))
        wide_ref[pl.ds(at + 1, chunk, stride=2), :] = jnp.where(left, pltpu.roll(g, rank, 1), u)
        both = wide_ref[pl.ds(pl.multiple_of(at, 128), 2 * chunk), :]
        a_gu_ref[pl.ds(pl.multiple_of(at, 128), 2 * chunk), :] = both.astype(jnp.bfloat16)
        return carry

    lax.fori_loop(0, n_wide // chunk, gate_up, 0, unroll=2)
    for i in range(n_unit // chunk):
        d = load(at_da + i * chunk)
        at = 2 * i * chunk
        wide_ref[pl.ds(at, chunk, stride=2), :] = jnp.where(left, d, 0.0)
        wide_ref[pl.ds(at + 1, chunk, stride=2), :] = jnp.where(left, pltpu.roll(d, rank, 1), 0.0)
        down_a_ref[at : at + 2 * chunk, :] = wide_ref[at : at + 2 * chunk, :].astype(jnp.bfloat16)
    for start, b_ref in (
        (n_wide, gate_b_ref),
        (at_ub, up_b_ref),
        (at_da + n_unit, down_b_ref),
    ):
        tiles = b_ref.shape[1] // LANES
        for j in range(tiles):
            row = flat_ref[pl.ds(start + j, rank, stride=tiles), :]
            b_ref[:, j * LANES : (j + 1) * LANES] = row.astype(jnp.bfloat16)


def relayout_factors(place, here, there, width, units, rank, n):
    outer, middle, _ = split_axis(n)
    shapes = [(width, 2 * rank), (rank, units), (rank, units), (units, 2 * rank), (rank, width)]
    length = here[0].shape[1]
    return pl.pallas_call(
        functools.partial(relayout_kernel, outer, middle),
        out_shape=[jax.ShapeDtypeStruct(shape, jnp.bfloat16) for shape in shapes],
        in_specs=[pl.BlockSpec(memory_space=pltpu.SMEM)]
        + [pl.BlockSpec(memory_space=pltpu.VMEM)] * (2 * outer),
        scratch_shapes=[
            pltpu.VMEM((n * length, LANES), jnp.float32),
            pltpu.VMEM((width, LANES), jnp.float32),
        ],
        compiler_params=pltpu.CompilerParams(vmem_limit_bytes=GRANT),
        name="relayout_factors",
    )(place, *here, *there)


def expert_kernel(count, place_ref, *refs):
    pieces, refs = refs[:count], refs[count:]
    a_gu_hbm, gate_b_hbm, up_b_hbm, down_a_hbm, down_b_hbm = refs[:5]
    w_gate_hbm, w_up_hbm, w_down_hbm, kept_hbm, sent_hbm = refs[5:10]
    x_ref, a_gu_ref, gate_b_ref, up_b_ref, down_a_ref, down_b_ref = refs[10:16]
    w_gate_ref, w_up_ref, w_down_ref, kept_ref, sent_ref, sem, out_sem = refs[16:]
    rows = pieces[0].shape[0]
    units, width = w_down_ref.shape
    rank = gate_b_ref.shape[0]
    own = kept_ref.shape[0]
    begun = []

    def begin(src, dst):
        copy = pltpu.make_async_copy(src, dst, sem.at[len(begun)])
        copy.start()
        begun.append(copy)
        return copy

    def begin_rows(src, dst):
        quarter = src.shape[0] // 4
        cuts = [pl.ds(at, quarter) for at in range(0, src.shape[0], quarter)]
        return [begin(src.at[cut], dst.at[cut]) for cut in cuts]

    def wait(copies):
        for copy in copies:
            copy.wait()

    x_in = [begin(p, x_ref.at[pl.ds(i * rows, rows)]) for i, p in enumerate(pieces)]
    x_in.append(begin(a_gu_hbm, a_gu_ref))
    gate_in = begin_rows(w_gate_hbm, w_gate_ref) + [begin(gate_b_hbm, gate_b_ref)]
    up_in = begin_rows(w_up_hbm, w_up_ref) + [begin(up_b_hbm, up_b_ref)]
    down_in = [begin(down_a_hbm, down_a_ref), begin(down_b_hbm, down_b_ref)]
    down_in += begin_rows(w_down_hbm, w_down_ref)
    wait(x_in)

    def run_piece(i, carry):
        here = pl.ds(pl.multiple_of(i * rows, rows), rows)
        gates = x_ref[here, width:].astype(jnp.float32)
        lane = lax.broadcasted_iota(jnp.int32, gates.shape, 1)
        mine = jnp.sum(jnp.where(lane == place_ref[1], gates, 0.0), axis=1, keepdims=True)
        low = (adapter_scale * dot(x_ref[here, :width], a_gu_ref[...])).astype(jnp.bfloat16)
        pl.when(i == 0)(lambda: wait(gate_in))
        g = dot(x_ref[here, :width], w_gate_ref[...]) + dot(low[:, :rank], gate_b_ref[...])
        pl.when(i == 0)(lambda: wait(up_in))
        u = dot(x_ref[here, :width], w_up_ref[...]) + dot(low[:, rank:], up_b_ref[...])
        inner = (g / (1.0 + jnp.exp(-g)) * u).astype(jnp.bfloat16)
        pl.when(i == 0)(lambda: wait(down_in))
        low = (adapter_scale * dot(inner, down_a_ref[...])).astype(jnp.bfloat16)[:, :rank]
        out = (dot(inner, w_down_ref[...]) + dot(low, down_b_ref[...])) * mine

        @pl.when(i < len(pieces) // 2)
        def _():
            kept_ref[here, :] = out
            pltpu.make_async_copy(
                kept_ref.at[here], kept_hbm.at[here], out_sem.at[i]
            ).start()

        @pl.when(i >= len(pieces) // 2)
        def _():
            there = pl.ds(pl.multiple_of(i * rows - own, rows), rows)
            sent_ref[there, :] = out.astype(jnp.bfloat16)
            pltpu.make_async_copy(
                sent_ref.at[there], sent_hbm.at[there], out_sem.at[i]
            ).start()

        return carry

    lax.fori_loop(0, len(pieces), run_piece, 0)
    for i in range(len(pieces)):
        src, dst = (kept_ref, kept_hbm) if i < len(pieces) // 2 else (sent_ref, sent_hbm)
        at = pl.ds(i % (len(pieces) // 2) * rows, rows)
        pltpu.make_async_copy(src.at[at], dst.at[at], out_sem.at[i]).wait()


def run_expert(place, pieces, low_rank, w_gate, w_up, w_down):
    units, width = w_down.shape
    total = sum(p.shape[0] for p in pieces)
    own = total // 2
    a_gu, gate_b, up_b, down_a, down_b = low_rank
    rank = down_b.shape[0]
    outs = [
        jax.ShapeDtypeStruct((own, width), jnp.float32),
        jax.ShapeDtypeStruct((total - own, width), jnp.bfloat16),
    ]
    kept = [a_gu, gate_b, up_b, down_a, down_b, w_gate, w_up, w_down]
    copies = len(pieces) + 5 + 3 * 4
    return pl.pallas_call(
        functools.partial(expert_kernel, len(pieces)),
        out_shape=outs,
        in_specs=[pl.BlockSpec(memory_space=pltpu.SMEM)]
        + [pl.BlockSpec(memory_space=pl.ANY)] * (len(pieces) + len(low_rank))
        + [pl.BlockSpec(memory_space=pltpu.HBM)] * 3,
        out_specs=[pl.BlockSpec(memory_space=pl.ANY)] * 2,
        scratch_shapes=[pltpu.VMEM((total, pieces[0].shape[1]), jnp.bfloat16)]
        + [pltpu.VMEM(a.shape, a.dtype) for a in kept]
        + [
            pltpu.VMEM(outs[0].shape, outs[0].dtype),
            pltpu.VMEM(outs[1].shape, outs[1].dtype),
            pltpu.SemaphoreType.DMA((copies,)),
            pltpu.SemaphoreType.DMA((len(pieces),)),
        ],
        compiler_params=pltpu.CompilerParams(vmem_limit_bytes=EXPERT_GRANT),
        cost_estimate=pl.CostEstimate(
            flops=2 * total * units * (3 * width + 4 * rank) + 8 * total * width * rank,
            bytes_accessed=6 * units * width + 5 * total * width,
            transcendentals=total * units,
        ),
        name="run_expert",
    )(place, *pieces, *kept)


def dense_shards(
    hidden, route_ids, route_logits, placement, factors, w_gate, w_up, down_weight
):
    owners = lax.axis_size("expert")
    experts = placement.shape[0]
    steps, rows, width = hidden.shape
    units = w_gate.shape[2]
    rank = factors.shape[1] * owners // (3 * (width + units))
    outer, middle, cores = split_axis(owners)
    along_outer, along_middle = (middle * cores, outer), (cores, middle)
    place = jnp.stack([lax.axis_index("group"), lax.axis_index("expert")]).astype(jnp.int32)

    first = max(1, steps * 2 // 3)
    head, tail = make_payload(hidden, route_ids, route_logits, experts, first)
    head, factors = lax.optimization_barrier((head, factors))
    tail = gather_along(tail, owners, *along_middle)
    head = gather_along(head, owners, *along_outer)
    blocks = order_factors(place, placement, factors, owners)
    blocks = [blocks[0]] + [shift(blocks[r], owners, *along_middle, r) for r in range(1, middle)]
    head, blocks = lax.optimization_barrier((head, blocks))
    here, there = exchange_factors(blocks, owners)
    heads = [head] + [shift(head, owners, *along_middle, k) for k in range(1, middle)]
    heads += [shift(p, owners, 1, cores, 1) for p in heads]
    tail, there = lax.optimization_barrier((tail, there))
    tail = gather_along(tail, owners, *along_outer)
    tails = [tail, shift(tail, owners, 1, cores, 1)]

    low_rank = relayout_factors(place, here, there, width, units, rank, owners)
    weights = (w_gate[0], w_up[0], down_weight[0])
    head, head_sent = run_expert(place, heads, low_rank, *weights)
    tail, tail_sent = run_expert(place, tails, low_rank, *weights)
    head = head + shift(head_sent, owners, 1, cores, 1).astype(jnp.float32)
    tail = tail + shift(tail_sent, owners, 1, cores, 1).astype(jnp.float32)
    head = scatter_along(head, owners, *along_middle)
    tail = scatter_along(tail, owners, *along_outer)
    head = scatter_along(head, owners, *along_outer)
    tail = scatter_along(tail, owners, *along_middle)
    return jnp.concatenate([head, tail]).astype(jnp.bfloat16).reshape(steps, rows, width)


def row_capacity(rows, top, experts):
    return min(rows, 3 * max(1, rows * top // experts))


def unpack_factors(flat_factors, width, hidden_units, rank_size):
    layouts = [
        (width, rank_size),
        (rank_size, hidden_units),
        (width, rank_size),
        (rank_size, hidden_units),
        (hidden_units, rank_size),
        (rank_size, width),
    ]
    offset = 0
    segments = []
    for leading, trailing in layouts:
        segments.append(
            flat_factors[offset : offset + leading * trailing].reshape(leading, trailing)
        )
        offset = offset + leading * trailing
    return segments


def merge_weight(loaded_weights, factor_a, factor_b):
    adapter_delta = jnp.dot(factor_a, factor_b, preferred_element_type=jnp.float32)
    return (loaded_weights.astype(jnp.float32) + adapter_scale * adapter_delta).astype(jnp.bfloat16)


def apply_expert_block(inputs, merged_gate, merged_up, combined_down_weight):
    gate_part = jnp.dot(inputs, merged_gate, preferred_element_type=jnp.float32)
    up_part = jnp.dot(inputs, merged_up, preferred_element_type=jnp.float32)
    inner = (jax.nn.silu(gate_part) * up_part).astype(jnp.bfloat16)
    return jnp.dot(inner, combined_down_weight, preferred_element_type=jnp.float32).astype(
        jnp.bfloat16
    )


def sparse_shards(hidden, route_ids, route_logits, placement, factors, w_gate, w_up, down_weight):
    owners = lax.axis_size("expert")
    experts = placement.shape[0]
    steps_count, row_count, width = hidden.shape
    top_count = route_ids.shape[2]
    hidden_units = w_gate.shape[2]
    rank_size = factors.shape[1] * owners // (3 * (width + hidden_units))
    capacity = row_capacity(row_count, top_count, experts)
    slot_of = (
        jnp.zeros((experts,), jnp.int32).at[placement].set(jnp.arange(experts, dtype=jnp.int32))
    )
    ordered = jnp.take(factors, slot_of, axis=0)
    received = lax.all_to_all(ordered, "expert", split_axis=0, concat_axis=1, tiled=True)
    segments = unpack_factors(received[0], width, hidden_units, rank_size)
    merged_gate = merge_weight(w_gate[0], segments[0], segments[1])
    merged_up = merge_weight(w_up[0], segments[2], segments[3])
    combined_down_weight = merge_weight(down_weight[0], segments[4], segments[5])

    def layout(step_index):
        ids_flat = route_ids[step_index].reshape(-1)
        onehot = (ids_flat[:, None] == jnp.arange(experts, dtype=jnp.int32)[None, :]).astype(
            jnp.int32
        )
        position = jnp.sum((jnp.cumsum(onehot, axis=0) - 1) * onehot, axis=1)
        target = ids_flat * capacity + position
        placed = (
            jnp.arange(experts * capacity, dtype=jnp.int32)[:, None] == target[None, :]
        ).astype(jnp.bfloat16)
        pair_rows = jnp.repeat(hidden[step_index], top_count, axis=0)
        outgoing = jnp.dot(placed, pair_rows, preferred_element_type=jnp.float32).astype(
            jnp.bfloat16
        )
        outgoing = outgoing.reshape(experts, 1, capacity, width)
        gates = route_gates(route_logits[step_index]).reshape(-1)
        weighted = placed * gates[None, :]
        return (outgoing, weighted)

    layouts_all = [layout(step_index) for step_index in range(steps_count)]
    results = []
    for step_index in range(steps_count):
        outgoing, weighted = layouts_all[step_index]
        arrived = lax.all_to_all(outgoing, "expert", split_axis=0, concat_axis=1, tiled=True)
        outputs = apply_expert_block(
            arrived.reshape(-1, width), merged_gate, merged_up, combined_down_weight
        )
        outputs = outputs.reshape(arrived.shape)
        returned = lax.all_to_all(outputs, "expert", split_axis=1, concat_axis=0, tiled=True)
        flat_back = returned.reshape(experts * capacity, width)
        pair_out = jnp.einsum("cp,cd->pd", weighted, flat_back, preferred_element_type=jnp.float32)
        results.append(
            pair_out.reshape(row_count, top_count, width).sum(axis=1).astype(jnp.bfloat16)
        )
    return jnp.stack(results, axis=0)


def shards(hidden, route_ids, route_logits, placement, factors, w_gate, w_up, down_weight):
    rows, top = route_ids.shape[1:]
    width, units = w_gate.shape[1:]
    owners = lax.axis_size("expert")
    rank = factors.shape[1] * owners // (3 * (width + units))
    dense = row_capacity(rows, top, placement.shape[0]) == rows
    dense = dense and lax.axis_size("group") == 2 and split_axis(owners)[2] == 2
    dense = dense and 2 * rank == LANES and width % 256 == 0 and units % 256 == 0
    dense = dense and factors.shape[1] % (8 * LANES) == 0 and hidden.shape[0] > 1
    return (dense_shards if dense else sparse_shards)(
        hidden, route_ids, route_logits, placement, factors, w_gate, w_up, down_weight
    )


def solution(mesh):
    placed = (
        P(None, ("group", "expert"), None),
        P(None, ("group", "expert"), None),
        P(None, ("group", "expert"), None),
        P(),
        P(None, "expert"),
        P("expert", None, None),
        P("expert", None, None),
        P("expert", None, None),
    )
    return jax.shard_map(
        shards,
        mesh=mesh,
        in_specs=placed,
        out_specs=P(None, ("group", "expert"), None),
        check_vma=False,
    )
```

```python
import functools

import jax
import jax.numpy as jnp
from jax import lax
from jax.experimental import pallas as pl
from jax.experimental.pallas import tpu as pltpu
from jax.sharding import PartitionSpec as P

adapter_scale = 2.0
LANES = 128
GRANT = 16 << 20
EXPERT_GRANT = 32 << 20
WHOLE_GRANT = 60 << 20


def route_gates(logits):
    highest = jnp.max(logits, axis=-1, keepdims=True)
    router_scores = jnp.exp(logits - highest)
    return (router_scores / jnp.sum(router_scores, axis=-1, keepdims=True)).astype(jnp.bfloat16)


def split_axis(n):
    cores = 2 if n % 2 == 0 else 1
    chips = n // cores
    middle = 1
    while chips % (2 * middle) == 0 and 4 * middle * middle <= chips:
        middle *= 2
    return chips // middle, middle, cores


def swap(x, n, stride, k):
    return lax.ppermute(x, "expert", [(i, i ^ (k * stride)) for i in range(n)])


def scatter_along(total, n, stride, size):
    count = total.shape[0] // size
    result = total[:count]
    for k in range(1, size):
        part = total[k * count : (k + 1) * count].astype(jnp.bfloat16)
        result = result + swap(part, n, stride, k).astype(jnp.float32)
    return result


def exchange_factors(blocks, n):
    outer, middle, cores = split_axis(n)
    here, there = [], []
    for q in range(outer):
        pairs = []
        for g in range(2):
            for i in range(n):
                pairs.append((g * n + i, g * n + (i ^ (q * middle * cores) ^ g)))
        part = jnp.stack([block[q] for block in blocks])
        part = lax.ppermute(part, ("group", "expert"), pairs)
        here.append(part)
        there.append(lax.ppermute(part, "group", [(0, 1), (1, 0)]))
    return here, there


def dot(a, b):
    return jnp.dot(a, b, preferred_element_type=jnp.float32)


def payload_kernel(hidden_ref, ids_ref, logits_ref, *refs):
    out_refs, turned_ref = refs[:-1], refs[-1]
    steps, top, rows = ids_ref.shape
    width = hidden_ref.shape[2]
    turned_ref[...] = jnp.zeros_like(turned_ref)
    for s in range(steps):
        logits, ids = logits_ref[s], ids_ref[s]
        scores = jnp.exp(logits - jnp.max(logits, axis=0, keepdims=True))
        gates = scores / jnp.sum(scores, axis=0, keepdims=True)
        expert = lax.broadcasted_iota(jnp.int32, (turned_ref.shape[0], rows), 0)
        dense = jnp.zeros(expert.shape, jnp.float32)
        for k in range(top):
            dense += jnp.where(ids[k : k + 1, :] == expert, gates[k : k + 1, :], 0.0)
        turned_ref[:, s * rows : (s + 1) * rows] = dense
    dense = turned_ref[...].T.astype(jnp.bfloat16)
    s = 0
    for out_ref in out_refs:
        for at in range(0, out_ref.shape[0], rows):
            out_ref[at : at + rows, :width] = hidden_ref[s]
            out_ref[at : at + rows, width:] = dense[s * rows : (s + 1) * rows, :]
            s += 1


def make_payload(hidden, route_ids, route_logits, experts, first):
    steps, rows, width = hidden.shape
    padded = -(-experts // LANES) * LANES
    return pl.pallas_call(
        payload_kernel,
        out_shape=[
            jax.ShapeDtypeStruct((count * rows, width + padded), jnp.bfloat16)
            for count in (first, steps - first)
        ],
        scratch_shapes=[pltpu.VMEM((padded, -(-steps * rows // LANES) * LANES), jnp.float32)],
        compiler_params=pltpu.CompilerParams(vmem_limit_bytes=WHOLE_GRANT),
        name="payload",
    )(hidden, jnp.swapaxes(route_ids, 1, 2), jnp.swapaxes(route_logits, 1, 2))


def order_kernel(middle, place_ref, placement_ref, factors_ref, *refs):
    out_refs, wide_ref = refs[:-1], refs[-1]
    slots = factors_ref.shape[0]
    length, lanes = out_refs[0].shape[1:]
    group, me = place_ref[0], place_ref[1]

    def cut(t, carry):
        start = pl.multiple_of(t * lanes, lanes)
        tile = factors_ref[:, pl.ds(start, lanes)].astype(jnp.float32)
        wide_ref[pl.ds(t, slots, stride=length), :] = tile
        return carry

    lax.fori_loop(0, length, cut, 0, unroll=8)

    def put(s, carry):
        to = placement_ref[s]
        away = to ^ me
        aside, ahead = lax.rem(away // 2, middle), away // (2 * middle)
        ours = lax.rem(away, 2) == group
        rows = wide_ref[pl.ds(pl.multiple_of(s * length, 8), length), :].astype(jnp.bfloat16)
        for r, out_ref in enumerate(out_refs):

            @pl.when(jnp.logical_and(ours, aside == r))
            def _():
                out_ref[ahead] = rows

        return carry

    lax.fori_loop(0, slots, put, 0)


def order_factors(place, placement, factors, n):
    outer, middle, _ = split_axis(n)
    slots, entries = factors.shape
    length = entries // LANES
    return pl.pallas_call(
        functools.partial(order_kernel, middle),
        out_shape=[jax.ShapeDtypeStruct((outer, length, LANES), jnp.bfloat16)] * middle,
        in_specs=[
            pl.BlockSpec(memory_space=pltpu.SMEM),
            pl.BlockSpec(memory_space=pltpu.SMEM),
            pl.BlockSpec(memory_space=pltpu.VMEM),
        ],
        scratch_shapes=[pltpu.VMEM((slots * length, LANES), jnp.float32)],
        compiler_params=pltpu.CompilerParams(vmem_limit_bytes=WHOLE_GRANT),
        name="order_factors",
    )(place, placement, factors)


def relayout_kernel(outer, middle, place_ref, *refs):
    pieces = refs[: 2 * outer]
    a_gu_ref, gate_b_ref, up_b_ref, down_a_ref, down_b_ref, flat_ref, wide_ref = refs[2 * outer :]
    width, units = a_gu_ref.shape[0], gate_b_ref.shape[1]
    rank = gate_b_ref.shape[0]
    length = pieces[0].shape[1]
    group, me = place_ref[0], place_ref[1]
    for i, piece in enumerate(pieces):
        swapped, q = i // outer, i % outer
        core = group if swapped == 0 else 1 - group
        for r in range(middle):
            source = me ^ ((q * middle + r) * 2 + core)
            start = pl.multiple_of(source * length, 8)
            flat_ref[pl.ds(start, length), :] = piece[r].astype(jnp.float32)

    n_wide, n_unit = width // 2, units // 2
    at_ub = 2 * n_wide + n_unit
    at_da = 2 * n_wide + 2 * n_unit
    chunk = 128
    left = lax.broadcasted_iota(jnp.int32, (chunk, LANES), 1) < rank

    def load(start):
        return flat_ref[pl.ds(pl.multiple_of(start, 128), chunk), :]

    def gate_up(i, carry):
        g, u = load(i * chunk), load(n_wide + n_unit + i * chunk)
        at = 2 * i * chunk
        wide_ref[pl.ds(at, chunk, stride=2), :] = jnp.where(left, g, pltpu.roll(u, rank, 1))
        wide_ref[pl.ds(at + 1, chunk, stride=2), :] = jnp.where(left, pltpu.roll(g, rank, 1), u)
        both = wide_ref[pl.ds(pl.multiple_of(at, 128), 2 * chunk), :]
        a_gu_ref[pl.ds(pl.multiple_of(at, 128), 2 * chunk), :] = both.astype(jnp.bfloat16)
        return carry

    lax.fori_loop(0, n_wide // chunk, gate_up, 0, unroll=2)
    for i in range(n_unit // chunk):
        d = load(at_da + i * chunk)
        at = 2 * i * chunk
        wide_ref[pl.ds(at, chunk, stride=2), :] = jnp.where(left, d, 0.0)
        wide_ref[pl.ds(at + 1, chunk, stride=2), :] = jnp.where(left, pltpu.roll(d, rank, 1), 0.0)
        down_a_ref[at : at + 2 * chunk, :] = wide_ref[at : at + 2 * chunk, :].astype(jnp.bfloat16)
    for start, b_ref in (
        (n_wide, gate_b_ref),
        (at_ub, up_b_ref),
        (at_da + n_unit, down_b_ref),
    ):
        tiles = b_ref.shape[1] // LANES
        for j in range(tiles):
            row = flat_ref[pl.ds(start + j, rank, stride=tiles), :]
            b_ref[:, j * LANES : (j + 1) * LANES] = row.astype(jnp.bfloat16)


def relayout_factors(place, here, there, width, units, rank, n):
    outer, middle, _ = split_axis(n)
    shapes = [(width, 2 * rank), (rank, units), (rank, units), (units, 2 * rank), (rank, width)]
    length = here[0].shape[1]
    return pl.pallas_call(
        functools.partial(relayout_kernel, outer, middle),
        out_shape=[jax.ShapeDtypeStruct(shape, jnp.bfloat16) for shape in shapes],
        in_specs=[pl.BlockSpec(memory_space=pltpu.SMEM)]
        + [pl.BlockSpec(memory_space=pltpu.VMEM)] * (2 * outer),
        scratch_shapes=[
            pltpu.VMEM((n * length, LANES), jnp.float32),
            pltpu.VMEM((width, LANES), jnp.float32),
        ],
        compiler_params=pltpu.CompilerParams(vmem_limit_bytes=GRANT),
        name="relayout_factors",
    )(place, *here, *there)


class Loads:
    def __init__(self, sem):
        self.sem, self.count = sem, 0

    def begin(self, src, dst):
        copy = pltpu.make_async_copy(src, dst, self.sem.at[self.count])
        copy.start()
        self.count += 1
        return [copy]

    def begin_rows(self, src, dst, parts=4):
        step = src.shape[0] // parts
        cuts = [pl.ds(at, step) for at in range(0, src.shape[0], step)]
        return sum([self.begin(src.at[cut], dst.at[cut]) for cut in cuts], [])


def wait(copies):
    for copy in copies:
        copy.wait()


def base_kernel(count, *refs):
    pieces = refs[:count]
    w_gate_hbm, w_up_hbm, gate_hbm, up_hbm, x_ref, w_gate_ref, w_up_ref = refs[count : count + 7]
    gate_ref, up_ref, sem, out_sem = refs[count + 7 :]
    rows = pieces[0].shape[0]
    width = w_gate_ref.shape[0]
    total = gate_ref.shape[0]
    block = min(128, total)
    loads = Loads(sem)
    x_in = [loads.begin(p, x_ref.at[pl.ds(i * rows, rows)]) for i, p in enumerate(pieces)]
    x_in = sum(x_in, [])
    gate_in = loads.begin_rows(w_gate_hbm, w_gate_ref)
    up_in = loads.begin_rows(w_up_hbm, w_up_ref)
    wait(x_in)

    def store(i):
        here = pl.ds(pl.multiple_of(i * block, block), block)
        return [
            pltpu.make_async_copy(src.at[here], dst.at[here], out_sem.at[j, i])
            for j, (src, dst) in enumerate(((gate_ref, gate_hbm), (up_ref, up_hbm)))
        ]

    def run_block(i, carry):
        here = pl.ds(pl.multiple_of(i * block, block), block)
        pl.when(i == 0)(lambda: wait(gate_in))
        gate_ref[here, :] = dot(x_ref[here, :width], w_gate_ref[...])
        pl.when(i == 0)(lambda: wait(up_in))
        up_ref[here, :] = dot(x_ref[here, :width], w_up_ref[...])
        for copy in store(i):
            copy.start()
        return carry

    lax.fori_loop(0, total // block, run_block, 0)
    for i in range(total // block):
        wait(store(i))


def base_products(pieces, w_gate, w_up):
    width, units = w_gate.shape
    total = sum(p.shape[0] for p in pieces)
    out = jax.ShapeDtypeStruct((total, units), jnp.float32)
    return pl.pallas_call(
        functools.partial(base_kernel, len(pieces)),
        out_shape=[out, out],
        in_specs=[pl.BlockSpec(memory_space=pl.ANY)] * len(pieces)
        + [pl.BlockSpec(memory_space=pltpu.HBM)] * 2,
        out_specs=[pl.BlockSpec(memory_space=pl.ANY)] * 2,
        scratch_shapes=[
            pltpu.VMEM((total, pieces[0].shape[1]), jnp.bfloat16),
            pltpu.VMEM(w_gate.shape, w_gate.dtype),
            pltpu.VMEM(w_up.shape, w_up.dtype),
            pltpu.VMEM(out.shape, out.dtype),
            pltpu.VMEM(out.shape, out.dtype),
            pltpu.SemaphoreType.DMA((len(pieces) + 8,)),
            pltpu.SemaphoreType.DMA((2, total // min(128, total))),
        ],
        compiler_params=pltpu.CompilerParams(vmem_limit_bytes=EXPERT_GRANT),
        cost_estimate=pl.CostEstimate(
            flops=4 * total * width * units,
            bytes_accessed=4 * width * units + 2 * total * width + 8 * total * units,
            transcendentals=0,
        ),
        name="base_products",
    )(*pieces, w_gate, w_up)


def finish_kernel(count, first, rows, place_ref, *refs):
    pieces, refs = refs[:count], refs[count:]
    gate_hbm, up_hbm, a_gu_hbm, gate_b_hbm, up_b_hbm, down_a_hbm, down_b_hbm = refs[:7]
    w_down_hbm, kept_hbm, sent_hbm, x_ref, gate_ref, up_ref = refs[7:13]
    a_gu_ref, gate_b_ref, up_b_ref, down_a_ref, down_b_ref, w_down_ref = refs[13:19]
    kept_ref, sent_ref, sem, out_sem = refs[19:]
    span = pieces[0].shape[0]
    units, width = w_down_ref.shape
    rank = gate_b_ref.shape[0]
    own = kept_ref.shape[0]
    block = min(128, own)
    loads = Loads(sem)
    x_in, base_in = [], []
    for i, piece in enumerate(pieces):
        x_in += loads.begin(piece.at[pl.ds(first, rows)], x_ref.at[pl.ds(i * rows, rows)])
    x_in += loads.begin(a_gu_hbm, a_gu_ref)
    x_in += loads.begin(gate_b_hbm, gate_b_ref) + loads.begin(up_b_hbm, up_b_ref)
    for i in range(count):
        src, dst = pl.ds(i * span + first, rows), pl.ds(i * rows, rows)
        base_in += loads.begin(gate_hbm.at[src], gate_ref.at[dst])
        base_in += loads.begin(up_hbm.at[src], up_ref.at[dst])
    down_in = loads.begin(down_a_hbm, down_a_ref) + loads.begin(down_b_hbm, down_b_ref)
    down_in += loads.begin_rows(w_down_hbm, w_down_ref)
    wait(x_in)

    def run_block(i, carry):
        here = pl.ds(pl.multiple_of(i * block, block), block)
        gates = x_ref[here, width:].astype(jnp.float32)
        lane = lax.broadcasted_iota(jnp.int32, gates.shape, 1)
        mine = jnp.sum(jnp.where(lane == place_ref[1], gates, 0.0), axis=1, keepdims=True)
        low = (adapter_scale * dot(x_ref[here, :width], a_gu_ref[...])).astype(jnp.bfloat16)
        pl.when(i == 0)(lambda: wait(base_in))
        g = gate_ref[here, :] + dot(low[:, :rank], gate_b_ref[...])
        u = up_ref[here, :] + dot(low[:, rank:], up_b_ref[...])
        inner = (g / (1.0 + jnp.exp(-g)) * u).astype(jnp.bfloat16)
        pl.when(i == 0)(lambda: wait(down_in))
        low = (adapter_scale * dot(inner, down_a_ref[...])).astype(jnp.bfloat16)[:, :rank]
        out = (dot(inner, w_down_ref[...]) + dot(low, down_b_ref[...])) * mine

        @pl.when(i < own // block)
        def _():
            kept_ref[here, :] = out
            pltpu.make_async_copy(kept_ref.at[here], kept_hbm.at[here], out_sem.at[i]).start()

        @pl.when(i >= own // block)
        def _():
            there = pl.ds(pl.multiple_of(i * block - own, block), block)
            sent_ref[there, :] = out.astype(jnp.bfloat16)
            pltpu.make_async_copy(sent_ref.at[there], sent_hbm.at[there], out_sem.at[i]).start()

        return carry

    lax.fori_loop(0, 2 * own // block, run_block, 0)
    for i in range(2 * own // block):
        src, dst = (kept_ref, kept_hbm) if i < own // block else (sent_ref, sent_hbm)
        at = pl.ds(i % (own // block) * block, block)
        pltpu.make_async_copy(src.at[at], dst.at[at], out_sem.at[i]).wait()


def finish_step(place, pieces, base, first, rows, low_rank, w_down):
    units, width = w_down.shape
    total = rows * len(pieces)
    own = total // 2
    a_gu, gate_b, up_b, down_a, down_b = low_rank
    rank = down_b.shape[0]
    outs = [
        jax.ShapeDtypeStruct((own, width), jnp.float32),
        jax.ShapeDtypeStruct((own, width), jnp.bfloat16),
    ]
    held = [*low_rank, w_down]
    return pl.pallas_call(
        functools.partial(finish_kernel, len(pieces), first, rows),
        out_shape=outs,
        in_specs=[pl.BlockSpec(memory_space=pltpu.SMEM)]
        + [pl.BlockSpec(memory_space=pl.ANY)] * (len(pieces) + 2 + len(low_rank))
        + [pl.BlockSpec(memory_space=pltpu.HBM)],
        out_specs=[pl.BlockSpec(memory_space=pl.ANY)] * 2,
        scratch_shapes=[
            pltpu.VMEM((total, pieces[0].shape[1]), jnp.bfloat16),
            pltpu.VMEM((total, units), jnp.float32),
            pltpu.VMEM((total, units), jnp.float32),
        ]
        + [pltpu.VMEM(a.shape, a.dtype) for a in held]
        + [pltpu.VMEM(o.shape, o.dtype) for o in outs]
        + [
            pltpu.SemaphoreType.DMA((3 * len(pieces) + 9,)),
            pltpu.SemaphoreType.DMA((2 * own // min(128, own),)),
        ],
        compiler_params=pltpu.CompilerParams(vmem_limit_bytes=EXPERT_GRANT),
        cost_estimate=pl.CostEstimate(
            flops=2 * total * units * (width + 4 * rank) + 8 * total * width * rank,
            bytes_accessed=2 * units * width + 5 * total * width + 8 * total * units,
            transcendentals=total * units,
        ),
        name="finish_step",
    )(place, *pieces, *base, *held)


def dense_shards(
    hidden, route_ids, route_logits, placement, factors, w_gate, w_up, down_weight
):
    owners = lax.axis_size("expert")
    experts = placement.shape[0]
    steps, rows, width = hidden.shape
    units = w_gate.shape[2]
    rank = factors.shape[1] * owners // (3 * (width + units))
    outer, middle, cores = split_axis(owners)
    along_outer, along_middle = (middle * cores, outer), (cores, middle)
    place = jnp.stack([lax.axis_index("group"), lax.axis_index("expert")]).astype(jnp.int32)

    def along(x, stride, size):
        return [x] + [swap(x, owners, stride, k) for k in range(1, size)]

    def by_step(pieces, count):
        column = jnp.stack([p.reshape(count, rows, -1) for p in pieces], axis=1)
        return column.reshape(count * outer * rows, -1)

    def across(column):
        sheet = along(column, *along_middle)
        return sheet + [swap(p, owners, 1, 1) for p in sheet]

    first = max(1, steps * 2 // 3)
    head, tail = make_payload(hidden, route_ids, route_logits, experts, first)
    head, factors = lax.optimization_barrier((head, factors))
    head = by_step(along(head, *along_outer), first)
    blocks = order_factors(place, placement, factors, owners)
    blocks = [blocks[0]] + [swap(blocks[r], owners, cores, r) for r in range(1, middle)]
    head, blocks = lax.optimization_barrier((head, blocks))
    here, there = exchange_factors(blocks, owners)
    heads = across(head)
    tail, here[1], heads[1] = lax.optimization_barrier((tail, here[1], heads[1]))
    tails = across(by_step(along(tail, *along_outer), steps - first))
    head_base = base_products(heads, w_gate[0], w_up[0])
    here, there, head_base = lax.optimization_barrier((here, there, head_base))
    low_rank = relayout_factors(place, here, there, width, units, rank, owners)

    span = outer * rows
    results = []
    for s in range(steps):
        at = s if s < first else s - first
        pieces, base = (heads, head_base) if s < first else (tails, None)
        if base is None:
            pieces, summed = lax.optimization_barrier((pieces, results[0]))
            results[0] = summed
            base = base_products(pieces, w_gate[0], w_up[0])
        kept, sent = finish_step(
            place, pieces, base, at * span, span, low_rank, down_weight[0]
        )
        results.append(kept + swap(sent, owners, 1, 1).astype(jnp.float32))
    results = [scatter_along(total, owners, *along_middle) for total in results]
    results = [scatter_along(total, owners, *along_outer) for total in results]
    return jnp.stack(results).astype(jnp.bfloat16)


def row_capacity(rows, top, experts):
    return min(rows, 3 * max(1, rows * top // experts))


def unpack_factors(flat_factors, width, hidden_units, rank_size):
    layouts = [
        (width, rank_size),
        (rank_size, hidden_units),
        (width, rank_size),
        (rank_size, hidden_units),
        (hidden_units, rank_size),
        (rank_size, width),
    ]
    offset = 0
    segments = []
    for leading, trailing in layouts:
        segments.append(
            flat_factors[offset : offset + leading * trailing].reshape(leading, trailing)
        )
        offset = offset + leading * trailing
    return segments


def merge_weight(loaded_weights, factor_a, factor_b):
    adapter_delta = jnp.dot(factor_a, factor_b, preferred_element_type=jnp.float32)
    return (loaded_weights.astype(jnp.float32) + adapter_scale * adapter_delta).astype(jnp.bfloat16)


def apply_expert_block(inputs, merged_gate, merged_up, combined_down_weight):
    gate_part = jnp.dot(inputs, merged_gate, preferred_element_type=jnp.float32)
    up_part = jnp.dot(inputs, merged_up, preferred_element_type=jnp.float32)
    inner = (jax.nn.silu(gate_part) * up_part).astype(jnp.bfloat16)
    return jnp.dot(inner, combined_down_weight, preferred_element_type=jnp.float32).astype(
        jnp.bfloat16
    )


def sparse_shards(hidden, route_ids, route_logits, placement, factors, w_gate, w_up, down_weight):
    owners = lax.axis_size("expert")
    experts = placement.shape[0]
    steps_count, row_count, width = hidden.shape
    top_count = route_ids.shape[2]
    hidden_units = w_gate.shape[2]
    rank_size = factors.shape[1] * owners // (3 * (width + hidden_units))
    capacity = row_capacity(row_count, top_count, experts)
    slot_of = (
        jnp.zeros((experts,), jnp.int32).at[placement].set(jnp.arange(experts, dtype=jnp.int32))
    )
    ordered = jnp.take(factors, slot_of, axis=0)
    received = lax.all_to_all(ordered, "expert", split_axis=0, concat_axis=1, tiled=True)
    segments = unpack_factors(received[0], width, hidden_units, rank_size)
    merged_gate = merge_weight(w_gate[0], segments[0], segments[1])
    merged_up = merge_weight(w_up[0], segments[2], segments[3])
    combined_down_weight = merge_weight(down_weight[0], segments[4], segments[5])

    def layout(step_index):
        ids_flat = route_ids[step_index].reshape(-1)
        onehot = (ids_flat[:, None] == jnp.arange(experts, dtype=jnp.int32)[None, :]).astype(
            jnp.int32
        )
        position = jnp.sum((jnp.cumsum(onehot, axis=0) - 1) * onehot, axis=1)
        target = ids_flat * capacity + position
        placed = (
            jnp.arange(experts * capacity, dtype=jnp.int32)[:, None] == target[None, :]
        ).astype(jnp.bfloat16)
        pair_rows = jnp.repeat(hidden[step_index], top_count, axis=0)
        outgoing = jnp.dot(placed, pair_rows, preferred_element_type=jnp.float32).astype(
            jnp.bfloat16
        )
        outgoing = outgoing.reshape(experts, 1, capacity, width)
        gates = route_gates(route_logits[step_index]).reshape(-1)
        weighted = placed * gates[None, :]
        return (outgoing, weighted)

    layouts_all = [layout(step_index) for step_index in range(steps_count)]
    results = []
    for step_index in range(steps_count):
        outgoing, weighted = layouts_all[step_index]
        arrived = lax.all_to_all(outgoing, "expert", split_axis=0, concat_axis=1, tiled=True)
        outputs = apply_expert_block(
            arrived.reshape(-1, width), merged_gate, merged_up, combined_down_weight
        )
        outputs = outputs.reshape(arrived.shape)
        returned = lax.all_to_all(outputs, "expert", split_axis=1, concat_axis=0, tiled=True)
        flat_back = returned.reshape(experts * capacity, width)
        pair_out = jnp.einsum("cp,cd->pd", weighted, flat_back, preferred_element_type=jnp.float32)
        results.append(
            pair_out.reshape(row_count, top_count, width).sum(axis=1).astype(jnp.bfloat16)
        )
    return jnp.stack(results, axis=0)


def shards(hidden, route_ids, route_logits, placement, factors, w_gate, w_up, down_weight):
    rows, top = route_ids.shape[1:]
    width, units = w_gate.shape[1:]
    owners = lax.axis_size("expert")
    rank = factors.shape[1] * owners // (3 * (width + units))
    dense = row_capacity(rows, top, placement.shape[0]) == rows
    dense = dense and lax.axis_size("group") == 2 and split_axis(owners)[2] == 2
    outer = split_axis(owners)[0]
    dense = dense and outer > 1 and outer & (outer - 1) == 0 and split_axis(owners)[1] > 1
    dense = dense and 2 * rank == LANES and width % 256 == 0 and units % 256 == 0
    dense = dense and factors.shape[1] % (8 * LANES) == 0 and hidden.shape[0] > 1
    return (dense_shards if dense else sparse_shards)(
        hidden, route_ids, route_logits, placement, factors, w_gate, w_up, down_weight
    )


def solution(mesh):
    placed = (
        P(None, ("group", "expert"), None),
        P(None, ("group", "expert"), None),
        P(None, ("group", "expert"), None),
        P(),
        P(None, "expert"),
        P("expert", None, None),
        P("expert", None, None),
        P("expert", None, None),
    )
    return jax.shard_map(
        shards,
        mesh=mesh,
        in_specs=placed,
        out_specs=P(None, ("group", "expert"), None),
        check_vma=False,
    )
```

```python
import functools

import jax
import jax.numpy as jnp
from jax import lax
from jax.experimental import pallas as pl
from jax.experimental.pallas import tpu as pltpu
from jax.sharding import PartitionSpec as P

adapter_scale = 2.0
LANES = 128
GRANT = 16 << 20
EXPERT_GRANT = 32 << 20
WHOLE_GRANT = 60 << 20
LITTLE = pl.CostEstimate(flops=1, bytes_accessed=1, transcendentals=0)


def route_gates(logits):
    highest = jnp.max(logits, axis=-1, keepdims=True)
    router_scores = jnp.exp(logits - highest)
    return (router_scores / jnp.sum(router_scores, axis=-1, keepdims=True)).astype(jnp.bfloat16)


def split_axis(n):
    cores = 2 if n % 2 == 0 else 1
    chips = n // cores
    middle = 1
    while chips % (2 * middle) == 0 and 4 * middle * middle <= chips:
        middle *= 2
    return chips // middle, middle, cores


def swap(x, n, stride, k):
    return lax.ppermute(x, "expert", [(i, i ^ (k * stride)) for i in range(n)])


def scatter_along(total, n, stride, size):
    count = total.shape[0] // size
    result = total[:count]
    for k in range(1, size):
        part = total[k * count : (k + 1) * count].astype(jnp.bfloat16)
        result = result + swap(part, n, stride, k).astype(jnp.float32)
    return result


def exchange_factors(blocks, n):
    outer, middle, cores = split_axis(n)
    here, there = [], []
    for q in range(outer):
        pairs = []
        for g in range(2):
            for i in range(n):
                pairs.append((g * n + i, g * n + (i ^ (q * middle * cores) ^ g)))
        part = jnp.stack([block[q] for block in blocks])
        part = lax.ppermute(part, ("group", "expert"), pairs)
        here.append(part)
        there.append(lax.ppermute(part, "group", [(0, 1), (1, 0)]))
    return here, there


def dot(a, b):
    return jnp.dot(a, b, preferred_element_type=jnp.float32)


def payload_kernel(hidden_ref, ids_ref, logits_ref, *refs):
    out_refs, turned_ref = refs[:-1], refs[-1]
    steps, top, rows = ids_ref.shape
    width = hidden_ref.shape[2]
    turned_ref[...] = jnp.zeros_like(turned_ref)
    for s in range(steps):
        logits, ids = logits_ref[s], ids_ref[s]
        scores = jnp.exp(logits - jnp.max(logits, axis=0, keepdims=True))
        gates = scores / jnp.sum(scores, axis=0, keepdims=True)
        expert = lax.broadcasted_iota(jnp.int32, (turned_ref.shape[0], rows), 0)
        dense = jnp.zeros(expert.shape, jnp.float32)
        for k in range(top):
            dense += jnp.where(ids[k : k + 1, :] == expert, gates[k : k + 1, :], 0.0)
        turned_ref[:, s * rows : (s + 1) * rows] = dense
    dense = turned_ref[...].T.astype(jnp.bfloat16)
    s = 0
    for out_ref in out_refs:
        for at in range(0, out_ref.shape[0], rows):
            out_ref[at : at + rows, :width] = hidden_ref[s]
            out_ref[at : at + rows, width:] = dense[s * rows : (s + 1) * rows, :]
            s += 1


def make_payload(hidden, route_ids, route_logits, experts, first):
    steps, rows, width = hidden.shape
    padded = -(-experts // LANES) * LANES
    return pl.pallas_call(
        payload_kernel,
        out_shape=[
            jax.ShapeDtypeStruct((count * rows, width + padded), jnp.bfloat16)
            for count in (first, steps - first)
        ],
        scratch_shapes=[pltpu.VMEM((padded, -(-steps * rows // LANES) * LANES), jnp.float32)],
        compiler_params=pltpu.CompilerParams(vmem_limit_bytes=WHOLE_GRANT),
        cost_estimate=LITTLE,
        name="payload",
    )(hidden, jnp.swapaxes(route_ids, 1, 2), jnp.swapaxes(route_logits, 1, 2))


def order_kernel(middle, place_ref, placement_ref, factors_ref, *refs):
    out_refs, wide_ref = refs[:-1], refs[-1]
    slots = factors_ref.shape[0]
    length, lanes = out_refs[0].shape[1:]
    group, me = place_ref[0], place_ref[1]

    def cut(t, carry):
        start = pl.multiple_of(t * lanes, lanes)
        tile = factors_ref[:, pl.ds(start, lanes)].astype(jnp.float32)
        wide_ref[pl.ds(t, slots, stride=length), :] = tile
        return carry

    lax.fori_loop(0, length, cut, 0, unroll=8)

    def put(s, carry):
        to = placement_ref[s]
        away = to ^ me
        aside, ahead = lax.rem(away // 2, middle), away // (2 * middle)
        ours = lax.rem(away, 2) == group
        rows = wide_ref[pl.ds(pl.multiple_of(s * length, 8), length), :].astype(jnp.bfloat16)
        for r, out_ref in enumerate(out_refs):

            @pl.when(jnp.logical_and(ours, aside == r))
            def _():
                out_ref[ahead] = rows

        return carry

    lax.fori_loop(0, slots, put, 0)


def order_factors(place, placement, factors, n):
    outer, middle, _ = split_axis(n)
    slots, entries = factors.shape
    length = entries // LANES
    return pl.pallas_call(
        functools.partial(order_kernel, middle),
        out_shape=[jax.ShapeDtypeStruct((outer, length, LANES), jnp.bfloat16)] * middle,
        in_specs=[
            pl.BlockSpec(memory_space=pltpu.SMEM),
            pl.BlockSpec(memory_space=pltpu.SMEM),
            pl.BlockSpec(memory_space=pltpu.VMEM),
        ],
        scratch_shapes=[pltpu.VMEM((slots * length, LANES), jnp.float32)],
        compiler_params=pltpu.CompilerParams(vmem_limit_bytes=WHOLE_GRANT),
        cost_estimate=LITTLE,
        name="order_factors",
    )(place, placement, factors)


def relayout_kernel(outer, middle, place_ref, *refs):
    pieces = refs[: 2 * outer]
    a_gu_ref, gate_b_ref, up_b_ref, down_a_ref, down_b_ref, flat_ref, wide_ref = refs[2 * outer :]
    width, units = a_gu_ref.shape[0], gate_b_ref.shape[1]
    rank = gate_b_ref.shape[0]
    length = pieces[0].shape[1]
    group, me = place_ref[0], place_ref[1]
    for i, piece in enumerate(pieces):
        swapped, q = i // outer, i % outer
        core = group if swapped == 0 else 1 - group
        for r in range(middle):
            source = me ^ ((q * middle + r) * 2 + core)
            start = pl.multiple_of(source * length, 8)
            flat_ref[pl.ds(start, length), :] = piece[r].astype(jnp.float32)

    n_wide, n_unit = width // 2, units // 2
    at_ub = 2 * n_wide + n_unit
    at_da = 2 * n_wide + 2 * n_unit
    chunk = 128
    left = lax.broadcasted_iota(jnp.int32, (chunk, LANES), 1) < rank

    def load(start):
        return flat_ref[pl.ds(pl.multiple_of(start, 128), chunk), :]

    def gate_up(i, carry):
        g, u = load(i * chunk), load(n_wide + n_unit + i * chunk)
        at = 2 * i * chunk
        wide_ref[pl.ds(at, chunk, stride=2), :] = jnp.where(left, g, pltpu.roll(u, rank, 1))
        wide_ref[pl.ds(at + 1, chunk, stride=2), :] = jnp.where(left, pltpu.roll(g, rank, 1), u)
        both = wide_ref[pl.ds(pl.multiple_of(at, 128), 2 * chunk), :]
        a_gu_ref[pl.ds(pl.multiple_of(at, 128), 2 * chunk), :] = both.astype(jnp.bfloat16)
        return carry

    lax.fori_loop(0, n_wide // chunk, gate_up, 0, unroll=2)
    for i in range(n_unit // chunk):
        d = load(at_da + i * chunk)
        at = 2 * i * chunk
        wide_ref[pl.ds(at, chunk, stride=2), :] = jnp.where(left, d, 0.0)
        wide_ref[pl.ds(at + 1, chunk, stride=2), :] = jnp.where(left, pltpu.roll(d, rank, 1), 0.0)
        down_a_ref[at : at + 2 * chunk, :] = wide_ref[at : at + 2 * chunk, :].astype(jnp.bfloat16)
    for start, b_ref in (
        (n_wide, gate_b_ref),
        (at_ub, up_b_ref),
        (at_da + n_unit, down_b_ref),
    ):
        tiles = b_ref.shape[1] // LANES
        for j in range(tiles):
            row = flat_ref[pl.ds(start + j, rank, stride=tiles), :]
            b_ref[:, j * LANES : (j + 1) * LANES] = row.astype(jnp.bfloat16)


def relayout_factors(place, here, there, width, units, rank, n):
    outer, middle, _ = split_axis(n)
    shapes = [(width, 2 * rank), (rank, units), (rank, units), (units, 2 * rank), (rank, width)]
    length = here[0].shape[1]
    return pl.pallas_call(
        functools.partial(relayout_kernel, outer, middle),
        out_shape=[jax.ShapeDtypeStruct(shape, jnp.bfloat16) for shape in shapes],
        in_specs=[pl.BlockSpec(memory_space=pltpu.SMEM)]
        + [pl.BlockSpec(memory_space=pltpu.VMEM)] * (2 * outer),
        scratch_shapes=[
            pltpu.VMEM((n * length, LANES), jnp.float32),
            pltpu.VMEM((width, LANES), jnp.float32),
        ],
        compiler_params=pltpu.CompilerParams(vmem_limit_bytes=GRANT),
        cost_estimate=LITTLE,
        name="relayout_factors",
    )(place, *here, *there)


class Loads:
    def __init__(self, sem):
        self.sem, self.count = sem, 0

    def begin(self, src, dst):
        copy = pltpu.make_async_copy(src, dst, self.sem.at[self.count])
        copy.start()
        self.count += 1
        return [copy]

    def begin_rows(self, src, dst, parts=4):
        step = src.shape[0] // parts
        cuts = [pl.ds(at, step) for at in range(0, src.shape[0], step)]
        return sum([self.begin(src.at[cut], dst.at[cut]) for cut in cuts], [])


def wait(copies):
    for copy in copies:
        copy.wait()


def base_kernel(count, *refs):
    pieces = refs[:count]
    w_gate_hbm, w_up_hbm, gate_hbm, up_hbm, x_ref, w_gate_ref, w_up_ref = refs[count : count + 7]
    gate_ref, up_ref, sem, out_sem = refs[count + 7 :]
    rows = pieces[0].shape[0]
    width = w_gate_ref.shape[0]
    total = gate_ref.shape[0]
    block = min(128, total)
    loads = Loads(sem)
    x_in = [loads.begin(p, x_ref.at[pl.ds(i * rows, rows)]) for i, p in enumerate(pieces)]
    x_in = sum(x_in, [])
    gate_in = loads.begin_rows(w_gate_hbm, w_gate_ref)
    up_in = loads.begin_rows(w_up_hbm, w_up_ref)
    wait(x_in + gate_in + up_in)

    def store(i):
        here = pl.ds(pl.multiple_of(i * block, block), block)
        return [
            pltpu.make_async_copy(src.at[here], dst.at[here], out_sem.at[j, i])
            for j, (src, dst) in enumerate(((gate_ref, gate_hbm), (up_ref, up_hbm)))
        ]

    def run_block(i, carry):
        here = pl.ds(pl.multiple_of(i * block, block), block)
        gate_ref[here, :] = dot(x_ref[here, :width], w_gate_ref[...])
        up_ref[here, :] = dot(x_ref[here, :width], w_up_ref[...])
        for copy in store(i):
            copy.start()
        return carry

    lax.fori_loop(0, total // block, run_block, 0)
    for i in range(total // block):
        wait(store(i))


def base_products(pieces, w_gate, w_up):
    width, units = w_gate.shape
    total = sum(p.shape[0] for p in pieces)
    out = jax.ShapeDtypeStruct((total, units), jnp.float32)
    return pl.pallas_call(
        functools.partial(base_kernel, len(pieces)),
        out_shape=[out, out],
        in_specs=[pl.BlockSpec(memory_space=pl.ANY)] * len(pieces)
        + [pl.BlockSpec(memory_space=pltpu.HBM)] * 2,
        out_specs=[pl.BlockSpec(memory_space=pl.ANY)] * 2,
        scratch_shapes=[
            pltpu.VMEM((total, pieces[0].shape[1]), jnp.bfloat16),
            pltpu.VMEM(w_gate.shape, w_gate.dtype),
            pltpu.VMEM(w_up.shape, w_up.dtype),
            pltpu.VMEM(out.shape, out.dtype),
            pltpu.VMEM(out.shape, out.dtype),
            pltpu.SemaphoreType.DMA((len(pieces) + 8,)),
            pltpu.SemaphoreType.DMA((2, total // min(128, total))),
        ],
        compiler_params=pltpu.CompilerParams(vmem_limit_bytes=EXPERT_GRANT),
        cost_estimate=LITTLE,
        name="base_products",
    )(*pieces, w_gate, w_up)


def finish_kernel(count, first, rows, place_ref, *refs):
    pieces, refs = refs[:count], refs[count:]
    gate_hbm, up_hbm, a_gu_hbm, gate_b_hbm, up_b_hbm, down_a_hbm, down_b_hbm = refs[:7]
    w_down_hbm, kept_hbm, sent_hbm, x_ref, gate_ref, up_ref = refs[7:13]
    a_gu_ref, gate_b_ref, up_b_ref, down_a_ref, down_b_ref, w_down_ref = refs[13:19]
    inner_ref, mine_ref, kept_ref, sent_ref, sem, out_sem = refs[19:]
    span = pieces[0].shape[0]
    units, width = w_down_ref.shape
    rank = gate_b_ref.shape[0]
    own = kept_ref.shape[0]
    block = min(128, own)
    loads = Loads(sem)
    x_in, base_in = [], []
    for i, piece in enumerate(pieces):
        x_in += loads.begin(piece.at[pl.ds(first, rows)], x_ref.at[pl.ds(i * rows, rows)])
    x_in += loads.begin(a_gu_hbm, a_gu_ref)
    x_in += loads.begin(gate_b_hbm, gate_b_ref) + loads.begin(up_b_hbm, up_b_ref)
    for i in range(count):
        src, dst = pl.ds(i * span + first, rows), pl.ds(i * rows, rows)
        base_in += loads.begin(gate_hbm.at[src], gate_ref.at[dst])
        base_in += loads.begin(up_hbm.at[src], up_ref.at[dst])
    down_in = loads.begin(down_a_hbm, down_a_ref) + loads.begin(down_b_hbm, down_b_ref)
    down_in += loads.begin_rows(w_down_hbm, w_down_ref)
    wait(x_in + base_in)

    def run_inner(i, carry):
        here = pl.ds(pl.multiple_of(i * block, block), block)
        gates = x_ref[here, width:].astype(jnp.float32)
        lane = lax.broadcasted_iota(jnp.int32, gates.shape, 1)
        mine = jnp.sum(jnp.where(lane == place_ref[1], gates, 0.0), axis=1, keepdims=True)
        low = (adapter_scale * dot(x_ref[here, :width], a_gu_ref[...])).astype(jnp.bfloat16)
        g = gate_ref[here, :] + dot(low[:, :rank], gate_b_ref[...])
        u = up_ref[here, :] + dot(low[:, rank:], up_b_ref[...])
        inner_ref[here, :] = (g / (1.0 + jnp.exp(-g)) * u).astype(jnp.bfloat16)
        mine_ref[here, :] = jnp.broadcast_to(mine, (block, LANES))
        return carry

    def run_down(i, carry):
        here = pl.ds(pl.multiple_of(i * block, block), block)
        inner, mine = inner_ref[here, :], mine_ref[here, :1]
        low = (adapter_scale * dot(inner, down_a_ref[...])).astype(jnp.bfloat16)[:, :rank]
        half = width // 2
        left = dot(inner, w_down_ref[:, :half]) + dot(low, down_b_ref[:, :half])
        right = dot(inner, w_down_ref[:, half:]) + dot(low, down_b_ref[:, half:])
        out = jnp.concatenate([left * mine, right * mine], axis=1)

        @pl.when(i < own // block)
        def _():
            kept_ref[here, :] = out
            pltpu.make_async_copy(kept_ref.at[here], kept_hbm.at[here], out_sem.at[i]).start()

        @pl.when(i >= own // block)
        def _():
            there = pl.ds(pl.multiple_of(i * block - own, block), block)
            sent_ref[there, :] = out.astype(jnp.bfloat16)
            pltpu.make_async_copy(sent_ref.at[there], sent_hbm.at[there], out_sem.at[i]).start()

        return carry

    lax.fori_loop(0, 2 * own // block, run_inner, 0)
    wait(down_in)
    lax.fori_loop(0, 2 * own // block, run_down, 0)
    for i in range(2 * own // block):
        src, dst = (kept_ref, kept_hbm) if i < own // block else (sent_ref, sent_hbm)
        at = pl.ds(i % (own // block) * block, block)
        pltpu.make_async_copy(src.at[at], dst.at[at], out_sem.at[i]).wait()


def finish_step(place, pieces, base, first, rows, low_rank, w_down):
    units, width = w_down.shape
    total = rows * len(pieces)
    own = total // 2
    a_gu, gate_b, up_b, down_a, down_b = low_rank
    rank = down_b.shape[0]
    outs = [
        jax.ShapeDtypeStruct((own, width), jnp.float32),
        jax.ShapeDtypeStruct((own, width), jnp.bfloat16),
    ]
    held = [*low_rank, w_down]
    return pl.pallas_call(
        functools.partial(finish_kernel, len(pieces), first, rows),
        out_shape=outs,
        in_specs=[pl.BlockSpec(memory_space=pltpu.SMEM)]
        + [pl.BlockSpec(memory_space=pl.ANY)] * (len(pieces) + 2 + len(low_rank))
        + [pl.BlockSpec(memory_space=pltpu.HBM)],
        out_specs=[pl.BlockSpec(memory_space=pl.ANY)] * 2,
        scratch_shapes=[
            pltpu.VMEM((total, pieces[0].shape[1]), jnp.bfloat16),
            pltpu.VMEM((total, units), jnp.float32),
            pltpu.VMEM((total, units), jnp.float32),
        ]
        + [pltpu.VMEM(a.shape, a.dtype) for a in held]
        + [pltpu.VMEM((total, units), jnp.bfloat16), pltpu.VMEM((total, LANES), jnp.float32)]
        + [pltpu.VMEM(o.shape, o.dtype) for o in outs]
        + [
            pltpu.SemaphoreType.DMA((3 * len(pieces) + 9,)),
            pltpu.SemaphoreType.DMA((2 * own // min(128, own),)),
        ],
        compiler_params=pltpu.CompilerParams(vmem_limit_bytes=EXPERT_GRANT),
        cost_estimate=LITTLE,
        name="finish_step",
    )(place, *pieces, *base, *held)


def dense_shards(
    hidden, route_ids, route_logits, placement, factors, w_gate, w_up, down_weight
):
    owners = lax.axis_size("expert")
    experts = placement.shape[0]
    steps, rows, width = hidden.shape
    units = w_gate.shape[2]
    rank = factors.shape[1] * owners // (3 * (width + units))
    outer, middle, cores = split_axis(owners)
    along_outer, along_middle = (middle * cores, outer), (cores, middle)
    place = jnp.stack([lax.axis_index("group"), lax.axis_index("expert")]).astype(jnp.int32)

    def along(x, stride, size):
        return [x] + [swap(x, owners, stride, k) for k in range(1, size)]

    def by_step(pieces, count):
        column = jnp.stack([p.reshape(count, rows, -1) for p in pieces], axis=1)
        return column.reshape(count * outer * rows, -1)

    def to_other_core(sheet):
        return sheet + [swap(p, owners, 1, 1) for p in sheet]

    first = max(1, steps * 2 // 3)
    head, tail = make_payload(hidden, route_ids, route_logits, experts, first)
    head, factors = lax.optimization_barrier((head, factors))
    head = by_step(along(head, *along_outer), first)
    blocks = order_factors(place, placement, factors, owners)
    blocks = [blocks[0]] + [swap(blocks[r], owners, cores, r) for r in range(1, middle)]
    head, blocks = lax.optimization_barrier((head, blocks))
    here, there = exchange_factors(blocks, owners)
    heads = along(head, *along_middle)
    tail, here, heads[1:] = lax.optimization_barrier((tail, here, heads[1:]))
    heads = to_other_core(heads)
    tails = by_step(along(tail, *along_outer), steps - first)
    tails = to_other_core(along(tails, *along_middle))
    head_base = base_products(heads, w_gate[0], w_up[0])
    here, there, head_base = lax.optimization_barrier((here, there, head_base))
    low_rank = relayout_factors(place, here, there, width, units, rank, owners)

    span = outer * rows
    results = []
    for s in range(steps):
        at = s if s < first else s - first
        pieces, base = (heads, head_base) if s < first else (tails, None)
        if base is None:
            pieces, summed = lax.optimization_barrier((pieces, results[0]))
            results[0] = summed
            base = base_products(pieces, w_gate[0], w_up[0])
        kept, sent = finish_step(
            place, pieces, base, at * span, span, low_rank, down_weight[0]
        )
        results.append(kept + swap(sent, owners, 1, 1).astype(jnp.float32))
    results = [scatter_along(total, owners, *along_middle) for total in results]
    results = [scatter_along(total, owners, *along_outer) for total in results]
    return jnp.stack(results).astype(jnp.bfloat16)


def row_capacity(rows, top, experts):
    return min(rows, 3 * max(1, rows * top // experts))


def unpack_factors(flat_factors, width, hidden_units, rank_size):
    layouts = [
        (width, rank_size),
        (rank_size, hidden_units),
        (width, rank_size),
        (rank_size, hidden_units),
        (hidden_units, rank_size),
        (rank_size, width),
    ]
    offset = 0
    segments = []
    for leading, trailing in layouts:
        segments.append(
            flat_factors[offset : offset + leading * trailing].reshape(leading, trailing)
        )
        offset = offset + leading * trailing
    return segments


def merge_weight(loaded_weights, factor_a, factor_b):
    adapter_delta = jnp.dot(factor_a, factor_b, preferred_element_type=jnp.float32)
    return (loaded_weights.astype(jnp.float32) + adapter_scale * adapter_delta).astype(jnp.bfloat16)


def apply_expert_block(inputs, merged_gate, merged_up, combined_down_weight):
    gate_part = jnp.dot(inputs, merged_gate, preferred_element_type=jnp.float32)
    up_part = jnp.dot(inputs, merged_up, preferred_element_type=jnp.float32)
    inner = (jax.nn.silu(gate_part) * up_part).astype(jnp.bfloat16)
    return jnp.dot(inner, combined_down_weight, preferred_element_type=jnp.float32).astype(
        jnp.bfloat16
    )


def sparse_shards(hidden, route_ids, route_logits, placement, factors, w_gate, w_up, down_weight):
    owners = lax.axis_size("expert")
    experts = placement.shape[0]
    steps_count, row_count, width = hidden.shape
    top_count = route_ids.shape[2]
    hidden_units = w_gate.shape[2]
    rank_size = factors.shape[1] * owners // (3 * (width + hidden_units))
    capacity = row_capacity(row_count, top_count, experts)
    slot_of = (
        jnp.zeros((experts,), jnp.int32).at[placement].set(jnp.arange(experts, dtype=jnp.int32))
    )
    ordered = jnp.take(factors, slot_of, axis=0)
    received = lax.all_to_all(ordered, "expert", split_axis=0, concat_axis=1, tiled=True)
    segments = unpack_factors(received[0], width, hidden_units, rank_size)
    merged_gate = merge_weight(w_gate[0], segments[0], segments[1])
    merged_up = merge_weight(w_up[0], segments[2], segments[3])
    combined_down_weight = merge_weight(down_weight[0], segments[4], segments[5])

    def layout(step_index):
        ids_flat = route_ids[step_index].reshape(-1)
        onehot = (ids_flat[:, None] == jnp.arange(experts, dtype=jnp.int32)[None, :]).astype(
            jnp.int32
        )
        position = jnp.sum((jnp.cumsum(onehot, axis=0) - 1) * onehot, axis=1)
        target = ids_flat * capacity + position
        placed = (
            jnp.arange(experts * capacity, dtype=jnp.int32)[:, None] == target[None, :]
        ).astype(jnp.bfloat16)
        pair_rows = jnp.repeat(hidden[step_index], top_count, axis=0)
        outgoing = jnp.dot(placed, pair_rows, preferred_element_type=jnp.float32).astype(
            jnp.bfloat16
        )
        outgoing = outgoing.reshape(experts, 1, capacity, width)
        gates = route_gates(route_logits[step_index]).reshape(-1)
        weighted = placed * gates[None, :]
        return (outgoing, weighted)

    layouts_all = [layout(step_index) for step_index in range(steps_count)]
    results = []
    for step_index in range(steps_count):
        outgoing, weighted = layouts_all[step_index]
        arrived = lax.all_to_all(outgoing, "expert", split_axis=0, concat_axis=1, tiled=True)
        outputs = apply_expert_block(
            arrived.reshape(-1, width), merged_gate, merged_up, combined_down_weight
        )
        outputs = outputs.reshape(arrived.shape)
        returned = lax.all_to_all(outputs, "expert", split_axis=1, concat_axis=0, tiled=True)
        flat_back = returned.reshape(experts * capacity, width)
        pair_out = jnp.einsum("cp,cd->pd", weighted, flat_back, preferred_element_type=jnp.float32)
        results.append(
            pair_out.reshape(row_count, top_count, width).sum(axis=1).astype(jnp.bfloat16)
        )
    return jnp.stack(results, axis=0)


def shards(hidden, route_ids, route_logits, placement, factors, w_gate, w_up, down_weight):
    rows, top = route_ids.shape[1:]
    width, units = w_gate.shape[1:]
    owners = lax.axis_size("expert")
    rank = factors.shape[1] * owners // (3 * (width + units))
    dense = row_capacity(rows, top, placement.shape[0]) == rows
    dense = dense and lax.axis_size("group") == 2 and split_axis(owners)[2] == 2
    outer = split_axis(owners)[0]
    dense = dense and outer > 1 and outer & (outer - 1) == 0 and split_axis(owners)[1] > 1
    dense = dense and 2 * rank == LANES and width % 256 == 0 and units % 256 == 0
    dense = dense and factors.shape[1] % (8 * LANES) == 0 and hidden.shape[0] > 1
    return (dense_shards if dense else sparse_shards)(
        hidden, route_ids, route_logits, placement, factors, w_gate, w_up, down_weight
    )


def solution(mesh):
    placed = (
        P(None, ("group", "expert"), None),
        P(None, ("group", "expert"), None),
        P(None, ("group", "expert"), None),
        P(),
        P(None, "expert"),
        P("expert", None, None),
        P("expert", None, None),
        P("expert", None, None),
    )
    return jax.shard_map(
        shards,
        mesh=mesh,
        in_specs=placed,
        out_specs=P(None, ("group", "expert"), None),
        check_vma=False,
    )
```

```python
import functools

import jax
import jax.numpy as jnp
from jax import lax
from jax.experimental import pallas as pl
from jax.experimental.pallas import tpu as pltpu
from jax.sharding import PartitionSpec as P

adapter_scale = 2.0
LANES = 128
GRANT = 16 << 20
EXPERT_GRANT = 32 << 20
WHOLE_GRANT = 60 << 20
LITTLE = pl.CostEstimate(flops=1, bytes_accessed=1, transcendentals=0)


def route_gates(logits):
    highest = jnp.max(logits, axis=-1, keepdims=True)
    router_scores = jnp.exp(logits - highest)
    return (router_scores / jnp.sum(router_scores, axis=-1, keepdims=True)).astype(jnp.bfloat16)


def split_axis(n):
    cores = 2 if n % 2 == 0 else 1
    chips = n // cores
    middle = 1
    while chips % (2 * middle) == 0 and 4 * middle * middle <= chips:
        middle *= 2
    return chips // middle, middle, cores


def swap(x, n, stride, k):
    return lax.ppermute(x, "expert", [(i, i ^ (k * stride)) for i in range(n)])


def scatter_along(total, n, stride, size):
    count = total.shape[0] // size
    result = total[:count]
    for k in range(1, size):
        part = total[k * count : (k + 1) * count].astype(jnp.bfloat16)
        result = result + swap(part, n, stride, k).astype(jnp.float32)
    return result


def exchange_factors(blocks, n):
    outer, middle, cores = split_axis(n)
    here = []
    for q in range(outer):
        pairs = []
        for g in range(2):
            for i in range(n):
                pairs.append((g * n + i, g * n + (i ^ (q * middle * cores) ^ g)))
        part = jnp.stack([block[q] for block in blocks])
        here.append(lax.ppermute(part, ("group", "expert"), pairs))
    return here


def dot(a, b):
    return jnp.dot(a, b, preferred_element_type=jnp.float32)


def payload_kernel(hidden_ref, ids_ref, logits_ref, out_ref, turned_ref):
    steps, top, rows = ids_ref.shape
    width = hidden_ref.shape[2]
    turned_ref[...] = jnp.zeros_like(turned_ref)
    for s in range(steps):
        logits, ids = logits_ref[s], ids_ref[s]
        scores = jnp.exp(logits - jnp.max(logits, axis=0, keepdims=True))
        gates = scores / jnp.sum(scores, axis=0, keepdims=True)
        expert = lax.broadcasted_iota(jnp.int32, (turned_ref.shape[0], rows), 0)
        dense = jnp.zeros(expert.shape, jnp.float32)
        for k in range(top):
            dense += jnp.where(ids[k : k + 1, :] == expert, gates[k : k + 1, :], 0.0)
        turned_ref[:, s * rows : (s + 1) * rows] = dense
    dense = turned_ref[...].T.astype(jnp.bfloat16)
    for s in range(steps):
        out_ref[s * rows : (s + 1) * rows, :width] = hidden_ref[s]
    out_ref[:, width:] = dense[: steps * rows]


def make_payload(hidden, route_ids, route_logits, experts):
    steps, rows, width = hidden.shape
    padded = -(-experts // LANES) * LANES
    return pl.pallas_call(
        payload_kernel,
        out_shape=jax.ShapeDtypeStruct((steps * rows, width + padded), jnp.bfloat16),
        scratch_shapes=[pltpu.VMEM((padded, -(-steps * rows // LANES) * LANES), jnp.float32)],
        compiler_params=pltpu.CompilerParams(vmem_limit_bytes=WHOLE_GRANT),
        cost_estimate=LITTLE,
        name="payload",
    )(hidden, jnp.swapaxes(route_ids, 1, 2), jnp.swapaxes(route_logits, 1, 2))


def order_kernel(middle, place_ref, placement_ref, factors_ref, *refs):
    out_refs, wide_ref = refs[:-1], refs[-1]
    slots = factors_ref.shape[0]
    length, lanes = out_refs[0].shape[1:]
    group, me = place_ref[0], place_ref[1]

    def cut(t, carry):
        start = pl.multiple_of(t * lanes, lanes)
        tile = factors_ref[:, pl.ds(start, lanes)].astype(jnp.float32)
        wide_ref[pl.ds(t, slots, stride=length), :] = tile
        return carry

    lax.fori_loop(0, length, cut, 0, unroll=8)

    def put(s, carry):
        to = placement_ref[s]
        away = to ^ me
        aside, ahead = lax.rem(away // 2, middle), away // (2 * middle)
        ours = lax.rem(away, 2) == group
        rows = wide_ref[pl.ds(pl.multiple_of(s * length, 8), length), :].astype(jnp.bfloat16)
        for r, out_ref in enumerate(out_refs):

            @pl.when(jnp.logical_and(ours, aside == r))
            def _():
                out_ref[ahead] = rows

        return carry

    lax.fori_loop(0, slots, put, 0)


def order_factors(place, placement, factors, n):
    outer, middle, _ = split_axis(n)
    slots, entries = factors.shape
    length = entries // LANES
    return pl.pallas_call(
        functools.partial(order_kernel, middle),
        out_shape=[jax.ShapeDtypeStruct((outer, length, LANES), jnp.bfloat16)] * middle,
        in_specs=[
            pl.BlockSpec(memory_space=pltpu.SMEM),
            pl.BlockSpec(memory_space=pltpu.SMEM),
            pl.BlockSpec(memory_space=pltpu.VMEM),
        ],
        scratch_shapes=[pltpu.VMEM((slots * length, LANES), jnp.float32)],
        compiler_params=pltpu.CompilerParams(vmem_limit_bytes=WHOLE_GRANT),
        cost_estimate=LITTLE,
        name="order_factors",
    )(place, placement, factors)


def relayout_kernel(outer, middle, place_ref, *refs):
    a_gu_ref, gate_b_ref, up_b_ref, down_a_ref, down_b_ref, flat_ref, wide_ref = refs[2:]
    width, units = a_gu_ref.shape[0], gate_b_ref.shape[1]
    rank = gate_b_ref.shape[0]
    length = refs[0].shape[2]
    group, me = place_ref[0], place_ref[1]
    for swapped, part in enumerate(refs[:2]):
        core = group if swapped == 0 else 1 - group
        for q in range(outer):
            for r in range(middle):
                source = me ^ ((q * middle + r) * 2 + core)
                start = pl.multiple_of(source * length, 8)
                flat_ref[pl.ds(start, length), :] = part[q, r].astype(jnp.float32)

    n_wide, n_unit = width // 2, units // 2
    at_ub = 2 * n_wide + n_unit
    at_da = 2 * n_wide + 2 * n_unit
    chunk = 128
    left = lax.broadcasted_iota(jnp.int32, (chunk, LANES), 1) < rank

    def load(start):
        return flat_ref[pl.ds(pl.multiple_of(start, 128), chunk), :]

    def gate_up(i, carry):
        g, u = load(i * chunk), load(n_wide + n_unit + i * chunk)
        at = 2 * i * chunk
        wide_ref[pl.ds(at, chunk, stride=2), :] = jnp.where(left, g, pltpu.roll(u, rank, 1))
        wide_ref[pl.ds(at + 1, chunk, stride=2), :] = jnp.where(left, pltpu.roll(g, rank, 1), u)
        both = wide_ref[pl.ds(pl.multiple_of(at, 128), 2 * chunk), :]
        a_gu_ref[pl.ds(pl.multiple_of(at, 128), 2 * chunk), :] = both.astype(jnp.bfloat16)
        return carry

    lax.fori_loop(0, n_wide // chunk, gate_up, 0, unroll=2)
    for i in range(n_unit // chunk):
        d = load(at_da + i * chunk)
        at = 2 * i * chunk
        wide_ref[pl.ds(at, chunk, stride=2), :] = jnp.where(left, d, 0.0)
        wide_ref[pl.ds(at + 1, chunk, stride=2), :] = jnp.where(left, pltpu.roll(d, rank, 1), 0.0)
        down_a_ref[at : at + 2 * chunk, :] = wide_ref[at : at + 2 * chunk, :].astype(jnp.bfloat16)
    for start, b_ref in (
        (n_wide, gate_b_ref),
        (at_ub, up_b_ref),
        (at_da + n_unit, down_b_ref),
    ):
        tiles = b_ref.shape[1] // LANES
        for j in range(tiles):
            row = flat_ref[pl.ds(start + j, rank, stride=tiles), :]
            b_ref[:, j * LANES : (j + 1) * LANES] = row.astype(jnp.bfloat16)


def relayout_factors(place, here, there, width, units, rank, n):
    outer, middle, _ = split_axis(n)
    shapes = [(width, 2 * rank), (rank, units), (rank, units), (units, 2 * rank), (rank, width)]
    length = here.shape[2]
    return pl.pallas_call(
        functools.partial(relayout_kernel, outer, middle),
        out_shape=[jax.ShapeDtypeStruct(shape, jnp.bfloat16) for shape in shapes],
        in_specs=[pl.BlockSpec(memory_space=pltpu.SMEM)]
        + [pl.BlockSpec(memory_space=pltpu.VMEM)] * 2,
        scratch_shapes=[
            pltpu.VMEM((n * length, LANES), jnp.float32),
            pltpu.VMEM((width, LANES), jnp.float32),
        ],
        compiler_params=pltpu.CompilerParams(vmem_limit_bytes=GRANT),
        cost_estimate=LITTLE,
        name="relayout_factors",
    )(place, here, there)


class Loads:
    def __init__(self, sem):
        self.sem, self.count = sem, 0

    def begin(self, src, dst):
        copy = pltpu.make_async_copy(src, dst, self.sem.at[self.count])
        copy.start()
        self.count += 1
        return [copy]

    def begin_rows(self, src, dst, parts=4):
        step = src.shape[0] // parts
        cuts = [pl.ds(at, step) for at in range(0, src.shape[0], step)]
        return sum([self.begin(src.at[cut], dst.at[cut]) for cut in cuts], [])


def wait(copies):
    for copy in copies:
        copy.wait()


def base_kernel(count, *refs):
    pieces = refs[:count]
    w_gate_hbm, w_up_hbm, gate_hbm, up_hbm, x_ref, w_gate_ref, w_up_ref = refs[count : count + 7]
    gate_ref, up_ref, sem, out_sem = refs[count + 7 :]
    rows = pieces[0].shape[0]
    width = w_gate_ref.shape[0]
    total = gate_ref.shape[0]
    block = min(128, total)
    loads = Loads(sem)
    x_in = [loads.begin(p, x_ref.at[pl.ds(i * rows, rows)]) for i, p in enumerate(pieces)]
    x_in = sum(x_in, [])
    gate_in = loads.begin_rows(w_gate_hbm, w_gate_ref)
    up_in = loads.begin_rows(w_up_hbm, w_up_ref)
    wait(x_in + gate_in + up_in)

    def store(i):
        here = pl.ds(pl.multiple_of(i * block, block), block)
        return [
            pltpu.make_async_copy(src.at[here], dst.at[here], out_sem.at[j, i])
            for j, (src, dst) in enumerate(((gate_ref, gate_hbm), (up_ref, up_hbm)))
        ]

    def run_block(i, carry):
        here = pl.ds(pl.multiple_of(i * block, block), block)
        gate_ref[here, :] = dot(x_ref[here, :width], w_gate_ref[...])
        up_ref[here, :] = dot(x_ref[here, :width], w_up_ref[...])
        for copy in store(i):
            copy.start()
        return carry

    lax.fori_loop(0, total // block, run_block, 0)
    for i in range(total // block):
        wait(store(i))


def base_products(pieces, w_gate, w_up):
    width, units = w_gate.shape
    total = sum(p.shape[0] for p in pieces)
    out = jax.ShapeDtypeStruct((total, units), jnp.float32)
    return pl.pallas_call(
        functools.partial(base_kernel, len(pieces)),
        out_shape=[out, out],
        in_specs=[pl.BlockSpec(memory_space=pl.ANY)] * len(pieces)
        + [pl.BlockSpec(memory_space=pltpu.HBM)] * 2,
        out_specs=[pl.BlockSpec(memory_space=pl.ANY)] * 2,
        scratch_shapes=[
            pltpu.VMEM((total, pieces[0].shape[1]), jnp.bfloat16),
            pltpu.VMEM(w_gate.shape, w_gate.dtype),
            pltpu.VMEM(w_up.shape, w_up.dtype),
            pltpu.VMEM(out.shape, out.dtype),
            pltpu.VMEM(out.shape, out.dtype),
            pltpu.SemaphoreType.DMA((len(pieces) + 8,)),
            pltpu.SemaphoreType.DMA((2, total // min(128, total))),
        ],
        compiler_params=pltpu.CompilerParams(vmem_limit_bytes=EXPERT_GRANT),
        cost_estimate=LITTLE,
        name="base_products",
    )(*pieces, w_gate, w_up)


def finish_kernel(count, first, rows, place_ref, *refs):
    pieces, refs = refs[:count], refs[count:]
    gate_hbm, up_hbm, a_gu_hbm, gate_b_hbm, up_b_hbm, down_a_hbm, down_b_hbm = refs[:7]
    w_down_hbm, kept_hbm, sent_hbm, x_ref, gate_ref, up_ref = refs[7:13]
    a_gu_ref, gate_b_ref, up_b_ref, down_a_ref, down_b_ref, w_down_ref = refs[13:19]
    inner_ref, kept_ref, sent_ref, sem, out_sem = refs[19:]
    span = pieces[0].shape[0]
    units, width = w_down_ref.shape
    rank = gate_b_ref.shape[0]
    own = kept_ref.shape[0]
    block = min(128, own)
    loads = Loads(sem)
    x_in, base_in = [], []
    for i, piece in enumerate(pieces):
        x_in += loads.begin(piece.at[pl.ds(first, rows)], x_ref.at[pl.ds(i * rows, rows)])
    x_in += loads.begin(a_gu_hbm, a_gu_ref)
    x_in += loads.begin(gate_b_hbm, gate_b_ref) + loads.begin(up_b_hbm, up_b_ref)
    for i in range(count):
        src, dst = pl.ds(i * span + first, rows), pl.ds(i * rows, rows)
        base_in += loads.begin(gate_hbm.at[src], gate_ref.at[dst])
        base_in += loads.begin(up_hbm.at[src], up_ref.at[dst])
    down_in = loads.begin(down_a_hbm, down_a_ref) + loads.begin(down_b_hbm, down_b_ref)
    down_in += loads.begin_rows(w_down_hbm, w_down_ref)
    cuts = [slice(at, at + block) for at in range(0, 2 * own, block)]
    wait(x_in)
    lows = []
    for cut in cuts:
        low = adapter_scale * dot(x_ref[cut, :width], a_gu_ref[...])
        lows.append(low.astype(jnp.bfloat16))
    wait(base_in)
    for cut, low in zip(cuts, lows):
        g = gate_ref[cut, :] + dot(low[:, :rank], gate_b_ref[...])
        u = up_ref[cut, :] + dot(low[:, rank:], up_b_ref[...])
        inner_ref[cut, :] = (g / (1.0 + jnp.exp(-g)) * u).astype(jnp.bfloat16)
    wait(down_in)
    lows = []
    for cut in cuts:
        low = adapter_scale * dot(inner_ref[cut, :], down_a_ref[...])
        lows.append(low.astype(jnp.bfloat16)[:, :rank])
    out_copies = []
    for cut, low in zip(cuts, lows):
        gates = x_ref[cut, width:].astype(jnp.float32)
        lane = lax.broadcasted_iota(jnp.int32, gates.shape, 1)
        mine = jnp.sum(jnp.where(lane == place_ref[1], gates, 0.0), axis=1, keepdims=True)
        out = (dot(inner_ref[cut, :], w_down_ref[...]) + dot(low, down_b_ref[...])) * mine
        keep = cut.start < own
        out_ref, out_hbm = (kept_ref, kept_hbm) if keep else (sent_ref, sent_hbm)
        at = pl.ds(cut.start if keep else cut.start - own, block)
        out_ref[at, :] = out.astype(out_ref.dtype)
        sem_out = out_sem.at[len(out_copies)]
        out_copies.append(pltpu.make_async_copy(out_ref.at[at], out_hbm.at[at], sem_out))
        out_copies[-1].start()
    wait(out_copies)


def finish_step(place, pieces, base, first, rows, low_rank, w_down):
    units, width = w_down.shape
    total = rows * len(pieces)
    own = total // 2
    a_gu, gate_b, up_b, down_a, down_b = low_rank
    rank = down_b.shape[0]
    outs = [
        jax.ShapeDtypeStruct((own, width), jnp.float32),
        jax.ShapeDtypeStruct((own, width), jnp.bfloat16),
    ]
    held = [*low_rank, w_down]
    return pl.pallas_call(
        functools.partial(finish_kernel, len(pieces), first, rows),
        out_shape=outs,
        in_specs=[pl.BlockSpec(memory_space=pltpu.SMEM)]
        + [pl.BlockSpec(memory_space=pl.ANY)] * (len(pieces) + 2 + len(low_rank))
        + [pl.BlockSpec(memory_space=pltpu.HBM)],
        out_specs=[pl.BlockSpec(memory_space=pl.ANY)] * 2,
        scratch_shapes=[
            pltpu.VMEM((total, pieces[0].shape[1]), jnp.bfloat16),
            pltpu.VMEM((total, units), jnp.float32),
            pltpu.VMEM((total, units), jnp.float32),
        ]
        + [pltpu.VMEM(a.shape, a.dtype) for a in held]
        + [pltpu.VMEM((total, units), jnp.bfloat16)]
        + [pltpu.VMEM(o.shape, o.dtype) for o in outs]
        + [
            pltpu.SemaphoreType.DMA((3 * len(pieces) + 9,)),
            pltpu.SemaphoreType.DMA((2 * own // min(128, own),)),
        ],
        compiler_params=pltpu.CompilerParams(vmem_limit_bytes=EXPERT_GRANT),
        cost_estimate=LITTLE,
        name="finish_step",
    )(place, *pieces, *base, *held)


def dense_shards(
    hidden, route_ids, route_logits, placement, factors, w_gate, w_up, down_weight
):
    owners = lax.axis_size("expert")
    experts = placement.shape[0]
    steps, rows, width = hidden.shape
    units = w_gate.shape[2]
    rank = factors.shape[1] * owners // (3 * (width + units))
    outer, middle, cores = split_axis(owners)
    along_outer, along_middle = (middle * cores, outer), (cores, middle)
    place = jnp.stack([lax.axis_index("group"), lax.axis_index("expert")]).astype(jnp.int32)

    def along(x, stride, size):
        return [x] + [swap(x, owners, stride, k) for k in range(1, size)]

    rows_in = make_payload(hidden, route_ids, route_logits, experts)
    rows_in, factors = lax.optimization_barrier((rows_in, factors))
    column = [p.reshape(steps, rows, -1) for p in along(rows_in, *along_outer)]
    column = jnp.stack(column, axis=1).reshape(steps * outer * rows, -1)
    blocks = order_factors(place, placement, factors, owners)
    blocks = [blocks[0]] + [swap(blocks[r], owners, cores, r) for r in range(1, middle)]
    column, blocks = lax.optimization_barrier((column, blocks))
    here = exchange_factors(blocks, owners)
    sheet = along(column, *along_middle)
    here, sheet[1:] = lax.optimization_barrier((here, sheet[1:]))
    here = jnp.stack(here)
    there = lax.ppermute(here, "group", [(0, 1), (1, 0)])
    pieces = sheet + [swap(p, owners, 1, 1) for p in sheet]
    base = base_products(pieces, w_gate[0], w_up[0])
    here, there, base = lax.optimization_barrier((here, there, base))
    low_rank = relayout_factors(place, here, there, width, units, rank, owners)

    span = outer * rows
    results = []
    for s in range(steps):
        if s >= 2:
            pieces, results[s - 2] = lax.optimization_barrier((pieces, results[s - 2]))
        kept, sent = finish_step(place, pieces, base, s * span, span, low_rank, down_weight[0])
        results.append(kept + swap(sent, owners, 1, 1).astype(jnp.float32))
    results = [scatter_along(total, owners, *along_middle) for total in results]
    results = [scatter_along(total, owners, *along_outer) for total in results]
    return jnp.stack(results).astype(jnp.bfloat16)


def row_capacity(rows, top, experts):
    return min(rows, 3 * max(1, rows * top // experts))


def unpack_factors(flat_factors, width, hidden_units, rank_size):
    layouts = [
        (width, rank_size),
        (rank_size, hidden_units),
        (width, rank_size),
        (rank_size, hidden_units),
        (hidden_units, rank_size),
        (rank_size, width),
    ]
    offset = 0
    segments = []
    for leading, trailing in layouts:
        segments.append(
            flat_factors[offset : offset + leading * trailing].reshape(leading, trailing)
        )
        offset = offset + leading * trailing
    return segments


def merge_weight(loaded_weights, factor_a, factor_b):
    adapter_delta = jnp.dot(factor_a, factor_b, preferred_element_type=jnp.float32)
    return (loaded_weights.astype(jnp.float32) + adapter_scale * adapter_delta).astype(jnp.bfloat16)


def apply_expert_block(inputs, merged_gate, merged_up, combined_down_weight):
    gate_part = jnp.dot(inputs, merged_gate, preferred_element_type=jnp.float32)
    up_part = jnp.dot(inputs, merged_up, preferred_element_type=jnp.float32)
    inner = (jax.nn.silu(gate_part) * up_part).astype(jnp.bfloat16)
    return jnp.dot(inner, combined_down_weight, preferred_element_type=jnp.float32).astype(
        jnp.bfloat16
    )


def sparse_shards(hidden, route_ids, route_logits, placement, factors, w_gate, w_up, down_weight):
    owners = lax.axis_size("expert")
    experts = placement.shape[0]
    steps_count, row_count, width = hidden.shape
    top_count = route_ids.shape[2]
    hidden_units = w_gate.shape[2]
    rank_size = factors.shape[1] * owners // (3 * (width + hidden_units))
    capacity = row_capacity(row_count, top_count, experts)
    slot_of = (
        jnp.zeros((experts,), jnp.int32).at[placement].set(jnp.arange(experts, dtype=jnp.int32))
    )
    ordered = jnp.take(factors, slot_of, axis=0)
    received = lax.all_to_all(ordered, "expert", split_axis=0, concat_axis=1, tiled=True)
    segments = unpack_factors(received[0], width, hidden_units, rank_size)
    merged_gate = merge_weight(w_gate[0], segments[0], segments[1])
    merged_up = merge_weight(w_up[0], segments[2], segments[3])
    combined_down_weight = merge_weight(down_weight[0], segments[4], segments[5])

    def layout(step_index):
        ids_flat = route_ids[step_index].reshape(-1)
        onehot = (ids_flat[:, None] == jnp.arange(experts, dtype=jnp.int32)[None, :]).astype(
            jnp.int32
        )
        position = jnp.sum((jnp.cumsum(onehot, axis=0) - 1) * onehot, axis=1)
        target = ids_flat * capacity + position
        placed = (
            jnp.arange(experts * capacity, dtype=jnp.int32)[:, None] == target[None, :]
        ).astype(jnp.bfloat16)
        pair_rows = jnp.repeat(hidden[step_index], top_count, axis=0)
        outgoing = jnp.dot(placed, pair_rows, preferred_element_type=jnp.float32).astype(
            jnp.bfloat16
        )
        outgoing = outgoing.reshape(experts, 1, capacity, width)
        gates = route_gates(route_logits[step_index]).reshape(-1)
        weighted = placed * gates[None, :]
        return (outgoing, weighted)

    layouts_all = [layout(step_index) for step_index in range(steps_count)]
    results = []
    for step_index in range(steps_count):
        outgoing, weighted = layouts_all[step_index]
        arrived = lax.all_to_all(outgoing, "expert", split_axis=0, concat_axis=1, tiled=True)
        outputs = apply_expert_block(
            arrived.reshape(-1, width), merged_gate, merged_up, combined_down_weight
        )
        outputs = outputs.reshape(arrived.shape)
        returned = lax.all_to_all(outputs, "expert", split_axis=1, concat_axis=0, tiled=True)
        flat_back = returned.reshape(experts * capacity, width)
        pair_out = jnp.einsum("cp,cd->pd", weighted, flat_back, preferred_element_type=jnp.float32)
        results.append(
            pair_out.reshape(row_count, top_count, width).sum(axis=1).astype(jnp.bfloat16)
        )
    return jnp.stack(results, axis=0)


def shards(hidden, route_ids, route_logits, placement, factors, w_gate, w_up, down_weight):
    rows, top = route_ids.shape[1:]
    width, units = w_gate.shape[1:]
    owners = lax.axis_size("expert")
    rank = factors.shape[1] * owners // (3 * (width + units))
    dense = row_capacity(rows, top, placement.shape[0]) == rows
    dense = dense and lax.axis_size("group") == 2 and split_axis(owners)[2] == 2
    outer = split_axis(owners)[0]
    dense = dense and outer > 1 and outer & (outer - 1) == 0 and split_axis(owners)[1] > 1
    dense = dense and 2 * rank == LANES and width % 256 == 0 and units % 256 == 0
    dense = dense and factors.shape[1] % (8 * LANES) == 0
    return (dense_shards if dense else sparse_shards)(
        hidden, route_ids, route_logits, placement, factors, w_gate, w_up, down_weight
    )


def solution(mesh):
    placed = (
        P(None, ("group", "expert"), None),
        P(None, ("group", "expert"), None),
        P(None, ("group", "expert"), None),
        P(),
        P(None, "expert"),
        P("expert", None, None),
        P("expert", None, None),
        P("expert", None, None),
    )
    return jax.shard_map(
        shards,
        mesh=mesh,
        in_specs=placed,
        out_specs=P(None, ("group", "expert"), None),
        check_vma=False,
    )
```

```python
import functools

import jax
import jax.numpy as jnp
from jax import lax
from jax.experimental import pallas as pl
from jax.experimental.pallas import tpu as pltpu
from jax.sharding import PartitionSpec as P

adapter_scale = 2.0
LANES = 128
GRANT = 16 << 20
EXPERT_GRANT = 32 << 20
WHOLE_GRANT = 60 << 20
LITTLE = pl.CostEstimate(flops=1, bytes_accessed=1, transcendentals=0)


def route_gates(logits):
    highest = jnp.max(logits, axis=-1, keepdims=True)
    router_scores = jnp.exp(logits - highest)
    return (router_scores / jnp.sum(router_scores, axis=-1, keepdims=True)).astype(jnp.bfloat16)


def split_axis(n):
    cores = 2 if n % 2 == 0 else 1
    chips = n // cores
    middle = 1
    while chips % (2 * middle) == 0 and 4 * middle * middle <= chips:
        middle *= 2
    return chips // middle, middle, cores


def swap(x, n, stride, k):
    return lax.ppermute(x, "expert", [(i, i ^ (k * stride)) for i in range(n)])


def scatter_along(total, n, stride, size):
    count = total.shape[0] // size
    result = total[:count]
    for k in range(1, size):
        part = total[k * count : (k + 1) * count].astype(jnp.bfloat16)
        result = result + swap(part, n, stride, k).astype(jnp.float32)
    return result


def exchange_along(x, n, stride, size):
    lines = [
        [start + k * stride for k in range(size)]
        for start in range(n)
        if start // stride % size == 0
    ]
    return lax.all_to_all(x, "expert", 0, 0, axis_index_groups=lines, tiled=True)


def exchange_factors(blocks, n):
    outer, middle, cores = split_axis(n)
    here = []
    for q in range(outer):
        pairs = []
        for g in range(2):
            for i in range(n):
                pairs.append((g * n + i, g * n + (i ^ (q * middle * cores) ^ g)))
        part = jnp.stack([block[q] for block in blocks])
        here.append(lax.ppermute(part, ("group", "expert"), pairs))
    return here


def dot(a, b):
    return jnp.dot(a, b, preferred_element_type=jnp.float32)


def payload_kernel(hidden_ref, ids_ref, logits_ref, out_ref, turned_ref):
    steps, top, rows = ids_ref.shape
    width = hidden_ref.shape[2]
    turned_ref[...] = jnp.zeros_like(turned_ref)
    for s in range(steps):
        logits, ids = logits_ref[s], ids_ref[s]
        scores = jnp.exp(logits - jnp.max(logits, axis=0, keepdims=True))
        gates = scores / jnp.sum(scores, axis=0, keepdims=True)
        expert = lax.broadcasted_iota(jnp.int32, (turned_ref.shape[0], rows), 0)
        dense = jnp.zeros(expert.shape, jnp.float32)
        for k in range(top):
            dense += jnp.where(ids[k : k + 1, :] == expert, gates[k : k + 1, :], 0.0)
        turned_ref[:, s * rows : (s + 1) * rows] = dense
    dense = turned_ref[...].T.astype(jnp.bfloat16)
    for s in range(steps):
        out_ref[s * rows : (s + 1) * rows, :width] = hidden_ref[s]
    out_ref[:, width:] = dense[: steps * rows]


def make_payload(hidden, route_ids, route_logits, experts):
    steps, rows, width = hidden.shape
    padded = -(-experts // LANES) * LANES
    return pl.pallas_call(
        payload_kernel,
        out_shape=jax.ShapeDtypeStruct((steps * rows, width + padded), jnp.bfloat16),
        scratch_shapes=[pltpu.VMEM((padded, -(-steps * rows // LANES) * LANES), jnp.float32)],
        compiler_params=pltpu.CompilerParams(vmem_limit_bytes=WHOLE_GRANT),
        cost_estimate=LITTLE,
        name="payload",
    )(hidden, jnp.swapaxes(route_ids, 1, 2), jnp.swapaxes(route_logits, 1, 2))


def order_kernel(middle, place_ref, placement_ref, factors_ref, *refs):
    out_refs, wide_ref = refs[:-1], refs[-1]
    slots = factors_ref.shape[0]
    length, lanes = out_refs[0].shape[1:]
    group, me = place_ref[0], place_ref[1]

    def cut(t, carry):
        start = pl.multiple_of(t * lanes, lanes)
        tile = factors_ref[:, pl.ds(start, lanes)].astype(jnp.float32)
        wide_ref[pl.ds(t, slots, stride=length), :] = tile
        return carry

    lax.fori_loop(0, length, cut, 0, unroll=8)

    def put(s, carry):
        to = placement_ref[s]
        away = to ^ me
        aside, ahead = lax.rem(away // 2, middle), away // (2 * middle)
        ours = lax.rem(away, 2) == group
        rows = wide_ref[pl.ds(pl.multiple_of(s * length, 8), length), :].astype(jnp.bfloat16)
        for r, out_ref in enumerate(out_refs):

            @pl.when(jnp.logical_and(ours, aside == r))
            def _():
                out_ref[ahead] = rows

        return carry

    lax.fori_loop(0, slots, put, 0)


def order_factors(place, placement, factors, n):
    outer, middle, _ = split_axis(n)
    slots, entries = factors.shape
    length = entries // LANES
    return pl.pallas_call(
        functools.partial(order_kernel, middle),
        out_shape=[jax.ShapeDtypeStruct((outer, length, LANES), jnp.bfloat16)] * middle,
        in_specs=[
            pl.BlockSpec(memory_space=pltpu.SMEM),
            pl.BlockSpec(memory_space=pltpu.SMEM),
            pl.BlockSpec(memory_space=pltpu.VMEM),
        ],
        scratch_shapes=[pltpu.VMEM((slots * length, LANES), jnp.float32)],
        compiler_params=pltpu.CompilerParams(vmem_limit_bytes=WHOLE_GRANT),
        cost_estimate=LITTLE,
        name="order_factors",
    )(place, placement, factors)


def relayout_kernel(middle, place_ref, *refs):
    parts, refs = refs[:4], refs[4:]
    a_gu_ref, gate_b_ref, up_b_ref, down_a_ref, down_b_ref, flat_ref, wide_ref = refs
    width, units = a_gu_ref.shape[0], gate_b_ref.shape[1]
    rank = gate_b_ref.shape[0]
    half, _, length, _ = parts[0].shape
    group, me = place_ref[0], place_ref[1]
    for i, part in enumerate(parts):
        core = group if i < 2 else 1 - group
        for q in range(half):
            for r in range(middle):
                source = me ^ (((i % 2 * half + q) * middle + r) * 2 + core)
                start = pl.multiple_of(source * length, 8)
                flat_ref[pl.ds(start, length), :] = part[q, r].astype(jnp.float32)

    n_wide, n_unit = width // 2, units // 2
    at_ub = 2 * n_wide + n_unit
    at_da = 2 * n_wide + 2 * n_unit
    chunk = 128
    left = lax.broadcasted_iota(jnp.int32, (chunk, LANES), 1) < rank

    def load(start):
        return flat_ref[pl.ds(pl.multiple_of(start, 128), chunk), :]

    def gate_up(i, carry):
        g, u = load(i * chunk), load(n_wide + n_unit + i * chunk)
        at = 2 * i * chunk
        wide_ref[pl.ds(at, chunk, stride=2), :] = jnp.where(left, g, pltpu.roll(u, rank, 1))
        wide_ref[pl.ds(at + 1, chunk, stride=2), :] = jnp.where(left, pltpu.roll(g, rank, 1), u)
        both = wide_ref[pl.ds(pl.multiple_of(at, 128), 2 * chunk), :]
        a_gu_ref[pl.ds(pl.multiple_of(at, 128), 2 * chunk), :] = both.astype(jnp.bfloat16)
        return carry

    lax.fori_loop(0, n_wide // chunk, gate_up, 0, unroll=2)
    for i in range(n_unit // chunk):
        d = load(at_da + i * chunk)
        at = 2 * i * chunk
        wide_ref[pl.ds(at, chunk, stride=2), :] = jnp.where(left, d, 0.0)
        wide_ref[pl.ds(at + 1, chunk, stride=2), :] = jnp.where(left, pltpu.roll(d, rank, 1), 0.0)
        down_a_ref[at : at + 2 * chunk, :] = wide_ref[at : at + 2 * chunk, :].astype(jnp.bfloat16)
    for start, b_ref in (
        (n_wide, gate_b_ref),
        (at_ub, up_b_ref),
        (at_da + n_unit, down_b_ref),
    ):
        tiles = b_ref.shape[1] // LANES
        for j in range(tiles):
            row = flat_ref[pl.ds(start + j, rank, stride=tiles), :]
            b_ref[:, j * LANES : (j + 1) * LANES] = row.astype(jnp.bfloat16)


def relayout_factors(place, here, there, width, units, rank, n):
    middle = split_axis(n)[1]
    shapes = [(width, 2 * rank), (rank, units), (rank, units), (units, 2 * rank), (rank, width)]
    length = here[0].shape[2]
    return pl.pallas_call(
        functools.partial(relayout_kernel, middle),
        out_shape=[jax.ShapeDtypeStruct(shape, jnp.bfloat16) for shape in shapes],
        in_specs=[pl.BlockSpec(memory_space=pltpu.SMEM)]
        + [pl.BlockSpec(memory_space=pltpu.VMEM)] * 4,
        scratch_shapes=[
            pltpu.VMEM((n * length, LANES), jnp.float32),
            pltpu.VMEM((width, LANES), jnp.float32),
        ],
        compiler_params=pltpu.CompilerParams(vmem_limit_bytes=GRANT),
        cost_estimate=LITTLE,
        name="relayout_factors",
    )(place, *here, *there)


class Loads:
    def __init__(self, sem):
        self.sem, self.count = sem, 0

    def begin(self, src, dst):
        copy = pltpu.make_async_copy(src, dst, self.sem.at[self.count])
        copy.start()
        self.count += 1
        return [copy]

    def begin_rows(self, src, dst, parts=4):
        step = src.shape[0] // parts
        cuts = [pl.ds(at, step) for at in range(0, src.shape[0], step)]
        return sum([self.begin(src.at[cut], dst.at[cut]) for cut in cuts], [])


def wait(copies):
    for copy in copies:
        copy.wait()


def base_kernel(count, *refs):
    pieces = refs[:count]
    w_gate_hbm, w_up_hbm, gate_hbm, up_hbm, x_ref, w_gate_ref, w_up_ref = refs[count : count + 7]
    gate_ref, up_ref, sem, out_sem = refs[count + 7 :]
    rows = pieces[0].shape[0]
    width = w_gate_ref.shape[0]
    total = gate_ref.shape[0]
    block = min(128, total)
    loads = Loads(sem)
    x_in = [loads.begin(p, x_ref.at[pl.ds(i * rows, rows)]) for i, p in enumerate(pieces)]
    x_in = sum(x_in, [])
    gate_in = loads.begin_rows(w_gate_hbm, w_gate_ref)
    up_in = loads.begin_rows(w_up_hbm, w_up_ref)
    wait(x_in + gate_in + up_in)

    def store(i):
        here = pl.ds(pl.multiple_of(i * block, block), block)
        return [
            pltpu.make_async_copy(src.at[here], dst.at[here], out_sem.at[j, i])
            for j, (src, dst) in enumerate(((gate_ref, gate_hbm), (up_ref, up_hbm)))
        ]

    def run_block(i, carry):
        here = pl.ds(pl.multiple_of(i * block, block), block)
        gate_ref[here, :] = dot(x_ref[here, :width], w_gate_ref[...])
        up_ref[here, :] = dot(x_ref[here, :width], w_up_ref[...])
        for copy in store(i):
            copy.start()
        return carry

    lax.fori_loop(0, total // block, run_block, 0)
    for i in range(total // block):
        wait(store(i))


def base_products(pieces, w_gate, w_up):
    width, units = w_gate.shape
    total = sum(p.shape[0] for p in pieces)
    out = jax.ShapeDtypeStruct((total, units), jnp.float32)
    return pl.pallas_call(
        functools.partial(base_kernel, len(pieces)),
        out_shape=[out, out],
        in_specs=[pl.BlockSpec(memory_space=pl.ANY)] * len(pieces)
        + [pl.BlockSpec(memory_space=pltpu.HBM)] * 2,
        out_specs=[pl.BlockSpec(memory_space=pl.ANY)] * 2,
        scratch_shapes=[
            pltpu.VMEM((total, pieces[0].shape[1]), jnp.bfloat16),
            pltpu.VMEM(w_gate.shape, w_gate.dtype),
            pltpu.VMEM(w_up.shape, w_up.dtype),
            pltpu.VMEM(out.shape, out.dtype),
            pltpu.VMEM(out.shape, out.dtype),
            pltpu.SemaphoreType.DMA((len(pieces) + 8,)),
            pltpu.SemaphoreType.DMA((2, total // min(128, total))),
        ],
        compiler_params=pltpu.CompilerParams(vmem_limit_bytes=EXPERT_GRANT),
        cost_estimate=LITTLE,
        name="base_products",
    )(*pieces, w_gate, w_up)


def finish_kernel(count, first, rows, place_ref, *refs):
    pieces, refs = refs[:count], refs[count:]
    base, refs = refs[:count], refs[count:]
    a_gu_hbm, gate_b_hbm, up_b_hbm, down_a_hbm, down_b_hbm = refs[:5]
    w_down_hbm, kept_hbm, sent_hbm, x_ref, gate_ref, up_ref = refs[5:11]
    a_gu_ref, gate_b_ref, up_b_ref, down_a_ref, down_b_ref, w_down_ref = refs[11:17]
    inner_ref, kept_ref, sent_ref, sem, out_sem = refs[17:]
    span = pieces[0].shape[0]
    units, width = w_down_ref.shape
    rank = gate_b_ref.shape[0]
    own = kept_ref.shape[0]
    block = min(128, own)
    loads = Loads(sem)
    x_in, base_in = [], []
    for i, piece in enumerate(pieces):
        x_in += loads.begin(piece.at[pl.ds(first, rows)], x_ref.at[pl.ds(i * rows, rows)])
    x_in += loads.begin(a_gu_hbm, a_gu_ref)
    x_in += loads.begin(gate_b_hbm, gate_b_ref) + loads.begin(up_b_hbm, up_b_ref)
    for i in range(count):
        half, r = i // (count // 2), i % (count // 2)
        src, dst = pl.ds(half * span + first, rows), pl.ds(i * rows, rows)
        base_in += loads.begin(base[2 * r].at[src], gate_ref.at[dst])
        base_in += loads.begin(base[2 * r + 1].at[src], up_ref.at[dst])
    down_in = loads.begin(down_a_hbm, down_a_ref) + loads.begin(down_b_hbm, down_b_ref)
    down_in += loads.begin_rows(w_down_hbm, w_down_ref)
    cuts = [slice(at, at + block) for at in range(0, 2 * own, block)]
    wait(x_in)
    lows = []
    for cut in cuts:
        low = adapter_scale * dot(x_ref[cut, :width], a_gu_ref[...])
        lows.append(low.astype(jnp.bfloat16))
    wait(base_in)
    for cut, low in zip(cuts, lows):
        g = gate_ref[cut, :] + dot(low[:, :rank], gate_b_ref[...])
        u = up_ref[cut, :] + dot(low[:, rank:], up_b_ref[...])
        inner_ref[cut, :] = (g / (1.0 + jnp.exp(-g)) * u).astype(jnp.bfloat16)
    wait(down_in)
    lows = []
    for cut in cuts:
        low = adapter_scale * dot(inner_ref[cut, :], down_a_ref[...])
        lows.append(low.astype(jnp.bfloat16)[:, :rank])
    out_copies = []
    for cut, low in zip(cuts, lows):
        gates = x_ref[cut, width:].astype(jnp.float32)
        lane = lax.broadcasted_iota(jnp.int32, gates.shape, 1)
        mine = jnp.sum(jnp.where(lane == place_ref[1], gates, 0.0), axis=1, keepdims=True)
        out = (dot(inner_ref[cut, :], w_down_ref[...]) + dot(low, down_b_ref[...])) * mine
        keep = cut.start < own
        out_ref, out_hbm = (kept_ref, kept_hbm) if keep else (sent_ref, sent_hbm)
        at = pl.ds(cut.start if keep else cut.start - own, block)
        out_ref[at, :] = out.astype(out_ref.dtype)
        sem_out = out_sem.at[len(out_copies)]
        out_copies.append(pltpu.make_async_copy(out_ref.at[at], out_hbm.at[at], sem_out))
        out_copies[-1].start()
    wait(out_copies)


def finish_step(place, pieces, base, first, rows, low_rank, w_down):
    units, width = w_down.shape
    total = rows * len(pieces)
    own = total // 2
    a_gu, gate_b, up_b, down_a, down_b = low_rank
    rank = down_b.shape[0]
    outs = [
        jax.ShapeDtypeStruct((own, width), jnp.float32),
        jax.ShapeDtypeStruct((own, width), jnp.bfloat16),
    ]
    held = [*low_rank, w_down]
    return pl.pallas_call(
        functools.partial(finish_kernel, len(pieces), first, rows),
        out_shape=outs,
        in_specs=[pl.BlockSpec(memory_space=pltpu.SMEM)]
        + [pl.BlockSpec(memory_space=pl.ANY)] * (2 * len(pieces) + len(low_rank))
        + [pl.BlockSpec(memory_space=pltpu.HBM)],
        out_specs=[pl.BlockSpec(memory_space=pl.ANY)] * 2,
        scratch_shapes=[
            pltpu.VMEM((total, pieces[0].shape[1]), jnp.bfloat16),
            pltpu.VMEM((total, units), jnp.float32),
            pltpu.VMEM((total, units), jnp.float32),
        ]
        + [pltpu.VMEM(a.shape, a.dtype) for a in held]
        + [pltpu.VMEM((total, units), jnp.bfloat16)]
        + [pltpu.VMEM(o.shape, o.dtype) for o in outs]
        + [
            pltpu.SemaphoreType.DMA((3 * len(pieces) + 9,)),
            pltpu.SemaphoreType.DMA((2 * own // min(128, own),)),
        ],
        compiler_params=pltpu.CompilerParams(vmem_limit_bytes=EXPERT_GRANT),
        cost_estimate=LITTLE,
        name="finish_step",
    )(place, *pieces, *base, *held)


def dense_shards(
    hidden, route_ids, route_logits, placement, factors, w_gate, w_up, down_weight
):
    owners = lax.axis_size("expert")
    experts = placement.shape[0]
    steps, rows, width = hidden.shape
    units = w_gate.shape[2]
    rank = factors.shape[1] * owners // (3 * (width + units))
    outer, middle, cores = split_axis(owners)
    along_outer, along_middle = (middle * cores, outer), (cores, middle)
    place = jnp.stack([lax.axis_index("group"), lax.axis_index("expert")]).astype(jnp.int32)

    def along(x, stride, size):
        return [x] + [swap(x, owners, stride, k) for k in range(1, size)]

    rows_in = make_payload(hidden, route_ids, route_logits, experts)
    rows_in, factors = lax.optimization_barrier((rows_in, factors))
    column = jnp.broadcast_to(rows_in, (outer, *rows_in.shape))
    column = exchange_along(column, owners, *along_outer).reshape(outer, steps, rows, -1)
    column = jnp.swapaxes(column, 0, 1).reshape(steps * outer * rows, -1)
    blocks = order_factors(place, placement, factors, owners)
    blocks = [blocks[0]] + [swap(blocks[r], owners, cores, r) for r in range(1, middle)]
    column, blocks = lax.optimization_barrier((column, blocks))
    here = exchange_factors(blocks, owners)
    here = [jnp.stack(here[: outer // 2]), jnp.stack(here[outer // 2 :])]
    sheet = along(column, *along_middle)
    others = [swap(column, owners, 1, 1)]
    base = [base_products([sheet[0], others[0]], w_gate[0], w_up[0])]
    here[0], base = lax.optimization_barrier((here[0], base))
    there = [lax.ppermute(p, "group", [(0, 1), (1, 0)]) for p in here]
    for r in range(1, middle):
        others.append(swap(sheet[r], owners, 1, 1))
        base.append(base_products([sheet[r], others[r]], w_gate[0], w_up[0]))
    here, there, base = lax.optimization_barrier((here, there, base))
    low_rank = relayout_factors(place, here, there, width, units, rank, owners)
    pieces, base = sheet + others, [b for pair in base for b in pair]

    span = outer * rows
    results = []
    for s in range(steps):
        if s >= 2:
            pieces, results[s - 2] = lax.optimization_barrier((pieces, results[s - 2]))
        kept, sent = finish_step(place, pieces, base, s * span, span, low_rank, down_weight[0])
        results.append(kept + swap(sent, owners, 1, 1).astype(jnp.float32))
    results = [scatter_along(total, owners, *along_middle) for total in results]
    finals = []
    for total in results:
        parts = total.astype(jnp.bfloat16).reshape(outer, rows, width)
        parts = exchange_along(parts, owners, *along_outer)
        finals.append(jnp.sum(parts, axis=0, dtype=jnp.float32))
    return jnp.stack(finals).astype(jnp.bfloat16)


def row_capacity(rows, top, experts):
    return min(rows, 3 * max(1, rows * top // experts))


def unpack_factors(flat_factors, width, hidden_units, rank_size):
    layouts = [
        (width, rank_size),
        (rank_size, hidden_units),
        (width, rank_size),
        (rank_size, hidden_units),
        (hidden_units, rank_size),
        (rank_size, width),
    ]
    offset = 0
    segments = []
    for leading, trailing in layouts:
        segments.append(
            flat_factors[offset : offset + leading * trailing].reshape(leading, trailing)
        )
        offset = offset + leading * trailing
    return segments


def merge_weight(loaded_weights, factor_a, factor_b):
    adapter_delta = jnp.dot(factor_a, factor_b, preferred_element_type=jnp.float32)
    return (loaded_weights.astype(jnp.float32) + adapter_scale * adapter_delta).astype(jnp.bfloat16)


def apply_expert_block(inputs, merged_gate, merged_up, combined_down_weight):
    gate_part = jnp.dot(inputs, merged_gate, preferred_element_type=jnp.float32)
    up_part = jnp.dot(inputs, merged_up, preferred_element_type=jnp.float32)
    inner = (jax.nn.silu(gate_part) * up_part).astype(jnp.bfloat16)
    return jnp.dot(inner, combined_down_weight, preferred_element_type=jnp.float32).astype(
        jnp.bfloat16
    )


def sparse_shards(hidden, route_ids, route_logits, placement, factors, w_gate, w_up, down_weight):
    owners = lax.axis_size("expert")
    experts = placement.shape[0]
    steps_count, row_count, width = hidden.shape
    top_count = route_ids.shape[2]
    hidden_units = w_gate.shape[2]
    rank_size = factors.shape[1] * owners // (3 * (width + hidden_units))
    capacity = row_capacity(row_count, top_count, experts)
    slot_of = (
        jnp.zeros((experts,), jnp.int32).at[placement].set(jnp.arange(experts, dtype=jnp.int32))
    )
    ordered = jnp.take(factors, slot_of, axis=0)
    received = lax.all_to_all(ordered, "expert", split_axis=0, concat_axis=1, tiled=True)
    segments = unpack_factors(received[0], width, hidden_units, rank_size)
    merged_gate = merge_weight(w_gate[0], segments[0], segments[1])
    merged_up = merge_weight(w_up[0], segments[2], segments[3])
    combined_down_weight = merge_weight(down_weight[0], segments[4], segments[5])

    def layout(step_index):
        ids_flat = route_ids[step_index].reshape(-1)
        onehot = (ids_flat[:, None] == jnp.arange(experts, dtype=jnp.int32)[None, :]).astype(
            jnp.int32
        )
        position = jnp.sum((jnp.cumsum(onehot, axis=0) - 1) * onehot, axis=1)
        target = ids_flat * capacity + position
        placed = (
            jnp.arange(experts * capacity, dtype=jnp.int32)[:, None] == target[None, :]
        ).astype(jnp.bfloat16)
        pair_rows = jnp.repeat(hidden[step_index], top_count, axis=0)
        outgoing = jnp.dot(placed, pair_rows, preferred_element_type=jnp.float32).astype(
            jnp.bfloat16
        )
        outgoing = outgoing.reshape(experts, 1, capacity, width)
        gates = route_gates(route_logits[step_index]).reshape(-1)
        weighted = placed * gates[None, :]
        return (outgoing, weighted)

    layouts_all = [layout(step_index) for step_index in range(steps_count)]
    results = []
    for step_index in range(steps_count):
        outgoing, weighted = layouts_all[step_index]
        arrived = lax.all_to_all(outgoing, "expert", split_axis=0, concat_axis=1, tiled=True)
        outputs = apply_expert_block(
            arrived.reshape(-1, width), merged_gate, merged_up, combined_down_weight
        )
        outputs = outputs.reshape(arrived.shape)
        returned = lax.all_to_all(outputs, "expert", split_axis=1, concat_axis=0, tiled=True)
        flat_back = returned.reshape(experts * capacity, width)
        pair_out = jnp.einsum("cp,cd->pd", weighted, flat_back, preferred_element_type=jnp.float32)
        results.append(
            pair_out.reshape(row_count, top_count, width).sum(axis=1).astype(jnp.bfloat16)
        )
    return jnp.stack(results, axis=0)


def shards(hidden, route_ids, route_logits, placement, factors, w_gate, w_up, down_weight):
    rows, top = route_ids.shape[1:]
    width, units = w_gate.shape[1:]
    owners = lax.axis_size("expert")
    rank = factors.shape[1] * owners // (3 * (width + units))
    dense = row_capacity(rows, top, placement.shape[0]) == rows
    dense = dense and lax.axis_size("group") == 2 and split_axis(owners)[2] == 2
    outer = split_axis(owners)[0]
    dense = dense and outer > 1 and outer & (outer - 1) == 0 and split_axis(owners)[1] > 1
    dense = dense and 2 * rank == LANES and width % 256 == 0 and units % 256 == 0
    dense = dense and factors.shape[1] % (8 * LANES) == 0
    return (dense_shards if dense else sparse_shards)(
        hidden, route_ids, route_logits, placement, factors, w_gate, w_up, down_weight
    )


def solution(mesh):
    placed = (
        P(None, ("group", "expert"), None),
        P(None, ("group", "expert"), None),
        P(None, ("group", "expert"), None),
        P(),
        P(None, "expert"),
        P("expert", None, None),
        P("expert", None, None),
        P("expert", None, None),
    )
    return jax.shard_map(
        shards,
        mesh=mesh,
        in_specs=placed,
        out_specs=P(None, ("group", "expert"), None),
        check_vma=False,
    )
```

```python
import functools

import jax
import jax.numpy as jnp
from jax import lax
from jax.experimental import pallas as pl
from jax.experimental.pallas import tpu as pltpu
from jax.sharding import PartitionSpec as P

adapter_scale = 2.0
LANES = 128
GRANT = 16 << 20
EXPERT_GRANT = 32 << 20
WHOLE_GRANT = 60 << 20
LITTLE = pl.CostEstimate(flops=1, bytes_accessed=1, transcendentals=0)


def route_gates(logits):
    highest = jnp.max(logits, axis=-1, keepdims=True)
    router_scores = jnp.exp(logits - highest)
    return (router_scores / jnp.sum(router_scores, axis=-1, keepdims=True)).astype(jnp.bfloat16)


def split_axis(n):
    cores = 2 if n % 2 == 0 else 1
    chips = n // cores
    middle = 1
    while chips % (2 * middle) == 0 and 4 * middle * middle <= chips:
        middle *= 2
    return chips // middle, middle, cores


def swap(x, n, stride, k):
    return lax.ppermute(x, "expert", [(i, i ^ (k * stride)) for i in range(n)])


def double_along(x, n, stride, size):
    step = size // 2
    while step:
        x = jnp.concatenate([x, swap(x, n, stride, step)])
        step //= 2
    return x


def halve_along(total, n, stride, size):
    step = 1
    while step < size:
        half = total.shape[0] // 2
        sent = swap(total[half:].astype(jnp.bfloat16), n, stride, step)
        total = total[:half] + sent.astype(jnp.float32)
        step *= 2
    return total


def exchange_factors(blocks, n):
    outer, middle, cores = split_axis(n)
    here = []
    for q in range(outer):
        pairs = []
        for g in range(2):
            for i in range(n):
                pairs.append((g * n + i, g * n + (i ^ (q * middle * cores) ^ g)))
        part = jnp.stack([block[q] for block in blocks])
        here.append(lax.ppermute(part, ("group", "expert"), pairs))
    return here


def dot(a, b):
    return jnp.dot(a, b, preferred_element_type=jnp.float32)


def payload_kernel(hidden_ref, ids_ref, logits_ref, out_ref, turned_ref):
    steps, top, rows = ids_ref.shape
    width = hidden_ref.shape[2]
    turned_ref[...] = jnp.zeros_like(turned_ref)
    for s in range(steps):
        logits, ids = logits_ref[s], ids_ref[s]
        scores = jnp.exp(logits - jnp.max(logits, axis=0, keepdims=True))
        gates = scores / jnp.sum(scores, axis=0, keepdims=True)
        expert = lax.broadcasted_iota(jnp.int32, (turned_ref.shape[0], rows), 0)
        dense = jnp.zeros(expert.shape, jnp.float32)
        for k in range(top):
            dense += jnp.where(ids[k : k + 1, :] == expert, gates[k : k + 1, :], 0.0)
        turned_ref[:, s * rows : (s + 1) * rows] = dense
    dense = turned_ref[...].T.astype(jnp.bfloat16)
    for s in range(steps):
        out_ref[s * rows : (s + 1) * rows, :width] = hidden_ref[s]
    out_ref[:, width:] = dense[: steps * rows]


def make_payload(hidden, route_ids, route_logits, experts):
    steps, rows, width = hidden.shape
    padded = -(-experts // LANES) * LANES
    return pl.pallas_call(
        payload_kernel,
        out_shape=jax.ShapeDtypeStruct((steps * rows, width + padded), jnp.bfloat16),
        scratch_shapes=[pltpu.VMEM((padded, -(-steps * rows // LANES) * LANES), jnp.float32)],
        compiler_params=pltpu.CompilerParams(vmem_limit_bytes=WHOLE_GRANT),
        cost_estimate=LITTLE,
        name="payload",
    )(hidden, jnp.swapaxes(route_ids, 1, 2), jnp.swapaxes(route_logits, 1, 2))


def order_kernel(middle, place_ref, placement_ref, factors_ref, *refs):
    out_refs, wide_ref = refs[:-1], refs[-1]
    slots = factors_ref.shape[0]
    length, lanes = out_refs[0].shape[1:]
    group, me = place_ref[0], place_ref[1]

    def cut(t, carry):
        start = pl.multiple_of(t * lanes, lanes)
        tile = factors_ref[:, pl.ds(start, lanes)].astype(jnp.float32)
        wide_ref[pl.ds(t, slots, stride=length), :] = tile
        return carry

    lax.fori_loop(0, length, cut, 0, unroll=8)

    def put(s, carry):
        to = placement_ref[s]
        away = to ^ me
        aside, ahead = lax.rem(away // 2, middle), away // (2 * middle)
        ours = lax.rem(away, 2) == group
        rows = wide_ref[pl.ds(pl.multiple_of(s * length, 8), length), :].astype(jnp.bfloat16)
        for r, out_ref in enumerate(out_refs):

            @pl.when(jnp.logical_and(ours, aside == r))
            def _():
                out_ref[ahead] = rows

        return carry

    lax.fori_loop(0, slots, put, 0)


def order_factors(place, placement, factors, n):
    outer, middle, _ = split_axis(n)
    slots, entries = factors.shape
    length = entries // LANES
    return pl.pallas_call(
        functools.partial(order_kernel, middle),
        out_shape=[jax.ShapeDtypeStruct((outer, length, LANES), jnp.bfloat16)] * middle,
        in_specs=[
            pl.BlockSpec(memory_space=pltpu.SMEM),
            pl.BlockSpec(memory_space=pltpu.SMEM),
            pl.BlockSpec(memory_space=pltpu.VMEM),
        ],
        scratch_shapes=[pltpu.VMEM((slots * length, LANES), jnp.float32)],
        compiler_params=pltpu.CompilerParams(vmem_limit_bytes=WHOLE_GRANT),
        cost_estimate=LITTLE,
        name="order_factors",
    )(place, placement, factors)


def relayout_kernel(middle, place_ref, *refs):
    parts, refs = refs[:2], refs[2:]
    a_gu_ref, gate_b_ref, up_b_ref, down_a_ref, down_b_ref, flat_ref, wide_ref = refs
    width, units = a_gu_ref.shape[0], gate_b_ref.shape[1]
    rank = gate_b_ref.shape[0]
    outer, _, length, _ = parts[0].shape
    group, me = place_ref[0], place_ref[1]
    for swapped, part in enumerate(parts):
        core = group if swapped == 0 else 1 - group
        for q in range(outer):
            for r in range(middle):
                source = me ^ ((q * middle + r) * 2 + core)
                start = pl.multiple_of(source * length, 8)
                flat_ref[pl.ds(start, length), :] = part[q, r].astype(jnp.float32)

    n_wide, n_unit = width // 2, units // 2
    at_ub = 2 * n_wide + n_unit
    at_da = 2 * n_wide + 2 * n_unit
    chunk = 128
    left = lax.broadcasted_iota(jnp.int32, (chunk, LANES), 1) < rank

    def load(start):
        return flat_ref[pl.ds(pl.multiple_of(start, 128), chunk), :]

    def gate_up(i, carry):
        g, u = load(i * chunk), load(n_wide + n_unit + i * chunk)
        at = 2 * i * chunk
        wide_ref[pl.ds(at, chunk, stride=2), :] = jnp.where(left, g, pltpu.roll(u, rank, 1))
        wide_ref[pl.ds(at + 1, chunk, stride=2), :] = jnp.where(left, pltpu.roll(g, rank, 1), u)
        both = wide_ref[pl.ds(pl.multiple_of(at, 128), 2 * chunk), :]
        a_gu_ref[pl.ds(pl.multiple_of(at, 128), 2 * chunk), :] = both.astype(jnp.bfloat16)
        return carry

    lax.fori_loop(0, n_wide // chunk, gate_up, 0, unroll=2)
    for i in range(n_unit // chunk):
        d = load(at_da + i * chunk)
        at = 2 * i * chunk
        wide_ref[pl.ds(at, chunk, stride=2), :] = jnp.where(left, d, 0.0)
        wide_ref[pl.ds(at + 1, chunk, stride=2), :] = jnp.where(left, pltpu.roll(d, rank, 1), 0.0)
        down_a_ref[at : at + 2 * chunk, :] = wide_ref[at : at + 2 * chunk, :].astype(jnp.bfloat16)
    for start, b_ref in (
        (n_wide, gate_b_ref),
        (at_ub, up_b_ref),
        (at_da + n_unit, down_b_ref),
    ):
        tiles = b_ref.shape[1] // LANES
        for j in range(tiles):
            row = flat_ref[pl.ds(start + j, rank, stride=tiles), :]
            b_ref[:, j * LANES : (j + 1) * LANES] = row.astype(jnp.bfloat16)


def relayout_factors(place, here, there, width, units, rank, n):
    middle = split_axis(n)[1]
    shapes = [(width, 2 * rank), (rank, units), (rank, units), (units, 2 * rank), (rank, width)]
    length = here.shape[2]
    return pl.pallas_call(
        functools.partial(relayout_kernel, middle),
        out_shape=[jax.ShapeDtypeStruct(shape, jnp.bfloat16) for shape in shapes],
        in_specs=[pl.BlockSpec(memory_space=pltpu.SMEM)]
        + [pl.BlockSpec(memory_space=pltpu.VMEM)] * 2,
        scratch_shapes=[
            pltpu.VMEM((n * length, LANES), jnp.float32),
            pltpu.VMEM((width, LANES), jnp.float32),
        ],
        compiler_params=pltpu.CompilerParams(vmem_limit_bytes=GRANT),
        cost_estimate=LITTLE,
        name="relayout_factors",
    )(place, here, there)


class Loads:
    def __init__(self, sem):
        self.sem, self.count = sem, 0

    def begin(self, src, dst):
        copy = pltpu.make_async_copy(src, dst, self.sem.at[self.count])
        copy.start()
        self.count += 1
        return [copy]

    def begin_rows(self, src, dst, parts=4):
        step = src.shape[0] // parts
        cuts = [pl.ds(at, step) for at in range(0, src.shape[0], step)]
        return sum([self.begin(src.at[cut], dst.at[cut]) for cut in cuts], [])


def wait(copies):
    for copy in copies:
        copy.wait()


def base_kernel(count, *refs):
    pieces = refs[:count]
    w_gate_hbm, w_up_hbm, gate_hbm, up_hbm, x_ref, w_gate_ref, w_up_ref = refs[count : count + 7]
    gate_ref, up_ref, sem, out_sem = refs[count + 7 :]
    rows = pieces[0].shape[0]
    width = w_gate_ref.shape[0]
    total = gate_ref.shape[0]
    block = min(128, total)
    loads = Loads(sem)
    x_in = [loads.begin(p, x_ref.at[pl.ds(i * rows, rows)]) for i, p in enumerate(pieces)]
    x_in = sum(x_in, [])
    gate_in = loads.begin_rows(w_gate_hbm, w_gate_ref)
    up_in = loads.begin_rows(w_up_hbm, w_up_ref)
    wait(x_in + gate_in + up_in)

    def store(i):
        here = pl.ds(pl.multiple_of(i * block, block), block)
        return [
            pltpu.make_async_copy(src.at[here], dst.at[here], out_sem.at[j, i])
            for j, (src, dst) in enumerate(((gate_ref, gate_hbm), (up_ref, up_hbm)))
        ]

    def run_block(i, carry):
        here = pl.ds(pl.multiple_of(i * block, block), block)
        gate_ref[here, :] = dot(x_ref[here, :width], w_gate_ref[...])
        up_ref[here, :] = dot(x_ref[here, :width], w_up_ref[...])
        for copy in store(i):
            copy.start()
        return carry

    lax.fori_loop(0, total // block, run_block, 0)
    for i in range(total // block):
        wait(store(i))


def base_products(pieces, w_gate, w_up, cost):
    width, units = w_gate.shape
    total = sum(p.shape[0] for p in pieces)
    out = jax.ShapeDtypeStruct((total, units), jnp.float32)
    return pl.pallas_call(
        functools.partial(base_kernel, len(pieces)),
        out_shape=[out, out],
        in_specs=[pl.BlockSpec(memory_space=pl.ANY)] * len(pieces)
        + [pl.BlockSpec(memory_space=pltpu.HBM)] * 2,
        out_specs=[pl.BlockSpec(memory_space=pl.ANY)] * 2,
        scratch_shapes=[
            pltpu.VMEM((total, pieces[0].shape[1]), jnp.bfloat16),
            pltpu.VMEM(w_gate.shape, w_gate.dtype),
            pltpu.VMEM(w_up.shape, w_up.dtype),
            pltpu.VMEM(out.shape, out.dtype),
            pltpu.VMEM(out.shape, out.dtype),
            pltpu.SemaphoreType.DMA((len(pieces) + 8,)),
            pltpu.SemaphoreType.DMA((2, total // min(128, total))),
        ],
        compiler_params=pltpu.CompilerParams(vmem_limit_bytes=EXPERT_GRANT),
        cost_estimate=cost,
        name="base_products",
    )(*pieces, w_gate, w_up)


def finish_kernel(firsts, rows, place_ref, *refs):
    count = len(firsts)
    pieces, refs = refs[:count], refs[count:]
    base, refs = refs[:count], refs[count:]
    a_gu_hbm, gate_b_hbm, up_b_hbm, down_a_hbm, down_b_hbm = refs[:5]
    w_down_hbm, kept_hbm, sent_hbm, x_ref, gate_ref, up_ref = refs[5:11]
    a_gu_ref, gate_b_ref, up_b_ref, down_a_ref, down_b_ref, w_down_ref = refs[11:17]
    inner_ref, kept_ref, sent_ref, sem, out_sem = refs[17:]
    units, width = w_down_ref.shape
    rank = gate_b_ref.shape[0]
    own = kept_ref.shape[0]
    block = min(128, own)
    loads = Loads(sem)
    x_in, base_in = [], []
    for i, piece in enumerate(pieces):
        src = pl.ds(firsts[i], rows)
        x_in += loads.begin(piece.at[src], x_ref.at[pl.ds(i * rows, rows)])
    x_in += loads.begin(a_gu_hbm, a_gu_ref)
    x_in += loads.begin(gate_b_hbm, gate_b_ref) + loads.begin(up_b_hbm, up_b_ref)
    for i in range(count):
        half, r = i // (count // 2), i % (count // 2)
        src = pl.ds(half * pieces[i].shape[0] + firsts[i], rows)
        dst = pl.ds(i * rows, rows)
        base_in += loads.begin(base[2 * r].at[src], gate_ref.at[dst])
        base_in += loads.begin(base[2 * r + 1].at[src], up_ref.at[dst])
    down_in = loads.begin(down_a_hbm, down_a_ref) + loads.begin(down_b_hbm, down_b_ref)
    down_in += loads.begin_rows(w_down_hbm, w_down_ref)
    cuts = [slice(at, at + block) for at in range(0, 2 * own, block)]
    wait(x_in)
    lows = []
    for cut in cuts:
        low = adapter_scale * dot(x_ref[cut, :width], a_gu_ref[...])
        lows.append(low.astype(jnp.bfloat16))
    wait(base_in)
    for cut, low in zip(cuts, lows):
        g = gate_ref[cut, :] + dot(low[:, :rank], gate_b_ref[...])
        u = up_ref[cut, :] + dot(low[:, rank:], up_b_ref[...])
        inner_ref[cut, :] = (g / (1.0 + jnp.exp(-g)) * u).astype(jnp.bfloat16)
    wait(down_in)
    lows = []
    for cut in cuts:
        low = adapter_scale * dot(inner_ref[cut, :], down_a_ref[...])
        lows.append(low.astype(jnp.bfloat16)[:, :rank])
    out_copies = []
    for cut, low in zip(cuts, lows):
        gates = x_ref[cut, width:].astype(jnp.float32)
        lane = lax.broadcasted_iota(jnp.int32, gates.shape, 1)
        mine = jnp.sum(jnp.where(lane == place_ref[1], gates, 0.0), axis=1, keepdims=True)
        out = (dot(inner_ref[cut, :], w_down_ref[...]) + dot(low, down_b_ref[...])) * mine
        keep = cut.start < own
        out_ref, out_hbm = (kept_ref, kept_hbm) if keep else (sent_ref, sent_hbm)
        at = pl.ds(cut.start if keep else cut.start - own, block)
        out_ref[at, :] = out.astype(out_ref.dtype)
        sem_out = out_sem.at[len(out_copies)]
        out_copies.append(pltpu.make_async_copy(out_ref.at[at], out_hbm.at[at], sem_out))
        out_copies[-1].start()
    wait(out_copies)


def finish_step(place, pieces, base, firsts, rows, low_rank, w_down, cost):
    units, width = w_down.shape
    total = rows * len(pieces)
    own = total // 2
    a_gu, gate_b, up_b, down_a, down_b = low_rank
    rank = down_b.shape[0]
    outs = [
        jax.ShapeDtypeStruct((own, width), jnp.float32),
        jax.ShapeDtypeStruct((own, width), jnp.bfloat16),
    ]
    held = [*low_rank, w_down]
    return pl.pallas_call(
        functools.partial(finish_kernel, firsts, rows),
        out_shape=outs,
        in_specs=[pl.BlockSpec(memory_space=pltpu.SMEM)]
        + [pl.BlockSpec(memory_space=pl.ANY)] * (2 * len(pieces) + len(low_rank))
        + [pl.BlockSpec(memory_space=pltpu.HBM)],
        out_specs=[pl.BlockSpec(memory_space=pl.ANY)] * 2,
        scratch_shapes=[
            pltpu.VMEM((total, pieces[0].shape[1]), jnp.bfloat16),
            pltpu.VMEM((total, units), jnp.float32),
            pltpu.VMEM((total, units), jnp.float32),
        ]
        + [pltpu.VMEM(a.shape, a.dtype) for a in held]
        + [pltpu.VMEM((total, units), jnp.bfloat16)]
        + [pltpu.VMEM(o.shape, o.dtype) for o in outs]
        + [
            pltpu.SemaphoreType.DMA((3 * len(pieces) + 9,)),
            pltpu.SemaphoreType.DMA((2 * own // min(128, own),)),
        ],
        compiler_params=pltpu.CompilerParams(vmem_limit_bytes=EXPERT_GRANT),
        cost_estimate=cost,
        name="finish_step",
    )(place, *pieces, *base, *held)


def dense_shards(
    hidden, route_ids, route_logits, placement, factors, w_gate, w_up, down_weight
):
    owners = lax.axis_size("expert")
    experts = placement.shape[0]
    steps, rows, width = hidden.shape
    units = w_gate.shape[2]
    rank = factors.shape[1] * owners // (3 * (width + units))
    outer, middle, cores = split_axis(owners)
    along_outer, along_middle = (middle * cores, outer), (cores, middle)
    place = jnp.stack([lax.axis_index("group"), lax.axis_index("expert")]).astype(jnp.int32)

    blocks = order_factors(place, placement, factors, owners)
    hidden, blocks = lax.optimization_barrier((hidden, blocks))
    rows_in = make_payload(hidden, route_ids, route_logits, experts)
    blocks = [blocks[0]] + [swap(blocks[r], owners, cores, r) for r in range(1, middle)]
    here = jnp.stack(exchange_factors(blocks, owners))
    column = double_along(rows_in, owners, *along_outer)
    column, here = lax.optimization_barrier((column, here))
    there = lax.ppermute(here, "group", [(0, 1), (1, 0)])
    column = jnp.swapaxes(column.reshape(outer, steps, rows, -1), 0, 1)
    column = column.reshape(steps * outer * rows, -1)
    span = outer * rows
    weights = (w_gate[0], w_up[0])

    def with_other_core(piece):
        return [piece, swap(piece, owners, 1, 1)]

    def along_middle_of(part):
        return [swap(part, owners, cores, r) for r in range(1, middle)]

    near = with_other_core(column)
    flops = 8 * near[0].shape[0] * width * units
    cost = pl.CostEstimate(flops=flops, bytes_accessed=1, transcendentals=0)
    near_base = base_products(near, *weights, cost)
    far, near_base, rest = lax.optimization_barrier(
        (along_middle_of(column[:span]), near_base, column[span:])
    )
    rest_far = along_middle_of(rest)
    far = [with_other_core(part) for part in far]
    far_base = [base_products(pair, *weights, LITTLE) for pair in far]
    low_rank = relayout_factors(place, here, there, width, units, rank, owners)

    summed, across = [], []
    for s in range(steps):
        if s == 1:
            far = [with_other_core(part) for part in rest_far]
            far_base = [base_products(pair, *weights, LITTLE) for pair in far]
        at = max(0, s - 1) * span
        pairs = [near] + far
        firsts = [s * span] + [at] * len(far)
        pieces = [pair[0] for pair in pairs] + [pair[1] for pair in pairs]
        base = [b for pair in [near_base] + far_base for b in pair]
        if s >= 1:
            pieces, summed[s - 1] = lax.optimization_barrier((pieces, summed[s - 1]))
            across.append(halve_along(summed[s - 1], owners, *along_middle))
        if s >= 2:
            pieces, across[s - 2] = lax.optimization_barrier((pieces, across[s - 2]))
        kept, sent = finish_step(
            place, pieces, base, firsts * 2, span, low_rank, down_weight[0], cost if s >= 2 else LITTLE
        )
        summed.append(kept + swap(sent, owners, 1, 1).astype(jnp.float32))
    across.append(halve_along(summed[-1], owners, *along_middle))
    results = [halve_along(total, owners, *along_outer) for total in across]
    return jnp.stack(results).astype(jnp.bfloat16)


def row_capacity(rows, top, experts):
    return min(rows, 3 * max(1, rows * top // experts))


def unpack_factors(flat_factors, width, hidden_units, rank_size):
    layouts = [
        (width, rank_size),
        (rank_size, hidden_units),
        (width, rank_size),
        (rank_size, hidden_units),
        (hidden_units, rank_size),
        (rank_size, width),
    ]
    offset = 0
    segments = []
    for leading, trailing in layouts:
        segments.append(
            flat_factors[offset : offset + leading * trailing].reshape(leading, trailing)
        )
        offset = offset + leading * trailing
    return segments


def merge_weight(loaded_weights, factor_a, factor_b):
    adapter_delta = jnp.dot(factor_a, factor_b, preferred_element_type=jnp.float32)
    return (loaded_weights.astype(jnp.float32) + adapter_scale * adapter_delta).astype(jnp.bfloat16)


def apply_expert_block(inputs, merged_gate, merged_up, combined_down_weight):
    gate_part = jnp.dot(inputs, merged_gate, preferred_element_type=jnp.float32)
    up_part = jnp.dot(inputs, merged_up, preferred_element_type=jnp.float32)
    inner = (jax.nn.silu(gate_part) * up_part).astype(jnp.bfloat16)
    return jnp.dot(inner, combined_down_weight, preferred_element_type=jnp.float32).astype(
        jnp.bfloat16
    )


def sparse_shards(hidden, route_ids, route_logits, placement, factors, w_gate, w_up, down_weight):
    owners = lax.axis_size("expert")
    experts = placement.shape[0]
    steps_count, row_count, width = hidden.shape
    top_count = route_ids.shape[2]
    hidden_units = w_gate.shape[2]
    rank_size = factors.shape[1] * owners // (3 * (width + hidden_units))
    capacity = row_capacity(row_count, top_count, experts)
    slot_of = (
        jnp.zeros((experts,), jnp.int32).at[placement].set(jnp.arange(experts, dtype=jnp.int32))
    )
    ordered = jnp.take(factors, slot_of, axis=0)
    received = lax.all_to_all(ordered, "expert", split_axis=0, concat_axis=1, tiled=True)
    segments = unpack_factors(received[0], width, hidden_units, rank_size)
    merged_gate = merge_weight(w_gate[0], segments[0], segments[1])
    merged_up = merge_weight(w_up[0], segments[2], segments[3])
    combined_down_weight = merge_weight(down_weight[0], segments[4], segments[5])

    def layout(step_index):
        ids_flat = route_ids[step_index].reshape(-1)
        onehot = (ids_flat[:, None] == jnp.arange(experts, dtype=jnp.int32)[None, :]).astype(
            jnp.int32
        )
        position = jnp.sum((jnp.cumsum(onehot, axis=0) - 1) * onehot, axis=1)
        target = ids_flat * capacity + position
        placed = (
            jnp.arange(experts * capacity, dtype=jnp.int32)[:, None] == target[None, :]
        ).astype(jnp.bfloat16)
        pair_rows = jnp.repeat(hidden[step_index], top_count, axis=0)
        outgoing = jnp.dot(placed, pair_rows, preferred_element_type=jnp.float32).astype(
            jnp.bfloat16
        )
        outgoing = outgoing.reshape(experts, 1, capacity, width)
        gates = route_gates(route_logits[step_index]).reshape(-1)
        weighted = placed * gates[None, :]
        return (outgoing, weighted)

    layouts_all = [layout(step_index) for step_index in range(steps_count)]
    results = []
    for step_index in range(steps_count):
        outgoing, weighted = layouts_all[step_index]
        arrived = lax.all_to_all(outgoing, "expert", split_axis=0, concat_axis=1, tiled=True)
        outputs = apply_expert_block(
            arrived.reshape(-1, width), merged_gate, merged_up, combined_down_weight
        )
        outputs = outputs.reshape(arrived.shape)
        returned = lax.all_to_all(outputs, "expert", split_axis=1, concat_axis=0, tiled=True)
        flat_back = returned.reshape(experts * capacity, width)
        pair_out = jnp.einsum("cp,cd->pd", weighted, flat_back, preferred_element_type=jnp.float32)
        results.append(
            pair_out.reshape(row_count, top_count, width).sum(axis=1).astype(jnp.bfloat16)
        )
    return jnp.stack(results, axis=0)


def shards(hidden, route_ids, route_logits, placement, factors, w_gate, w_up, down_weight):
    rows, top = route_ids.shape[1:]
    width, units = w_gate.shape[1:]
    owners = lax.axis_size("expert")
    rank = factors.shape[1] * owners // (3 * (width + units))
    dense = row_capacity(rows, top, placement.shape[0]) == rows
    dense = dense and lax.axis_size("group") == 2 and split_axis(owners)[2] == 2
    outer = split_axis(owners)[0]
    dense = dense and outer > 1 and outer & (outer - 1) == 0 and split_axis(owners)[1] > 1
    dense = dense and 2 * rank == LANES and width % 256 == 0 and units % 256 == 0
    dense = dense and factors.shape[1] % (8 * LANES) == 0
    return (dense_shards if dense else sparse_shards)(
        hidden, route_ids, route_logits, placement, factors, w_gate, w_up, down_weight
    )


def solution(mesh):
    placed = (
        P(None, ("group", "expert"), None),
        P(None, ("group", "expert"), None),
        P(None, ("group", "expert"), None),
        P(),
        P(None, "expert"),
        P("expert", None, None),
        P("expert", None, None),
        P("expert", None, None),
    )
    return jax.shard_map(
        shards,
        mesh=mesh,
        in_specs=placed,
        out_specs=P(None, ("group", "expert"), None),
        check_vma=False,
    )
```

```python
import functools

import jax
import jax.numpy as jnp
from jax import lax
from jax.experimental import pallas as pl
from jax.experimental.pallas import tpu as pltpu
from jax.sharding import PartitionSpec as P

adapter_scale = 2.0
LANES = 128
GRANT = 16 << 20
EXPERT_GRANT = 32 << 20
WHOLE_GRANT = 60 << 20
MUCH = pl.CostEstimate(flops=1 << 33, bytes_accessed=1, transcendentals=0)
LITTLE = pl.CostEstimate(flops=1, bytes_accessed=1, transcendentals=0)


def route_gates(logits):
    highest = jnp.max(logits, axis=-1, keepdims=True)
    router_scores = jnp.exp(logits - highest)
    return (router_scores / jnp.sum(router_scores, axis=-1, keepdims=True)).astype(jnp.bfloat16)


def split_axis(n):
    cores = 2 if n % 2 == 0 else 1
    chips = n // cores
    middle = 1
    while chips % (2 * middle) == 0 and 4 * middle * middle <= chips:
        middle *= 2
    return chips // middle, middle, cores


def swap(x, n, stride, k):
    return lax.ppermute(x, "expert", [(i, i ^ (k * stride)) for i in range(n)])


def double_along(arrays, n, stride, size, first=lambda arrays: arrays):
    step = size // 2
    while step:
        arrays = [jnp.concatenate([x, swap(x, n, stride, step)]) for x in arrays]
        if step == size // 2:
            arrays = first(arrays)
        step //= 2
    return arrays


def scatter_along(total, n, stride, size):
    places = [0]
    step = size // 2
    while step:
        places += [k ^ step for k in places]
        step //= 2
    count = total.shape[0] // size
    result = total[:count]
    for i in range(1, size):
        part = total[i * count : (i + 1) * count].astype(jnp.bfloat16)
        result = result + swap(part, n, stride, places[i]).astype(jnp.float32)
    return result


def exchange_factors(blocks, n, stride):
    here = []
    for q in range(blocks[0].shape[0]):
        pairs = [(g * n + i, g * n + (i ^ (q * stride) ^ g)) for g in range(2) for i in range(n)]
        part = jnp.stack([block[q] for block in blocks])
        here.append(lax.ppermute(part, ("group", "expert"), pairs))
    return jnp.concatenate(here)


def dot(a, b):
    return jnp.dot(a, b, preferred_element_type=jnp.float32)


def gates_kernel(ids_ref, logits_ref, out_ref, turned_ref):
    steps, top, rows = ids_ref.shape
    turned_ref[...] = jnp.zeros_like(turned_ref)
    for s in range(steps):
        logits, ids = logits_ref[s], ids_ref[s]
        scores = jnp.exp(logits - jnp.max(logits, axis=0, keepdims=True))
        gates = scores / jnp.sum(scores, axis=0, keepdims=True)
        expert = lax.broadcasted_iota(jnp.int32, (turned_ref.shape[0], rows), 0)
        dense = jnp.zeros(expert.shape, jnp.float32)
        for k in range(top):
            dense += jnp.where(ids[k : k + 1, :] == expert, gates[k : k + 1, :], 0.0)
        turned_ref[:, s * rows : (s + 1) * rows] = dense
    out_ref[...] = turned_ref[...].T.astype(jnp.bfloat16)[: steps * rows]


def dense_gates(route_ids, route_logits, experts):
    steps, rows, _ = route_ids.shape
    padded = -(-experts // LANES) * LANES
    return pl.pallas_call(
        gates_kernel,
        out_shape=jax.ShapeDtypeStruct((steps * rows, padded), jnp.bfloat16),
        scratch_shapes=[pltpu.VMEM((padded, -(-steps * rows // LANES) * LANES), jnp.float32)],
        compiler_params=pltpu.CompilerParams(vmem_limit_bytes=WHOLE_GRANT),
        cost_estimate=MUCH,
        name="dense_gates",
    )(jnp.swapaxes(route_ids, 1, 2), jnp.swapaxes(route_logits, 1, 2))


def order_kernel(place_ref, placement_ref, factors_ref, *refs):
    out_refs, wide_ref, slot_ref = refs[:-2], refs[-2], refs[-1]
    slots = factors_ref.shape[0]
    outer, length, lanes = out_refs[0].shape
    group, me = place_ref[0], place_ref[1]

    def cut(t, carry):
        start = pl.multiple_of(t * lanes, lanes)
        tile = factors_ref[:, pl.ds(start, lanes)].astype(jnp.float32)
        wide_ref[pl.ds(t, slots, stride=length), :] = tile
        return carry

    lax.fori_loop(0, length, cut, 0, unroll=8)
    for s in range(slots):
        slot_ref[placement_ref[s]] = s
    for r, out_ref in enumerate(out_refs):
        for q in range(outer):
            slot = slot_ref[me ^ (2 * (q * len(out_refs) + r) + group)]
            rows = wide_ref[pl.ds(pl.multiple_of(slot * length, 8), length), :]
            out_ref[q] = rows.astype(jnp.bfloat16)


def order_factors(place, placement, factors, outer, middle):
    slots, entries = factors.shape
    length = entries // LANES
    return pl.pallas_call(
        order_kernel,
        out_shape=[jax.ShapeDtypeStruct((outer, length, LANES), jnp.bfloat16)] * middle,
        in_specs=[
            pl.BlockSpec(memory_space=pltpu.SMEM),
            pl.BlockSpec(memory_space=pltpu.SMEM),
            pl.BlockSpec(memory_space=pltpu.VMEM),
        ],
        scratch_shapes=[
            pltpu.VMEM((slots * length, LANES), jnp.float32),
            pltpu.SMEM((slots,), jnp.int32),
        ],
        compiler_params=pltpu.CompilerParams(vmem_limit_bytes=WHOLE_GRANT),
        cost_estimate=MUCH,
        name="order_factors",
    )(place, placement, factors)


def relayout_kernel(place_ref, *refs):
    parts, refs = refs[:2], refs[2:]
    a_gu_ref, gate_b_ref, up_b_ref, down_a_ref, down_b_ref, flat_ref, wide_ref = refs
    width, units = a_gu_ref.shape[0], gate_b_ref.shape[1]
    rank = gate_b_ref.shape[0]
    chips, length, _ = parts[0].shape
    group, me = place_ref[0], place_ref[1]
    for swapped, part in enumerate(parts):
        core = group if swapped == 0 else 1 - group
        for d in range(chips):
            start = pl.multiple_of((me ^ (2 * d + core)) * length, 8)
            flat_ref[pl.ds(start, length), :] = part[d].astype(jnp.float32)

    n_wide, n_unit = width // 2, units // 2
    at_ub = 2 * n_wide + n_unit
    at_da = 2 * n_wide + 2 * n_unit
    chunk = 128
    left = lax.broadcasted_iota(jnp.int32, (chunk, LANES), 1) < rank

    def load(start):
        return flat_ref[pl.ds(pl.multiple_of(start, 128), chunk), :]

    def gate_up(i, carry):
        g, u = load(i * chunk), load(n_wide + n_unit + i * chunk)
        at = 2 * i * chunk
        wide_ref[pl.ds(at, chunk, stride=2), :] = jnp.where(left, g, pltpu.roll(u, rank, 1))
        wide_ref[pl.ds(at + 1, chunk, stride=2), :] = jnp.where(left, pltpu.roll(g, rank, 1), u)
        both = wide_ref[pl.ds(pl.multiple_of(at, 128), 2 * chunk), :]
        a_gu_ref[pl.ds(pl.multiple_of(at, 128), 2 * chunk), :] = both.astype(jnp.bfloat16)
        return carry

    lax.fori_loop(0, n_wide // chunk, gate_up, 0, unroll=2)
    for i in range(n_unit // chunk):
        d = load(at_da + i * chunk)
        at = 2 * i * chunk
        wide_ref[pl.ds(at, chunk, stride=2), :] = jnp.where(left, d, 0.0)
        wide_ref[pl.ds(at + 1, chunk, stride=2), :] = jnp.where(left, pltpu.roll(d, rank, 1), 0.0)
        down_a_ref[at : at + 2 * chunk, :] = wide_ref[at : at + 2 * chunk, :].astype(jnp.bfloat16)
    for start, b_ref in (
        (n_wide, gate_b_ref),
        (at_ub, up_b_ref),
        (at_da + n_unit, down_b_ref),
    ):
        tiles = b_ref.shape[1] // LANES
        for j in range(tiles):
            row = flat_ref[pl.ds(start + j, rank, stride=tiles), :]
            b_ref[:, j * LANES : (j + 1) * LANES] = row.astype(jnp.bfloat16)


def relayout_factors(place, here, there, width, units, rank, n):
    shapes = [(width, 2 * rank), (rank, units), (rank, units), (units, 2 * rank), (rank, width)]
    length = here.shape[1]
    return pl.pallas_call(
        relayout_kernel,
        out_shape=[jax.ShapeDtypeStruct(shape, jnp.bfloat16) for shape in shapes],
        in_specs=[pl.BlockSpec(memory_space=pltpu.SMEM)]
        + [pl.BlockSpec(memory_space=pltpu.VMEM)] * 2,
        scratch_shapes=[
            pltpu.VMEM((n * length, LANES), jnp.float32),
            pltpu.VMEM((width, LANES), jnp.float32),
        ],
        compiler_params=pltpu.CompilerParams(vmem_limit_bytes=GRANT),
        cost_estimate=LITTLE,
        name="relayout_factors",
    )(place, here, there)


class Loads:
    def __init__(self, sem):
        self.sem, self.count = sem, 0

    def begin(self, src, dst):
        copy = pltpu.make_async_copy(src, dst, self.sem.at[self.count])
        copy.start()
        self.count += 1
        return [copy]

    def begin_rows(self, src, dst, parts=4):
        step = src.shape[0] // parts
        cuts = [pl.ds(at, step) for at in range(0, src.shape[0], step)]
        return sum([self.begin(src.at[cut], dst.at[cut]) for cut in cuts], [])


def wait(copies):
    for copy in copies:
        copy.wait()


def base_kernel(count, *refs):
    pieces = refs[:count]
    w_gate_hbm, w_up_hbm, gate_hbm, up_hbm, x_ref, w_gate_ref, w_up_ref = refs[count : count + 7]
    gate_ref, up_ref, sem, out_sem = refs[count + 7 :]
    rows = pieces[0].shape[0]
    width = w_gate_ref.shape[0]
    total = gate_ref.shape[0]
    block = min(128, total)
    loads = Loads(sem)
    x_in = [loads.begin(p, x_ref.at[pl.ds(i * rows, rows)]) for i, p in enumerate(pieces)]
    x_in = sum(x_in, [])
    gate_in = loads.begin_rows(w_gate_hbm, w_gate_ref)
    up_in = loads.begin_rows(w_up_hbm, w_up_ref)
    wait(x_in + gate_in + up_in)

    def store(i):
        here = pl.ds(pl.multiple_of(i * block, block), block)
        return [
            pltpu.make_async_copy(src.at[here], dst.at[here], out_sem.at[j, i])
            for j, (src, dst) in enumerate(((gate_ref, gate_hbm), (up_ref, up_hbm)))
        ]

    def run_block(i, carry):
        here = pl.ds(pl.multiple_of(i * block, block), block)
        gate_ref[here, :] = dot(x_ref[here, :width], w_gate_ref[...])
        up_ref[here, :] = dot(x_ref[here, :width], w_up_ref[...])
        for copy in store(i):
            copy.start()
        return carry

    lax.fori_loop(0, total // block, run_block, 0)
    for i in range(total // block):
        wait(store(i))


def base_products(pieces, w_gate, w_up, cost):
    width, units = w_gate.shape
    total = sum(p.shape[0] for p in pieces)
    out = jax.ShapeDtypeStruct((total, units), jnp.float32)
    return pl.pallas_call(
        functools.partial(base_kernel, len(pieces)),
        out_shape=[out, out],
        in_specs=[pl.BlockSpec(memory_space=pl.ANY)] * len(pieces)
        + [pl.BlockSpec(memory_space=pltpu.HBM)] * 2,
        out_specs=[pl.BlockSpec(memory_space=pl.ANY)] * 2,
        scratch_shapes=[
            pltpu.VMEM((total, pieces[0].shape[1]), jnp.bfloat16),
            pltpu.VMEM(w_gate.shape, w_gate.dtype),
            pltpu.VMEM(w_up.shape, w_up.dtype),
            pltpu.VMEM(out.shape, out.dtype),
            pltpu.VMEM(out.shape, out.dtype),
            pltpu.SemaphoreType.DMA((len(pieces) + 8,)),
            pltpu.SemaphoreType.DMA((2, total // min(128, total))),
        ],
        compiler_params=pltpu.CompilerParams(vmem_limit_bytes=EXPERT_GRANT),
        cost_estimate=cost,
        name="base_products",
    )(*pieces, w_gate, w_up)


def finish_kernel(firsts, rows, place_ref, *refs):
    count = len(firsts)
    pieces, refs = refs[:count], refs[count:]
    base, refs = refs[:count], refs[count:]
    a_gu_hbm, gate_b_hbm, up_b_hbm, down_a_hbm, down_b_hbm = refs[:5]
    w_down_hbm, kept_hbm, sent_hbm, x_ref, gate_ref, up_ref = refs[5:11]
    a_gu_ref, gate_b_ref, up_b_ref, down_a_ref, down_b_ref, w_down_ref = refs[11:17]
    inner_ref, kept_ref, sent_ref, sem, out_sem = refs[17:]
    units, width = w_down_ref.shape
    rank = gate_b_ref.shape[0]
    own = kept_ref.shape[0]
    block = min(128, own)
    loads = Loads(sem)
    x_in, base_in = [], []
    for i, piece in enumerate(pieces):
        src = pl.ds(firsts[i], rows)
        x_in += loads.begin(piece.at[src], x_ref.at[pl.ds(i * rows, rows)])
    x_in += loads.begin(a_gu_hbm, a_gu_ref)
    x_in += loads.begin(gate_b_hbm, gate_b_ref) + loads.begin(up_b_hbm, up_b_ref)
    for i in range(count):
        half, r = i // (count // 2), i % (count // 2)
        src = pl.ds(half * pieces[i].shape[0] + firsts[i], rows)
        dst = pl.ds(i * rows, rows)
        base_in += loads.begin(base[2 * r].at[src], gate_ref.at[dst])
        base_in += loads.begin(base[2 * r + 1].at[src], up_ref.at[dst])
    down_in = loads.begin(down_a_hbm, down_a_ref) + loads.begin(down_b_hbm, down_b_ref)
    down_in += loads.begin_rows(w_down_hbm, w_down_ref)
    cuts = [slice(at, at + block) for at in range(0, 2 * own, block)]
    wait(x_in)
    lows = []
    for cut in cuts:
        low = adapter_scale * dot(x_ref[cut, :width], a_gu_ref[...])
        lows.append(low.astype(jnp.bfloat16))
    wait(base_in)
    for cut, low in zip(cuts, lows):
        g = gate_ref[cut, :] + dot(low[:, :rank], gate_b_ref[...])
        u = up_ref[cut, :] + dot(low[:, rank:], up_b_ref[...])
        inner_ref[cut, :] = (g / (1.0 + jnp.exp(-g)) * u).astype(jnp.bfloat16)
    wait(down_in)
    lows = []
    for cut in cuts:
        low = adapter_scale * dot(inner_ref[cut, :], down_a_ref[...])
        lows.append(low.astype(jnp.bfloat16)[:, :rank])
    out_copies = []
    for cut, low in zip(cuts, lows):
        gates = x_ref[cut, width:].astype(jnp.float32)
        lane = lax.broadcasted_iota(jnp.int32, gates.shape, 1)
        mine = jnp.sum(jnp.where(lane == place_ref[1], gates, 0.0), axis=1, keepdims=True)
        out = (dot(inner_ref[cut, :], w_down_ref[...]) + dot(low, down_b_ref[...])) * mine
        keep = cut.start < own
        out_ref, out_hbm = (kept_ref, kept_hbm) if keep else (sent_ref, sent_hbm)
        at = pl.ds(cut.start if keep else cut.start - own, block)
        out_ref[at, :] = out.astype(out_ref.dtype)
        sem_out = out_sem.at[len(out_copies)]
        out_copies.append(pltpu.make_async_copy(out_ref.at[at], out_hbm.at[at], sem_out))
        out_copies[-1].start()
    wait(out_copies)


def finish_step(place, pieces, base, firsts, rows, low_rank, w_down, cost):
    units, width = w_down.shape
    total = rows * len(pieces)
    own = total // 2
    a_gu, gate_b, up_b, down_a, down_b = low_rank
    rank = down_b.shape[0]
    outs = [
        jax.ShapeDtypeStruct((own, width), jnp.float32),
        jax.ShapeDtypeStruct((own, width), jnp.bfloat16),
    ]
    held = [*low_rank, w_down]
    return pl.pallas_call(
        functools.partial(finish_kernel, firsts, rows),
        out_shape=outs,
        in_specs=[pl.BlockSpec(memory_space=pltpu.SMEM)]
        + [pl.BlockSpec(memory_space=pl.ANY)] * (2 * len(pieces) + len(low_rank))
        + [pl.BlockSpec(memory_space=pltpu.HBM)],
        out_specs=[pl.BlockSpec(memory_space=pl.ANY)] * 2,
        scratch_shapes=[
            pltpu.VMEM((total, pieces[0].shape[1]), jnp.bfloat16),
            pltpu.VMEM((total, units), jnp.float32),
            pltpu.VMEM((total, units), jnp.float32),
        ]
        + [pltpu.VMEM(a.shape, a.dtype) for a in held]
        + [pltpu.VMEM((total, units), jnp.bfloat16)]
        + [pltpu.VMEM(o.shape, o.dtype) for o in outs]
        + [
            pltpu.SemaphoreType.DMA((3 * len(pieces) + 9,)),
            pltpu.SemaphoreType.DMA((2 * own // min(128, own),)),
        ],
        compiler_params=pltpu.CompilerParams(vmem_limit_bytes=EXPERT_GRANT),
        cost_estimate=cost,
        name="finish_step",
    )(place, *pieces, *base, *held)


def dense_shards(
    hidden, route_ids, route_logits, placement, factors, w_gate, w_up, down_weight
):
    owners = lax.axis_size("expert")
    experts = placement.shape[0]
    steps, rows, width = hidden.shape
    units = w_gate.shape[2]
    rank = factors.shape[1] * owners // (3 * (width + units))
    outer, middle, cores = split_axis(owners)
    along_outer, along_middle = (middle * cores, outer), (cores, middle)
    place = jnp.stack([lax.axis_index("group"), lax.axis_index("expert")]).astype(jnp.int32)

    blocks = order_factors(place, placement, factors, outer, middle)
    blocks = [blocks[0]] + [swap(blocks[r], owners, cores, r) for r in range(1, middle)]
    gates = dense_gates(route_ids, route_logits, experts)
    arrays = [hidden.reshape(steps * rows, width), gates]

    def after_first(arrays):
        nonlocal blocks
        arrays, blocks = lax.optimization_barrier((arrays, blocks))
        return arrays

    column, gates = double_along(arrays, owners, *along_outer, after_first)
    here = exchange_factors(blocks, owners, along_outer[0])
    column, gates, here = lax.optimization_barrier((column, gates, here))
    there = lax.ppermute(here, "group", [(0, 1), (1, 0)])
    column = jnp.concatenate([column, gates], axis=1).reshape(outer, steps, rows, -1)
    column = jnp.swapaxes(column, 0, 1).reshape(steps * outer * rows, -1)
    span = outer * rows
    weights = (w_gate[0], w_up[0])

    def with_other_core(piece):
        return [piece, swap(piece, owners, 1, 1)]

    def along_middle_of(part):
        return [swap(part, owners, cores, r) for r in range(1, middle)]

    near = with_other_core(column)
    near_base = base_products(near, *weights, MUCH)
    far, near_base, rest = lax.optimization_barrier(
        (along_middle_of(column[:span]), near_base, column[span:])
    )
    rest_far = along_middle_of(rest)
    far = [with_other_core(part) for part in far]
    far_base = [base_products(pair, *weights, LITTLE) for pair in far]
    low_rank = relayout_factors(place, here, there, width, units, rank, owners)

    summed = []
    for s in range(steps):
        if s == 1:
            far = [with_other_core(part) for part in rest_far]
            far_base = [base_products(pair, *weights, LITTLE) for pair in far]
        at = max(0, s - 1) * span
        pairs = [near] + far
        firsts = [s * span] + [at] * len(far)
        pieces = [pair[0] for pair in pairs] + [pair[1] for pair in pairs]
        base = [b for pair in [near_base] + far_base for b in pair]
        if s >= 2:
            pieces, summed[s - 2] = lax.optimization_barrier((pieces, summed[s - 2]))
        kept, sent = finish_step(
            place, pieces, base, firsts * 2, span, low_rank, down_weight[0], LITTLE
        )
        summed.append(kept + swap(sent, owners, 1, 1).astype(jnp.float32))
    results = [scatter_along(total, owners, *along_middle) for total in summed]
    results = [scatter_along(total, owners, *along_outer) for total in results]
    return jnp.stack(results).astype(jnp.bfloat16)


def row_capacity(rows, top, experts):
    return min(rows, 3 * max(1, rows * top // experts))


def unpack_factors(flat_factors, width, hidden_units, rank_size):
    layouts = [
        (width, rank_size),
        (rank_size, hidden_units),
        (width, rank_size),
        (rank_size, hidden_units),
        (hidden_units, rank_size),
        (rank_size, width),
    ]
    offset = 0
    segments = []
    for leading, trailing in layouts:
        segments.append(
            flat_factors[offset : offset + leading * trailing].reshape(leading, trailing)
        )
        offset = offset + leading * trailing
    return segments


def merge_weight(loaded_weights, factor_a, factor_b):
    adapter_delta = jnp.dot(factor_a, factor_b, preferred_element_type=jnp.float32)
    return (loaded_weights.astype(jnp.float32) + adapter_scale * adapter_delta).astype(jnp.bfloat16)


def apply_expert_block(inputs, merged_gate, merged_up, combined_down_weight):
    gate_part = jnp.dot(inputs, merged_gate, preferred_element_type=jnp.float32)
    up_part = jnp.dot(inputs, merged_up, preferred_element_type=jnp.float32)
    inner = (jax.nn.silu(gate_part) * up_part).astype(jnp.bfloat16)
    return jnp.dot(inner, combined_down_weight, preferred_element_type=jnp.float32).astype(
        jnp.bfloat16
    )


def sparse_shards(hidden, route_ids, route_logits, placement, factors, w_gate, w_up, down_weight):
    owners = lax.axis_size("expert")
    experts = placement.shape[0]
    steps_count, row_count, width = hidden.shape
    top_count = route_ids.shape[2]
    hidden_units = w_gate.shape[2]
    rank_size = factors.shape[1] * owners // (3 * (width + hidden_units))
    capacity = row_capacity(row_count, top_count, experts)
    slot_of = (
        jnp.zeros((experts,), jnp.int32).at[placement].set(jnp.arange(experts, dtype=jnp.int32))
    )
    ordered = jnp.take(factors, slot_of, axis=0)
    received = lax.all_to_all(ordered, "expert", split_axis=0, concat_axis=1, tiled=True)
    segments = unpack_factors(received[0], width, hidden_units, rank_size)
    merged_gate = merge_weight(w_gate[0], segments[0], segments[1])
    merged_up = merge_weight(w_up[0], segments[2], segments[3])
    combined_down_weight = merge_weight(down_weight[0], segments[4], segments[5])

    def layout(step_index):
        ids_flat = route_ids[step_index].reshape(-1)
        onehot = (ids_flat[:, None] == jnp.arange(experts, dtype=jnp.int32)[None, :]).astype(
            jnp.int32
        )
        position = jnp.sum((jnp.cumsum(onehot, axis=0) - 1) * onehot, axis=1)
        target = ids_flat * capacity + position
        placed = (
            jnp.arange(experts * capacity, dtype=jnp.int32)[:, None] == target[None, :]
        ).astype(jnp.bfloat16)
        pair_rows = jnp.repeat(hidden[step_index], top_count, axis=0)
        outgoing = jnp.dot(placed, pair_rows, preferred_element_type=jnp.float32).astype(
            jnp.bfloat16
        )
        outgoing = outgoing.reshape(experts, 1, capacity, width)
        gates = route_gates(route_logits[step_index]).reshape(-1)
        weighted = placed * gates[None, :]
        return (outgoing, weighted)

    layouts_all = [layout(step_index) for step_index in range(steps_count)]
    results = []
    for step_index in range(steps_count):
        outgoing, weighted = layouts_all[step_index]
        arrived = lax.all_to_all(outgoing, "expert", split_axis=0, concat_axis=1, tiled=True)
        outputs = apply_expert_block(
            arrived.reshape(-1, width), merged_gate, merged_up, combined_down_weight
        )
        outputs = outputs.reshape(arrived.shape)
        returned = lax.all_to_all(outputs, "expert", split_axis=1, concat_axis=0, tiled=True)
        flat_back = returned.reshape(experts * capacity, width)
        pair_out = jnp.einsum("cp,cd->pd", weighted, flat_back, preferred_element_type=jnp.float32)
        results.append(
            pair_out.reshape(row_count, top_count, width).sum(axis=1).astype(jnp.bfloat16)
        )
    return jnp.stack(results, axis=0)


def shards(hidden, route_ids, route_logits, placement, factors, w_gate, w_up, down_weight):
    rows, top = route_ids.shape[1:]
    width, units = w_gate.shape[1:]
    owners = lax.axis_size("expert")
    rank = factors.shape[1] * owners // (3 * (width + units))
    dense = row_capacity(rows, top, placement.shape[0]) == rows
    dense = dense and lax.axis_size("group") == 2 and split_axis(owners)[2] == 2
    outer = split_axis(owners)[0]
    dense = dense and outer > 1 and outer & (outer - 1) == 0 and split_axis(owners)[1] > 1
    dense = dense and 2 * rank == LANES and width % 256 == 0 and units % 256 == 0
    dense = dense and factors.shape[1] % (8 * LANES) == 0
    return (dense_shards if dense else sparse_shards)(
        hidden, route_ids, route_logits, placement, factors, w_gate, w_up, down_weight
    )


def solution(mesh):
    placed = (
        P(None, ("group", "expert"), None),
        P(None, ("group", "expert"), None),
        P(None, ("group", "expert"), None),
        P(),
        P(None, "expert"),
        P("expert", None, None),
        P("expert", None, None),
        P("expert", None, None),
    )
    return jax.shard_map(
        shards,
        mesh=mesh,
        in_specs=placed,
        out_specs=P(None, ("group", "expert"), None),
        check_vma=False,
    )
```

```python
import functools

import jax
import jax.numpy as jnp
from jax import lax
from jax.experimental import pallas as pl
from jax.experimental.pallas import tpu as pltpu
from jax.sharding import PartitionSpec as P

adapter_scale = 2.0
LANES = 128
GRANT = 16 << 20
EXPERT_GRANT = 32 << 20
WHOLE_GRANT = 60 << 20
LITTLE = pl.CostEstimate(flops=1, bytes_accessed=1, transcendentals=0)


def route_gates(logits):
    highest = jnp.max(logits, axis=-1, keepdims=True)
    router_scores = jnp.exp(logits - highest)
    return (router_scores / jnp.sum(router_scores, axis=-1, keepdims=True)).astype(jnp.bfloat16)


def split_axis(n):
    cores = 2 if n % 2 == 0 else 1
    chips = n // cores
    middle = 1
    while chips % (2 * middle) == 0 and 4 * middle * middle <= chips:
        middle *= 2
    return chips // middle, middle, cores


def swap(x, n, stride, k):
    return lax.ppermute(x, "expert", [(i, i ^ (k * stride)) for i in range(n)])


def scatter_along(total, n, stride, size):
    count = total.shape[0] // size
    result = total[:count]
    for k in range(1, size):
        part = total[k * count : (k + 1) * count].astype(jnp.bfloat16)
        result = result + swap(part, n, stride, k).astype(jnp.float32)
    return result


def exchange_factors(blocks, n):
    outer, middle, cores = split_axis(n)
    here = []
    for q in range(outer):
        pairs = []
        for g in range(2):
            for i in range(n):
                pairs.append((g * n + i, g * n + (i ^ (q * middle * cores) ^ g)))
        part = jnp.stack([block[q] for block in blocks])
        here.append(lax.ppermute(part, ("group", "expert"), pairs))
    return here


def dot(a, b):
    return jnp.dot(a, b, preferred_element_type=jnp.float32)


def payload_kernel(hidden_ref, ids_ref, logits_ref, out_ref, turned_ref):
    steps, top, rows = ids_ref.shape
    width = hidden_ref.shape[2]
    turned_ref[...] = jnp.zeros_like(turned_ref)
    for s in range(steps):
        logits, ids = logits_ref[s], ids_ref[s]
        scores = jnp.exp(logits - jnp.max(logits, axis=0, keepdims=True))
        gates = scores / jnp.sum(scores, axis=0, keepdims=True)
        expert = lax.broadcasted_iota(jnp.int32, (turned_ref.shape[0], rows), 0)
        dense = jnp.zeros(expert.shape, jnp.float32)
        for k in range(top):
            dense += jnp.where(ids[k : k + 1, :] == expert, gates[k : k + 1, :], 0.0)
        turned_ref[:, s * rows : (s + 1) * rows] = dense
    dense = turned_ref[...].T.astype(jnp.bfloat16)
    for s in range(steps):
        out_ref[s * rows : (s + 1) * rows, :width] = hidden_ref[s]
    out_ref[:, width:] = dense[: steps * rows]


def make_payload(hidden, route_ids, route_logits, experts):
    steps, rows, width = hidden.shape
    padded = -(-experts // LANES) * LANES
    return pl.pallas_call(
        payload_kernel,
        out_shape=jax.ShapeDtypeStruct((steps * rows, width + padded), jnp.bfloat16),
        scratch_shapes=[pltpu.VMEM((padded, -(-steps * rows // LANES) * LANES), jnp.float32)],
        compiler_params=pltpu.CompilerParams(vmem_limit_bytes=WHOLE_GRANT),
        cost_estimate=LITTLE,
        name="payload",
    )(hidden, jnp.swapaxes(route_ids, 1, 2), jnp.swapaxes(route_logits, 1, 2))


def order_kernel(place_ref, placement_ref, factors_ref, *refs):
    out_refs, wide_ref, slot_ref = refs[:-2], refs[-2], refs[-1]
    slots = factors_ref.shape[0]
    outer, length, lanes = out_refs[0].shape
    group, me = place_ref[0], place_ref[1]

    def cut(t, carry):
        start = pl.multiple_of(t * lanes, lanes)
        tile = factors_ref[:, pl.ds(start, lanes)].astype(jnp.float32)
        wide_ref[pl.ds(t, slots, stride=length), :] = tile
        return carry

    lax.fori_loop(0, length, cut, 0, unroll=8)
    for s in range(slots):
        slot_ref[placement_ref[s]] = s
    for r, out_ref in enumerate(out_refs):
        for q in range(outer):
            slot = slot_ref[me ^ (2 * (q * len(out_refs) + r) + group)]
            rows = wide_ref[pl.ds(pl.multiple_of(slot * length, 8), length), :]
            out_ref[q] = rows.astype(jnp.bfloat16)


def order_factors(place, placement, factors, outer, middle):
    slots, entries = factors.shape
    length = entries // LANES
    return pl.pallas_call(
        order_kernel,
        out_shape=[jax.ShapeDtypeStruct((outer, length, LANES), jnp.bfloat16)] * middle,
        in_specs=[
            pl.BlockSpec(memory_space=pltpu.SMEM),
            pl.BlockSpec(memory_space=pltpu.SMEM),
            pl.BlockSpec(memory_space=pltpu.VMEM),
        ],
        scratch_shapes=[
            pltpu.VMEM((slots * length, LANES), jnp.float32),
            pltpu.SMEM((slots,), jnp.int32),
        ],
        compiler_params=pltpu.CompilerParams(vmem_limit_bytes=WHOLE_GRANT),
        cost_estimate=LITTLE,
        name="order_factors",
    )(place, placement, factors)


def relayout_kernel(middle, place_ref, *refs):
    parts, refs = refs[:4], refs[4:]
    a_gu_ref, gate_b_ref, up_b_ref, down_a_ref, down_b_ref, flat_ref, wide_ref = refs
    width, units = a_gu_ref.shape[0], gate_b_ref.shape[1]
    rank = gate_b_ref.shape[0]
    half, _, length, _ = parts[0].shape
    group, me = place_ref[0], place_ref[1]
    for i, part in enumerate(parts):
        core = group if i < 2 else 1 - group
        for q in range(half):
            for r in range(middle):
                source = me ^ (((i % 2 * half + q) * middle + r) * 2 + core)
                start = pl.multiple_of(source * length, 8)
                flat_ref[pl.ds(start, length), :] = part[q, r].astype(jnp.float32)

    n_wide, n_unit = width // 2, units // 2
    at_ub = 2 * n_wide + n_unit
    at_da = 2 * n_wide + 2 * n_unit
    chunk = 128
    left = lax.broadcasted_iota(jnp.int32, (chunk, LANES), 1) < rank

    def load(start):
        return flat_ref[pl.ds(pl.multiple_of(start, 128), chunk), :]

    def gate_up(i, carry):
        g, u = load(i * chunk), load(n_wide + n_unit + i * chunk)
        at = 2 * i * chunk
        wide_ref[pl.ds(at, chunk, stride=2), :] = jnp.where(left, g, pltpu.roll(u, rank, 1))
        wide_ref[pl.ds(at + 1, chunk, stride=2), :] = jnp.where(left, pltpu.roll(g, rank, 1), u)
        both = wide_ref[pl.ds(pl.multiple_of(at, 128), 2 * chunk), :]
        a_gu_ref[pl.ds(pl.multiple_of(at, 128), 2 * chunk), :] = both.astype(jnp.bfloat16)
        return carry

    lax.fori_loop(0, n_wide // chunk, gate_up, 0, unroll=2)
    for i in range(n_unit // chunk):
        d = load(at_da + i * chunk)
        at = 2 * i * chunk
        wide_ref[pl.ds(at, chunk, stride=2), :] = jnp.where(left, d, 0.0)
        wide_ref[pl.ds(at + 1, chunk, stride=2), :] = jnp.where(left, pltpu.roll(d, rank, 1), 0.0)
        down_a_ref[at : at + 2 * chunk, :] = wide_ref[at : at + 2 * chunk, :].astype(jnp.bfloat16)
    for start, b_ref in (
        (n_wide, gate_b_ref),
        (at_ub, up_b_ref),
        (at_da + n_unit, down_b_ref),
    ):
        tiles = b_ref.shape[1] // LANES
        for j in range(tiles):
            row = flat_ref[pl.ds(start + j, rank, stride=tiles), :]
            b_ref[:, j * LANES : (j + 1) * LANES] = row.astype(jnp.bfloat16)


def relayout_factors(place, here, there, width, units, rank, n):
    middle = split_axis(n)[1]
    shapes = [(width, 2 * rank), (rank, units), (rank, units), (units, 2 * rank), (rank, width)]
    length = here[0].shape[2]
    return pl.pallas_call(
        functools.partial(relayout_kernel, middle),
        out_shape=[jax.ShapeDtypeStruct(shape, jnp.bfloat16) for shape in shapes],
        in_specs=[pl.BlockSpec(memory_space=pltpu.SMEM)]
        + [pl.BlockSpec(memory_space=pltpu.VMEM)] * 4,
        scratch_shapes=[
            pltpu.VMEM((n * length, LANES), jnp.float32),
            pltpu.VMEM((width, LANES), jnp.float32),
        ],
        compiler_params=pltpu.CompilerParams(vmem_limit_bytes=GRANT),
        cost_estimate=LITTLE,
        name="relayout_factors",
    )(place, *here, *there)


class Loads:
    def __init__(self, sem):
        self.sem, self.count = sem, 0

    def begin(self, src, dst):
        copy = pltpu.make_async_copy(src, dst, self.sem.at[self.count])
        copy.start()
        self.count += 1
        return [copy]

    def begin_rows(self, src, dst, parts=4):
        step = src.shape[0] // parts
        cuts = [pl.ds(at, step) for at in range(0, src.shape[0], step)]
        return sum([self.begin(src.at[cut], dst.at[cut]) for cut in cuts], [])


def wait(copies):
    for copy in copies:
        copy.wait()


def base_kernel(count, *refs):
    pieces = refs[:count]
    w_gate_hbm, w_up_hbm, gate_hbm, up_hbm, x_ref, w_gate_ref, w_up_ref = refs[count : count + 7]
    gate_ref, up_ref, sem, out_sem = refs[count + 7 :]
    rows = pieces[0].shape[0]
    width = w_gate_ref.shape[0]
    total = gate_ref.shape[0]
    block = min(128, total)
    loads = Loads(sem)
    x_in = [loads.begin(p, x_ref.at[pl.ds(i * rows, rows)]) for i, p in enumerate(pieces)]
    x_in = sum(x_in, [])
    gate_in = loads.begin_rows(w_gate_hbm, w_gate_ref)
    up_in = loads.begin_rows(w_up_hbm, w_up_ref)
    wait(x_in + gate_in + up_in)

    def store(i):
        here = pl.ds(pl.multiple_of(i * block, block), block)
        return [
            pltpu.make_async_copy(src.at[here], dst.at[here], out_sem.at[j, i])
            for j, (src, dst) in enumerate(((gate_ref, gate_hbm), (up_ref, up_hbm)))
        ]

    def run_block(i, carry):
        here = pl.ds(pl.multiple_of(i * block, block), block)
        gate_ref[here, :] = dot(x_ref[here, :width], w_gate_ref[...])
        up_ref[here, :] = dot(x_ref[here, :width], w_up_ref[...])
        for copy in store(i):
            copy.start()
        return carry

    lax.fori_loop(0, total // block, run_block, 0)
    for i in range(total // block):
        wait(store(i))


def base_products(pieces, w_gate, w_up):
    width, units = w_gate.shape
    total = sum(p.shape[0] for p in pieces)
    out = jax.ShapeDtypeStruct((total, units), jnp.float32)
    return pl.pallas_call(
        functools.partial(base_kernel, len(pieces)),
        out_shape=[out, out],
        in_specs=[pl.BlockSpec(memory_space=pl.ANY)] * len(pieces)
        + [pl.BlockSpec(memory_space=pltpu.HBM)] * 2,
        out_specs=[pl.BlockSpec(memory_space=pl.ANY)] * 2,
        scratch_shapes=[
            pltpu.VMEM((total, pieces[0].shape[1]), jnp.bfloat16),
            pltpu.VMEM(w_gate.shape, w_gate.dtype),
            pltpu.VMEM(w_up.shape, w_up.dtype),
            pltpu.VMEM(out.shape, out.dtype),
            pltpu.VMEM(out.shape, out.dtype),
            pltpu.SemaphoreType.DMA((len(pieces) + 8,)),
            pltpu.SemaphoreType.DMA((2, total // min(128, total))),
        ],
        compiler_params=pltpu.CompilerParams(vmem_limit_bytes=EXPERT_GRANT),
        cost_estimate=LITTLE,
        name="base_products",
    )(*pieces, w_gate, w_up)


def finish_kernel(count, first, rows, place_ref, *refs):
    pieces, refs = refs[:count], refs[count:]
    base, refs = refs[:count], refs[count:]
    a_gu_hbm, gate_b_hbm, up_b_hbm, down_a_hbm, down_b_hbm = refs[:5]
    w_down_hbm, kept_hbm, sent_hbm, x_ref, gate_ref, up_ref = refs[5:11]
    a_gu_ref, gate_b_ref, up_b_ref, down_a_ref, down_b_ref, w_down_ref = refs[11:17]
    inner_ref, kept_ref, sent_ref, sem, out_sem = refs[17:]
    span = pieces[0].shape[0]
    units, width = w_down_ref.shape
    rank = gate_b_ref.shape[0]
    own = kept_ref.shape[0]
    block = min(128, own)
    loads = Loads(sem)
    x_in, base_in = [], []
    for i, piece in enumerate(pieces):
        x_in += loads.begin(piece.at[pl.ds(first, rows)], x_ref.at[pl.ds(i * rows, rows)])
    x_in += loads.begin(a_gu_hbm, a_gu_ref)
    x_in += loads.begin(gate_b_hbm, gate_b_ref) + loads.begin(up_b_hbm, up_b_ref)
    for i in range(count):
        half, r = i // (count // 2), i % (count // 2)
        src, dst = pl.ds(half * span + first, rows), pl.ds(i * rows, rows)
        base_in += loads.begin(base[2 * r].at[src], gate_ref.at[dst])
        base_in += loads.begin(base[2 * r + 1].at[src], up_ref.at[dst])
    down_in = loads.begin(down_a_hbm, down_a_ref) + loads.begin(down_b_hbm, down_b_ref)
    down_in += loads.begin_rows(w_down_hbm, w_down_ref)
    cuts = [slice(at, at + block) for at in range(0, 2 * own, block)]
    wait(x_in)
    lows = []
    for cut in cuts:
        low = adapter_scale * dot(x_ref[cut, :width], a_gu_ref[...])
        lows.append(low.astype(jnp.bfloat16))
    wait(base_in)
    for cut, low in zip(cuts, lows):
        g = gate_ref[cut, :] + dot(low[:, :rank], gate_b_ref[...])
        u = up_ref[cut, :] + dot(low[:, rank:], up_b_ref[...])
        inner_ref[cut, :] = (g / (1.0 + jnp.exp(-g)) * u).astype(jnp.bfloat16)
    wait(down_in)
    lows = []
    for cut in cuts:
        low = adapter_scale * dot(inner_ref[cut, :], down_a_ref[...])
        lows.append(low.astype(jnp.bfloat16)[:, :rank])
    out_copies = []
    for cut, low in zip(cuts, lows):
        gates = x_ref[cut, width:].astype(jnp.float32)
        lane = lax.broadcasted_iota(jnp.int32, gates.shape, 1)
        mine = jnp.sum(jnp.where(lane == place_ref[1], gates, 0.0), axis=1, keepdims=True)
        out = (dot(inner_ref[cut, :], w_down_ref[...]) + dot(low, down_b_ref[...])) * mine
        keep = cut.start < own
        out_ref, out_hbm = (kept_ref, kept_hbm) if keep else (sent_ref, sent_hbm)
        at = pl.ds(cut.start if keep else cut.start - own, block)
        out_ref[at, :] = out.astype(out_ref.dtype)
        sem_out = out_sem.at[len(out_copies)]
        out_copies.append(pltpu.make_async_copy(out_ref.at[at], out_hbm.at[at], sem_out))
        out_copies[-1].start()
    wait(out_copies)


def finish_step(place, pieces, base, first, rows, low_rank, w_down):
    units, width = w_down.shape
    total = rows * len(pieces)
    own = total // 2
    a_gu, gate_b, up_b, down_a, down_b = low_rank
    rank = down_b.shape[0]
    outs = [
        jax.ShapeDtypeStruct((own, width), jnp.float32),
        jax.ShapeDtypeStruct((own, width), jnp.bfloat16),
    ]
    held = [*low_rank, w_down]
    return pl.pallas_call(
        functools.partial(finish_kernel, len(pieces), first, rows),
        out_shape=outs,
        in_specs=[pl.BlockSpec(memory_space=pltpu.SMEM)]
        + [pl.BlockSpec(memory_space=pl.ANY)] * (2 * len(pieces) + len(low_rank))
        + [pl.BlockSpec(memory_space=pltpu.HBM)],
        out_specs=[pl.BlockSpec(memory_space=pl.ANY)] * 2,
        scratch_shapes=[
            pltpu.VMEM((total, pieces[0].shape[1]), jnp.bfloat16),
            pltpu.VMEM((total, units), jnp.float32),
            pltpu.VMEM((total, units), jnp.float32),
        ]
        + [pltpu.VMEM(a.shape, a.dtype) for a in held]
        + [pltpu.VMEM((total, units), jnp.bfloat16)]
        + [pltpu.VMEM(o.shape, o.dtype) for o in outs]
        + [
            pltpu.SemaphoreType.DMA((3 * len(pieces) + 9,)),
            pltpu.SemaphoreType.DMA((2 * own // min(128, own),)),
        ],
        compiler_params=pltpu.CompilerParams(vmem_limit_bytes=EXPERT_GRANT),
        cost_estimate=LITTLE,
        name="finish_step",
    )(place, *pieces, *base, *held)


def dense_shards(
    hidden, route_ids, route_logits, placement, factors, w_gate, w_up, down_weight
):
    owners = lax.axis_size("expert")
    experts = placement.shape[0]
    steps, rows, width = hidden.shape
    units = w_gate.shape[2]
    rank = factors.shape[1] * owners // (3 * (width + units))
    outer, middle, cores = split_axis(owners)
    along_outer, along_middle = (middle * cores, outer), (cores, middle)
    place = jnp.stack([lax.axis_index("group"), lax.axis_index("expert")]).astype(jnp.int32)

    def along(x, stride, size):
        return [x] + [swap(x, owners, stride, k) for k in range(1, size)]

    rows_in = make_payload(hidden, route_ids, route_logits, experts)
    rows_in, factors = lax.optimization_barrier((rows_in, factors))
    column = [p.reshape(steps, rows, -1) for p in along(rows_in, *along_outer)]
    column = jnp.stack(column, axis=1).reshape(steps * outer * rows, -1)
    blocks = order_factors(place, placement, factors, outer, middle)
    blocks = [blocks[0]] + [swap(blocks[r], owners, cores, r) for r in range(1, middle)]
    column, blocks = lax.optimization_barrier((column, blocks))
    here = exchange_factors(blocks, owners)
    here = [jnp.stack(here[: outer // 2]), jnp.stack(here[outer // 2 :])]
    sheet = along(column, *along_middle)
    others = [swap(column, owners, 1, 1)]
    base = [base_products([sheet[0], others[0]], w_gate[0], w_up[0])]
    there = [lax.ppermute(p, "group", [(0, 1), (1, 0)]) for p in here]
    early = (there[0], here[1], base, sheet[1:])
    there[0], here[1], base, sheet[1:] = lax.optimization_barrier(early)
    for r in range(1, middle):
        others.append(swap(sheet[r], owners, 1, 1))
        base.append(base_products([sheet[r], others[r]], w_gate[0], w_up[0]))
    here, there, base = lax.optimization_barrier((here, there, base))
    low_rank = relayout_factors(place, here, there, width, units, rank, owners)
    pieces, base = sheet + others, [b for pair in base for b in pair]

    span = outer * rows
    results = []
    for s in range(steps):
        if s >= 2:
            pieces, results[s - 2] = lax.optimization_barrier((pieces, results[s - 2]))
        kept, sent = finish_step(place, pieces, base, s * span, span, low_rank, down_weight[0])
        results.append(kept + swap(sent, owners, 1, 1).astype(jnp.float32))
    results = [scatter_along(total, owners, *along_middle) for total in results]
    results = [scatter_along(total, owners, *along_outer) for total in results]
    return jnp.stack(results).astype(jnp.bfloat16)


def row_capacity(rows, top, experts):
    return min(rows, 3 * max(1, rows * top // experts))


def unpack_factors(flat_factors, width, hidden_units, rank_size):
    layouts = [
        (width, rank_size),
        (rank_size, hidden_units),
        (width, rank_size),
        (rank_size, hidden_units),
        (hidden_units, rank_size),
        (rank_size, width),
    ]
    offset = 0
    segments = []
    for leading, trailing in layouts:
        segments.append(
            flat_factors[offset : offset + leading * trailing].reshape(leading, trailing)
        )
        offset = offset + leading * trailing
    return segments


def merge_weight(loaded_weights, factor_a, factor_b):
    adapter_delta = jnp.dot(factor_a, factor_b, preferred_element_type=jnp.float32)
    return (loaded_weights.astype(jnp.float32) + adapter_scale * adapter_delta).astype(jnp.bfloat16)


def apply_expert_block(inputs, merged_gate, merged_up, combined_down_weight):
    gate_part = jnp.dot(inputs, merged_gate, preferred_element_type=jnp.float32)
    up_part = jnp.dot(inputs, merged_up, preferred_element_type=jnp.float32)
    inner = (jax.nn.silu(gate_part) * up_part).astype(jnp.bfloat16)
    return jnp.dot(inner, combined_down_weight, preferred_element_type=jnp.float32).astype(
        jnp.bfloat16
    )


def sparse_shards(hidden, route_ids, route_logits, placement, factors, w_gate, w_up, down_weight):
    owners = lax.axis_size("expert")
    experts = placement.shape[0]
    steps_count, row_count, width = hidden.shape
    top_count = route_ids.shape[2]
    hidden_units = w_gate.shape[2]
    rank_size = factors.shape[1] * owners // (3 * (width + hidden_units))
    capacity = row_capacity(row_count, top_count, experts)
    slot_of = (
        jnp.zeros((experts,), jnp.int32).at[placement].set(jnp.arange(experts, dtype=jnp.int32))
    )
    ordered = jnp.take(factors, slot_of, axis=0)
    received = lax.all_to_all(ordered, "expert", split_axis=0, concat_axis=1, tiled=True)
    segments = unpack_factors(received[0], width, hidden_units, rank_size)
    merged_gate = merge_weight(w_gate[0], segments[0], segments[1])
    merged_up = merge_weight(w_up[0], segments[2], segments[3])
    combined_down_weight = merge_weight(down_weight[0], segments[4], segments[5])

    def layout(step_index):
        ids_flat = route_ids[step_index].reshape(-1)
        onehot = (ids_flat[:, None] == jnp.arange(experts, dtype=jnp.int32)[None, :]).astype(
            jnp.int32
        )
        position = jnp.sum((jnp.cumsum(onehot, axis=0) - 1) * onehot, axis=1)
        target = ids_flat * capacity + position
        placed = (
            jnp.arange(experts * capacity, dtype=jnp.int32)[:, None] == target[None, :]
        ).astype(jnp.bfloat16)
        pair_rows = jnp.repeat(hidden[step_index], top_count, axis=0)
        outgoing = jnp.dot(placed, pair_rows, preferred_element_type=jnp.float32).astype(
            jnp.bfloat16
        )
        outgoing = outgoing.reshape(experts, 1, capacity, width)
        gates = route_gates(route_logits[step_index]).reshape(-1)
        weighted = placed * gates[None, :]
        return (outgoing, weighted)

    layouts_all = [layout(step_index) for step_index in range(steps_count)]
    results = []
    for step_index in range(steps_count):
        outgoing, weighted = layouts_all[step_index]
        arrived = lax.all_to_all(outgoing, "expert", split_axis=0, concat_axis=1, tiled=True)
        outputs = apply_expert_block(
            arrived.reshape(-1, width), merged_gate, merged_up, combined_down_weight
        )
        outputs = outputs.reshape(arrived.shape)
        returned = lax.all_to_all(outputs, "expert", split_axis=1, concat_axis=0, tiled=True)
        flat_back = returned.reshape(experts * capacity, width)
        pair_out = jnp.einsum("cp,cd->pd", weighted, flat_back, preferred_element_type=jnp.float32)
        results.append(
            pair_out.reshape(row_count, top_count, width).sum(axis=1).astype(jnp.bfloat16)
        )
    return jnp.stack(results, axis=0)


def shards(hidden, route_ids, route_logits, placement, factors, w_gate, w_up, down_weight):
    rows, top = route_ids.shape[1:]
    width, units = w_gate.shape[1:]
    owners = lax.axis_size("expert")
    rank = factors.shape[1] * owners // (3 * (width + units))
    dense = row_capacity(rows, top, placement.shape[0]) == rows
    dense = dense and lax.axis_size("group") == 2 and split_axis(owners)[2] == 2
    outer = split_axis(owners)[0]
    dense = dense and outer > 1 and outer & (outer - 1) == 0 and split_axis(owners)[1] > 1
    dense = dense and 2 * rank == LANES and width % 256 == 0 and units % 256 == 0
    dense = dense and factors.shape[1] % (8 * LANES) == 0
    return (dense_shards if dense else sparse_shards)(
        hidden, route_ids, route_logits, placement, factors, w_gate, w_up, down_weight
    )


def solution(mesh):
    placed = (
        P(None, ("group", "expert"), None),
        P(None, ("group", "expert"), None),
        P(None, ("group", "expert"), None),
        P(),
        P(None, "expert"),
        P("expert", None, None),
        P("expert", None, None),
        P("expert", None, None),
    )
    return jax.shard_map(
        shards,
        mesh=mesh,
        in_specs=placed,
        out_specs=P(None, ("group", "expert"), None),
        check_vma=False,
    )
```

```python
import functools

import jax
import jax.numpy as jnp
from jax import lax
from jax.experimental import pallas as pl
from jax.experimental.pallas import tpu as pltpu
from jax.sharding import PartitionSpec as P

adapter_scale = 2.0
LANES = 128
GRANT = 16 << 20
EXPERT_GRANT = 32 << 20
WHOLE_GRANT = 60 << 20
LITTLE = pl.CostEstimate(flops=1, bytes_accessed=1, transcendentals=0)


def route_gates(logits):
    highest = jnp.max(logits, axis=-1, keepdims=True)
    router_scores = jnp.exp(logits - highest)
    return (router_scores / jnp.sum(router_scores, axis=-1, keepdims=True)).astype(jnp.bfloat16)


def split_axis(n):
    cores = 2 if n % 2 == 0 else 1
    chips = n // cores
    middle = 1
    while chips % (2 * middle) == 0 and 4 * middle * middle <= chips:
        middle *= 2
    return chips // middle, middle, cores


def swap(x, n, stride, k):
    return lax.ppermute(x, "expert", [(i, i ^ (k * stride)) for i in range(n)])


def scatter_along(total, n, stride, size):
    count = total.shape[0] // size
    result = total[:count]
    for k in range(1, size):
        part = total[k * count : (k + 1) * count].astype(jnp.bfloat16)
        result = result + swap(part, n, stride, k).astype(jnp.float32)
    return result


def halve_along(total, n, stride, size):
    count = total.shape[0] // size
    step = 1
    while step < size:
        total = total.reshape(-1, 2, count, total.shape[1])
        sent = total[:, 1].reshape(-1, total.shape[3]).astype(jnp.bfloat16)
        kept = total[:, 0].reshape(-1, total.shape[3])
        total = kept + swap(sent, n, stride, step).astype(jnp.float32)
        step *= 2
    return total


def exchange_factors(blocks, n):
    outer, middle, cores = split_axis(n)
    here = []
    for q in range(outer):
        pairs = []
        for g in range(2):
            for i in range(n):
                pairs.append((g * n + i, g * n + (i ^ (q * middle * cores) ^ g)))
        part = jnp.stack([block[q] for block in blocks])
        here.append(lax.ppermute(part, ("group", "expert"), pairs))
    return here


def dot(a, b):
    return jnp.dot(a, b, preferred_element_type=jnp.float32)


def payload_kernel(hidden_ref, ids_ref, logits_ref, out_ref, turned_ref):
    steps, top, rows = ids_ref.shape
    width = hidden_ref.shape[2]
    turned_ref[...] = jnp.zeros_like(turned_ref)
    for s in range(steps):
        logits, ids = logits_ref[s], ids_ref[s]
        scores = jnp.exp(logits - jnp.max(logits, axis=0, keepdims=True))
        gates = scores / jnp.sum(scores, axis=0, keepdims=True)
        expert = lax.broadcasted_iota(jnp.int32, (turned_ref.shape[0], rows), 0)
        dense = jnp.zeros(expert.shape, jnp.float32)
        for k in range(top):
            dense += jnp.where(ids[k : k + 1, :] == expert, gates[k : k + 1, :], 0.0)
        turned_ref[:, s * rows : (s + 1) * rows] = dense
    dense = turned_ref[...].T.astype(jnp.bfloat16)
    for s in range(steps):
        out_ref[s * rows : (s + 1) * rows, :width] = hidden_ref[s]
    out_ref[:, width:] = dense[: steps * rows]


def make_payload(hidden, route_ids, route_logits, experts):
    steps, rows, width = hidden.shape
    padded = -(-experts // LANES) * LANES
    return pl.pallas_call(
        payload_kernel,
        out_shape=jax.ShapeDtypeStruct((steps * rows, width + padded), jnp.bfloat16),
        scratch_shapes=[pltpu.VMEM((padded, -(-steps * rows // LANES) * LANES), jnp.float32)],
        compiler_params=pltpu.CompilerParams(vmem_limit_bytes=WHOLE_GRANT),
        cost_estimate=LITTLE,
        name="payload",
    )(hidden, jnp.swapaxes(route_ids, 1, 2), jnp.swapaxes(route_logits, 1, 2))


def order_kernel(place_ref, placement_ref, factors_ref, *refs):
    out_refs, wide_ref, slot_ref = refs[:-2], refs[-2], refs[-1]
    slots = factors_ref.shape[0]
    outer, length, lanes = out_refs[0].shape
    group, me = place_ref[0], place_ref[1]

    def cut(t, carry):
        start = pl.multiple_of(t * lanes, lanes)
        tile = factors_ref[:, pl.ds(start, lanes)].astype(jnp.float32)
        wide_ref[pl.ds(t, slots, stride=length), :] = tile
        return carry

    lax.fori_loop(0, length, cut, 0, unroll=8)
    for s in range(slots):
        slot_ref[placement_ref[s]] = s
    for r, out_ref in enumerate(out_refs):
        for q in range(outer):
            slot = slot_ref[me ^ (2 * (q * len(out_refs) + r) + group)]
            rows = wide_ref[pl.ds(pl.multiple_of(slot * length, 8), length), :]
            out_ref[q] = rows.astype(jnp.bfloat16)


def order_factors(place, placement, factors, outer, middle):
    slots, entries = factors.shape
    length = entries // LANES
    return pl.pallas_call(
        order_kernel,
        out_shape=[jax.ShapeDtypeStruct((outer, length, LANES), jnp.bfloat16)] * middle,
        in_specs=[
            pl.BlockSpec(memory_space=pltpu.SMEM),
            pl.BlockSpec(memory_space=pltpu.SMEM),
            pl.BlockSpec(memory_space=pltpu.VMEM),
        ],
        scratch_shapes=[
            pltpu.VMEM((slots * length, LANES), jnp.float32),
            pltpu.SMEM((slots,), jnp.int32),
        ],
        compiler_params=pltpu.CompilerParams(vmem_limit_bytes=WHOLE_GRANT),
        cost_estimate=LITTLE,
        name="order_factors",
    )(place, placement, factors)


def relayout_kernel(outer, middle, place_ref, *refs):
    a_gu_ref, gate_b_ref, up_b_ref, down_a_ref, down_b_ref, flat_ref, wide_ref = refs[2:]
    width, units = a_gu_ref.shape[0], gate_b_ref.shape[1]
    rank = gate_b_ref.shape[0]
    length = refs[0].shape[2]
    group, me = place_ref[0], place_ref[1]
    for swapped, part in enumerate(refs[:2]):
        core = group if swapped == 0 else 1 - group
        for q in range(outer):
            for r in range(middle):
                source = me ^ ((q * middle + r) * 2 + core)
                start = pl.multiple_of(source * length, 8)
                flat_ref[pl.ds(start, length), :] = part[q, r].astype(jnp.float32)

    n_wide, n_unit = width // 2, units // 2
    at_ub = 2 * n_wide + n_unit
    at_da = 2 * n_wide + 2 * n_unit
    chunk = 128
    left = lax.broadcasted_iota(jnp.int32, (chunk, LANES), 1) < rank

    def load(start):
        return flat_ref[pl.ds(pl.multiple_of(start, 128), chunk), :]

    def gate_up(i, carry):
        g, u = load(i * chunk), load(n_wide + n_unit + i * chunk)
        at = 2 * i * chunk
        wide_ref[pl.ds(at, chunk, stride=2), :] = jnp.where(left, g, pltpu.roll(u, rank, 1))
        wide_ref[pl.ds(at + 1, chunk, stride=2), :] = jnp.where(left, pltpu.roll(g, rank, 1), u)
        both = wide_ref[pl.ds(pl.multiple_of(at, 128), 2 * chunk), :]
        a_gu_ref[pl.ds(pl.multiple_of(at, 128), 2 * chunk), :] = both.astype(jnp.bfloat16)
        return carry

    lax.fori_loop(0, n_wide // chunk, gate_up, 0, unroll=2)
    for i in range(n_unit // chunk):
        d = load(at_da + i * chunk)
        at = 2 * i * chunk
        wide_ref[pl.ds(at, chunk, stride=2), :] = jnp.where(left, d, 0.0)
        wide_ref[pl.ds(at + 1, chunk, stride=2), :] = jnp.where(left, pltpu.roll(d, rank, 1), 0.0)
        down_a_ref[at : at + 2 * chunk, :] = wide_ref[at : at + 2 * chunk, :].astype(jnp.bfloat16)
    for start, b_ref in (
        (n_wide, gate_b_ref),
        (at_ub, up_b_ref),
        (at_da + n_unit, down_b_ref),
    ):
        tiles = b_ref.shape[1] // LANES
        for j in range(tiles):
            row = flat_ref[pl.ds(start + j, rank, stride=tiles), :]
            b_ref[:, j * LANES : (j + 1) * LANES] = row.astype(jnp.bfloat16)


def relayout_factors(place, here, there, width, units, rank, n):
    outer, middle, _ = split_axis(n)
    shapes = [(width, 2 * rank), (rank, units), (rank, units), (units, 2 * rank), (rank, width)]
    length = here.shape[2]
    return pl.pallas_call(
        functools.partial(relayout_kernel, outer, middle),
        out_shape=[jax.ShapeDtypeStruct(shape, jnp.bfloat16) for shape in shapes],
        in_specs=[pl.BlockSpec(memory_space=pltpu.SMEM)]
        + [pl.BlockSpec(memory_space=pltpu.VMEM)] * 2,
        scratch_shapes=[
            pltpu.VMEM((n * length, LANES), jnp.float32),
            pltpu.VMEM((width, LANES), jnp.float32),
        ],
        compiler_params=pltpu.CompilerParams(vmem_limit_bytes=GRANT),
        cost_estimate=LITTLE,
        name="relayout_factors",
    )(place, here, there)


class Loads:
    def __init__(self, sem):
        self.sem, self.count = sem, 0

    def begin(self, src, dst):
        copy = pltpu.make_async_copy(src, dst, self.sem.at[self.count])
        copy.start()
        self.count += 1
        return [copy]

    def begin_rows(self, src, dst, parts=4):
        step = src.shape[0] // parts
        cuts = [pl.ds(at, step) for at in range(0, src.shape[0], step)]
        return sum([self.begin(src.at[cut], dst.at[cut]) for cut in cuts], [])


def wait(copies):
    for copy in copies:
        copy.wait()


def base_kernel(count, *refs):
    pieces = refs[:count]
    w_gate_hbm, w_up_hbm, gate_hbm, up_hbm, x_ref, w_gate_ref, w_up_ref = refs[count : count + 7]
    gate_ref, up_ref, sem, out_sem = refs[count + 7 :]
    rows = pieces[0].shape[0]
    width = w_gate_ref.shape[0]
    total = gate_ref.shape[0]
    block = min(128, total)
    loads = Loads(sem)
    x_in = [loads.begin(p, x_ref.at[pl.ds(i * rows, rows)]) for i, p in enumerate(pieces)]
    x_in = sum(x_in, [])
    gate_in = loads.begin_rows(w_gate_hbm, w_gate_ref)
    up_in = loads.begin_rows(w_up_hbm, w_up_ref)
    wait(x_in + gate_in + up_in)

    def store(i):
        here = pl.ds(pl.multiple_of(i * block, block), block)
        return [
            pltpu.make_async_copy(src.at[here], dst.at[here], out_sem.at[j, i])
            for j, (src, dst) in enumerate(((gate_ref, gate_hbm), (up_ref, up_hbm)))
        ]

    def run_block(i, carry):
        here = pl.ds(pl.multiple_of(i * block, block), block)
        gate_ref[here, :] = dot(x_ref[here, :width], w_gate_ref[...])
        up_ref[here, :] = dot(x_ref[here, :width], w_up_ref[...])
        for copy in store(i):
            copy.start()
        return carry

    lax.fori_loop(0, total // block, run_block, 0)
    for i in range(total // block):
        wait(store(i))


def base_products(pieces, w_gate, w_up):
    width, units = w_gate.shape
    total = sum(p.shape[0] for p in pieces)
    out = jax.ShapeDtypeStruct((total, units), jnp.float32)
    return pl.pallas_call(
        functools.partial(base_kernel, len(pieces)),
        out_shape=[out, out],
        in_specs=[pl.BlockSpec(memory_space=pl.ANY)] * len(pieces)
        + [pl.BlockSpec(memory_space=pltpu.HBM)] * 2,
        out_specs=[pl.BlockSpec(memory_space=pl.ANY)] * 2,
        scratch_shapes=[
            pltpu.VMEM((total, pieces[0].shape[1]), jnp.bfloat16),
            pltpu.VMEM(w_gate.shape, w_gate.dtype),
            pltpu.VMEM(w_up.shape, w_up.dtype),
            pltpu.VMEM(out.shape, out.dtype),
            pltpu.VMEM(out.shape, out.dtype),
            pltpu.SemaphoreType.DMA((len(pieces) + 8,)),
            pltpu.SemaphoreType.DMA((2, total // min(128, total))),
        ],
        compiler_params=pltpu.CompilerParams(vmem_limit_bytes=EXPERT_GRANT),
        cost_estimate=LITTLE,
        name="base_products",
    )(*pieces, w_gate, w_up)


def finish_kernel(count, first, rows, place_ref, *refs):
    pieces, refs = refs[:count], refs[count:]
    gate_hbm, up_hbm, a_gu_hbm, gate_b_hbm, up_b_hbm, down_a_hbm, down_b_hbm = refs[:7]
    w_down_hbm, kept_hbm, sent_hbm, x_ref, gate_ref, up_ref = refs[7:13]
    a_gu_ref, gate_b_ref, up_b_ref, down_a_ref, down_b_ref, w_down_ref = refs[13:19]
    inner_ref, kept_ref, sent_ref, sem, out_sem = refs[19:]
    span = pieces[0].shape[0]
    units, width = w_down_ref.shape
    rank = gate_b_ref.shape[0]
    own = kept_ref.shape[0]
    block = min(128, own)
    loads = Loads(sem)
    x_in, base_in = [], []
    for i, piece in enumerate(pieces):
        x_in += loads.begin(piece.at[pl.ds(first, rows)], x_ref.at[pl.ds(i * rows, rows)])
    x_in += loads.begin(a_gu_hbm, a_gu_ref)
    x_in += loads.begin(gate_b_hbm, gate_b_ref) + loads.begin(up_b_hbm, up_b_ref)
    for i in range(count):
        src, dst = pl.ds(i * span + first, rows), pl.ds(i * rows, rows)
        base_in += loads.begin(gate_hbm.at[src], gate_ref.at[dst])
        base_in += loads.begin(up_hbm.at[src], up_ref.at[dst])
    down_in = loads.begin(down_a_hbm, down_a_ref) + loads.begin(down_b_hbm, down_b_ref)
    down_in += loads.begin_rows(w_down_hbm, w_down_ref)
    cuts = [slice(at, at + block) for at in range(0, 2 * own, block)]
    wait(x_in)
    lows = []
    for cut in cuts:
        low = adapter_scale * dot(x_ref[cut, :width], a_gu_ref[...])
        lows.append(low.astype(jnp.bfloat16))
    wait(base_in)
    for cut, low in zip(cuts, lows):
        g = gate_ref[cut, :] + dot(low[:, :rank], gate_b_ref[...])
        u = up_ref[cut, :] + dot(low[:, rank:], up_b_ref[...])
        inner_ref[cut, :] = (g / (1.0 + jnp.exp(-g)) * u).astype(jnp.bfloat16)
    wait(down_in)
    lows = []
    for cut in cuts:
        low = adapter_scale * dot(inner_ref[cut, :], down_a_ref[...])
        lows.append(low.astype(jnp.bfloat16)[:, :rank])
    out_copies = []
    for cut, low in zip(cuts, lows):
        gates = x_ref[cut, width:].astype(jnp.float32)
        lane = lax.broadcasted_iota(jnp.int32, gates.shape, 1)
        mine = jnp.sum(jnp.where(lane == place_ref[1], gates, 0.0), axis=1, keepdims=True)
        out = (dot(inner_ref[cut, :], w_down_ref[...]) + dot(low, down_b_ref[...])) * mine
        keep = cut.start < own
        out_ref, out_hbm = (kept_ref, kept_hbm) if keep else (sent_ref, sent_hbm)
        at = pl.ds(cut.start if keep else cut.start - own, block)
        out_ref[at, :] = out.astype(out_ref.dtype)
        sem_out = out_sem.at[len(out_copies)]
        out_copies.append(pltpu.make_async_copy(out_ref.at[at], out_hbm.at[at], sem_out))
        out_copies[-1].start()
    wait(out_copies)


def finish_step(place, pieces, base, first, rows, low_rank, w_down):
    units, width = w_down.shape
    total = rows * len(pieces)
    own = total // 2
    a_gu, gate_b, up_b, down_a, down_b = low_rank
    rank = down_b.shape[0]
    outs = [
        jax.ShapeDtypeStruct((own, width), jnp.float32),
        jax.ShapeDtypeStruct((own, width), jnp.bfloat16),
    ]
    held = [*low_rank, w_down]
    return pl.pallas_call(
        functools.partial(finish_kernel, len(pieces), first, rows),
        out_shape=outs,
        in_specs=[pl.BlockSpec(memory_space=pltpu.SMEM)]
        + [pl.BlockSpec(memory_space=pl.ANY)] * (len(pieces) + 2 + len(low_rank))
        + [pl.BlockSpec(memory_space=pltpu.HBM)],
        out_specs=[pl.BlockSpec(memory_space=pl.ANY)] * 2,
        scratch_shapes=[
            pltpu.VMEM((total, pieces[0].shape[1]), jnp.bfloat16),
            pltpu.VMEM((total, units), jnp.float32),
            pltpu.VMEM((total, units), jnp.float32),
        ]
        + [pltpu.VMEM(a.shape, a.dtype) for a in held]
        + [pltpu.VMEM((total, units), jnp.bfloat16)]
        + [pltpu.VMEM(o.shape, o.dtype) for o in outs]
        + [
            pltpu.SemaphoreType.DMA((3 * len(pieces) + 9,)),
            pltpu.SemaphoreType.DMA((2 * own // min(128, own),)),
        ],
        compiler_params=pltpu.CompilerParams(vmem_limit_bytes=EXPERT_GRANT),
        cost_estimate=LITTLE,
        name="finish_step",
    )(place, *pieces, *base, *held)


def dense_shards(
    hidden, route_ids, route_logits, placement, factors, w_gate, w_up, down_weight
):
    owners = lax.axis_size("expert")
    experts = placement.shape[0]
    steps, rows, width = hidden.shape
    units = w_gate.shape[2]
    rank = factors.shape[1] * owners // (3 * (width + units))
    outer, middle, cores = split_axis(owners)
    along_outer, along_middle = (middle * cores, outer), (cores, middle)
    place = jnp.stack([lax.axis_index("group"), lax.axis_index("expert")]).astype(jnp.int32)

    def along(x, stride, size):
        return [x] + [swap(x, owners, stride, k) for k in range(1, size)]

    rows_in = make_payload(hidden, route_ids, route_logits, experts)
    rows_in, factors = lax.optimization_barrier((rows_in, factors))
    column = [p.reshape(steps, rows, -1) for p in along(rows_in, *along_outer)]
    column = jnp.stack(column, axis=1).reshape(steps * outer * rows, -1)
    blocks = order_factors(place, placement, factors, outer, middle)
    blocks = [blocks[0]] + [swap(blocks[r], owners, cores, r) for r in range(1, middle)]
    column, blocks = lax.optimization_barrier((column, blocks))
    here = exchange_factors(blocks, owners)
    sheet = along(column, *along_middle)
    here, sheet[1:] = lax.optimization_barrier((here, sheet[1:]))
    here = jnp.stack(here)
    there = lax.ppermute(here, "group", [(0, 1), (1, 0)])
    pieces = sheet + [swap(p, owners, 1, 1) for p in sheet]
    base = base_products(pieces, w_gate[0], w_up[0])
    here, there, base = lax.optimization_barrier((here, there, base))
    low_rank = relayout_factors(place, here, there, width, units, rank, owners)

    span = outer * rows
    results = []
    for s in range(steps):
        if s >= 2:
            pieces, results[s - 2] = lax.optimization_barrier((pieces, results[s - 2]))
        kept, sent = finish_step(place, pieces, base, s * span, span, low_rank, down_weight[0])
        results.append(kept + swap(sent, owners, 1, 1).astype(jnp.float32))
    results[:-1] = [scatter_along(total, owners, *along_middle) for total in results[:-1]]
    results = lax.optimization_barrier(results)
    results[-1] = scatter_along(results[-1], owners, *along_middle)
    results[:-1] = [halve_along(total, owners, *along_outer) for total in results[:-1]]
    results[-1] = scatter_along(results[-1], owners, *along_outer)
    return jnp.stack(results).astype(jnp.bfloat16)


def row_capacity(rows, top, experts):
    return min(rows, 3 * max(1, rows * top // experts))


def unpack_factors(flat_factors, width, hidden_units, rank_size):
    layouts = [
        (width, rank_size),
        (rank_size, hidden_units),
        (width, rank_size),
        (rank_size, hidden_units),
        (hidden_units, rank_size),
        (rank_size, width),
    ]
    offset = 0
    segments = []
    for leading, trailing in layouts:
        segments.append(
            flat_factors[offset : offset + leading * trailing].reshape(leading, trailing)
        )
        offset = offset + leading * trailing
    return segments


def merge_weight(loaded_weights, factor_a, factor_b):
    adapter_delta = jnp.dot(factor_a, factor_b, preferred_element_type=jnp.float32)
    return (loaded_weights.astype(jnp.float32) + adapter_scale * adapter_delta).astype(jnp.bfloat16)


def apply_expert_block(inputs, merged_gate, merged_up, combined_down_weight):
    gate_part = jnp.dot(inputs, merged_gate, preferred_element_type=jnp.float32)
    up_part = jnp.dot(inputs, merged_up, preferred_element_type=jnp.float32)
    inner = (jax.nn.silu(gate_part) * up_part).astype(jnp.bfloat16)
    return jnp.dot(inner, combined_down_weight, preferred_element_type=jnp.float32).astype(
        jnp.bfloat16
    )


def sparse_shards(hidden, route_ids, route_logits, placement, factors, w_gate, w_up, down_weight):
    owners = lax.axis_size("expert")
    experts = placement.shape[0]
    steps_count, row_count, width = hidden.shape
    top_count = route_ids.shape[2]
    hidden_units = w_gate.shape[2]
    rank_size = factors.shape[1] * owners // (3 * (width + hidden_units))
    capacity = row_capacity(row_count, top_count, experts)
    slot_of = (
        jnp.zeros((experts,), jnp.int32).at[placement].set(jnp.arange(experts, dtype=jnp.int32))
    )
    ordered = jnp.take(factors, slot_of, axis=0)
    received = lax.all_to_all(ordered, "expert", split_axis=0, concat_axis=1, tiled=True)
    segments = unpack_factors(received[0], width, hidden_units, rank_size)
    merged_gate = merge_weight(w_gate[0], segments[0], segments[1])
    merged_up = merge_weight(w_up[0], segments[2], segments[3])
    combined_down_weight = merge_weight(down_weight[0], segments[4], segments[5])

    def layout(step_index):
        ids_flat = route_ids[step_index].reshape(-1)
        onehot = (ids_flat[:, None] == jnp.arange(experts, dtype=jnp.int32)[None, :]).astype(
            jnp.int32
        )
        position = jnp.sum((jnp.cumsum(onehot, axis=0) - 1) * onehot, axis=1)
        target = ids_flat * capacity + position
        placed = (
            jnp.arange(experts * capacity, dtype=jnp.int32)[:, None] == target[None, :]
        ).astype(jnp.bfloat16)
        pair_rows = jnp.repeat(hidden[step_index], top_count, axis=0)
        outgoing = jnp.dot(placed, pair_rows, preferred_element_type=jnp.float32).astype(
            jnp.bfloat16
        )
        outgoing = outgoing.reshape(experts, 1, capacity, width)
        gates = route_gates(route_logits[step_index]).reshape(-1)
        weighted = placed * gates[None, :]
        return (outgoing, weighted)

    layouts_all = [layout(step_index) for step_index in range(steps_count)]
    results = []
    for step_index in range(steps_count):
        outgoing, weighted = layouts_all[step_index]
        arrived = lax.all_to_all(outgoing, "expert", split_axis=0, concat_axis=1, tiled=True)
        outputs = apply_expert_block(
            arrived.reshape(-1, width), merged_gate, merged_up, combined_down_weight
        )
        outputs = outputs.reshape(arrived.shape)
        returned = lax.all_to_all(outputs, "expert", split_axis=1, concat_axis=0, tiled=True)
        flat_back = returned.reshape(experts * capacity, width)
        pair_out = jnp.einsum("cp,cd->pd", weighted, flat_back, preferred_element_type=jnp.float32)
        results.append(
            pair_out.reshape(row_count, top_count, width).sum(axis=1).astype(jnp.bfloat16)
        )
    return jnp.stack(results, axis=0)


def shards(hidden, route_ids, route_logits, placement, factors, w_gate, w_up, down_weight):
    rows, top = route_ids.shape[1:]
    width, units = w_gate.shape[1:]
    owners = lax.axis_size("expert")
    rank = factors.shape[1] * owners // (3 * (width + units))
    dense = row_capacity(rows, top, placement.shape[0]) == rows
    dense = dense and lax.axis_size("group") == 2 and split_axis(owners)[2] == 2
    outer = split_axis(owners)[0]
    dense = dense and outer > 1 and outer & (outer - 1) == 0 and split_axis(owners)[1] > 1
    dense = dense and 2 * rank == LANES and width % 256 == 0 and units % 256 == 0
    dense = dense and factors.shape[1] % (8 * LANES) == 0
    return (dense_shards if dense else sparse_shards)(
        hidden, route_ids, route_logits, placement, factors, w_gate, w_up, down_weight
    )


def solution(mesh):
    placed = (
        P(None, ("group", "expert"), None),
        P(None, ("group", "expert"), None),
        P(None, ("group", "expert"), None),
        P(),
        P(None, "expert"),
        P("expert", None, None),
        P("expert", None, None),
        P("expert", None, None),
    )
    return jax.shard_map(
        shards,
        mesh=mesh,
        in_specs=placed,
        out_specs=P(None, ("group", "expert"), None),
        check_vma=False,
    )
```

```python
import functools

import jax
import jax.numpy as jnp
from jax import lax
from jax.experimental import pallas as pl
from jax.experimental.pallas import tpu as pltpu
from jax.sharding import PartitionSpec as P

adapter_scale = 2.0
LANES = 128
GRANT = 16 << 20
EXPERT_GRANT = 32 << 20
WHOLE_GRANT = 60 << 20
MUCH = pl.CostEstimate(flops=1 << 33, bytes_accessed=1, transcendentals=0)
LITTLE = pl.CostEstimate(flops=1, bytes_accessed=1, transcendentals=0)


def route_gates(logits):
    highest = jnp.max(logits, axis=-1, keepdims=True)
    router_scores = jnp.exp(logits - highest)
    return (router_scores / jnp.sum(router_scores, axis=-1, keepdims=True)).astype(jnp.bfloat16)


def split_axis(n):
    cores = 2 if n % 2 == 0 else 1
    chips = n // cores
    middle = 1
    while chips % (2 * middle) == 0 and 4 * middle * middle <= chips:
        middle *= 2
    return chips // middle, middle, cores


def swap(x, n, stride, k):
    return lax.ppermute(x, "expert", [(i, i ^ (k * stride)) for i in range(n)])


def scatter_along(total, n, stride, size):
    count = total.shape[0] // size
    result = total[:count]
    for k in range(1, size):
        part = total[k * count : (k + 1) * count].astype(jnp.bfloat16)
        result = result + swap(part, n, stride, k).astype(jnp.float32)
    return result


def halve_along(total, n, stride, size):
    count = total.shape[0] // size
    step = 1
    while step < size:
        total = total.reshape(-1, 2, count, total.shape[1])
        sent = total[:, 1].reshape(-1, total.shape[3]).astype(jnp.bfloat16)
        kept = total[:, 0].reshape(-1, total.shape[3])
        total = kept + swap(sent, n, stride, step).astype(jnp.float32)
        step *= 2
    return total


def exchange_factors(blocks, n):
    _, middle, cores = split_axis(n)
    here = []
    for q, block in enumerate(blocks):
        turn = q * middle * cores
        pairs = [(g * n + i, g * n + (i ^ turn ^ g)) for g in range(2) for i in range(n)]
        here.append(lax.ppermute(block, ("group", "expert"), pairs))
    return here


def dot(a, b):
    return jnp.dot(a, b, preferred_element_type=jnp.float32)


def payload_kernel(hidden_ref, ids_ref, logits_ref, out_ref, turned_ref):
    steps, top, rows = ids_ref.shape
    width = hidden_ref.shape[2]
    turned_ref[...] = jnp.zeros_like(turned_ref)
    for s in range(steps):
        logits, ids = logits_ref[s], ids_ref[s]
        scores = jnp.exp(logits - jnp.max(logits, axis=0, keepdims=True))
        gates = scores / jnp.sum(scores, axis=0, keepdims=True)
        expert = lax.broadcasted_iota(jnp.int32, (turned_ref.shape[0], rows), 0)
        dense = jnp.zeros(expert.shape, jnp.float32)
        for k in range(top):
            dense += jnp.where(ids[k : k + 1, :] == expert, gates[k : k + 1, :], 0.0)
        turned_ref[:, s * rows : (s + 1) * rows] = dense
    dense = turned_ref[...].T.astype(jnp.bfloat16)
    for s in range(steps):
        out_ref[s * rows : (s + 1) * rows, :width] = hidden_ref[s]
    out_ref[:, width:] = dense[: steps * rows]


def make_payload(hidden, route_ids, route_logits, experts):
    steps, rows, width = hidden.shape
    padded = -(-experts // LANES) * LANES
    return pl.pallas_call(
        payload_kernel,
        out_shape=jax.ShapeDtypeStruct((steps * rows, width + padded), jnp.bfloat16),
        scratch_shapes=[pltpu.VMEM((padded, -(-steps * rows // LANES) * LANES), jnp.float32)],
        compiler_params=pltpu.CompilerParams(vmem_limit_bytes=WHOLE_GRANT),
        cost_estimate=LITTLE,
        name="payload",
    )(hidden, jnp.swapaxes(route_ids, 1, 2), jnp.swapaxes(route_logits, 1, 2))


def order_kernel(place_ref, placement_ref, factors_ref, *refs):
    out_refs, wide_ref, slot_ref = refs[:-2], refs[-2], refs[-1]
    slots = factors_ref.shape[0]
    outer, length, lanes = out_refs[0].shape
    group, me = place_ref[0], place_ref[1]

    def cut(t, carry):
        start = pl.multiple_of(t * lanes, lanes)
        tile = factors_ref[:, pl.ds(start, lanes)].astype(jnp.float32)
        wide_ref[pl.ds(t, slots, stride=length), :] = tile
        return carry

    lax.fori_loop(0, length, cut, 0, unroll=8)
    for s in range(slots):
        slot_ref[placement_ref[s]] = s
    for r, out_ref in enumerate(out_refs):
        for q in range(outer):
            slot = slot_ref[me ^ (2 * (q * len(out_refs) + r) + group)]
            rows = wide_ref[pl.ds(pl.multiple_of(slot * length, 8), length), :]
            out_ref[q] = rows.astype(jnp.bfloat16)


def order_factors(place, placement, factors, outer, middle):
    slots, entries = factors.shape
    length = entries // LANES
    return pl.pallas_call(
        order_kernel,
        out_shape=[jax.ShapeDtypeStruct((outer, length, LANES), jnp.bfloat16)] * middle,
        in_specs=[
            pl.BlockSpec(memory_space=pltpu.SMEM),
            pl.BlockSpec(memory_space=pltpu.SMEM),
            pl.BlockSpec(memory_space=pltpu.VMEM),
        ],
        scratch_shapes=[
            pltpu.VMEM((slots * length, LANES), jnp.float32),
            pltpu.SMEM((slots,), jnp.int32),
        ],
        compiler_params=pltpu.CompilerParams(vmem_limit_bytes=WHOLE_GRANT),
        cost_estimate=LITTLE,
        name="order_factors",
    )(place, placement, factors)


def relayout_kernel(outer, middle, place_ref, *refs):
    a_gu_ref, gate_b_ref, up_b_ref, down_a_ref, down_b_ref, flat_ref, wide_ref = refs[2:]
    width, units = a_gu_ref.shape[0], gate_b_ref.shape[1]
    rank = gate_b_ref.shape[0]
    length = refs[0].shape[2]
    group, me = place_ref[0], place_ref[1]
    for swapped, part in enumerate(refs[:2]):
        core = group if swapped == 0 else 1 - group
        for q in range(outer):
            for r in range(middle):
                source = me ^ ((q * middle + r) * 2 + core)
                start = pl.multiple_of(source * length, 8)
                flat_ref[pl.ds(start, length), :] = part[q, r].astype(jnp.float32)

    n_wide, n_unit = width // 2, units // 2
    at_ub = 2 * n_wide + n_unit
    at_da = 2 * n_wide + 2 * n_unit
    chunk = 128
    left = lax.broadcasted_iota(jnp.int32, (chunk, LANES), 1) < rank

    def load(start):
        return flat_ref[pl.ds(pl.multiple_of(start, 128), chunk), :]

    def gate_up(i, carry):
        g, u = load(i * chunk), load(n_wide + n_unit + i * chunk)
        at = 2 * i * chunk
        wide_ref[pl.ds(at, chunk, stride=2), :] = jnp.where(left, g, pltpu.roll(u, rank, 1))
        wide_ref[pl.ds(at + 1, chunk, stride=2), :] = jnp.where(left, pltpu.roll(g, rank, 1), u)
        both = wide_ref[pl.ds(pl.multiple_of(at, 128), 2 * chunk), :]
        a_gu_ref[pl.ds(pl.multiple_of(at, 128), 2 * chunk), :] = both.astype(jnp.bfloat16)
        return carry

    lax.fori_loop(0, n_wide // chunk, gate_up, 0, unroll=2)
    for i in range(n_unit // chunk):
        d = load(at_da + i * chunk)
        at = 2 * i * chunk
        wide_ref[pl.ds(at, chunk, stride=2), :] = jnp.where(left, d, 0.0)
        wide_ref[pl.ds(at + 1, chunk, stride=2), :] = jnp.where(left, pltpu.roll(d, rank, 1), 0.0)
        down_a_ref[at : at + 2 * chunk, :] = wide_ref[at : at + 2 * chunk, :].astype(jnp.bfloat16)
    for start, b_ref in (
        (n_wide, gate_b_ref),
        (at_ub, up_b_ref),
        (at_da + n_unit, down_b_ref),
    ):
        tiles = b_ref.shape[1] // LANES
        for j in range(tiles):
            row = flat_ref[pl.ds(start + j, rank, stride=tiles), :]
            b_ref[:, j * LANES : (j + 1) * LANES] = row.astype(jnp.bfloat16)


def relayout_factors(place, here, there, width, units, rank, n):
    outer, middle, _ = split_axis(n)
    shapes = [(width, 2 * rank), (rank, units), (rank, units), (units, 2 * rank), (rank, width)]
    length = here.shape[2]
    return pl.pallas_call(
        functools.partial(relayout_kernel, outer, middle),
        out_shape=[jax.ShapeDtypeStruct(shape, jnp.bfloat16) for shape in shapes],
        in_specs=[pl.BlockSpec(memory_space=pltpu.SMEM)]
        + [pl.BlockSpec(memory_space=pltpu.VMEM)] * 2,
        scratch_shapes=[
            pltpu.VMEM((n * length, LANES), jnp.float32),
            pltpu.VMEM((width, LANES), jnp.float32),
        ],
        compiler_params=pltpu.CompilerParams(vmem_limit_bytes=GRANT),
        cost_estimate=LITTLE,
        name="relayout_factors",
    )(place, here, there)


class Loads:
    def __init__(self, sem):
        self.sem, self.count = sem, 0

    def begin(self, src, dst):
        copy = pltpu.make_async_copy(src, dst, self.sem.at[self.count])
        copy.start()
        self.count += 1
        return [copy]

    def begin_rows(self, src, dst, parts=4):
        step = src.shape[0] // parts
        cuts = [pl.ds(at, step) for at in range(0, src.shape[0], step)]
        return sum([self.begin(src.at[cut], dst.at[cut]) for cut in cuts], [])


def wait(copies):
    for copy in copies:
        copy.wait()


def base_kernel(count, *refs):
    pieces = refs[:count]
    w_gate_hbm, w_up_hbm, gate_hbm, up_hbm, x_ref, w_gate_ref, w_up_ref = refs[count : count + 7]
    gate_ref, up_ref, sem, out_sem = refs[count + 7 :]
    rows = pieces[0].shape[0]
    width = w_gate_ref.shape[0]
    total = gate_ref.shape[0]
    block = min(128, total)
    loads = Loads(sem)
    x_in = [loads.begin(p, x_ref.at[pl.ds(i * rows, rows)]) for i, p in enumerate(pieces)]
    x_in = sum(x_in, [])
    gate_in = loads.begin_rows(w_gate_hbm, w_gate_ref)
    up_in = loads.begin_rows(w_up_hbm, w_up_ref)
    wait(x_in + gate_in + up_in)

    def store(i):
        here = pl.ds(pl.multiple_of(i * block, block), block)
        return [
            pltpu.make_async_copy(src.at[here], dst.at[here], out_sem.at[j, i])
            for j, (src, dst) in enumerate(((gate_ref, gate_hbm), (up_ref, up_hbm)))
        ]

    def run_block(i, carry):
        here = pl.ds(pl.multiple_of(i * block, block), block)
        gate_ref[here, :] = dot(x_ref[here, :width], w_gate_ref[...])
        up_ref[here, :] = dot(x_ref[here, :width], w_up_ref[...])
        for copy in store(i):
            copy.start()
        return carry

    lax.fori_loop(0, total // block, run_block, 0)
    for i in range(total // block):
        wait(store(i))


def base_products(pieces, w_gate, w_up):
    width, units = w_gate.shape
    total = sum(p.shape[0] for p in pieces)
    out = jax.ShapeDtypeStruct((total, units), jnp.float32)
    return pl.pallas_call(
        functools.partial(base_kernel, len(pieces)),
        out_shape=[out, out],
        in_specs=[pl.BlockSpec(memory_space=pl.ANY)] * len(pieces)
        + [pl.BlockSpec(memory_space=pltpu.HBM)] * 2,
        out_specs=[pl.BlockSpec(memory_space=pl.ANY)] * 2,
        scratch_shapes=[
            pltpu.VMEM((total, pieces[0].shape[1]), jnp.bfloat16),
            pltpu.VMEM(w_gate.shape, w_gate.dtype),
            pltpu.VMEM(w_up.shape, w_up.dtype),
            pltpu.VMEM(out.shape, out.dtype),
            pltpu.VMEM(out.shape, out.dtype),
            pltpu.SemaphoreType.DMA((len(pieces) + 8,)),
            pltpu.SemaphoreType.DMA((2, total // min(128, total))),
        ],
        compiler_params=pltpu.CompilerParams(vmem_limit_bytes=EXPERT_GRANT),
        cost_estimate=LITTLE,
        name="base_products",
    )(*pieces, w_gate, w_up)


def finish_kernel(count, first, rows, block, parts, place_ref, *refs):
    pieces, refs = refs[:count], refs[count:]
    gate_hbm, up_hbm, a_gu_hbm, gate_b_hbm, up_b_hbm, down_a_hbm, down_b_hbm = refs[:7]
    w_down_hbm, kept_hbm, sent_hbm, x_ref, gate_ref, up_ref = refs[7:13]
    a_gu_ref, gate_b_ref, up_b_ref, down_a_ref, down_b_ref, w_down_ref = refs[13:19]
    inner_ref, kept_ref, sent_ref, sem, out_sem = refs[19:]
    span = pieces[0].shape[0]
    units, width = w_down_ref.shape
    rank = gate_b_ref.shape[0]
    own = kept_ref.shape[0]
    loads = Loads(sem)
    x_in, base_in = [], []
    for i, piece in enumerate(pieces):
        x_in += loads.begin(piece.at[pl.ds(first, rows)], x_ref.at[pl.ds(i * rows, rows)])
    x_in += loads.begin(a_gu_hbm, a_gu_ref)
    x_in += loads.begin(gate_b_hbm, gate_b_ref) + loads.begin(up_b_hbm, up_b_ref)
    for i in range(count):
        src, dst = pl.ds(i * span + first, rows), pl.ds(i * rows, rows)
        base_in += loads.begin(gate_hbm.at[src], gate_ref.at[dst])
        base_in += loads.begin(up_hbm.at[src], up_ref.at[dst])
    down_in = loads.begin(down_a_hbm, down_a_ref) + loads.begin(down_b_hbm, down_b_ref)
    down_in += loads.begin_rows(w_down_hbm, w_down_ref)
    cuts = [slice(at, at + block) for at in range(0, 2 * own, block)]
    wait(x_in)
    lows = []
    for cut in cuts:
        low = adapter_scale * dot(x_ref[cut, :width], a_gu_ref[...])
        lows.append(low.astype(jnp.bfloat16))
    wait(base_in)
    for cut, low in zip(cuts, lows):
        g = gate_ref[cut, :] + dot(low[:, :rank], gate_b_ref[...])
        u = up_ref[cut, :] + dot(low[:, rank:], up_b_ref[...])
        inner_ref[cut, :] = (g / (1.0 + jnp.exp(-g)) * u).astype(jnp.bfloat16)
    wait(down_in)
    lows = []
    for cut in cuts:
        low = adapter_scale * dot(inner_ref[cut, :], down_a_ref[...])
        lows.append(low.astype(jnp.bfloat16)[:, :rank])
    out_copies = []
    half = width // parts
    columns = [slice(at, at + half) for at in range(0, width, half)]
    for cut, low in zip(cuts, lows):
        gates = x_ref[cut, width:].astype(jnp.float32)
        lane = lax.broadcasted_iota(jnp.int32, gates.shape, 1)
        mine = jnp.sum(jnp.where(lane == place_ref[1], gates, 0.0), axis=1, keepdims=True)
        outs = [
            (dot(inner_ref[cut, :], w_down_ref[:, c]) + dot(low, down_b_ref[:, c])) * mine
            for c in columns
        ]
        ends = [(kept_ref, kept_hbm, 0), (sent_ref, sent_hbm, own)]
        for out_ref, out_hbm, start in ends:
            at, to = max(cut.start, start), min(cut.stop, start + own)
            if at < to:
                for c, out in zip(columns, outs):
                    part = out[at - cut.start : to - cut.start]
                    out_ref[at - start : to - start, c] = part.astype(out_ref.dtype)
                rows_out = pl.ds(at - start, to - at)
                sem_out = out_sem.at[len(out_copies)]
                copy = pltpu.make_async_copy(out_ref.at[rows_out], out_hbm.at[rows_out], sem_out)
                copy.start()
                out_copies.append(copy)
    wait(out_copies)


def finish_step(place, pieces, base, first, rows, low_rank, w_down, block, parts):
    units, width = w_down.shape
    total = rows * len(pieces)
    own = total // 2
    a_gu, gate_b, up_b, down_a, down_b = low_rank
    rank = down_b.shape[0]
    outs = [
        jax.ShapeDtypeStruct((own, width), jnp.float32),
        jax.ShapeDtypeStruct((own, width), jnp.bfloat16),
    ]
    held = [*low_rank, w_down]
    return pl.pallas_call(
        functools.partial(finish_kernel, len(pieces), first, rows, block, parts),
        out_shape=outs,
        in_specs=[pl.BlockSpec(memory_space=pltpu.SMEM)]
        + [pl.BlockSpec(memory_space=pl.ANY)] * (len(pieces) + 2 + len(low_rank))
        + [pl.BlockSpec(memory_space=pltpu.HBM)],
        out_specs=[pl.BlockSpec(memory_space=pl.ANY)] * 2,
        scratch_shapes=[
            pltpu.VMEM((total, pieces[0].shape[1]), jnp.bfloat16),
            pltpu.VMEM((total, units), jnp.float32),
            pltpu.VMEM((total, units), jnp.float32),
        ]
        + [pltpu.VMEM(a.shape, a.dtype) for a in held]
        + [pltpu.VMEM((total, units), jnp.bfloat16)]
        + [pltpu.VMEM(o.shape, o.dtype) for o in outs]
        + [
            pltpu.SemaphoreType.DMA((3 * len(pieces) + 9,)),
            pltpu.SemaphoreType.DMA((2 * own // min(block, own),)),
        ],
        compiler_params=pltpu.CompilerParams(vmem_limit_bytes=EXPERT_GRANT),
        cost_estimate=MUCH,
        name="finish_step",
    )(place, *pieces, *base, *held)


def dense_shards(
    hidden, route_ids, route_logits, placement, factors, w_gate, w_up, down_weight
):
    owners = lax.axis_size("expert")
    experts = placement.shape[0]
    steps, rows, width = hidden.shape
    units = w_gate.shape[2]
    rank = factors.shape[1] * owners // (3 * (width + units))
    outer, middle, cores = split_axis(owners)
    along_outer, along_middle = (middle * cores, outer), (cores, middle)
    place = jnp.stack([lax.axis_index("group"), lax.axis_index("expert")]).astype(jnp.int32)

    def along(x, stride, size):
        return [x] + [swap(x, owners, stride, k) for k in range(1, size)]

    rows_in = make_payload(hidden, route_ids, route_logits, experts)
    rows_in, factors = lax.optimization_barrier((rows_in, factors))
    column = [p.reshape(steps, rows, -1) for p in along(rows_in, *along_outer)]
    column = jnp.stack(column, axis=1).reshape(steps * outer * rows, -1)
    blocks = order_factors(place, placement, factors, outer, middle)
    blocks = [blocks[0]] + [swap(blocks[r], owners, cores, r) for r in range(1, middle)]
    blocks = [jnp.stack([block[q] for block in blocks]) for q in range(outer)]
    column, blocks = lax.optimization_barrier((column, blocks))
    here = exchange_factors(blocks, owners)
    sheet = along(column, *along_middle)
    here, sheet[1:] = lax.optimization_barrier((here, sheet[1:]))
    here = jnp.stack(here)
    there = lax.ppermute(here, "group", [(0, 1), (1, 0)])
    pieces = sheet + [swap(p, owners, 1, 1) for p in sheet]
    base = base_products(pieces, w_gate[0], w_up[0])
    here, there, base = lax.optimization_barrier((here, there, base))
    low_rank = relayout_factors(place, here, there, width, units, rank, owners)

    span = outer * rows
    def after(x, other):
        return lax.optimization_barrier((x, other))[0]

    summed, across = [], []
    for s in range(steps):
        if s >= 1:
            pieces = lax.optimization_barrier((pieces, summed[s - 1], across[: s - 1]))[0]
        block, parts = [(128, 1), (256, 1), (256, 2)][s % 3]
        kept, sent = finish_step(
            place, pieces, base, s * span, span, low_rank, down_weight[0], block, parts
        )
        summed.append(kept + swap(sent, owners, 1, 1).astype(jnp.float32))
        across.append(scatter_along(summed[s], owners, *along_middle))
    across[:-1] = [after(total, summed[-1]) for total in across[:-1]]
    results = [halve_along(total, owners, *along_outer) for total in across[:-1]]
    results.append(scatter_along(across[-1], owners, *along_outer))
    return jnp.stack(results).astype(jnp.bfloat16)


def row_capacity(rows, top, experts):
    return min(rows, 3 * max(1, rows * top // experts))


def unpack_factors(flat_factors, width, hidden_units, rank_size):
    layouts = [
        (width, rank_size),
        (rank_size, hidden_units),
        (width, rank_size),
        (rank_size, hidden_units),
        (hidden_units, rank_size),
        (rank_size, width),
    ]
    offset = 0
    segments = []
    for leading, trailing in layouts:
        segments.append(
            flat_factors[offset : offset + leading * trailing].reshape(leading, trailing)
        )
        offset = offset + leading * trailing
    return segments


def merge_weight(loaded_weights, factor_a, factor_b):
    adapter_delta = jnp.dot(factor_a, factor_b, preferred_element_type=jnp.float32)
    return (loaded_weights.astype(jnp.float32) + adapter_scale * adapter_delta).astype(jnp.bfloat16)


def apply_expert_block(inputs, merged_gate, merged_up, combined_down_weight):
    gate_part = jnp.dot(inputs, merged_gate, preferred_element_type=jnp.float32)
    up_part = jnp.dot(inputs, merged_up, preferred_element_type=jnp.float32)
    inner = (jax.nn.silu(gate_part) * up_part).astype(jnp.bfloat16)
    return jnp.dot(inner, combined_down_weight, preferred_element_type=jnp.float32).astype(
        jnp.bfloat16
    )


def sparse_shards(hidden, route_ids, route_logits, placement, factors, w_gate, w_up, down_weight):
    owners = lax.axis_size("expert")
    experts = placement.shape[0]
    steps_count, row_count, width = hidden.shape
    top_count = route_ids.shape[2]
    hidden_units = w_gate.shape[2]
    rank_size = factors.shape[1] * owners // (3 * (width + hidden_units))
    capacity = row_capacity(row_count, top_count, experts)
    slot_of = (
        jnp.zeros((experts,), jnp.int32).at[placement].set(jnp.arange(experts, dtype=jnp.int32))
    )
    ordered = jnp.take(factors, slot_of, axis=0)
    received = lax.all_to_all(ordered, "expert", split_axis=0, concat_axis=1, tiled=True)
    segments = unpack_factors(received[0], width, hidden_units, rank_size)
    merged_gate = merge_weight(w_gate[0], segments[0], segments[1])
    merged_up = merge_weight(w_up[0], segments[2], segments[3])
    combined_down_weight = merge_weight(down_weight[0], segments[4], segments[5])

    def layout(step_index):
        ids_flat = route_ids[step_index].reshape(-1)
        onehot = (ids_flat[:, None] == jnp.arange(experts, dtype=jnp.int32)[None, :]).astype(
            jnp.int32
        )
        position = jnp.sum((jnp.cumsum(onehot, axis=0) - 1) * onehot, axis=1)
        target = ids_flat * capacity + position
        placed = (
            jnp.arange(experts * capacity, dtype=jnp.int32)[:, None] == target[None, :]
        ).astype(jnp.bfloat16)
        pair_rows = jnp.repeat(hidden[step_index], top_count, axis=0)
        outgoing = jnp.dot(placed, pair_rows, preferred_element_type=jnp.float32).astype(
            jnp.bfloat16
        )
        outgoing = outgoing.reshape(experts, 1, capacity, width)
        gates = route_gates(route_logits[step_index]).reshape(-1)
        weighted = placed * gates[None, :]
        return (outgoing, weighted)

    layouts_all = [layout(step_index) for step_index in range(steps_count)]
    results = []
    for step_index in range(steps_count):
        outgoing, weighted = layouts_all[step_index]
        arrived = lax.all_to_all(outgoing, "expert", split_axis=0, concat_axis=1, tiled=True)
        outputs = apply_expert_block(
            arrived.reshape(-1, width), merged_gate, merged_up, combined_down_weight
        )
        outputs = outputs.reshape(arrived.shape)
        returned = lax.all_to_all(outputs, "expert", split_axis=1, concat_axis=0, tiled=True)
        flat_back = returned.reshape(experts * capacity, width)
        pair_out = jnp.einsum("cp,cd->pd", weighted, flat_back, preferred_element_type=jnp.float32)
        results.append(
            pair_out.reshape(row_count, top_count, width).sum(axis=1).astype(jnp.bfloat16)
        )
    return jnp.stack(results, axis=0)


def shards(hidden, route_ids, route_logits, placement, factors, w_gate, w_up, down_weight):
    rows, top = route_ids.shape[1:]
    width, units = w_gate.shape[1:]
    owners = lax.axis_size("expert")
    rank = factors.shape[1] * owners // (3 * (width + units))
    dense = row_capacity(rows, top, placement.shape[0]) == rows
    dense = dense and lax.axis_size("group") == 2 and split_axis(owners)[2] == 2
    outer = split_axis(owners)[0]
    dense = dense and outer > 1 and outer & (outer - 1) == 0 and split_axis(owners)[1] > 1
    dense = dense and 2 * rank == LANES and width % 256 == 0 and units % 256 == 0
    dense = dense and factors.shape[1] % (8 * LANES) == 0
    return (dense_shards if dense else sparse_shards)(
        hidden, route_ids, route_logits, placement, factors, w_gate, w_up, down_weight
    )


def solution(mesh):
    placed = (
        P(None, ("group", "expert"), None),
        P(None, ("group", "expert"), None),
        P(None, ("group", "expert"), None),
        P(),
        P(None, "expert"),
        P("expert", None, None),
        P("expert", None, None),
        P("expert", None, None),
    )
    return jax.shard_map(
        shards,
        mesh=mesh,
        in_specs=placed,
        out_specs=P(None, ("group", "expert"), None),
        check_vma=False,
    )
```

```python
import functools

import jax
import jax.numpy as jnp
from jax import lax
from jax.experimental import pallas as pl
from jax.experimental.pallas import tpu as pltpu
from jax.sharding import PartitionSpec as P

adapter_scale = 2.0
LANES = 128
GRANT = 16 << 20
EXPERT_GRANT = 32 << 20
WHOLE_GRANT = 60 << 20
MUCH = pl.CostEstimate(flops=1 << 33, bytes_accessed=1, transcendentals=0)
LITTLE = pl.CostEstimate(flops=1, bytes_accessed=1, transcendentals=0)


def route_gates(logits):
    highest = jnp.max(logits, axis=-1, keepdims=True)
    router_scores = jnp.exp(logits - highest)
    return (router_scores / jnp.sum(router_scores, axis=-1, keepdims=True)).astype(jnp.bfloat16)


def split_axis(n):
    cores = 2 if n % 2 == 0 else 1
    chips = n // cores
    middle = 1
    while chips % (2 * middle) == 0 and 4 * middle * middle <= chips:
        middle *= 2
    return chips // middle, middle, cores


def swap(x, n, stride, k):
    return lax.ppermute(x, "expert", [(i, i ^ (k * stride)) for i in range(n)])


def scatter_along(total, n, stride, size, received=None):
    count = total.shape[0] // size
    received = [] if received is None else received
    for k in range(1, size):
        part = total[k * count : (k + 1) * count].astype(jnp.bfloat16)
        received.append(swap(part, n, stride, k))
    return sum([part.astype(jnp.float32) for part in received], total[:count])


def halve_along(total, n, stride, size, last):
    count = total.shape[0] // size
    step = 1
    while step < size:
        total = total.reshape(-1, 2, count, total.shape[1])
        sent = total[:, 1].reshape(-1, total.shape[3]).astype(jnp.bfloat16)
        kept = total[:, 0].reshape(-1, total.shape[3])
        sent = swap(sent, n, stride, step)
        if 2 * step == size:
            sent = lax.optimization_barrier((sent, last))[0]
        total = kept + sent.astype(jnp.float32)
        step *= 2
    return total


def exchange_factors(blocks, n):
    _, middle, cores = split_axis(n)
    here = []
    for q, block in enumerate(blocks):
        turn = q * middle * cores
        pairs = [(g * n + i, g * n + (i ^ turn ^ g)) for g in range(2) for i in range(n)]
        here.append(lax.ppermute(block, ("group", "expert"), pairs))
    return here


def dot(a, b):
    return jnp.dot(a, b, preferred_element_type=jnp.float32)


def payload_kernel(hidden_ref, ids_ref, logits_ref, out_ref, turned_ref):
    steps, top, rows = ids_ref.shape
    width = hidden_ref.shape[2]
    turned_ref[...] = jnp.zeros_like(turned_ref)
    for s in range(steps):
        logits, ids = logits_ref[s], ids_ref[s]
        scores = jnp.exp(logits - jnp.max(logits, axis=0, keepdims=True))
        gates = scores / jnp.sum(scores, axis=0, keepdims=True)
        expert = lax.broadcasted_iota(jnp.int32, (turned_ref.shape[0], rows), 0)
        dense = jnp.zeros(expert.shape, jnp.float32)
        for k in range(top):
            dense += jnp.where(ids[k : k + 1, :] == expert, gates[k : k + 1, :], 0.0)
        turned_ref[:, s * rows : (s + 1) * rows] = dense
    dense = turned_ref[...].T.astype(jnp.bfloat16)
    for s in range(steps):
        out_ref[s * rows : (s + 1) * rows, :width] = hidden_ref[s]
    out_ref[:, width:] = dense[: steps * rows]


def make_payload(hidden, route_ids, route_logits, experts):
    steps, rows, width = hidden.shape
    padded = -(-experts // LANES) * LANES
    return pl.pallas_call(
        payload_kernel,
        out_shape=jax.ShapeDtypeStruct((steps * rows, width + padded), jnp.bfloat16),
        scratch_shapes=[pltpu.VMEM((padded, -(-steps * rows // LANES) * LANES), jnp.float32)],
        compiler_params=pltpu.CompilerParams(vmem_limit_bytes=WHOLE_GRANT),
        cost_estimate=LITTLE,
        name="payload",
    )(hidden, jnp.swapaxes(route_ids, 1, 2), jnp.swapaxes(route_logits, 1, 2))


def order_kernel(place_ref, placement_ref, factors_ref, *refs):
    out_refs, wide_ref, slot_ref = refs[:-2], refs[-2], refs[-1]
    slots = factors_ref.shape[0]
    outer, length, lanes = out_refs[0].shape
    group, me = place_ref[0], place_ref[1]

    def cut(t, carry):
        start = pl.multiple_of(t * lanes, lanes)
        tile = factors_ref[:, pl.ds(start, lanes)].astype(jnp.float32)
        wide_ref[pl.ds(t, slots, stride=length), :] = tile
        return carry

    lax.fori_loop(0, length, cut, 0, unroll=8)
    for s in range(slots):
        slot_ref[placement_ref[s]] = s
    for r, out_ref in enumerate(out_refs):
        for q in range(outer):
            slot = slot_ref[me ^ (2 * (q * len(out_refs) + r) + group)]
            rows = wide_ref[pl.ds(pl.multiple_of(slot * length, 8), length), :]
            out_ref[q] = rows.astype(jnp.bfloat16)


def order_factors(place, placement, factors, outer, middle):
    slots, entries = factors.shape
    length = entries // LANES
    return pl.pallas_call(
        order_kernel,
        out_shape=[jax.ShapeDtypeStruct((outer, length, LANES), jnp.bfloat16)] * middle,
        in_specs=[
            pl.BlockSpec(memory_space=pltpu.SMEM),
            pl.BlockSpec(memory_space=pltpu.SMEM),
            pl.BlockSpec(memory_space=pltpu.VMEM),
        ],
        scratch_shapes=[
            pltpu.VMEM((slots * length, LANES), jnp.float32),
            pltpu.SMEM((slots,), jnp.int32),
        ],
        compiler_params=pltpu.CompilerParams(vmem_limit_bytes=WHOLE_GRANT),
        cost_estimate=LITTLE,
        name="order_factors",
    )(place, placement, factors)


def relayout_kernel(outer, middle, place_ref, *refs):
    a_gu_ref, gate_b_ref, up_b_ref, down_a_ref, down_b_ref, flat_ref, wide_ref = refs[2:]
    width, units = a_gu_ref.shape[0], gate_b_ref.shape[1]
    rank = gate_b_ref.shape[0]
    length = refs[0].shape[2]
    group, me = place_ref[0], place_ref[1]
    for swapped, part in enumerate(refs[:2]):
        core = group if swapped == 0 else 1 - group
        for q in range(outer):
            for r in range(middle):
                source = me ^ ((q * middle + r) * 2 + core)
                start = pl.multiple_of(source * length, 8)
                flat_ref[pl.ds(start, length), :] = part[q, r].astype(jnp.float32)

    n_wide, n_unit = width // 2, units // 2
    at_ub = 2 * n_wide + n_unit
    at_da = 2 * n_wide + 2 * n_unit
    chunk = 128
    left = lax.broadcasted_iota(jnp.int32, (chunk, LANES), 1) < rank

    def load(start):
        return flat_ref[pl.ds(pl.multiple_of(start, 128), chunk), :]

    def gate_up(i, carry):
        g, u = load(i * chunk), load(n_wide + n_unit + i * chunk)
        at = 2 * i * chunk
        wide_ref[pl.ds(at, chunk, stride=2), :] = jnp.where(left, g, pltpu.roll(u, rank, 1))
        wide_ref[pl.ds(at + 1, chunk, stride=2), :] = jnp.where(left, pltpu.roll(g, rank, 1), u)
        both = wide_ref[pl.ds(pl.multiple_of(at, 128), 2 * chunk), :]
        a_gu_ref[pl.ds(pl.multiple_of(at, 128), 2 * chunk), :] = both.astype(jnp.bfloat16)
        return carry

    lax.fori_loop(0, n_wide // chunk, gate_up, 0, unroll=2)
    for i in range(n_unit // chunk):
        d = load(at_da + i * chunk)
        at = 2 * i * chunk
        wide_ref[pl.ds(at, chunk, stride=2), :] = jnp.where(left, d, 0.0)
        wide_ref[pl.ds(at + 1, chunk, stride=2), :] = jnp.where(left, pltpu.roll(d, rank, 1), 0.0)
        down_a_ref[at : at + 2 * chunk, :] = wide_ref[at : at + 2 * chunk, :].astype(jnp.bfloat16)
    for start, b_ref in (
        (n_wide, gate_b_ref),
        (at_ub, up_b_ref),
        (at_da + n_unit, down_b_ref),
    ):
        tiles = b_ref.shape[1] // LANES
        for j in range(tiles):
            row = flat_ref[pl.ds(start + j, rank, stride=tiles), :]
            b_ref[:, j * LANES : (j + 1) * LANES] = row.astype(jnp.bfloat16)


def relayout_factors(place, here, there, width, units, rank, n):
    outer, middle, _ = split_axis(n)
    shapes = [(width, 2 * rank), (rank, units), (rank, units), (units, 2 * rank), (rank, width)]
    length = here.shape[2]
    return pl.pallas_call(
        functools.partial(relayout_kernel, outer, middle),
        out_shape=[jax.ShapeDtypeStruct(shape, jnp.bfloat16) for shape in shapes],
        in_specs=[pl.BlockSpec(memory_space=pltpu.SMEM)]
        + [pl.BlockSpec(memory_space=pltpu.VMEM)] * 2,
        scratch_shapes=[
            pltpu.VMEM((n * length, LANES), jnp.float32),
            pltpu.VMEM((width, LANES), jnp.float32),
        ],
        compiler_params=pltpu.CompilerParams(vmem_limit_bytes=GRANT),
        cost_estimate=LITTLE,
        name="relayout_factors",
    )(place, here, there)


class Loads:
    def __init__(self, sem):
        self.sem, self.count = sem, 0

    def begin(self, src, dst):
        copy = pltpu.make_async_copy(src, dst, self.sem.at[self.count])
        copy.start()
        self.count += 1
        return [copy]

    def begin_rows(self, src, dst, parts=4):
        step = src.shape[0] // parts
        cuts = [pl.ds(at, step) for at in range(0, src.shape[0], step)]
        return sum([self.begin(src.at[cut], dst.at[cut]) for cut in cuts], [])


def wait(copies):
    for copy in copies:
        copy.wait()


def base_kernel(count, *refs):
    pieces = refs[:count]
    w_gate_hbm, w_up_hbm, gate_hbm, up_hbm, x_ref, w_gate_ref, w_up_ref = refs[count : count + 7]
    gate_ref, up_ref, sem, out_sem = refs[count + 7 :]
    rows = pieces[0].shape[0]
    width = w_gate_ref.shape[0]
    total = gate_ref.shape[0]
    block = min(128, total)
    loads = Loads(sem)
    x_in = [loads.begin(p, x_ref.at[pl.ds(i * rows, rows)]) for i, p in enumerate(pieces)]
    x_in = sum(x_in, [])
    gate_in = loads.begin_rows(w_gate_hbm, w_gate_ref)
    up_in = loads.begin_rows(w_up_hbm, w_up_ref)
    wait(x_in + gate_in + up_in)

    def store(i):
        here = pl.ds(pl.multiple_of(i * block, block), block)
        return [
            pltpu.make_async_copy(src.at[here], dst.at[here], out_sem.at[j, i])
            for j, (src, dst) in enumerate(((gate_ref, gate_hbm), (up_ref, up_hbm)))
        ]

    def run_block(i, carry):
        here = pl.ds(pl.multiple_of(i * block, block), block)
        gate_ref[here, :] = dot(x_ref[here, :width], w_gate_ref[...])
        up_ref[here, :] = dot(x_ref[here, :width], w_up_ref[...])
        for copy in store(i):
            copy.start()
        return carry

    lax.fori_loop(0, total // block, run_block, 0)
    for i in range(total // block):
        wait(store(i))


def base_products(pieces, w_gate, w_up):
    width, units = w_gate.shape
    total = sum(p.shape[0] for p in pieces)
    out = jax.ShapeDtypeStruct((total, units), jnp.float32)
    return pl.pallas_call(
        functools.partial(base_kernel, len(pieces)),
        out_shape=[out, out],
        in_specs=[pl.BlockSpec(memory_space=pl.ANY)] * len(pieces)
        + [pl.BlockSpec(memory_space=pltpu.HBM)] * 2,
        out_specs=[pl.BlockSpec(memory_space=pl.ANY)] * 2,
        scratch_shapes=[
            pltpu.VMEM((total, pieces[0].shape[1]), jnp.bfloat16),
            pltpu.VMEM(w_gate.shape, w_gate.dtype),
            pltpu.VMEM(w_up.shape, w_up.dtype),
            pltpu.VMEM(out.shape, out.dtype),
            pltpu.VMEM(out.shape, out.dtype),
            pltpu.SemaphoreType.DMA((len(pieces) + 8,)),
            pltpu.SemaphoreType.DMA((2, total // min(128, total))),
        ],
        compiler_params=pltpu.CompilerParams(vmem_limit_bytes=EXPERT_GRANT),
        cost_estimate=LITTLE,
        name="base_products",
    )(*pieces, w_gate, w_up)


def finish_kernel(count, first, rows, place_ref, *refs):
    pieces, refs = refs[:count], refs[count:]
    gate_hbm, up_hbm, a_gu_hbm, gate_b_hbm, up_b_hbm, down_a_hbm, down_b_hbm = refs[:7]
    w_down_hbm, kept_hbm, sent_hbm, x_ref, gate_ref, up_ref = refs[7:13]
    a_gu_ref, gate_b_ref, up_b_ref, down_a_ref, down_b_ref, w_down_ref = refs[13:19]
    inner_ref, kept_ref, sent_ref, sem, out_sem = refs[19:]
    span = pieces[0].shape[0]
    units, width = w_down_ref.shape
    rank = gate_b_ref.shape[0]
    own = kept_ref.shape[0]
    loads = Loads(sem)
    x_in, base_in = [], []
    for i, piece in enumerate(pieces):
        x_in += loads.begin(piece.at[pl.ds(first, rows)], x_ref.at[pl.ds(i * rows, rows)])
    x_in += loads.begin(a_gu_hbm, a_gu_ref)
    x_in += loads.begin(gate_b_hbm, gate_b_ref) + loads.begin(up_b_hbm, up_b_ref)
    for i in range(count):
        src, dst = pl.ds(i * span + first, rows), pl.ds(i * rows, rows)
        base_in += loads.begin(gate_hbm.at[src], gate_ref.at[dst])
        base_in += loads.begin(up_hbm.at[src], up_ref.at[dst])
    down_in = loads.begin(down_a_hbm, down_a_ref) + loads.begin(down_b_hbm, down_b_ref)
    down_in += loads.begin_rows(w_down_hbm, w_down_ref)
    wait(x_in)
    low = (adapter_scale * dot(x_ref[:, :width], a_gu_ref[...])).astype(jnp.bfloat16)
    gates = x_ref[:, width:].astype(jnp.float32)
    lane = lax.broadcasted_iota(jnp.int32, gates.shape, 1)
    mine = jnp.sum(jnp.where(lane == place_ref[1], gates, 0.0), axis=1, keepdims=True)
    wait(base_in)
    g = gate_ref[...] + dot(low[:, :rank], gate_b_ref[...])
    u = up_ref[...] + dot(low[:, rank:], up_b_ref[...])
    half = 0.5 * g
    inner_ref[...] = ((half + half * jnp.tanh(half)) * u).astype(jnp.bfloat16)
    wait(down_in)
    low = (adapter_scale * dot(inner_ref[...], down_a_ref[...])).astype(jnp.bfloat16)[:, :rank]
    out = (dot(inner_ref[...], w_down_ref[...]) + dot(low, down_b_ref[...])) * mine
    sent_ref[...] = out[own:].astype(jnp.bfloat16)
    sent_out = pltpu.make_async_copy(sent_ref, sent_hbm, out_sem.at[0])
    sent_out.start()
    kept_ref[...] = out[:own]
    kept_out = pltpu.make_async_copy(kept_ref, kept_hbm, out_sem.at[1])
    kept_out.start()
    wait([sent_out, kept_out])


def finish_step(place, pieces, base, first, rows, low_rank, w_down):
    units, width = w_down.shape
    total = rows * len(pieces)
    own = total // 2
    a_gu, gate_b, up_b, down_a, down_b = low_rank
    rank = down_b.shape[0]
    outs = [
        jax.ShapeDtypeStruct((own, width), jnp.float32),
        jax.ShapeDtypeStruct((own, width), jnp.bfloat16),
    ]
    held = [*low_rank, w_down]
    return pl.pallas_call(
        functools.partial(finish_kernel, len(pieces), first, rows),
        out_shape=outs,
        in_specs=[pl.BlockSpec(memory_space=pltpu.SMEM)]
        + [pl.BlockSpec(memory_space=pl.ANY)] * (len(pieces) + 2 + len(low_rank))
        + [pl.BlockSpec(memory_space=pltpu.HBM)],
        out_specs=[pl.BlockSpec(memory_space=pl.ANY)] * 2,
        scratch_shapes=[
            pltpu.VMEM((total, pieces[0].shape[1]), jnp.bfloat16),
            pltpu.VMEM((total, units), jnp.float32),
            pltpu.VMEM((total, units), jnp.float32),
        ]
        + [pltpu.VMEM(a.shape, a.dtype) for a in held]
        + [pltpu.VMEM((total, units), jnp.bfloat16)]
        + [pltpu.VMEM(o.shape, o.dtype) for o in outs]
        + [
            pltpu.SemaphoreType.DMA((3 * len(pieces) + 9,)),
            pltpu.SemaphoreType.DMA((2,)),
        ],
        compiler_params=pltpu.CompilerParams(vmem_limit_bytes=EXPERT_GRANT),
        cost_estimate=MUCH,
        name="finish_step",
    )(place, *pieces, *base, *held)


def dense_shards(
    hidden, route_ids, route_logits, placement, factors, w_gate, w_up, down_weight
):
    owners = lax.axis_size("expert")
    experts = placement.shape[0]
    steps, rows, width = hidden.shape
    units = w_gate.shape[2]
    rank = factors.shape[1] * owners // (3 * (width + units))
    outer, middle, cores = split_axis(owners)
    along_outer, along_middle = (middle * cores, outer), (cores, middle)
    place = jnp.stack([lax.axis_index("group"), lax.axis_index("expert")]).astype(jnp.int32)

    def along(x, stride, size):
        return [x] + [swap(x, owners, stride, k) for k in range(1, size)]

    rows_in = make_payload(hidden, route_ids, route_logits, experts)
    rows_in, factors = lax.optimization_barrier((rows_in, factors))
    column = [p.reshape(steps, rows, -1) for p in along(rows_in, *along_outer)]
    column = jnp.stack(column, axis=1).reshape(steps * outer * rows, -1)
    blocks = order_factors(place, placement, factors, outer, middle)
    blocks = [blocks[0]] + [swap(blocks[r], owners, cores, r) for r in range(1, middle)]
    blocks = [jnp.stack([block[q] for block in blocks]) for q in range(outer)]
    column, blocks = lax.optimization_barrier((column, blocks))
    here = exchange_factors(blocks, owners)
    sheet = along(column, *along_middle)
    here, sheet[1:] = lax.optimization_barrier((here, sheet[1:]))
    here = jnp.stack(here)
    there = lax.ppermute(here, "group", [(0, 1), (1, 0)])
    pieces = sheet + [swap(p, owners, 1, 1) for p in sheet]
    base = base_products(pieces, w_gate[0], w_up[0])
    here, there, base = lax.optimization_barrier((here, there, base))
    low_rank = relayout_factors(place, here, there, width, units, rank, owners)

    span = outer * rows
    def after(x, other):
        return lax.optimization_barrier((x, other))[0]

    summed, across = [], []
    for s in range(steps):
        if s >= 1:
            pieces = lax.optimization_barrier((pieces, summed[s - 1], across[: s - 1]))[0]
        kept, sent = finish_step(
            place, pieces, base, s * span, span, low_rank, down_weight[0]
        )
        summed.append(kept + swap(sent, owners, 1, 1).astype(jnp.float32))
        across.append(scatter_along(summed[s], owners, *along_middle))
    across[:-1] = [after(total, summed[-1]) for total in across[:-1]]
    ends = []
    final = scatter_along(across[-1], owners, *along_outer, ends)
    results = [halve_along(total, owners, *along_outer, ends[0]) for total in across[:-1]]
    return jnp.stack(results + [final]).astype(jnp.bfloat16)


def row_capacity(rows, top, experts):
    return min(rows, 3 * max(1, rows * top // experts))


def unpack_factors(flat_factors, width, hidden_units, rank_size):
    layouts = [
        (width, rank_size),
        (rank_size, hidden_units),
        (width, rank_size),
        (rank_size, hidden_units),
        (hidden_units, rank_size),
        (rank_size, width),
    ]
    offset = 0
    segments = []
    for leading, trailing in layouts:
        segments.append(
            flat_factors[offset : offset + leading * trailing].reshape(leading, trailing)
        )
        offset = offset + leading * trailing
    return segments


def merge_weight(loaded_weights, factor_a, factor_b):
    adapter_delta = jnp.dot(factor_a, factor_b, preferred_element_type=jnp.float32)
    return (loaded_weights.astype(jnp.float32) + adapter_scale * adapter_delta).astype(jnp.bfloat16)


def apply_expert_block(inputs, merged_gate, merged_up, combined_down_weight):
    gate_part = jnp.dot(inputs, merged_gate, preferred_element_type=jnp.float32)
    up_part = jnp.dot(inputs, merged_up, preferred_element_type=jnp.float32)
    inner = (jax.nn.silu(gate_part) * up_part).astype(jnp.bfloat16)
    return jnp.dot(inner, combined_down_weight, preferred_element_type=jnp.float32).astype(
        jnp.bfloat16
    )


def sparse_shards(hidden, route_ids, route_logits, placement, factors, w_gate, w_up, down_weight):
    owners = lax.axis_size("expert")
    experts = placement.shape[0]
    steps_count, row_count, width = hidden.shape
    top_count = route_ids.shape[2]
    hidden_units = w_gate.shape[2]
    rank_size = factors.shape[1] * owners // (3 * (width + hidden_units))
    capacity = row_capacity(row_count, top_count, experts)
    slot_of = (
        jnp.zeros((experts,), jnp.int32).at[placement].set(jnp.arange(experts, dtype=jnp.int32))
    )
    ordered = jnp.take(factors, slot_of, axis=0)
    received = lax.all_to_all(ordered, "expert", split_axis=0, concat_axis=1, tiled=True)
    segments = unpack_factors(received[0], width, hidden_units, rank_size)
    merged_gate = merge_weight(w_gate[0], segments[0], segments[1])
    merged_up = merge_weight(w_up[0], segments[2], segments[3])
    combined_down_weight = merge_weight(down_weight[0], segments[4], segments[5])

    def layout(step_index):
        ids_flat = route_ids[step_index].reshape(-1)
        onehot = (ids_flat[:, None] == jnp.arange(experts, dtype=jnp.int32)[None, :]).astype(
            jnp.int32
        )
        position = jnp.sum((jnp.cumsum(onehot, axis=0) - 1) * onehot, axis=1)
        target = ids_flat * capacity + position
        placed = (
            jnp.arange(experts * capacity, dtype=jnp.int32)[:, None] == target[None, :]
        ).astype(jnp.bfloat16)
        pair_rows = jnp.repeat(hidden[step_index], top_count, axis=0)
        outgoing = jnp.dot(placed, pair_rows, preferred_element_type=jnp.float32).astype(
            jnp.bfloat16
        )
        outgoing = outgoing.reshape(experts, 1, capacity, width)
        gates = route_gates(route_logits[step_index]).reshape(-1)
        weighted = placed * gates[None, :]
        return (outgoing, weighted)

    layouts_all = [layout(step_index) for step_index in range(steps_count)]
    results = []
    for step_index in range(steps_count):
        outgoing, weighted = layouts_all[step_index]
        arrived = lax.all_to_all(outgoing, "expert", split_axis=0, concat_axis=1, tiled=True)
        outputs = apply_expert_block(
            arrived.reshape(-1, width), merged_gate, merged_up, combined_down_weight
        )
        outputs = outputs.reshape(arrived.shape)
        returned = lax.all_to_all(outputs, "expert", split_axis=1, concat_axis=0, tiled=True)
        flat_back = returned.reshape(experts * capacity, width)
        pair_out = jnp.einsum("cp,cd->pd", weighted, flat_back, preferred_element_type=jnp.float32)
        results.append(
            pair_out.reshape(row_count, top_count, width).sum(axis=1).astype(jnp.bfloat16)
        )
    return jnp.stack(results, axis=0)


def shards(hidden, route_ids, route_logits, placement, factors, w_gate, w_up, down_weight):
    rows, top = route_ids.shape[1:]
    width, units = w_gate.shape[1:]
    owners = lax.axis_size("expert")
    rank = factors.shape[1] * owners // (3 * (width + units))
    dense = row_capacity(rows, top, placement.shape[0]) == rows
    dense = dense and lax.axis_size("group") == 2 and split_axis(owners)[2] == 2
    outer = split_axis(owners)[0]
    dense = dense and outer > 1 and outer & (outer - 1) == 0 and split_axis(owners)[1] > 1
    dense = dense and 2 * rank == LANES and width % 256 == 0 and units % 256 == 0
    dense = dense and factors.shape[1] % (8 * LANES) == 0
    return (dense_shards if dense else sparse_shards)(
        hidden, route_ids, route_logits, placement, factors, w_gate, w_up, down_weight
    )


def solution(mesh):
    placed = (
        P(None, ("group", "expert"), None),
        P(None, ("group", "expert"), None),
        P(None, ("group", "expert"), None),
        P(),
        P(None, "expert"),
        P("expert", None, None),
        P("expert", None, None),
        P("expert", None, None),
    )
    return jax.shard_map(
        shards,
        mesh=mesh,
        in_specs=placed,
        out_specs=P(None, ("group", "expert"), None),
        check_vma=False,
    )
```

```python
import functools

import jax
import jax.numpy as jnp
from jax import lax
from jax.experimental import pallas as pl
from jax.experimental.pallas import tpu as pltpu
from jax.sharding import PartitionSpec as P

adapter_scale = 2.0
LANES = 128
GRANT = 16 << 20
EXPERT_GRANT = 30 << 20
WHOLE_GRANT = 60 << 20
MUCH = pl.CostEstimate(flops=1 << 33, bytes_accessed=1, transcendentals=0)
LITTLE = pl.CostEstimate(flops=1, bytes_accessed=1, transcendentals=0)


def route_gates(logits):
    highest = jnp.max(logits, axis=-1, keepdims=True)
    router_scores = jnp.exp(logits - highest)
    return (router_scores / jnp.sum(router_scores, axis=-1, keepdims=True)).astype(jnp.bfloat16)


def split_axis(n):
    cores = 2 if n % 2 == 0 else 1
    chips = n // cores
    middle = 1
    while chips % (2 * middle) == 0 and 4 * middle * middle <= chips:
        middle *= 2
    return chips // middle, middle, cores


def swap(x, n, stride, k):
    return lax.ppermute(x, "expert", [(i, i ^ (k * stride)) for i in range(n)])


def scatter_along(total, n, stride, size, received=None):
    count = total.shape[0] // size
    received = [] if received is None else received
    for k in range(1, size):
        part = total[k * count : (k + 1) * count].astype(jnp.bfloat16)
        received.append(swap(part, n, stride, k))
    return sum([part.astype(jnp.float32) for part in received], total[:count])


def halve_along(total, n, stride, size, count, last):
    step = 1
    while step < size:
        total = total.reshape(-1, 2, count, total.shape[1])
        sent = total[:, 1].reshape(-1, total.shape[3]).astype(jnp.bfloat16)
        kept = total[:, 0].reshape(-1, total.shape[3])
        sent = swap(sent, n, stride, step)
        if 2 * step == size:
            sent = lax.optimization_barrier((sent, last))[0]
        total = kept + sent.astype(jnp.float32)
        step *= 2
    return total


def exchange_factors(blocks, n):
    _, middle, cores = split_axis(n)
    here = []
    for q, block in enumerate(blocks):
        turn = q * middle * cores
        pairs = [(g * n + i, g * n + (i ^ turn ^ g)) for g in range(2) for i in range(n)]
        here.append(lax.ppermute(block, ("group", "expert"), pairs))
    return here


def dot(a, b):
    return jnp.dot(a, b, preferred_element_type=jnp.float32)


def payload_kernel(hidden_ref, ids_ref, logits_ref, out_ref, turned_ref):
    steps, top, rows = ids_ref.shape
    width = hidden_ref.shape[2]
    turned_ref[...] = jnp.zeros_like(turned_ref)
    for s in range(steps):
        logits, ids = logits_ref[s], ids_ref[s]
        scores = jnp.exp(logits - jnp.max(logits, axis=0, keepdims=True))
        gates = scores / jnp.sum(scores, axis=0, keepdims=True)
        expert = lax.broadcasted_iota(jnp.int32, (turned_ref.shape[0], rows), 0)
        dense = jnp.zeros(expert.shape, jnp.float32)
        for k in range(top):
            dense += jnp.where(ids[k : k + 1, :] == expert, gates[k : k + 1, :], 0.0)
        turned_ref[:, s * rows : (s + 1) * rows] = dense
    dense = turned_ref[...].T.astype(jnp.bfloat16)
    for s in range(steps):
        out_ref[s * rows : (s + 1) * rows, :width] = hidden_ref[s]
    out_ref[:, width:] = dense[: steps * rows]


def make_payload(hidden, route_ids, route_logits, experts):
    steps, rows, width = hidden.shape
    padded = -(-experts // LANES) * LANES
    return pl.pallas_call(
        payload_kernel,
        out_shape=jax.ShapeDtypeStruct((steps * rows, width + padded), jnp.bfloat16),
        scratch_shapes=[pltpu.VMEM((padded, -(-steps * rows // LANES) * LANES), jnp.float32)],
        compiler_params=pltpu.CompilerParams(vmem_limit_bytes=WHOLE_GRANT),
        cost_estimate=LITTLE,
        name="payload",
    )(hidden, jnp.swapaxes(route_ids, 1, 2), jnp.swapaxes(route_logits, 1, 2))


def order_kernel(place_ref, placement_ref, factors_ref, *refs):
    out_refs, wide_ref, slot_ref = refs[:-2], refs[-2], refs[-1]
    slots = factors_ref.shape[0]
    outer, length, lanes = out_refs[0].shape
    group, me = place_ref[0], place_ref[1]

    def cut(t, carry):
        start = pl.multiple_of(t * lanes, lanes)
        tile = factors_ref[:, pl.ds(start, lanes)].astype(jnp.float32)
        wide_ref[pl.ds(t, slots, stride=length), :] = tile
        return carry

    lax.fori_loop(0, length, cut, 0, unroll=8)
    for s in range(slots):
        slot_ref[placement_ref[s]] = s
    for r, out_ref in enumerate(out_refs):
        for q in range(outer):
            slot = slot_ref[me ^ (2 * (q * len(out_refs) + r) + group)]
            rows = wide_ref[pl.ds(pl.multiple_of(slot * length, 8), length), :]
            out_ref[q] = rows.astype(jnp.bfloat16)


def order_factors(place, placement, factors, outer, middle):
    slots, entries = factors.shape
    length = entries // LANES
    return pl.pallas_call(
        order_kernel,
        out_shape=[jax.ShapeDtypeStruct((outer, length, LANES), jnp.bfloat16)] * middle,
        in_specs=[
            pl.BlockSpec(memory_space=pltpu.SMEM),
            pl.BlockSpec(memory_space=pltpu.SMEM),
            pl.BlockSpec(memory_space=pltpu.VMEM),
        ],
        scratch_shapes=[
            pltpu.VMEM((slots * length, LANES), jnp.float32),
            pltpu.SMEM((slots,), jnp.int32),
        ],
        compiler_params=pltpu.CompilerParams(vmem_limit_bytes=WHOLE_GRANT),
        cost_estimate=LITTLE,
        name="order_factors",
    )(place, placement, factors)


def relayout_kernel(outer, middle, place_ref, *refs):
    a_gu_ref, gate_b_ref, up_b_ref, down_a_ref, down_b_ref, flat_ref, wide_ref = refs[2:]
    width, units = a_gu_ref.shape[0], gate_b_ref.shape[1]
    rank = gate_b_ref.shape[0]
    length = refs[0].shape[2]
    group, me = place_ref[0], place_ref[1]
    for swapped, part in enumerate(refs[:2]):
        core = group if swapped == 0 else 1 - group
        for q in range(outer):
            for r in range(middle):
                source = me ^ ((q * middle + r) * 2 + core)
                start = pl.multiple_of(source * length, 8)
                flat_ref[pl.ds(start, length), :] = part[q, r].astype(jnp.float32)

    n_wide, n_unit = width // 2, units // 2
    at_ub = 2 * n_wide + n_unit
    at_da = 2 * n_wide + 2 * n_unit
    chunk = 128
    left = lax.broadcasted_iota(jnp.int32, (chunk, LANES), 1) < rank

    def load(start):
        return flat_ref[pl.ds(pl.multiple_of(start, 128), chunk), :]

    def gate_up(i, carry):
        g, u = load(i * chunk), load(n_wide + n_unit + i * chunk)
        at = 2 * i * chunk
        wide_ref[pl.ds(at, chunk, stride=2), :] = jnp.where(left, g, pltpu.roll(u, rank, 1))
        wide_ref[pl.ds(at + 1, chunk, stride=2), :] = jnp.where(left, pltpu.roll(g, rank, 1), u)
        both = wide_ref[pl.ds(pl.multiple_of(at, 128), 2 * chunk), :]
        a_gu_ref[pl.ds(pl.multiple_of(at, 128), 2 * chunk), :] = both.astype(jnp.bfloat16)
        return carry

    lax.fori_loop(0, n_wide // chunk, gate_up, 0, unroll=2)
    for i in range(n_unit // chunk):
        d = load(at_da + i * chunk)
        at = 2 * i * chunk
        wide_ref[pl.ds(at, chunk, stride=2), :] = jnp.where(left, d, 0.0)
        wide_ref[pl.ds(at + 1, chunk, stride=2), :] = jnp.where(left, pltpu.roll(d, rank, 1), 0.0)
        down_a_ref[at : at + 2 * chunk, :] = wide_ref[at : at + 2 * chunk, :].astype(jnp.bfloat16)
    for start, b_ref in (
        (n_wide, gate_b_ref),
        (at_ub, up_b_ref),
        (at_da + n_unit, down_b_ref),
    ):
        tiles = b_ref.shape[1] // LANES
        for j in range(tiles):
            row = flat_ref[pl.ds(start + j, rank, stride=tiles), :]
            b_ref[:, j * LANES : (j + 1) * LANES] = row.astype(jnp.bfloat16)


def relayout_factors(place, here, there, width, units, rank, n):
    outer, middle, _ = split_axis(n)
    shapes = [(width, 2 * rank), (rank, units), (rank, units), (units, 2 * rank), (rank, width)]
    length = here.shape[2]
    return pl.pallas_call(
        functools.partial(relayout_kernel, outer, middle),
        out_shape=[jax.ShapeDtypeStruct(shape, jnp.bfloat16) for shape in shapes],
        in_specs=[pl.BlockSpec(memory_space=pltpu.SMEM)]
        + [pl.BlockSpec(memory_space=pltpu.VMEM)] * 2,
        scratch_shapes=[
            pltpu.VMEM((n * length, LANES), jnp.float32),
            pltpu.VMEM((width, LANES), jnp.float32),
        ],
        compiler_params=pltpu.CompilerParams(vmem_limit_bytes=GRANT),
        cost_estimate=LITTLE,
        name="relayout_factors",
    )(place, here, there)


class Loads:
    def __init__(self, sem):
        self.sem, self.count = sem, 0

    def begin(self, src, dst):
        copy = pltpu.make_async_copy(src, dst, self.sem.at[self.count])
        copy.start()
        self.count += 1
        return [copy]

    def begin_rows(self, src, dst, parts=4):
        step = src.shape[0] // parts
        cuts = [pl.ds(at, step) for at in range(0, src.shape[0], step)]
        return sum([self.begin(src.at[cut], dst.at[cut]) for cut in cuts], [])


def wait(copies):
    for copy in copies:
        copy.wait()


def base_kernel(count, *refs):
    pieces = refs[:count]
    w_gate_hbm, w_up_hbm, gate_hbm, up_hbm, x_ref, w_gate_ref, w_up_ref = refs[count : count + 7]
    gate_ref, up_ref, sem, out_sem = refs[count + 7 :]
    rows = pieces[0].shape[0]
    width = w_gate_ref.shape[0]
    total = gate_ref.shape[0]
    block = min(128, total)
    loads = Loads(sem)
    x_in = [loads.begin(p, x_ref.at[pl.ds(i * rows, rows)]) for i, p in enumerate(pieces)]
    x_in = sum(x_in, [])
    gate_in = loads.begin_rows(w_gate_hbm, w_gate_ref)
    up_in = loads.begin_rows(w_up_hbm, w_up_ref)
    wait(x_in + gate_in + up_in)

    def store(i):
        here = pl.ds(pl.multiple_of(i * block, block), block)
        return [
            pltpu.make_async_copy(src.at[here], dst.at[here], out_sem.at[j, i])
            for j, (src, dst) in enumerate(((gate_ref, gate_hbm), (up_ref, up_hbm)))
        ]

    def run_block(i, carry):
        here = pl.ds(pl.multiple_of(i * block, block), block)
        gate_ref[here, :] = dot(x_ref[here, :width], w_gate_ref[...])
        up_ref[here, :] = dot(x_ref[here, :width], w_up_ref[...])
        for copy in store(i):
            copy.start()
        return carry

    lax.fori_loop(0, total // block, run_block, 0)
    for i in range(total // block):
        wait(store(i))


def base_products(pieces, w_gate, w_up):
    width, units = w_gate.shape
    total = sum(p.shape[0] for p in pieces)
    out = jax.ShapeDtypeStruct((total, units), jnp.float32)
    return pl.pallas_call(
        functools.partial(base_kernel, len(pieces)),
        out_shape=[out, out],
        in_specs=[pl.BlockSpec(memory_space=pl.ANY)] * len(pieces)
        + [pl.BlockSpec(memory_space=pltpu.HBM)] * 2,
        out_specs=[pl.BlockSpec(memory_space=pl.ANY)] * 2,
        scratch_shapes=[
            pltpu.VMEM((total, pieces[0].shape[1]), jnp.bfloat16),
            pltpu.VMEM(w_gate.shape, w_gate.dtype),
            pltpu.VMEM(w_up.shape, w_up.dtype),
            pltpu.VMEM(out.shape, out.dtype),
            pltpu.VMEM(out.shape, out.dtype),
            pltpu.SemaphoreType.DMA((len(pieces) + 8,)),
            pltpu.SemaphoreType.DMA((2, total // min(128, total))),
        ],
        compiler_params=pltpu.CompilerParams(vmem_limit_bytes=EXPERT_GRANT),
        cost_estimate=LITTLE,
        name="base_products",
    )(*pieces, w_gate, w_up)


def finish_kernel(count, first, rows, place_ref, *refs):
    pieces, refs = refs[:count], refs[count:]
    gate_ref, up_ref, a_gu_ref, gate_b_ref, up_b_ref, down_a_ref, down_b_ref = refs[:7]
    w_down_ref, kept_ref, sent_ref, x_ref, inner_ref = refs[7:]
    width = w_down_ref.shape[1]
    rank = gate_b_ref.shape[0]
    span = pieces[0].shape[0]
    own = kept_ref.shape[0]
    for i, piece in enumerate(pieces):
        x_ref[i * rows : (i + 1) * rows, :] = piece[first : first + rows, :]

    def of_step(ref):
        starts = [i * span + first for i in range(count)]
        return jnp.concatenate([ref[at : at + rows, :] for at in starts])

    low = (adapter_scale * dot(x_ref[:, :width], a_gu_ref[...])).astype(jnp.bfloat16)
    gates = x_ref[:, width:].astype(jnp.float32)
    lane = lax.broadcasted_iota(jnp.int32, gates.shape, 1)
    mine = jnp.sum(jnp.where(lane == place_ref[1], gates, 0.0), axis=1, keepdims=True)
    g = of_step(gate_ref) + dot(low[:, :rank], gate_b_ref[...])
    u = of_step(up_ref) + dot(low[:, rank:], up_b_ref[...])
    half = 0.5 * g
    inner_ref[...] = ((half + half * jnp.tanh(half)) * u).astype(jnp.bfloat16)
    low = (adapter_scale * dot(inner_ref[...], down_a_ref[...])).astype(jnp.bfloat16)[:, :rank]
    out = (dot(inner_ref[...], w_down_ref[...]) + dot(low, down_b_ref[...])) * mine
    kept_ref[...] = out[:own]
    sent_ref[...] = out[own:].astype(jnp.bfloat16)


def finish_step(place, pieces, base, first, rows, low_rank, w_down):
    units, width = w_down.shape
    total = rows * len(pieces)
    own = total // 2
    operands = [*pieces, *base, *low_rank, w_down]
    return pl.pallas_call(
        functools.partial(finish_kernel, len(pieces), first, rows),
        out_shape=[
            jax.ShapeDtypeStruct((own, width), jnp.float32),
            jax.ShapeDtypeStruct((own, width), jnp.bfloat16),
        ],
        in_specs=[pl.BlockSpec(memory_space=pltpu.SMEM)]
        + [pl.BlockSpec(memory_space=pltpu.VMEM)] * len(operands),
        scratch_shapes=[
            pltpu.VMEM((total, pieces[0].shape[1]), jnp.bfloat16),
            pltpu.VMEM((total, units), jnp.bfloat16),
        ],
        compiler_params=pltpu.CompilerParams(vmem_limit_bytes=EXPERT_GRANT),
        cost_estimate=MUCH,
        name="finish_step",
    )(place, *operands)


def dense_shards(
    hidden, route_ids, route_logits, placement, factors, w_gate, w_up, down_weight
):
    owners = lax.axis_size("expert")
    experts = placement.shape[0]
    steps, rows, width = hidden.shape
    units = w_gate.shape[2]
    rank = factors.shape[1] * owners // (3 * (width + units))
    outer, middle, cores = split_axis(owners)
    along_outer, along_middle = (middle * cores, outer), (cores, middle)
    place = jnp.stack([lax.axis_index("group"), lax.axis_index("expert")]).astype(jnp.int32)

    def along(x, stride, size):
        return [x] + [swap(x, owners, stride, k) for k in range(1, size)]

    rows_in = make_payload(hidden, route_ids, route_logits, experts)
    rows_in, factors = lax.optimization_barrier((rows_in, factors))
    column = [p.reshape(steps, rows, -1) for p in along(rows_in, *along_outer)]
    column = jnp.stack(column, axis=1).reshape(steps * outer * rows, -1)
    blocks = order_factors(place, placement, factors, outer, middle)
    blocks = [blocks[0]] + [swap(blocks[r], owners, cores, r) for r in range(1, middle)]
    blocks = [jnp.stack([block[q] for block in blocks]) for q in range(outer)]
    column, blocks = lax.optimization_barrier((column, blocks))
    here = exchange_factors(blocks, owners)
    sheet = along(column, *along_middle)
    here, sheet[1:] = lax.optimization_barrier((here, sheet[1:]))
    here = jnp.stack(here)
    there = lax.ppermute(here, "group", [(0, 1), (1, 0)])
    pieces = sheet + [swap(p, owners, 1, 1) for p in sheet]
    base = base_products(pieces, w_gate[0], w_up[0])
    here, there, base = lax.optimization_barrier((here, there, base))
    low_rank = relayout_factors(place, here, there, width, units, rank, owners)

    span = outer * rows
    def after(x, other):
        return lax.optimization_barrier((x, other))[0]

    summed, across = [], []
    for s in range(steps):
        if s >= 1:
            pieces = lax.optimization_barrier((pieces, summed[s - 1], across[: s - 1]))[0]
        kept, sent = finish_step(
            place, pieces, base, s * span, span, low_rank, down_weight[0]
        )
        if s >= 1:
            kept = after(kept, across[s - 1])
        summed.append(kept + swap(sent, owners, 1, 1).astype(jnp.float32))
        across.append(scatter_along(summed[s], owners, *along_middle))
    across[:-1] = [after(total, summed[-1]) for total in across[:-1]]
    ends = []
    final = scatter_along(across[-1], owners, *along_outer, ends)
    others = halve_along(jnp.concatenate(across[:-1]), owners, *along_outer, rows, ends[0])
    return jnp.concatenate([others, final]).astype(jnp.bfloat16).reshape(hidden.shape)


def row_capacity(rows, top, experts):
    return min(rows, 3 * max(1, rows * top // experts))


def unpack_factors(flat_factors, width, hidden_units, rank_size):
    layouts = [
        (width, rank_size),
        (rank_size, hidden_units),
        (width, rank_size),
        (rank_size, hidden_units),
        (hidden_units, rank_size),
        (rank_size, width),
    ]
    offset = 0
    segments = []
    for leading, trailing in layouts:
        segments.append(
            flat_factors[offset : offset + leading * trailing].reshape(leading, trailing)
        )
        offset = offset + leading * trailing
    return segments


def merge_weight(loaded_weights, factor_a, factor_b):
    adapter_delta = jnp.dot(factor_a, factor_b, preferred_element_type=jnp.float32)
    return (loaded_weights.astype(jnp.float32) + adapter_scale * adapter_delta).astype(jnp.bfloat16)


def apply_expert_block(inputs, merged_gate, merged_up, combined_down_weight):
    gate_part = jnp.dot(inputs, merged_gate, preferred_element_type=jnp.float32)
    up_part = jnp.dot(inputs, merged_up, preferred_element_type=jnp.float32)
    inner = (jax.nn.silu(gate_part) * up_part).astype(jnp.bfloat16)
    return jnp.dot(inner, combined_down_weight, preferred_element_type=jnp.float32).astype(
        jnp.bfloat16
    )


def sparse_shards(hidden, route_ids, route_logits, placement, factors, w_gate, w_up, down_weight):
    owners = lax.axis_size("expert")
    experts = placement.shape[0]
    steps_count, row_count, width = hidden.shape
    top_count = route_ids.shape[2]
    hidden_units = w_gate.shape[2]
    rank_size = factors.shape[1] * owners // (3 * (width + hidden_units))
    capacity = row_capacity(row_count, top_count, experts)
    slot_of = (
        jnp.zeros((experts,), jnp.int32).at[placement].set(jnp.arange(experts, dtype=jnp.int32))
    )
    ordered = jnp.take(factors, slot_of, axis=0)
    received = lax.all_to_all(ordered, "expert", split_axis=0, concat_axis=1, tiled=True)
    segments = unpack_factors(received[0], width, hidden_units, rank_size)
    merged_gate = merge_weight(w_gate[0], segments[0], segments[1])
    merged_up = merge_weight(w_up[0], segments[2], segments[3])
    combined_down_weight = merge_weight(down_weight[0], segments[4], segments[5])

    def layout(step_index):
        ids_flat = route_ids[step_index].reshape(-1)
        onehot = (ids_flat[:, None] == jnp.arange(experts, dtype=jnp.int32)[None, :]).astype(
            jnp.int32
        )
        position = jnp.sum((jnp.cumsum(onehot, axis=0) - 1) * onehot, axis=1)
        target = ids_flat * capacity + position
        placed = (
            jnp.arange(experts * capacity, dtype=jnp.int32)[:, None] == target[None, :]
        ).astype(jnp.bfloat16)
        pair_rows = jnp.repeat(hidden[step_index], top_count, axis=0)
        outgoing = jnp.dot(placed, pair_rows, preferred_element_type=jnp.float32).astype(
            jnp.bfloat16
        )
        outgoing = outgoing.reshape(experts, 1, capacity, width)
        gates = route_gates(route_logits[step_index]).reshape(-1)
        weighted = placed * gates[None, :]
        return (outgoing, weighted)

    layouts_all = [layout(step_index) for step_index in range(steps_count)]
    results = []
    for step_index in range(steps_count):
        outgoing, weighted = layouts_all[step_index]
        arrived = lax.all_to_all(outgoing, "expert", split_axis=0, concat_axis=1, tiled=True)
        outputs = apply_expert_block(
            arrived.reshape(-1, width), merged_gate, merged_up, combined_down_weight
        )
        outputs = outputs.reshape(arrived.shape)
        returned = lax.all_to_all(outputs, "expert", split_axis=1, concat_axis=0, tiled=True)
        flat_back = returned.reshape(experts * capacity, width)
        pair_out = jnp.einsum("cp,cd->pd", weighted, flat_back, preferred_element_type=jnp.float32)
        results.append(
            pair_out.reshape(row_count, top_count, width).sum(axis=1).astype(jnp.bfloat16)
        )
    return jnp.stack(results, axis=0)


def shards(hidden, route_ids, route_logits, placement, factors, w_gate, w_up, down_weight):
    rows, top = route_ids.shape[1:]
    width, units = w_gate.shape[1:]
    owners = lax.axis_size("expert")
    rank = factors.shape[1] * owners // (3 * (width + units))
    dense = row_capacity(rows, top, placement.shape[0]) == rows
    dense = dense and lax.axis_size("group") == 2 and split_axis(owners)[2] == 2
    outer = split_axis(owners)[0]
    dense = dense and outer > 1 and outer & (outer - 1) == 0 and split_axis(owners)[1] > 1
    dense = dense and 2 * rank == LANES and width % 256 == 0 and units % 256 == 0
    dense = dense and factors.shape[1] % (8 * LANES) == 0
    return (dense_shards if dense else sparse_shards)(
        hidden, route_ids, route_logits, placement, factors, w_gate, w_up, down_weight
    )


def solution(mesh):
    placed = (
        P(None, ("group", "expert"), None),
        P(None, ("group", "expert"), None),
        P(None, ("group", "expert"), None),
        P(),
        P(None, "expert"),
        P("expert", None, None),
        P("expert", None, None),
        P("expert", None, None),
    )
    return jax.shard_map(
        shards,
        mesh=mesh,
        in_specs=placed,
        out_specs=P(None, ("group", "expert"), None),
        check_vma=False,
    )
```

```python
import functools

import jax
import jax.numpy as jnp
from jax import lax
from jax.experimental import pallas as pl
from jax.experimental.pallas import tpu as pltpu
from jax.sharding import PartitionSpec as P

adapter_scale = 2.0
LANES = 128
GRANT = 16 << 20
EXPERT_GRANT = 30 << 20
WHOLE_GRANT = 60 << 20
MUCH = pl.CostEstimate(flops=1 << 33, bytes_accessed=1, transcendentals=0)
LITTLE = pl.CostEstimate(flops=1, bytes_accessed=1, transcendentals=0)


def route_gates(logits):
    highest = jnp.max(logits, axis=-1, keepdims=True)
    router_scores = jnp.exp(logits - highest)
    return (router_scores / jnp.sum(router_scores, axis=-1, keepdims=True)).astype(jnp.bfloat16)


def split_axis(n):
    cores = 2 if n % 2 == 0 else 1
    chips = n // cores
    middle = 1
    while chips % (2 * middle) == 0 and 4 * middle * middle <= chips:
        middle *= 2
    return chips // middle, middle, cores


def swap(x, n, stride, k):
    return lax.ppermute(x, "expert", [(i, i ^ (k * stride)) for i in range(n)])


def scatter_along(total, n, stride, size, received=None):
    count = total.shape[0] // size
    received = [] if received is None else received
    for k in range(1, size):
        part = total[k * count : (k + 1) * count].astype(jnp.bfloat16)
        received.append(swap(part, n, stride, k))
    return sum([part.astype(jnp.float32) for part in received], total[:count])


def halve_along(total, n, stride, size, count, last):
    step = 1
    while step < size:
        total = total.reshape(-1, 2, count, total.shape[1])
        sent = total[:, 1].reshape(-1, total.shape[3]).astype(jnp.bfloat16)
        kept = total[:, 0].reshape(-1, total.shape[3])
        sent = swap(sent, n, stride, step)
        if 2 * step == size:
            sent = lax.optimization_barrier((sent, last))[0]
        total = kept + sent.astype(jnp.float32)
        step *= 2
    return total


def dot(a, b):
    return jnp.dot(a, b, preferred_element_type=jnp.float32)


def payload_kernel(hidden_ref, ids_ref, logits_ref, out_ref, turned_ref):
    steps, top, rows = ids_ref.shape
    width = hidden_ref.shape[2]
    turned_ref[...] = jnp.zeros_like(turned_ref)
    for s in range(steps):
        logits, ids = logits_ref[s], ids_ref[s]
        scores = jnp.exp(logits - jnp.max(logits, axis=0, keepdims=True))
        gates = scores / jnp.sum(scores, axis=0, keepdims=True)
        expert = lax.broadcasted_iota(jnp.int32, (turned_ref.shape[0], rows), 0)
        dense = jnp.zeros(expert.shape, jnp.float32)
        for k in range(top):
            dense += jnp.where(ids[k : k + 1, :] == expert, gates[k : k + 1, :], 0.0)
        turned_ref[:, s * rows : (s + 1) * rows] = dense
    dense = turned_ref[...].T.astype(jnp.bfloat16)
    for s in range(steps):
        out_ref[s * rows : (s + 1) * rows, :width] = hidden_ref[s]
    out_ref[:, width:] = dense[: steps * rows]


def make_payload(hidden, route_ids, route_logits, experts):
    steps, rows, width = hidden.shape
    padded = -(-experts // LANES) * LANES
    return pl.pallas_call(
        payload_kernel,
        out_shape=jax.ShapeDtypeStruct((steps * rows, width + padded), jnp.bfloat16),
        scratch_shapes=[pltpu.VMEM((padded, -(-steps * rows // LANES) * LANES), jnp.float32)],
        compiler_params=pltpu.CompilerParams(vmem_limit_bytes=WHOLE_GRANT),
        cost_estimate=LITTLE,
        name="payload",
    )(hidden, jnp.swapaxes(route_ids, 1, 2), jnp.swapaxes(route_logits, 1, 2))


def order_kernel(place_ref, placement_ref, factors_ref, *refs):
    out_refs, wide_ref, slot_ref = refs[:-2], refs[-2], refs[-1]
    slots = factors_ref.shape[0]
    middle, outer, length, lanes = out_refs[0].shape

    def cut(t, carry):
        start = pl.multiple_of(t * lanes, lanes)
        tile = factors_ref[:, pl.ds(start, lanes)].astype(jnp.float32)
        wide_ref[pl.ds(t, slots, stride=length), :] = tile
        return carry

    lax.fori_loop(0, length, cut, 0, unroll=8)
    for s in range(slots):
        slot_ref[placement_ref[s]] = s
    for core, out_ref in enumerate(out_refs):
        for r in range(middle):
            for q in range(outer):
                slot = slot_ref[place_ref[0] ^ ((q * middle + r) * len(out_refs) + core)]
                rows = wide_ref[pl.ds(pl.multiple_of(slot * length, 8), length), :]
                out_ref[r, q] = rows.astype(jnp.bfloat16)


def order_factors(place, placement, factors, outer, middle, cores):
    slots, entries = factors.shape
    length = entries // LANES
    shape = jax.ShapeDtypeStruct((middle, outer, length, LANES), jnp.bfloat16)
    return pl.pallas_call(
        order_kernel,
        out_shape=[shape] * cores,
        in_specs=[
            pl.BlockSpec(memory_space=pltpu.SMEM),
            pl.BlockSpec(memory_space=pltpu.SMEM),
            pl.BlockSpec(memory_space=pltpu.VMEM),
        ],
        scratch_shapes=[
            pltpu.VMEM((slots * length, LANES), jnp.float32),
            pltpu.SMEM((slots,), jnp.int32),
        ],
        compiler_params=pltpu.CompilerParams(vmem_limit_bytes=WHOLE_GRANT),
        cost_estimate=MUCH,
        name="order_factors",
    )(place, placement, factors)


def relayout_kernel(place_ref, *refs):
    parts, refs = refs[:-7], refs[-7:]
    a_gu_ref, gate_b_ref, up_b_ref, down_a_ref, down_b_ref, flat_ref, wide_ref = refs
    width, units = a_gu_ref.shape[0], gate_b_ref.shape[1]
    rank = gate_b_ref.shape[0]
    near, length, _ = parts[0].shape
    for q, part in enumerate(parts):
        for j in range(near):
            start = pl.multiple_of((place_ref[0] ^ (near * q + j)) * length, 8)
            flat_ref[pl.ds(start, length), :] = part[j].astype(jnp.float32)

    n_wide, n_unit = width // 2, units // 2
    at_ub = 2 * n_wide + n_unit
    at_da = 2 * n_wide + 2 * n_unit
    chunk = 128
    left = lax.broadcasted_iota(jnp.int32, (chunk, LANES), 1) < rank

    def load(start):
        return flat_ref[pl.ds(pl.multiple_of(start, 128), chunk), :]

    def gate_up(i, carry):
        g, u = load(i * chunk), load(n_wide + n_unit + i * chunk)
        at = 2 * i * chunk
        wide_ref[pl.ds(at, chunk, stride=2), :] = jnp.where(left, g, pltpu.roll(u, rank, 1))
        wide_ref[pl.ds(at + 1, chunk, stride=2), :] = jnp.where(left, pltpu.roll(g, rank, 1), u)
        both = wide_ref[pl.ds(pl.multiple_of(at, 128), 2 * chunk), :]
        a_gu_ref[pl.ds(pl.multiple_of(at, 128), 2 * chunk), :] = both.astype(jnp.bfloat16)
        return carry

    lax.fori_loop(0, n_wide // chunk, gate_up, 0, unroll=2)
    for i in range(n_unit // chunk):
        d = load(at_da + i * chunk)
        at = 2 * i * chunk
        wide_ref[pl.ds(at, chunk, stride=2), :] = jnp.where(left, d, 0.0)
        wide_ref[pl.ds(at + 1, chunk, stride=2), :] = jnp.where(left, pltpu.roll(d, rank, 1), 0.0)
        down_a_ref[at : at + 2 * chunk, :] = wide_ref[at : at + 2 * chunk, :].astype(jnp.bfloat16)
    for start, b_ref in (
        (n_wide, gate_b_ref),
        (at_ub, up_b_ref),
        (at_da + n_unit, down_b_ref),
    ):
        tiles = b_ref.shape[1] // LANES
        for j in range(tiles):
            row = flat_ref[pl.ds(start + j, rank, stride=tiles), :]
            b_ref[:, j * LANES : (j + 1) * LANES] = row.astype(jnp.bfloat16)


def relayout_factors(place, parts, width, units, rank, n):
    shapes = [(width, 2 * rank), (rank, units), (rank, units), (units, 2 * rank), (rank, width)]
    length = parts[0].shape[1]
    return pl.pallas_call(
        relayout_kernel,
        out_shape=[jax.ShapeDtypeStruct(shape, jnp.bfloat16) for shape in shapes],
        in_specs=[pl.BlockSpec(memory_space=pltpu.SMEM)]
        + [pl.BlockSpec(memory_space=pltpu.VMEM)] * len(parts),
        scratch_shapes=[
            pltpu.VMEM((n * length, LANES), jnp.float32),
            pltpu.VMEM((width, LANES), jnp.float32),
        ],
        compiler_params=pltpu.CompilerParams(vmem_limit_bytes=GRANT),
        cost_estimate=LITTLE,
        name="relayout_factors",
    )(place, *parts)


def base_kernel(x_ref, other_ref, w_gate_ref, w_up_ref, gate_ref, up_ref):
    width, rows = w_gate_ref.shape[0], x_ref.shape[0]
    for i, piece in enumerate((x_ref, other_ref)):
        at = slice(i * rows, (i + 1) * rows)
        gate_ref[at, :] = dot(piece[:, :width], w_gate_ref[...])
        up_ref[at, :] = dot(piece[:, :width], w_up_ref[...])


def base_products(pieces, w_gate, w_up):
    total = sum(p.shape[0] for p in pieces)
    out = jax.ShapeDtypeStruct((total, w_gate.shape[1]), jnp.float32)
    return pl.pallas_call(
        base_kernel,
        out_shape=[out, out],
        in_specs=[pl.BlockSpec(memory_space=pltpu.VMEM)] * 4,
        compiler_params=pltpu.CompilerParams(vmem_limit_bytes=EXPERT_GRANT),
        cost_estimate=LITTLE,
        name="base_products",
    )(*pieces, w_gate, w_up)


def finish_kernel(count, first, rows, place_ref, *refs):
    pieces, refs = refs[:count], refs[count:]
    base, refs = refs[:count], refs[count:]
    a_gu_ref, gate_b_ref, up_b_ref, down_a_ref, down_b_ref, w_down_ref = refs[:6]
    kept_ref, sent_ref, x_ref, inner_ref = refs[6:]
    width = w_down_ref.shape[1]
    rank = gate_b_ref.shape[0]
    span = pieces[0].shape[0]
    own = kept_ref.shape[0]
    for i, piece in enumerate(pieces):
        x_ref[i * rows : (i + 1) * rows, :] = piece[first : first + rows, :]

    def of_step(refs):
        at = [first, span + first]
        return jnp.concatenate([ref[i : i + rows, :] for i in at for ref in refs])

    low = (adapter_scale * dot(x_ref[:, :width], a_gu_ref[...])).astype(jnp.bfloat16)
    gates = x_ref[:, width:].astype(jnp.float32)
    lane = lax.broadcasted_iota(jnp.int32, gates.shape, 1)
    mine = jnp.sum(jnp.where(lane == place_ref[0], gates, 0.0), axis=1, keepdims=True)
    g = of_step(base[::2]) + dot(low[:, :rank], gate_b_ref[...])
    u = of_step(base[1::2]) + dot(low[:, rank:], up_b_ref[...])
    half = 0.5 * g
    inner_ref[...] = ((half + half * jnp.tanh(half)) * u).astype(jnp.bfloat16)
    low = (adapter_scale * dot(inner_ref[...], down_a_ref[...])).astype(jnp.bfloat16)[:, :rank]
    out = (dot(inner_ref[...], w_down_ref[...]) + dot(low, down_b_ref[...])) * mine
    kept_ref[...] = out[:own]
    sent_ref[...] = out[own:].astype(jnp.bfloat16)


def finish_step(place, pieces, base, first, rows, low_rank, w_down):
    units, width = w_down.shape
    total = rows * len(pieces)
    own = total // 2
    operands = [*pieces, *base, *low_rank, w_down]
    return pl.pallas_call(
        functools.partial(finish_kernel, len(pieces), first, rows),
        out_shape=[
            jax.ShapeDtypeStruct((own, width), jnp.float32),
            jax.ShapeDtypeStruct((own, width), jnp.bfloat16),
        ],
        in_specs=[pl.BlockSpec(memory_space=pltpu.SMEM)]
        + [pl.BlockSpec(memory_space=pltpu.VMEM)] * len(operands),
        scratch_shapes=[
            pltpu.VMEM((total, pieces[0].shape[1]), jnp.bfloat16),
            pltpu.VMEM((total, units), jnp.bfloat16),
        ],
        compiler_params=pltpu.CompilerParams(vmem_limit_bytes=EXPERT_GRANT),
        cost_estimate=MUCH,
        name="finish_step",
    )(place, *operands)


def dense_shards(
    hidden, route_ids, route_logits, placement, factors, w_gate, w_up, down_weight
):
    owners = lax.axis_size("expert")
    experts = placement.shape[0]
    steps, rows, width = hidden.shape
    units = w_gate.shape[2]
    rank = factors.shape[1] * owners // (3 * (width + units))
    outer, middle, cores = split_axis(owners)
    along_outer, along_middle = (middle * cores, outer), (cores, middle)
    place = lax.axis_index("expert").astype(jnp.int32).reshape(1)

    def along(x, stride, size):
        return [x] + [swap(x, owners, stride, k) for k in range(1, size)]

    rows_in = make_payload(hidden, route_ids, route_logits, experts)
    rows_in, factors = lax.optimization_barrier((rows_in, factors))
    column = [p.reshape(steps, rows, -1) for p in along(rows_in, *along_outer)]
    column = jnp.stack(column, axis=1).reshape(steps * outer * rows, -1)
    kept, sent = order_factors(place, placement, factors, outer, middle, cores)
    blocks = jnp.stack([kept, swap(sent, owners, 1, 1)])
    blocks = [blocks[:, 0], swap(blocks[:, 1], owners, cores, 1)]
    blocks = [jnp.concatenate([block[:, q] for block in blocks]) for q in range(outer)]
    column, blocks = lax.optimization_barrier((column, blocks))
    here = blocks[:1] + [
        swap(block, owners, middle * cores, q) for q, block in enumerate(blocks) if q
    ]
    sheet = along(column, *along_middle)
    others = [swap(column, owners, 1, 1)]
    weights = (w_gate[0], w_up[0])
    base = [base_products([column, others[0]], *weights)]
    here, sheet[1:], base = lax.optimization_barrier((here, sheet[1:], base))
    for r in range(1, middle):
        others.append(swap(sheet[r], owners, 1, 1))
        base.append(base_products([sheet[r], others[r]], *weights))
    low_rank = relayout_factors(place, here, width, units, rank, owners)
    pieces, base = sheet + others, [b for pair in base for b in pair]
    span = outer * rows

    def after(x, other):
        return lax.optimization_barrier((x, other))[0]

    summed, across = [], []
    for s in range(steps):
        if s >= 1:
            pieces = lax.optimization_barrier((pieces, summed[s - 1], across[: s - 1]))[0]
        kept, sent = finish_step(
            place, pieces, base, s * span, span, low_rank, down_weight[0]
        )
        if s >= 1:
            kept = after(kept, across[s - 1])
        summed.append(kept + swap(sent, owners, 1, 1).astype(jnp.float32))
        across.append(scatter_along(summed[s], owners, *along_middle))
    across[:-1] = [after(total, summed[-1]) for total in across[:-1]]
    ends = []
    final = scatter_along(across[-1], owners, *along_outer, ends)
    others = halve_along(jnp.concatenate(across[:-1]), owners, *along_outer, rows, ends[0])
    return jnp.concatenate([others, final]).astype(jnp.bfloat16).reshape(hidden.shape)


def row_capacity(rows, top, experts):
    return min(rows, 3 * max(1, rows * top // experts))


def unpack_factors(flat_factors, width, hidden_units, rank_size):
    layouts = [
        (width, rank_size),
        (rank_size, hidden_units),
        (width, rank_size),
        (rank_size, hidden_units),
        (hidden_units, rank_size),
        (rank_size, width),
    ]
    offset = 0
    segments = []
    for leading, trailing in layouts:
        segments.append(
            flat_factors[offset : offset + leading * trailing].reshape(leading, trailing)
        )
        offset = offset + leading * trailing
    return segments


def merge_weight(loaded_weights, factor_a, factor_b):
    adapter_delta = jnp.dot(factor_a, factor_b, preferred_element_type=jnp.float32)
    return (loaded_weights.astype(jnp.float32) + adapter_scale * adapter_delta).astype(jnp.bfloat16)


def apply_expert_block(inputs, merged_gate, merged_up, combined_down_weight):
    gate_part = jnp.dot(inputs, merged_gate, preferred_element_type=jnp.float32)
    up_part = jnp.dot(inputs, merged_up, preferred_element_type=jnp.float32)
    inner = (jax.nn.silu(gate_part) * up_part).astype(jnp.bfloat16)
    return jnp.dot(inner, combined_down_weight, preferred_element_type=jnp.float32).astype(
        jnp.bfloat16
    )


def sparse_shards(hidden, route_ids, route_logits, placement, factors, w_gate, w_up, down_weight):
    owners = lax.axis_size("expert")
    experts = placement.shape[0]
    steps_count, row_count, width = hidden.shape
    top_count = route_ids.shape[2]
    hidden_units = w_gate.shape[2]
    rank_size = factors.shape[1] * owners // (3 * (width + hidden_units))
    capacity = row_capacity(row_count, top_count, experts)
    slot_of = (
        jnp.zeros((experts,), jnp.int32).at[placement].set(jnp.arange(experts, dtype=jnp.int32))
    )
    ordered = jnp.take(factors, slot_of, axis=0)
    received = lax.all_to_all(ordered, "expert", split_axis=0, concat_axis=1, tiled=True)
    segments = unpack_factors(received[0], width, hidden_units, rank_size)
    merged_gate = merge_weight(w_gate[0], segments[0], segments[1])
    merged_up = merge_weight(w_up[0], segments[2], segments[3])
    combined_down_weight = merge_weight(down_weight[0], segments[4], segments[5])

    def layout(step_index):
        ids_flat = route_ids[step_index].reshape(-1)
        onehot = (ids_flat[:, None] == jnp.arange(experts, dtype=jnp.int32)[None, :]).astype(
            jnp.int32
        )
        position = jnp.sum((jnp.cumsum(onehot, axis=0) - 1) * onehot, axis=1)
        target = ids_flat * capacity + position
        placed = (
            jnp.arange(experts * capacity, dtype=jnp.int32)[:, None] == target[None, :]
        ).astype(jnp.bfloat16)
        pair_rows = jnp.repeat(hidden[step_index], top_count, axis=0)
        outgoing = jnp.dot(placed, pair_rows, preferred_element_type=jnp.float32).astype(
            jnp.bfloat16
        )
        outgoing = outgoing.reshape(experts, 1, capacity, width)
        gates = route_gates(route_logits[step_index]).reshape(-1)
        weighted = placed * gates[None, :]
        return (outgoing, weighted)

    layouts_all = [layout(step_index) for step_index in range(steps_count)]
    results = []
    for step_index in range(steps_count):
        outgoing, weighted = layouts_all[step_index]
        arrived = lax.all_to_all(outgoing, "expert", split_axis=0, concat_axis=1, tiled=True)
        outputs = apply_expert_block(
            arrived.reshape(-1, width), merged_gate, merged_up, combined_down_weight
        )
        outputs = outputs.reshape(arrived.shape)
        returned = lax.all_to_all(outputs, "expert", split_axis=1, concat_axis=0, tiled=True)
        flat_back = returned.reshape(experts * capacity, width)
        pair_out = jnp.einsum("cp,cd->pd", weighted, flat_back, preferred_element_type=jnp.float32)
        results.append(
            pair_out.reshape(row_count, top_count, width).sum(axis=1).astype(jnp.bfloat16)
        )
    return jnp.stack(results, axis=0)


def shards(hidden, route_ids, route_logits, placement, factors, w_gate, w_up, down_weight):
    rows, top = route_ids.shape[1:]
    width, units = w_gate.shape[1:]
    owners = lax.axis_size("expert")
    rank = factors.shape[1] * owners // (3 * (width + units))
    dense = row_capacity(rows, top, placement.shape[0]) == rows
    dense = dense and split_axis(owners)[1:] == (2, 2)
    outer = split_axis(owners)[0]
    dense = dense and outer > 1 and outer & (outer - 1) == 0 and split_axis(owners)[1] > 1
    dense = dense and 2 * rank == LANES and width % 256 == 0 and units % 256 == 0
    dense = dense and factors.shape[1] % (8 * LANES) == 0
    return (dense_shards if dense else sparse_shards)(
        hidden, route_ids, route_logits, placement, factors, w_gate, w_up, down_weight
    )


def solution(mesh):
    placed = (
        P(None, ("group", "expert"), None),
        P(None, ("group", "expert"), None),
        P(None, ("group", "expert"), None),
        P(),
        P(None, "expert"),
        P("expert", None, None),
        P("expert", None, None),
        P("expert", None, None),
    )
    return jax.shard_map(
        shards,
        mesh=mesh,
        in_specs=placed,
        out_specs=P(None, ("group", "expert"), None),
        check_vma=False,
    )
```

```python
import functools

import jax
import jax.numpy as jnp
from jax import lax
from jax.experimental import pallas as pl
from jax.experimental.pallas import tpu as pltpu
from jax.sharding import PartitionSpec as P

adapter_scale = 2.0
LANES = 128
GRANT = 16 << 20
EXPERT_GRANT = 30 << 20
WHOLE_GRANT = 60 << 20
MUCH = pl.CostEstimate(flops=1 << 33, bytes_accessed=1, transcendentals=0)
LITTLE = pl.CostEstimate(flops=1, bytes_accessed=1, transcendentals=0)


def route_gates(logits):
    highest = jnp.max(logits, axis=-1, keepdims=True)
    router_scores = jnp.exp(logits - highest)
    return (router_scores / jnp.sum(router_scores, axis=-1, keepdims=True)).astype(jnp.bfloat16)


def split_axis(n):
    cores = 2 if n % 2 == 0 else 1
    chips = n // cores
    middle = 1
    while chips % (2 * middle) == 0 and 4 * middle * middle <= chips:
        middle *= 2
    return chips // middle, middle, cores


def swap(x, n, stride, k):
    return lax.ppermute(x, "expert", [(i, i ^ (k * stride)) for i in range(n)])


def scatter_along(total, n, stride, size, received=None):
    count = total.shape[0] // size
    received = [] if received is None else received
    for k in range(1, size):
        part = total[k * count : (k + 1) * count].astype(jnp.bfloat16)
        received.append(swap(part, n, stride, k))
    return sum([part.astype(jnp.float32) for part in received], total[:count])


def halve_along(total, n, stride, size, count, last):
    step = 1
    while step < size:
        total = total.reshape(-1, 2, count, total.shape[1])
        sent = total[:, 1].reshape(-1, total.shape[3]).astype(jnp.bfloat16)
        kept = total[:, 0].reshape(-1, total.shape[3])
        sent = swap(sent, n, stride, step)
        if 2 * step == size:
            sent = lax.optimization_barrier((sent, last))[0]
        total = kept + sent.astype(jnp.float32)
        step *= 2
    return total


def dot(a, b):
    return jnp.dot(a, b, preferred_element_type=jnp.float32)


def payload_kernel(hidden_ref, ids_ref, logits_ref, out_ref, turned_ref):
    steps, top, rows = ids_ref.shape
    width = hidden_ref.shape[2]
    turned_ref[...] = jnp.zeros_like(turned_ref)
    for s in range(steps):
        logits, ids = logits_ref[s], ids_ref[s]
        scores = jnp.exp(logits - jnp.max(logits, axis=0, keepdims=True))
        gates = scores / jnp.sum(scores, axis=0, keepdims=True)
        expert = lax.broadcasted_iota(jnp.int32, (turned_ref.shape[0], rows), 0)
        dense = jnp.zeros(expert.shape, jnp.float32)
        for k in range(top):
            dense += jnp.where(ids[k : k + 1, :] == expert, gates[k : k + 1, :], 0.0)
        turned_ref[:, s * rows : (s + 1) * rows] = dense
    dense = turned_ref[...].T.astype(jnp.bfloat16)
    for s in range(steps):
        out_ref[s * rows : (s + 1) * rows, :width] = hidden_ref[s]
    out_ref[:, width:] = dense[: steps * rows]


def make_payload(hidden, route_ids, route_logits, experts):
    steps, rows, width = hidden.shape
    padded = -(-experts // LANES) * LANES
    return pl.pallas_call(
        payload_kernel,
        out_shape=jax.ShapeDtypeStruct((steps * rows, width + padded), jnp.bfloat16),
        scratch_shapes=[pltpu.VMEM((padded, -(-steps * rows // LANES) * LANES), jnp.float32)],
        compiler_params=pltpu.CompilerParams(vmem_limit_bytes=WHOLE_GRANT),
        cost_estimate=LITTLE,
        name="payload",
    )(hidden, jnp.swapaxes(route_ids, 1, 2), jnp.swapaxes(route_logits, 1, 2))


def order_kernel(place_ref, placement_ref, factors_ref, *refs):
    out_refs, wide_ref, slot_ref = refs[:-2], refs[-2], refs[-1]
    slots = factors_ref.shape[0]
    middle, outer, length, lanes = out_refs[0].shape

    def cut(t, carry):
        start = pl.multiple_of(t * lanes, lanes)
        tile = factors_ref[:, pl.ds(start, lanes)].astype(jnp.float32)
        wide_ref[pl.ds(t, slots, stride=length), :] = tile
        return carry

    lax.fori_loop(0, length, cut, 0, unroll=8)
    for s in range(slots):
        slot_ref[placement_ref[s]] = s
    for core, out_ref in enumerate(out_refs):
        for r in range(middle):
            for q in range(outer):
                slot = slot_ref[place_ref[0] ^ ((q * middle + r) * len(out_refs) + core)]
                rows = wide_ref[pl.ds(pl.multiple_of(slot * length, 8), length), :]
                out_ref[r, q] = rows.astype(jnp.bfloat16)


def order_factors(place, placement, factors, outer, middle, cores):
    slots, entries = factors.shape
    length = entries // LANES
    shape = jax.ShapeDtypeStruct((middle, outer, length, LANES), jnp.bfloat16)
    return pl.pallas_call(
        order_kernel,
        out_shape=[shape] * cores,
        in_specs=[
            pl.BlockSpec(memory_space=pltpu.SMEM),
            pl.BlockSpec(memory_space=pltpu.SMEM),
            pl.BlockSpec(memory_space=pltpu.VMEM),
        ],
        scratch_shapes=[
            pltpu.VMEM((slots * length, LANES), jnp.float32),
            pltpu.SMEM((slots,), jnp.int32),
        ],
        compiler_params=pltpu.CompilerParams(vmem_limit_bytes=WHOLE_GRANT),
        cost_estimate=MUCH,
        name="order_factors",
    )(place, placement, factors)


def relayout_kernel(place_ref, *refs):
    parts, refs = refs[:-7], refs[-7:]
    a_gu_ref, gate_b_ref, up_b_ref, down_a_ref, down_b_ref, flat_ref, wide_ref = refs
    width, units = a_gu_ref.shape[0], gate_b_ref.shape[1]
    rank = gate_b_ref.shape[0]
    near, length, _ = parts[0].shape
    for q, part in enumerate(parts):
        for j in range(near):
            start = pl.multiple_of((place_ref[0] ^ (near * q + j)) * length, 8)
            flat_ref[pl.ds(start, length), :] = part[j].astype(jnp.float32)

    n_wide, n_unit = width // 2, units // 2
    at_ub = 2 * n_wide + n_unit
    at_da = 2 * n_wide + 2 * n_unit
    chunk = 128
    left = lax.broadcasted_iota(jnp.int32, (chunk, LANES), 1) < rank

    def load(start):
        return flat_ref[pl.ds(pl.multiple_of(start, 128), chunk), :]

    def gate_up(i, carry):
        g, u = load(i * chunk), load(n_wide + n_unit + i * chunk)
        at = 2 * i * chunk
        wide_ref[pl.ds(at, chunk, stride=2), :] = jnp.where(left, g, pltpu.roll(u, rank, 1))
        wide_ref[pl.ds(at + 1, chunk, stride=2), :] = jnp.where(left, pltpu.roll(g, rank, 1), u)
        both = wide_ref[pl.ds(pl.multiple_of(at, 128), 2 * chunk), :]
        a_gu_ref[pl.ds(pl.multiple_of(at, 128), 2 * chunk), :] = both.astype(jnp.bfloat16)
        return carry

    lax.fori_loop(0, n_wide // chunk, gate_up, 0, unroll=2)
    for i in range(n_unit // chunk):
        d = load(at_da + i * chunk)
        at = 2 * i * chunk
        wide_ref[pl.ds(at, chunk, stride=2), :] = jnp.where(left, d, 0.0)
        wide_ref[pl.ds(at + 1, chunk, stride=2), :] = jnp.where(left, pltpu.roll(d, rank, 1), 0.0)
        down_a_ref[at : at + 2 * chunk, :] = wide_ref[at : at + 2 * chunk, :].astype(jnp.bfloat16)
    for start, b_ref in (
        (n_wide, gate_b_ref),
        (at_ub, up_b_ref),
        (at_da + n_unit, down_b_ref),
    ):
        tiles = b_ref.shape[1] // LANES
        for j in range(tiles):
            row = flat_ref[pl.ds(start + j, rank, stride=tiles), :]
            b_ref[:, j * LANES : (j + 1) * LANES] = row.astype(jnp.bfloat16)


def relayout_factors(place, parts, width, units, rank, n):
    shapes = [(width, 2 * rank), (rank, units), (rank, units), (units, 2 * rank), (rank, width)]
    length = parts[0].shape[1]
    return pl.pallas_call(
        relayout_kernel,
        out_shape=[jax.ShapeDtypeStruct(shape, jnp.bfloat16) for shape in shapes],
        in_specs=[pl.BlockSpec(memory_space=pltpu.SMEM)]
        + [pl.BlockSpec(memory_space=pltpu.VMEM)] * len(parts),
        scratch_shapes=[
            pltpu.VMEM((n * length, LANES), jnp.float32),
            pltpu.VMEM((width, LANES), jnp.float32),
        ],
        compiler_params=pltpu.CompilerParams(vmem_limit_bytes=GRANT),
        cost_estimate=LITTLE,
        name="relayout_factors",
    )(place, *parts)


def base_kernel(x_ref, other_ref, w_gate_ref, w_up_ref, gate_ref, up_ref):
    width, rows = w_gate_ref.shape[0], x_ref.shape[0]
    for i, piece in enumerate((x_ref, other_ref)):
        at = slice(i * rows, (i + 1) * rows)
        gate_ref[at, :] = dot(piece[:, :width], w_gate_ref[...])
        up_ref[at, :] = dot(piece[:, :width], w_up_ref[...])


def base_products(pieces, w_gate, w_up):
    total = sum(p.shape[0] for p in pieces)
    out = jax.ShapeDtypeStruct((total, w_gate.shape[1]), jnp.float32)
    return pl.pallas_call(
        base_kernel,
        out_shape=[out, out],
        in_specs=[pl.BlockSpec(memory_space=pltpu.VMEM)] * 4,
        compiler_params=pltpu.CompilerParams(vmem_limit_bytes=EXPERT_GRANT),
        cost_estimate=LITTLE,
        name="base_products",
    )(*pieces, w_gate, w_up)


def finish_kernel(count, first, rows, place_ref, *refs):
    pieces, refs = refs[:count], refs[count:]
    base, refs = refs[:count], refs[count:]
    a_gu_ref, gate_b_ref, up_b_ref, down_a_ref, down_b_ref, w_down_ref = refs[:6]
    kept_ref, sent_ref, x_ref, inner_ref = refs[6:]
    width = w_down_ref.shape[1]
    rank = gate_b_ref.shape[0]
    span = pieces[0].shape[0]
    own = kept_ref.shape[0]
    for i, piece in enumerate(pieces):
        x_ref[i * rows : (i + 1) * rows, :] = piece[first : first + rows, :]

    def of_step(refs):
        at = [first, span + first]
        return jnp.concatenate([ref[i : i + rows, :] for i in at for ref in refs])

    low = (adapter_scale * dot(x_ref[:, :width], a_gu_ref[...])).astype(jnp.bfloat16)
    gates = x_ref[:, width:].astype(jnp.float32)
    lane = lax.broadcasted_iota(jnp.int32, gates.shape, 1)
    mine = jnp.sum(jnp.where(lane == place_ref[0], gates, 0.0), axis=1, keepdims=True)
    g = of_step(base[::2]) + dot(low[:, :rank], gate_b_ref[...])
    u = of_step(base[1::2]) + dot(low[:, rank:], up_b_ref[...])
    half = 0.5 * g
    inner_ref[...] = ((half + half * jnp.tanh(half)) * u).astype(jnp.bfloat16)
    low = (adapter_scale * dot(inner_ref[...], down_a_ref[...])).astype(jnp.bfloat16)[:, :rank]
    out = (dot(inner_ref[...], w_down_ref[...]) + dot(low, down_b_ref[...])) * mine
    kept_ref[...] = out[:own]
    sent_ref[...] = out[own:].astype(jnp.bfloat16)


def finish_step(place, pieces, base, first, rows, low_rank, w_down):
    units, width = w_down.shape
    total = rows * len(pieces)
    own = total // 2
    operands = [*pieces, *base, *low_rank, w_down]
    return pl.pallas_call(
        functools.partial(finish_kernel, len(pieces), first, rows),
        out_shape=[
            jax.ShapeDtypeStruct((own, width), jnp.float32),
            jax.ShapeDtypeStruct((own, width), jnp.bfloat16),
        ],
        in_specs=[pl.BlockSpec(memory_space=pltpu.SMEM)]
        + [pl.BlockSpec(memory_space=pltpu.VMEM)] * len(operands),
        scratch_shapes=[
            pltpu.VMEM((total, pieces[0].shape[1]), jnp.bfloat16),
            pltpu.VMEM((total, units), jnp.bfloat16),
        ],
        compiler_params=pltpu.CompilerParams(vmem_limit_bytes=EXPERT_GRANT),
        cost_estimate=MUCH,
        name="finish_step",
    )(place, *operands)


def dense_shards(
    hidden, route_ids, route_logits, placement, factors, w_gate, w_up, down_weight
):
    owners = lax.axis_size("expert")
    experts = placement.shape[0]
    steps, rows, width = hidden.shape
    units = w_gate.shape[2]
    rank = factors.shape[1] * owners // (3 * (width + units))
    outer, middle, cores = split_axis(owners)
    along_outer, along_middle = (middle * cores, outer), (cores, middle)
    place = lax.axis_index("expert").astype(jnp.int32).reshape(1)

    def along(x, stride, size):
        return [x] + [swap(x, owners, stride, k) for k in range(1, size)]

    rows_in = make_payload(hidden, route_ids, route_logits, experts)
    rows_in, factors = lax.optimization_barrier((rows_in, factors))
    column = [p.reshape(steps, rows, -1) for p in along(rows_in, *along_outer)]
    column = jnp.stack(column, axis=1).reshape(steps * outer * rows, -1)
    kept, sent = order_factors(place, placement, factors, outer, middle, cores)
    blocks = jnp.stack([kept, swap(sent, owners, 1, 1)])
    blocks = [blocks[:, 0], swap(blocks[:, 1], owners, cores, 1)]
    blocks = [jnp.concatenate([block[:, q] for block in blocks]) for q in range(outer)]
    column, blocks = lax.optimization_barrier((column, blocks))
    here = blocks[:1] + [
        swap(block, owners, middle * cores, q) for q, block in enumerate(blocks) if q
    ]
    sheet = along(column, *along_middle)
    others = [swap(column, owners, 1, 1)]
    weights = (w_gate[0], w_up[0])
    base = [base_products([column, others[0]], *weights)]
    here, sheet[1:], base = lax.optimization_barrier((here, sheet[1:], base))
    for r in range(1, middle):
        others.append(swap(sheet[r], owners, 1, 1))
        base.append(base_products([sheet[r], others[r]], *weights))
    low_rank = relayout_factors(place, here, width, units, rank, owners)
    pieces, base = sheet + others, [b for pair in base for b in pair]
    span = outer * rows

    def after(x, other):
        return lax.optimization_barrier((x, other))[0]

    summed, across = [], []
    for s in range(steps):
        if s >= 2:
            pieces = lax.optimization_barrier((pieces, summed[s - 2]))[0]
        kept, sent = finish_step(
            place, pieces, base, s * span, span, low_rank, down_weight[0]
        )
        if s == 2:
            kept = after(kept, across[0])
        summed.append(kept + swap(sent, owners, 1, 1).astype(jnp.float32))
        across.append(scatter_along(summed[s], owners, *along_middle))
    ends = []
    final = scatter_along(across[-1], owners, *along_outer, ends)
    others = [halve_along(total, owners, *along_outer, rows, ends[0]) for total in across[:-1]]
    return jnp.stack(others + [final]).astype(jnp.bfloat16)


def row_capacity(rows, top, experts):
    return min(rows, 3 * max(1, rows * top // experts))


def unpack_factors(flat_factors, width, hidden_units, rank_size):
    layouts = [
        (width, rank_size),
        (rank_size, hidden_units),
        (width, rank_size),
        (rank_size, hidden_units),
        (hidden_units, rank_size),
        (rank_size, width),
    ]
    offset = 0
    segments = []
    for leading, trailing in layouts:
        segments.append(
            flat_factors[offset : offset + leading * trailing].reshape(leading, trailing)
        )
        offset = offset + leading * trailing
    return segments


def merge_weight(loaded_weights, factor_a, factor_b):
    adapter_delta = jnp.dot(factor_a, factor_b, preferred_element_type=jnp.float32)
    return (loaded_weights.astype(jnp.float32) + adapter_scale * adapter_delta).astype(jnp.bfloat16)


def apply_expert_block(inputs, merged_gate, merged_up, combined_down_weight):
    gate_part = jnp.dot(inputs, merged_gate, preferred_element_type=jnp.float32)
    up_part = jnp.dot(inputs, merged_up, preferred_element_type=jnp.float32)
    inner = (jax.nn.silu(gate_part) * up_part).astype(jnp.bfloat16)
    return jnp.dot(inner, combined_down_weight, preferred_element_type=jnp.float32).astype(
        jnp.bfloat16
    )


def sparse_shards(hidden, route_ids, route_logits, placement, factors, w_gate, w_up, down_weight):
    owners = lax.axis_size("expert")
    experts = placement.shape[0]
    steps_count, row_count, width = hidden.shape
    top_count = route_ids.shape[2]
    hidden_units = w_gate.shape[2]
    rank_size = factors.shape[1] * owners // (3 * (width + hidden_units))
    capacity = row_capacity(row_count, top_count, experts)
    slot_of = (
        jnp.zeros((experts,), jnp.int32).at[placement].set(jnp.arange(experts, dtype=jnp.int32))
    )
    ordered = jnp.take(factors, slot_of, axis=0)
    received = lax.all_to_all(ordered, "expert", split_axis=0, concat_axis=1, tiled=True)
    segments = unpack_factors(received[0], width, hidden_units, rank_size)
    merged_gate = merge_weight(w_gate[0], segments[0], segments[1])
    merged_up = merge_weight(w_up[0], segments[2], segments[3])
    combined_down_weight = merge_weight(down_weight[0], segments[4], segments[5])

    def layout(step_index):
        ids_flat = route_ids[step_index].reshape(-1)
        onehot = (ids_flat[:, None] == jnp.arange(experts, dtype=jnp.int32)[None, :]).astype(
            jnp.int32
        )
        position = jnp.sum((jnp.cumsum(onehot, axis=0) - 1) * onehot, axis=1)
        target = ids_flat * capacity + position
        placed = (
            jnp.arange(experts * capacity, dtype=jnp.int32)[:, None] == target[None, :]
        ).astype(jnp.bfloat16)
        pair_rows = jnp.repeat(hidden[step_index], top_count, axis=0)
        outgoing = jnp.dot(placed, pair_rows, preferred_element_type=jnp.float32).astype(
            jnp.bfloat16
        )
        outgoing = outgoing.reshape(experts, 1, capacity, width)
        gates = route_gates(route_logits[step_index]).reshape(-1)
        weighted = placed * gates[None, :]
        return (outgoing, weighted)

    layouts_all = [layout(step_index) for step_index in range(steps_count)]
    results = []
    for step_index in range(steps_count):
        outgoing, weighted = layouts_all[step_index]
        arrived = lax.all_to_all(outgoing, "expert", split_axis=0, concat_axis=1, tiled=True)
        outputs = apply_expert_block(
            arrived.reshape(-1, width), merged_gate, merged_up, combined_down_weight
        )
        outputs = outputs.reshape(arrived.shape)
        returned = lax.all_to_all(outputs, "expert", split_axis=1, concat_axis=0, tiled=True)
        flat_back = returned.reshape(experts * capacity, width)
        pair_out = jnp.einsum("cp,cd->pd", weighted, flat_back, preferred_element_type=jnp.float32)
        results.append(
            pair_out.reshape(row_count, top_count, width).sum(axis=1).astype(jnp.bfloat16)
        )
    return jnp.stack(results, axis=0)


def shards(hidden, route_ids, route_logits, placement, factors, w_gate, w_up, down_weight):
    rows, top = route_ids.shape[1:]
    width, units = w_gate.shape[1:]
    owners = lax.axis_size("expert")
    rank = factors.shape[1] * owners // (3 * (width + units))
    dense = row_capacity(rows, top, placement.shape[0]) == rows
    dense = dense and split_axis(owners)[1:] == (2, 2)
    outer = split_axis(owners)[0]
    dense = dense and outer > 1 and outer & (outer - 1) == 0 and split_axis(owners)[1] > 1
    dense = dense and 2 * rank == LANES and width % 256 == 0 and units % 256 == 0
    dense = dense and factors.shape[1] % (8 * LANES) == 0
    return (dense_shards if dense else sparse_shards)(
        hidden, route_ids, route_logits, placement, factors, w_gate, w_up, down_weight
    )


def solution(mesh):
    placed = (
        P(None, ("group", "expert"), None),
        P(None, ("group", "expert"), None),
        P(None, ("group", "expert"), None),
        P(),
        P(None, "expert"),
        P("expert", None, None),
        P("expert", None, None),
        P("expert", None, None),
    )
    return jax.shard_map(
        shards,
        mesh=mesh,
        in_specs=placed,
        out_specs=P(None, ("group", "expert"), None),
        check_vma=False,
    )
```

```python
import functools

import jax
import jax.numpy as jnp
from jax import lax
from jax.experimental import pallas as pl
from jax.experimental.pallas import tpu as pltpu
from jax.sharding import PartitionSpec as P

adapter_scale = 2.0
LANES = 128
GRANT = 16 << 20
EXPERT_GRANT = 30 << 20
WHOLE_GRANT = 60 << 20
MUCH = pl.CostEstimate(flops=1 << 33, bytes_accessed=1, transcendentals=0)
LITTLE = pl.CostEstimate(flops=1, bytes_accessed=1, transcendentals=0)


def route_gates(logits):
    highest = jnp.max(logits, axis=-1, keepdims=True)
    router_scores = jnp.exp(logits - highest)
    return (router_scores / jnp.sum(router_scores, axis=-1, keepdims=True)).astype(jnp.bfloat16)


def split_axis(n):
    cores = 2 if n % 2 == 0 else 1
    chips = n // cores
    middle = 1
    while chips % (2 * middle) == 0 and 4 * middle * middle <= chips:
        middle *= 2
    return chips // middle, middle, cores


def swap(x, n, stride, k):
    return lax.ppermute(x, "expert", [(i, i ^ (k * stride)) for i in range(n)])


def scatter_along(total, n, stride, size):
    count = total.shape[0] // size
    received = []
    for k in range(1, size):
        part = total[k * count : (k + 1) * count].astype(jnp.bfloat16)
        received.append(swap(part, n, stride, k))
    return sum([part.astype(jnp.float32) for part in received], total[:count])


def dot(a, b):
    return jnp.dot(a, b, preferred_element_type=jnp.float32)


def payload_kernel(hidden_ref, ids_ref, logits_ref, out_ref, turned_ref):
    steps, top, rows = ids_ref.shape
    width = hidden_ref.shape[2]
    turned_ref[...] = jnp.zeros_like(turned_ref)
    for s in range(steps):
        logits, ids = logits_ref[s], ids_ref[s]
        scores = jnp.exp(logits - jnp.max(logits, axis=0, keepdims=True))
        gates = scores / jnp.sum(scores, axis=0, keepdims=True)
        expert = lax.broadcasted_iota(jnp.int32, (turned_ref.shape[0], rows), 0)
        dense = jnp.zeros(expert.shape, jnp.float32)
        for k in range(top):
            dense += jnp.where(ids[k : k + 1, :] == expert, gates[k : k + 1, :], 0.0)
        turned_ref[:, s * rows : (s + 1) * rows] = dense
    dense = turned_ref[...].T.astype(jnp.bfloat16)
    for s in range(steps):
        out_ref[s * rows : (s + 1) * rows, :width] = hidden_ref[s]
    out_ref[:, width:] = dense[: steps * rows]


def make_payload(hidden, route_ids, route_logits, experts):
    steps, rows, width = hidden.shape
    padded = -(-experts // LANES) * LANES
    return pl.pallas_call(
        payload_kernel,
        out_shape=jax.ShapeDtypeStruct((steps * rows, width + padded), jnp.bfloat16),
        scratch_shapes=[pltpu.VMEM((padded, -(-steps * rows // LANES) * LANES), jnp.float32)],
        compiler_params=pltpu.CompilerParams(vmem_limit_bytes=WHOLE_GRANT),
        cost_estimate=LITTLE,
        name="payload",
    )(hidden, jnp.swapaxes(route_ids, 1, 2), jnp.swapaxes(route_logits, 1, 2))


def order_kernel(place_ref, placement_ref, factors_ref, *refs):
    out_refs, wide_ref, slot_ref = refs[:-2], refs[-2], refs[-1]
    slots = factors_ref.shape[0]
    middle, outer, length, lanes = out_refs[0].shape

    def cut(t, carry):
        start = pl.multiple_of(t * lanes, lanes)
        tile = factors_ref[:, pl.ds(start, lanes)].astype(jnp.float32)
        wide_ref[pl.ds(t, slots, stride=length), :] = tile
        return carry

    lax.fori_loop(0, length, cut, 0, unroll=8)
    for s in range(slots):
        slot_ref[placement_ref[s]] = s
    for core, out_ref in enumerate(out_refs):
        for r in range(middle):
            for q in range(outer):
                slot = slot_ref[place_ref[0] ^ ((q * middle + r) * len(out_refs) + core)]
                rows = wide_ref[pl.ds(pl.multiple_of(slot * length, 8), length), :]
                out_ref[r, q] = rows.astype(jnp.bfloat16)


def order_factors(place, placement, factors, outer, middle, cores):
    slots, entries = factors.shape
    length = entries // LANES
    shape = jax.ShapeDtypeStruct((middle, outer, length, LANES), jnp.bfloat16)
    return pl.pallas_call(
        order_kernel,
        out_shape=[shape] * cores,
        in_specs=[
            pl.BlockSpec(memory_space=pltpu.SMEM),
            pl.BlockSpec(memory_space=pltpu.SMEM),
            pl.BlockSpec(memory_space=pltpu.VMEM),
        ],
        scratch_shapes=[
            pltpu.VMEM((slots * length, LANES), jnp.float32),
            pltpu.SMEM((slots,), jnp.int32),
        ],
        compiler_params=pltpu.CompilerParams(vmem_limit_bytes=WHOLE_GRANT),
        cost_estimate=MUCH,
        name="order_factors",
    )(place, placement, factors)


def relayout_kernel(place_ref, *refs):
    parts, refs = refs[:-7], refs[-7:]
    a_gu_ref, gate_b_ref, up_b_ref, down_a_ref, down_b_ref, flat_ref, wide_ref = refs
    width, units = a_gu_ref.shape[0], gate_b_ref.shape[1]
    rank = gate_b_ref.shape[0]
    near, length, _ = parts[0].shape
    for q, part in enumerate(parts):
        for j in range(near):
            start = pl.multiple_of((place_ref[0] ^ (near * q + j)) * length, 8)
            flat_ref[pl.ds(start, length), :] = part[j].astype(jnp.float32)

    n_wide, n_unit = width // 2, units // 2
    at_ub = 2 * n_wide + n_unit
    at_da = 2 * n_wide + 2 * n_unit
    chunk = 128
    left = lax.broadcasted_iota(jnp.int32, (chunk, LANES), 1) < rank

    def load(start):
        return flat_ref[pl.ds(pl.multiple_of(start, 128), chunk), :]

    def gate_up(i, carry):
        g, u = load(i * chunk), load(n_wide + n_unit + i * chunk)
        at = 2 * i * chunk
        wide_ref[pl.ds(at, chunk, stride=2), :] = jnp.where(left, g, pltpu.roll(u, rank, 1))
        wide_ref[pl.ds(at + 1, chunk, stride=2), :] = jnp.where(left, pltpu.roll(g, rank, 1), u)
        both = wide_ref[pl.ds(pl.multiple_of(at, 128), 2 * chunk), :]
        a_gu_ref[pl.ds(pl.multiple_of(at, 128), 2 * chunk), :] = both.astype(jnp.bfloat16)
        return carry

    lax.fori_loop(0, n_wide // chunk, gate_up, 0, unroll=2)
    for i in range(n_unit // chunk):
        d = load(at_da + i * chunk)
        at = 2 * i * chunk
        wide_ref[pl.ds(at, chunk, stride=2), :] = jnp.where(left, d, 0.0)
        wide_ref[pl.ds(at + 1, chunk, stride=2), :] = jnp.where(left, pltpu.roll(d, rank, 1), 0.0)
        down_a_ref[at : at + 2 * chunk, :] = wide_ref[at : at + 2 * chunk, :].astype(jnp.bfloat16)
    for start, b_ref in (
        (n_wide, gate_b_ref),
        (at_ub, up_b_ref),
        (at_da + n_unit, down_b_ref),
    ):
        tiles = b_ref.shape[1] // LANES
        for j in range(tiles):
            row = flat_ref[pl.ds(start + j, rank, stride=tiles), :]
            b_ref[:, j * LANES : (j + 1) * LANES] = row.astype(jnp.bfloat16)


def relayout_factors(place, parts, width, units, rank, n):
    shapes = [(width, 2 * rank), (rank, units), (rank, units), (units, 2 * rank), (rank, width)]
    length = parts[0].shape[1]
    return pl.pallas_call(
        relayout_kernel,
        out_shape=[jax.ShapeDtypeStruct(shape, jnp.bfloat16) for shape in shapes],
        in_specs=[pl.BlockSpec(memory_space=pltpu.SMEM)]
        + [pl.BlockSpec(memory_space=pltpu.VMEM)] * len(parts),
        scratch_shapes=[
            pltpu.VMEM((n * length, LANES), jnp.float32),
            pltpu.VMEM((width, LANES), jnp.float32),
        ],
        compiler_params=pltpu.CompilerParams(vmem_limit_bytes=GRANT),
        cost_estimate=LITTLE,
        name="relayout_factors",
    )(place, *parts)


def base_kernel(x_ref, other_ref, w_gate_ref, w_up_ref, gate_ref, up_ref):
    width, rows = w_gate_ref.shape[0], x_ref.shape[0]
    for i, piece in enumerate((x_ref, other_ref)):
        at = slice(i * rows, (i + 1) * rows)
        gate_ref[at, :] = dot(piece[:, :width], w_gate_ref[...])
        up_ref[at, :] = dot(piece[:, :width], w_up_ref[...])


def base_products(pieces, w_gate, w_up):
    total = sum(p.shape[0] for p in pieces)
    out = jax.ShapeDtypeStruct((total, w_gate.shape[1]), jnp.float32)
    return pl.pallas_call(
        base_kernel,
        out_shape=[out, out],
        in_specs=[pl.BlockSpec(memory_space=pltpu.VMEM)] * 4,
        compiler_params=pltpu.CompilerParams(vmem_limit_bytes=EXPERT_GRANT),
        cost_estimate=LITTLE,
        name="base_products",
    )(*pieces, w_gate, w_up)


def finish_kernel(count, first, rows, place_ref, *refs):
    pieces, refs = refs[:count], refs[count:]
    base, refs = refs[:count], refs[count:]
    a_gu_ref, gate_b_ref, up_b_ref, down_a_ref, down_b_ref, w_down_ref = refs[:6]
    kept_ref, sent_ref, x_ref, inner_ref = refs[6:]
    width = w_down_ref.shape[1]
    rank = gate_b_ref.shape[0]
    span = pieces[0].shape[0]
    own = kept_ref.shape[0]
    for i, piece in enumerate(pieces):
        x_ref[i * rows : (i + 1) * rows, :] = piece[first : first + rows, :]

    def of_step(refs):
        at = [first, span + first]
        return jnp.concatenate([ref[i : i + rows, :] for i in at for ref in refs])

    low = (adapter_scale * dot(x_ref[:, :width], a_gu_ref[...])).astype(jnp.bfloat16)
    gates = x_ref[:, width:].astype(jnp.float32)
    lane = lax.broadcasted_iota(jnp.int32, gates.shape, 1)
    mine = jnp.sum(jnp.where(lane == place_ref[0], gates, 0.0), axis=1, keepdims=True)
    g = of_step(base[::2]) + dot(low[:, :rank], gate_b_ref[...])
    u = of_step(base[1::2]) + dot(low[:, rank:], up_b_ref[...])
    half = 0.5 * g
    inner_ref[...] = ((half + half * jnp.tanh(half)) * u).astype(jnp.bfloat16)
    low = (adapter_scale * dot(inner_ref[...], down_a_ref[...])).astype(jnp.bfloat16)[:, :rank]
    out = (dot(inner_ref[...], w_down_ref[...]) + dot(low, down_b_ref[...])) * mine
    kept_ref[...] = out[:own]
    sent_ref[...] = out[own:].astype(jnp.bfloat16)


def finish_step(place, pieces, base, first, rows, low_rank, w_down):
    units, width = w_down.shape
    total = rows * len(pieces)
    own = total // 2
    operands = [*pieces, *base, *low_rank, w_down]
    return pl.pallas_call(
        functools.partial(finish_kernel, len(pieces), first, rows),
        out_shape=[
            jax.ShapeDtypeStruct((own, width), jnp.float32),
            jax.ShapeDtypeStruct((own, width), jnp.bfloat16),
        ],
        in_specs=[pl.BlockSpec(memory_space=pltpu.SMEM)]
        + [pl.BlockSpec(memory_space=pltpu.VMEM)] * len(operands),
        scratch_shapes=[
            pltpu.VMEM((total, pieces[0].shape[1]), jnp.bfloat16),
            pltpu.VMEM((total, units), jnp.bfloat16),
        ],
        compiler_params=pltpu.CompilerParams(vmem_limit_bytes=EXPERT_GRANT),
        cost_estimate=MUCH,
        name="finish_step",
    )(place, *operands)


def dense_shards(
    hidden, route_ids, route_logits, placement, factors, w_gate, w_up, down_weight
):
    owners = lax.axis_size("expert")
    experts = placement.shape[0]
    steps, rows, width = hidden.shape
    units = w_gate.shape[2]
    rank = factors.shape[1] * owners // (3 * (width + units))
    outer, middle, cores = split_axis(owners)
    along_outer, along_middle = (middle * cores, outer), (cores, middle)
    place = lax.axis_index("expert").astype(jnp.int32).reshape(1)

    def along(x, stride, size):
        return [x] + [swap(x, owners, stride, k) for k in range(1, size)]

    rows_in = make_payload(hidden, route_ids, route_logits, experts)
    rows_in, factors = lax.optimization_barrier((rows_in, factors))
    column = [p.reshape(steps, rows, -1) for p in along(rows_in, *along_outer)]
    column = jnp.stack(column, axis=1).reshape(steps * outer * rows, -1)
    kept, sent = order_factors(place, placement, factors, outer, middle, cores)
    blocks = jnp.stack([kept, swap(sent, owners, 1, 1)])
    blocks = [blocks[:, 0], swap(blocks[:, 1], owners, cores, 1)]
    blocks = [jnp.concatenate([block[:, q] for block in blocks]) for q in range(outer)]
    column, blocks = lax.optimization_barrier((column, blocks))
    here = blocks[:1] + [
        swap(block, owners, middle * cores, q) for q, block in enumerate(blocks) if q
    ]
    sheet = along(column, *along_middle)
    others = [swap(column, owners, 1, 1)]
    weights = (w_gate[0], w_up[0])
    base = [base_products([column, others[0]], *weights)]
    here, sheet[1:], base = lax.optimization_barrier((here, sheet[1:], base))
    for r in range(1, middle):
        others.append(swap(sheet[r], owners, 1, 1))
        base.append(base_products([sheet[r], others[r]], *weights))
    low_rank = relayout_factors(place, here, width, units, rank, owners)
    pieces, base = sheet + others, [b for pair in base for b in pair]
    span = outer * rows

    summed = []
    for s in range(steps):
        kept, sent = finish_step(place, pieces, base, s * span, span, low_rank, down_weight[0])
        total = kept + swap(sent, owners, 1, 1).astype(jnp.float32)
        summed.append(total.reshape(middle, outer, rows, width))
    first = jnp.stack(summed[:-1], axis=1).reshape(-1, width)
    last = jnp.swapaxes(summed[-1], 0, 1).reshape(-1, width)
    first = scatter_along(first, owners, *along_middle)
    last = scatter_along(last, owners, *along_outer)
    first, last = lax.optimization_barrier((first, last))
    first = jnp.swapaxes(first.reshape(steps - 1, outer, rows, width), 0, 1).reshape(-1, width)
    first = scatter_along(first, owners, *along_outer)
    last = scatter_along(last, owners, *along_middle)
    return jnp.concatenate([first, last]).astype(jnp.bfloat16).reshape(hidden.shape)


def row_capacity(rows, top, experts):
    return min(rows, 3 * max(1, rows * top // experts))


def unpack_factors(flat_factors, width, hidden_units, rank_size):
    layouts = [
        (width, rank_size),
        (rank_size, hidden_units),
        (width, rank_size),
        (rank_size, hidden_units),
        (hidden_units, rank_size),
        (rank_size, width),
    ]
    offset = 0
    segments = []
    for leading, trailing in layouts:
        segments.append(
            flat_factors[offset : offset + leading * trailing].reshape(leading, trailing)
        )
        offset = offset + leading * trailing
    return segments


def merge_weight(loaded_weights, factor_a, factor_b):
    adapter_delta = jnp.dot(factor_a, factor_b, preferred_element_type=jnp.float32)
    return (loaded_weights.astype(jnp.float32) + adapter_scale * adapter_delta).astype(jnp.bfloat16)


def apply_expert_block(inputs, merged_gate, merged_up, combined_down_weight):
    gate_part = jnp.dot(inputs, merged_gate, preferred_element_type=jnp.float32)
    up_part = jnp.dot(inputs, merged_up, preferred_element_type=jnp.float32)
    inner = (jax.nn.silu(gate_part) * up_part).astype(jnp.bfloat16)
    return jnp.dot(inner, combined_down_weight, preferred_element_type=jnp.float32).astype(
        jnp.bfloat16
    )


def sparse_shards(hidden, route_ids, route_logits, placement, factors, w_gate, w_up, down_weight):
    owners = lax.axis_size("expert")
    experts = placement.shape[0]
    steps_count, row_count, width = hidden.shape
    top_count = route_ids.shape[2]
    hidden_units = w_gate.shape[2]
    rank_size = factors.shape[1] * owners // (3 * (width + hidden_units))
    capacity = row_capacity(row_count, top_count, experts)
    slot_of = (
        jnp.zeros((experts,), jnp.int32).at[placement].set(jnp.arange(experts, dtype=jnp.int32))
    )
    ordered = jnp.take(factors, slot_of, axis=0)
    received = lax.all_to_all(ordered, "expert", split_axis=0, concat_axis=1, tiled=True)
    segments = unpack_factors(received[0], width, hidden_units, rank_size)
    merged_gate = merge_weight(w_gate[0], segments[0], segments[1])
    merged_up = merge_weight(w_up[0], segments[2], segments[3])
    combined_down_weight = merge_weight(down_weight[0], segments[4], segments[5])

    def layout(step_index):
        ids_flat = route_ids[step_index].reshape(-1)
        onehot = (ids_flat[:, None] == jnp.arange(experts, dtype=jnp.int32)[None, :]).astype(
            jnp.int32
        )
        position = jnp.sum((jnp.cumsum(onehot, axis=0) - 1) * onehot, axis=1)
        target = ids_flat * capacity + position
        placed = (
            jnp.arange(experts * capacity, dtype=jnp.int32)[:, None] == target[None, :]
        ).astype(jnp.bfloat16)
        pair_rows = jnp.repeat(hidden[step_index], top_count, axis=0)
        outgoing = jnp.dot(placed, pair_rows, preferred_element_type=jnp.float32).astype(
            jnp.bfloat16
        )
        outgoing = outgoing.reshape(experts, 1, capacity, width)
        gates = route_gates(route_logits[step_index]).reshape(-1)
        weighted = placed * gates[None, :]
        return (outgoing, weighted)

    layouts_all = [layout(step_index) for step_index in range(steps_count)]
    results = []
    for step_index in range(steps_count):
        outgoing, weighted = layouts_all[step_index]
        arrived = lax.all_to_all(outgoing, "expert", split_axis=0, concat_axis=1, tiled=True)
        outputs = apply_expert_block(
            arrived.reshape(-1, width), merged_gate, merged_up, combined_down_weight
        )
        outputs = outputs.reshape(arrived.shape)
        returned = lax.all_to_all(outputs, "expert", split_axis=1, concat_axis=0, tiled=True)
        flat_back = returned.reshape(experts * capacity, width)
        pair_out = jnp.einsum("cp,cd->pd", weighted, flat_back, preferred_element_type=jnp.float32)
        results.append(
            pair_out.reshape(row_count, top_count, width).sum(axis=1).astype(jnp.bfloat16)
        )
    return jnp.stack(results, axis=0)


def shards(hidden, route_ids, route_logits, placement, factors, w_gate, w_up, down_weight):
    rows, top = route_ids.shape[1:]
    width, units = w_gate.shape[1:]
    owners = lax.axis_size("expert")
    rank = factors.shape[1] * owners // (3 * (width + units))
    dense = row_capacity(rows, top, placement.shape[0]) == rows
    dense = dense and split_axis(owners)[1:] == (2, 2)
    outer = split_axis(owners)[0]
    dense = dense and outer > 1 and outer & (outer - 1) == 0 and split_axis(owners)[1] > 1
    dense = dense and 2 * rank == LANES and width % 256 == 0 and units % 256 == 0
    dense = dense and factors.shape[1] % (8 * LANES) == 0
    return (dense_shards if dense else sparse_shards)(
        hidden, route_ids, route_logits, placement, factors, w_gate, w_up, down_weight
    )


def solution(mesh):
    placed = (
        P(None, ("group", "expert"), None),
        P(None, ("group", "expert"), None),
        P(None, ("group", "expert"), None),
        P(),
        P(None, "expert"),
        P("expert", None, None),
        P("expert", None, None),
        P("expert", None, None),
    )
    return jax.shard_map(
        shards,
        mesh=mesh,
        in_specs=placed,
        out_specs=P(None, ("group", "expert"), None),
        check_vma=False,
    )
```

```python
import functools

import jax
import jax.numpy as jnp
from jax import lax
from jax.experimental import pallas as pl
from jax.experimental.pallas import tpu as pltpu
from jax.sharding import PartitionSpec as P

adapter_scale = 2.0
LANES = 128
GRANT = 16 << 20
EXPERT_GRANT = 30 << 20
WHOLE_GRANT = 60 << 20
MUCH = pl.CostEstimate(flops=1 << 33, bytes_accessed=1, transcendentals=0)
LITTLE = pl.CostEstimate(flops=1, bytes_accessed=1, transcendentals=0)


def route_gates(logits):
    highest = jnp.max(logits, axis=-1, keepdims=True)
    router_scores = jnp.exp(logits - highest)
    return (router_scores / jnp.sum(router_scores, axis=-1, keepdims=True)).astype(jnp.bfloat16)


def split_axis(n):
    cores = 2 if n % 2 == 0 else 1
    chips = n // cores
    middle = 1
    while chips % (2 * middle) == 0 and 4 * middle * middle <= chips:
        middle *= 2
    return chips // middle, middle, cores


def swap(x, n, stride, k):
    return lax.ppermute(x, "expert", [(i, i ^ (k * stride)) for i in range(n)])


def scatter_along(total, n, stride, size):
    count = total.shape[0] // size
    received = []
    for k in range(1, size):
        part = total[k * count : (k + 1) * count].astype(jnp.bfloat16)
        received.append(swap(part, n, stride, k))
    return sum([part.astype(jnp.float32) for part in received], total[:count])


def dot(a, b):
    return jnp.dot(a, b, preferred_element_type=jnp.float32)


def payload_kernel(hidden_ref, ids_ref, logits_ref, out_ref, turned_ref):
    steps, top, rows = ids_ref.shape
    width = hidden_ref.shape[2]
    turned_ref[...] = jnp.zeros_like(turned_ref)
    for s in range(steps):
        logits, ids = logits_ref[s], ids_ref[s]
        scores = jnp.exp(logits - jnp.max(logits, axis=0, keepdims=True))
        gates = scores / jnp.sum(scores, axis=0, keepdims=True)
        expert = lax.broadcasted_iota(jnp.int32, (turned_ref.shape[0], rows), 0)
        dense = jnp.zeros(expert.shape, jnp.float32)
        for k in range(top):
            dense += jnp.where(ids[k : k + 1, :] == expert, gates[k : k + 1, :], 0.0)
        turned_ref[:, s * rows : (s + 1) * rows] = dense
    dense = turned_ref[...].T.astype(jnp.bfloat16)
    for s in range(steps):
        out_ref[s * rows : (s + 1) * rows, :width] = hidden_ref[s]
    out_ref[:, width:] = dense[: steps * rows]


def make_payload(hidden, route_ids, route_logits, experts):
    steps, rows, width = hidden.shape
    padded = -(-experts // LANES) * LANES
    return pl.pallas_call(
        payload_kernel,
        out_shape=jax.ShapeDtypeStruct((steps * rows, width + padded), jnp.bfloat16),
        scratch_shapes=[pltpu.VMEM((padded, -(-steps * rows // LANES) * LANES), jnp.float32)],
        compiler_params=pltpu.CompilerParams(vmem_limit_bytes=WHOLE_GRANT),
        cost_estimate=LITTLE,
        name="payload",
    )(hidden, jnp.swapaxes(route_ids, 1, 2), jnp.swapaxes(route_logits, 1, 2))


def order_kernel(place_ref, placement_ref, factors_ref, *refs):
    out_refs, wide_ref, slot_ref = refs[:-2], refs[-2], refs[-1]
    slots = factors_ref.shape[0]
    middle, outer, length, lanes = out_refs[0].shape

    def cut(t, carry):
        start = pl.multiple_of(t * lanes, lanes)
        tile = factors_ref[:, pl.ds(start, lanes)].astype(jnp.float32)
        wide_ref[pl.ds(t, slots, stride=length), :] = tile
        return carry

    lax.fori_loop(0, length, cut, 0, unroll=8)
    for s in range(slots):
        slot_ref[placement_ref[s]] = s
    for core, out_ref in enumerate(out_refs):
        for r in range(middle):
            for q in range(outer):
                slot = slot_ref[place_ref[0] ^ ((q * middle + r) * len(out_refs) + core)]
                rows = wide_ref[pl.ds(pl.multiple_of(slot * length, 8), length), :]
                out_ref[r, q] = rows.astype(jnp.bfloat16)


def order_factors(place, placement, factors, outer, middle, cores):
    slots, entries = factors.shape
    length = entries // LANES
    shape = jax.ShapeDtypeStruct((middle, outer, length, LANES), jnp.bfloat16)
    return pl.pallas_call(
        order_kernel,
        out_shape=[shape] * cores,
        in_specs=[
            pl.BlockSpec(memory_space=pltpu.SMEM),
            pl.BlockSpec(memory_space=pltpu.SMEM),
            pl.BlockSpec(memory_space=pltpu.VMEM),
        ],
        scratch_shapes=[
            pltpu.VMEM((slots * length, LANES), jnp.float32),
            pltpu.SMEM((slots,), jnp.int32),
        ],
        compiler_params=pltpu.CompilerParams(vmem_limit_bytes=WHOLE_GRANT),
        cost_estimate=MUCH,
        name="order_factors",
    )(place, placement, factors)


def relayout_kernel(place_ref, *refs):
    parts, refs = refs[:-7], refs[-7:]
    a_gu_ref, gate_b_ref, up_b_ref, down_a_ref, down_b_ref, flat_ref, wide_ref = refs
    width, units = a_gu_ref.shape[0], gate_b_ref.shape[1]
    rank = gate_b_ref.shape[0]
    near, length, _ = parts[0].shape
    for q, part in enumerate(parts):
        for j in range(near):
            start = pl.multiple_of((place_ref[0] ^ (near * q + j)) * length, 8)
            flat_ref[pl.ds(start, length), :] = part[j].astype(jnp.float32)

    n_wide, n_unit = width // 2, units // 2
    at_ub = 2 * n_wide + n_unit
    at_da = 2 * n_wide + 2 * n_unit
    chunk = 128
    left = lax.broadcasted_iota(jnp.int32, (chunk, LANES), 1) < rank

    def load(start):
        return flat_ref[pl.ds(pl.multiple_of(start, 128), chunk), :]

    def gate_up(i, carry):
        g, u = load(i * chunk), load(n_wide + n_unit + i * chunk)
        at = 2 * i * chunk
        wide_ref[pl.ds(at, chunk, stride=2), :] = jnp.where(left, g, pltpu.roll(u, rank, 1))
        wide_ref[pl.ds(at + 1, chunk, stride=2), :] = jnp.where(left, pltpu.roll(g, rank, 1), u)
        both = wide_ref[pl.ds(pl.multiple_of(at, 128), 2 * chunk), :]
        a_gu_ref[pl.ds(pl.multiple_of(at, 128), 2 * chunk), :] = both.astype(jnp.bfloat16)
        return carry

    lax.fori_loop(0, n_wide // chunk, gate_up, 0, unroll=2)
    for i in range(n_unit // chunk):
        d = load(at_da + i * chunk)
        at = 2 * i * chunk
        wide_ref[pl.ds(at, chunk, stride=2), :] = jnp.where(left, d, 0.0)
        wide_ref[pl.ds(at + 1, chunk, stride=2), :] = jnp.where(left, pltpu.roll(d, rank, 1), 0.0)
        down_a_ref[at : at + 2 * chunk, :] = wide_ref[at : at + 2 * chunk, :].astype(jnp.bfloat16)
    for start, b_ref in (
        (n_wide, gate_b_ref),
        (at_ub, up_b_ref),
        (at_da + n_unit, down_b_ref),
    ):
        tiles = b_ref.shape[1] // LANES
        for j in range(tiles):
            row = flat_ref[pl.ds(start + j, rank, stride=tiles), :]
            b_ref[:, j * LANES : (j + 1) * LANES] = row.astype(jnp.bfloat16)


def relayout_factors(place, parts, width, units, rank, n):
    shapes = [(width, 2 * rank), (rank, units), (rank, units), (units, 2 * rank), (rank, width)]
    length = parts[0].shape[1]
    return pl.pallas_call(
        relayout_kernel,
        out_shape=[jax.ShapeDtypeStruct(shape, jnp.bfloat16) for shape in shapes],
        in_specs=[pl.BlockSpec(memory_space=pltpu.SMEM)]
        + [pl.BlockSpec(memory_space=pltpu.VMEM)] * len(parts),
        scratch_shapes=[
            pltpu.VMEM((n * length, LANES), jnp.float32),
            pltpu.VMEM((width, LANES), jnp.float32),
        ],
        compiler_params=pltpu.CompilerParams(vmem_limit_bytes=GRANT),
        cost_estimate=LITTLE,
        name="relayout_factors",
    )(place, *parts)


def base_kernel(x_ref, other_ref, w_gate_ref, w_up_ref, gate_ref, up_ref):
    width, rows = w_gate_ref.shape[0], x_ref.shape[0]
    for i, piece in enumerate((x_ref, other_ref)):
        at = slice(i * rows, (i + 1) * rows)
        gate_ref[at, :] = dot(piece[:, :width], w_gate_ref[...])
        up_ref[at, :] = dot(piece[:, :width], w_up_ref[...])


def base_products(pieces, w_gate, w_up):
    total = sum(p.shape[0] for p in pieces)
    out = jax.ShapeDtypeStruct((total, w_gate.shape[1]), jnp.float32)
    return pl.pallas_call(
        base_kernel,
        out_shape=[out, out],
        in_specs=[pl.BlockSpec(memory_space=pltpu.VMEM)] * 4,
        compiler_params=pltpu.CompilerParams(vmem_limit_bytes=EXPERT_GRANT),
        cost_estimate=LITTLE,
        name="base_products",
    )(*pieces, w_gate, w_up)


def finish_kernel(count, first, rows, place_ref, *refs):
    pieces, refs = refs[:count], refs[count:]
    base, refs = refs[:count], refs[count:]
    a_gu_ref, gate_b_ref, up_b_ref, down_a_ref, down_b_ref, w_down_ref = refs[:6]
    kept_ref, sent_ref, x_ref, inner_ref = refs[6:]
    width = w_down_ref.shape[1]
    rank = gate_b_ref.shape[0]
    span = pieces[0].shape[0]
    own = kept_ref.shape[0]
    for i, piece in enumerate(pieces):
        x_ref[i * rows : (i + 1) * rows, :] = piece[first : first + rows, :]

    def of_step(refs):
        at = [first, span + first]
        return jnp.concatenate([ref[i : i + rows, :] for i in at for ref in refs])

    low = (adapter_scale * dot(x_ref[:, :width], a_gu_ref[...])).astype(jnp.bfloat16)
    gates = x_ref[:, width:].astype(jnp.float32)
    lane = lax.broadcasted_iota(jnp.int32, gates.shape, 1)
    mine = jnp.sum(jnp.where(lane == place_ref[0], gates, 0.0), axis=1, keepdims=True)
    g = of_step(base[::2]) + dot(low[:, :rank], gate_b_ref[...])
    u = of_step(base[1::2]) + dot(low[:, rank:], up_b_ref[...])
    half = 0.5 * g
    inner_ref[...] = ((half + half * jnp.tanh(half)) * u).astype(jnp.bfloat16)
    low = (adapter_scale * dot(inner_ref[...], down_a_ref[...])).astype(jnp.bfloat16)[:, :rank]
    out = (dot(inner_ref[...], w_down_ref[...]) + dot(low, down_b_ref[...])) * mine
    kept_ref[...] = out[:own]
    sent_ref[...] = out[own:].astype(jnp.bfloat16)


def finish_step(place, pieces, base, first, rows, low_rank, w_down):
    units, width = w_down.shape
    total = rows * len(pieces)
    own = total // 2
    operands = [*pieces, *base, *low_rank, w_down]
    return pl.pallas_call(
        functools.partial(finish_kernel, len(pieces), first, rows),
        out_shape=[
            jax.ShapeDtypeStruct((own, width), jnp.float32),
            jax.ShapeDtypeStruct((own, width), jnp.bfloat16),
        ],
        in_specs=[pl.BlockSpec(memory_space=pltpu.SMEM)]
        + [pl.BlockSpec(memory_space=pltpu.VMEM)] * len(operands),
        scratch_shapes=[
            pltpu.VMEM((total, pieces[0].shape[1]), jnp.bfloat16),
            pltpu.VMEM((total, units), jnp.bfloat16),
        ],
        compiler_params=pltpu.CompilerParams(vmem_limit_bytes=EXPERT_GRANT),
        cost_estimate=MUCH,
        name="finish_step",
    )(place, *operands)


def dense_shards(
    hidden, route_ids, route_logits, placement, factors, w_gate, w_up, down_weight
):
    owners = lax.axis_size("expert")
    experts = placement.shape[0]
    steps, rows, width = hidden.shape
    units = w_gate.shape[2]
    rank = factors.shape[1] * owners // (3 * (width + units))
    outer, middle, cores = split_axis(owners)
    along_outer, along_middle = (middle * cores, outer), (cores, middle)
    place = lax.axis_index("expert").astype(jnp.int32).reshape(1)

    def along(x, stride, size):
        return [x] + [swap(x, owners, stride, k) for k in range(1, size)]

    rows_in = make_payload(hidden, route_ids, route_logits, experts)
    rows_in, factors = lax.optimization_barrier((rows_in, factors))
    column = [p.reshape(steps, rows, -1) for p in along(rows_in, *along_outer)]
    column = jnp.stack(column, axis=1).reshape(steps * outer * rows, -1)
    kept, sent = order_factors(place, placement, factors, outer, middle, cores)
    blocks = jnp.stack([kept, swap(sent, owners, 1, 1)])
    blocks = [blocks[:, 0], swap(blocks[:, 1], owners, cores, 1)]
    blocks = [jnp.concatenate([block[:, q] for block in blocks]) for q in range(outer)]
    column, blocks = lax.optimization_barrier((column, blocks))
    here = blocks[:1] + [
        swap(block, owners, middle * cores, q) for q, block in enumerate(blocks) if q
    ]
    sheet = along(column, *along_middle)
    others = [swap(column, owners, 1, 1)]
    weights = (w_gate[0], w_up[0])
    base = [base_products([column, others[0]], *weights)]
    here, sheet[1:], base = lax.optimization_barrier((here, sheet[1:], base))
    for r in range(1, middle):
        others.append(swap(sheet[r], owners, 1, 1))
        base.append(base_products([sheet[r], others[r]], *weights))
    low_rank = relayout_factors(place, here, width, units, rank, owners)
    pieces, base = sheet + others, [b for pair in base for b in pair]
    span = outer * rows

    summed = []
    for s in range(steps):
        kept, sent = finish_step(place, pieces, base, s * span, span, low_rank, down_weight[0])
        if s == steps - 2:
            pieces, kept = lax.optimization_barrier((pieces, kept))
        total = kept + swap(sent, owners, 1, 1).astype(jnp.float32)
        summed.append(total.reshape(middle, outer, rows, width))
    first = jnp.stack(summed[:-1], axis=1).reshape(-1, width)
    last = jnp.swapaxes(summed[-1], 0, 1).reshape(-1, width)
    first = scatter_along(first, owners, *along_middle)
    last = scatter_along(last, owners, *along_outer)
    first, last = lax.optimization_barrier((first, last))
    first = jnp.swapaxes(first.reshape(steps - 1, outer, rows, width), 0, 1).reshape(-1, width)
    first = scatter_along(first, owners, *along_outer)
    last = scatter_along(last, owners, *along_middle)
    return jnp.concatenate([first, last]).astype(jnp.bfloat16).reshape(hidden.shape)


def row_capacity(rows, top, experts):
    return min(rows, 3 * max(1, rows * top // experts))


def unpack_factors(flat_factors, width, hidden_units, rank_size):
    layouts = [
        (width, rank_size),
        (rank_size, hidden_units),
        (width, rank_size),
        (rank_size, hidden_units),
        (hidden_units, rank_size),
        (rank_size, width),
    ]
    offset = 0
    segments = []
    for leading, trailing in layouts:
        segments.append(
            flat_factors[offset : offset + leading * trailing].reshape(leading, trailing)
        )
        offset = offset + leading * trailing
    return segments


def merge_weight(loaded_weights, factor_a, factor_b):
    adapter_delta = jnp.dot(factor_a, factor_b, preferred_element_type=jnp.float32)
    return (loaded_weights.astype(jnp.float32) + adapter_scale * adapter_delta).astype(jnp.bfloat16)


def apply_expert_block(inputs, merged_gate, merged_up, combined_down_weight):
    gate_part = jnp.dot(inputs, merged_gate, preferred_element_type=jnp.float32)
    up_part = jnp.dot(inputs, merged_up, preferred_element_type=jnp.float32)
    inner = (jax.nn.silu(gate_part) * up_part).astype(jnp.bfloat16)
    return jnp.dot(inner, combined_down_weight, preferred_element_type=jnp.float32).astype(
        jnp.bfloat16
    )


def sparse_shards(hidden, route_ids, route_logits, placement, factors, w_gate, w_up, down_weight):
    owners = lax.axis_size("expert")
    experts = placement.shape[0]
    steps_count, row_count, width = hidden.shape
    top_count = route_ids.shape[2]
    hidden_units = w_gate.shape[2]
    rank_size = factors.shape[1] * owners // (3 * (width + hidden_units))
    capacity = row_capacity(row_count, top_count, experts)
    slot_of = (
        jnp.zeros((experts,), jnp.int32).at[placement].set(jnp.arange(experts, dtype=jnp.int32))
    )
    ordered = jnp.take(factors, slot_of, axis=0)
    received = lax.all_to_all(ordered, "expert", split_axis=0, concat_axis=1, tiled=True)
    segments = unpack_factors(received[0], width, hidden_units, rank_size)
    merged_gate = merge_weight(w_gate[0], segments[0], segments[1])
    merged_up = merge_weight(w_up[0], segments[2], segments[3])
    combined_down_weight = merge_weight(down_weight[0], segments[4], segments[5])

    def layout(step_index):
        ids_flat = route_ids[step_index].reshape(-1)
        onehot = (ids_flat[:, None] == jnp.arange(experts, dtype=jnp.int32)[None, :]).astype(
            jnp.int32
        )
        position = jnp.sum((jnp.cumsum(onehot, axis=0) - 1) * onehot, axis=1)
        target = ids_flat * capacity + position
        placed = (
            jnp.arange(experts * capacity, dtype=jnp.int32)[:, None] == target[None, :]
        ).astype(jnp.bfloat16)
        pair_rows = jnp.repeat(hidden[step_index], top_count, axis=0)
        outgoing = jnp.dot(placed, pair_rows, preferred_element_type=jnp.float32).astype(
            jnp.bfloat16
        )
        outgoing = outgoing.reshape(experts, 1, capacity, width)
        gates = route_gates(route_logits[step_index]).reshape(-1)
        weighted = placed * gates[None, :]
        return (outgoing, weighted)

    layouts_all = [layout(step_index) for step_index in range(steps_count)]
    results = []
    for step_index in range(steps_count):
        outgoing, weighted = layouts_all[step_index]
        arrived = lax.all_to_all(outgoing, "expert", split_axis=0, concat_axis=1, tiled=True)
        outputs = apply_expert_block(
            arrived.reshape(-1, width), merged_gate, merged_up, combined_down_weight
        )
        outputs = outputs.reshape(arrived.shape)
        returned = lax.all_to_all(outputs, "expert", split_axis=1, concat_axis=0, tiled=True)
        flat_back = returned.reshape(experts * capacity, width)
        pair_out = jnp.einsum("cp,cd->pd", weighted, flat_back, preferred_element_type=jnp.float32)
        results.append(
            pair_out.reshape(row_count, top_count, width).sum(axis=1).astype(jnp.bfloat16)
        )
    return jnp.stack(results, axis=0)


def shards(hidden, route_ids, route_logits, placement, factors, w_gate, w_up, down_weight):
    rows, top = route_ids.shape[1:]
    width, units = w_gate.shape[1:]
    owners = lax.axis_size("expert")
    rank = factors.shape[1] * owners // (3 * (width + units))
    dense = row_capacity(rows, top, placement.shape[0]) == rows
    dense = dense and split_axis(owners)[1:] == (2, 2)
    outer = split_axis(owners)[0]
    dense = dense and outer > 1 and outer & (outer - 1) == 0 and split_axis(owners)[1] > 1
    dense = dense and 2 * rank == LANES and width % 256 == 0 and units % 256 == 0
    dense = dense and factors.shape[1] % (8 * LANES) == 0
    return (dense_shards if dense else sparse_shards)(
        hidden, route_ids, route_logits, placement, factors, w_gate, w_up, down_weight
    )


def solution(mesh):
    placed = (
        P(None, ("group", "expert"), None),
        P(None, ("group", "expert"), None),
        P(None, ("group", "expert"), None),
        P(),
        P(None, "expert"),
        P("expert", None, None),
        P("expert", None, None),
        P("expert", None, None),
    )
    return jax.shard_map(
        shards,
        mesh=mesh,
        in_specs=placed,
        out_specs=P(None, ("group", "expert"), None),
        check_vma=False,
    )
```

```python
import functools

import jax
import jax.numpy as jnp
from jax import lax
from jax.experimental import pallas as pl
from jax.experimental.pallas import tpu as pltpu
from jax.sharding import PartitionSpec as P

adapter_scale = 2.0
LANES = 128
GRANT = 16 << 20
EXPERT_GRANT = 30 << 20
WHOLE_GRANT = 60 << 20
MUCH = pl.CostEstimate(flops=1 << 33, bytes_accessed=1, transcendentals=0)
LITTLE = pl.CostEstimate(flops=1, bytes_accessed=1, transcendentals=0)


def route_gates(logits):
    highest = jnp.max(logits, axis=-1, keepdims=True)
    router_scores = jnp.exp(logits - highest)
    return (router_scores / jnp.sum(router_scores, axis=-1, keepdims=True)).astype(jnp.bfloat16)


def split_axis(n):
    cores = 2 if n % 2 == 0 else 1
    chips = n // cores
    middle = 1
    while chips % (2 * middle) == 0 and 4 * middle * middle <= chips:
        middle *= 2
    return chips // middle, middle, cores


def swap(x, n, stride, k):
    return lax.ppermute(x, "expert", [(i, i ^ (k * stride)) for i in range(n)])


def scatter_along(total, n, stride, size):
    count = total.shape[0] // size
    received = []
    for k in range(1, size):
        part = total[k * count : (k + 1) * count].astype(jnp.bfloat16)
        received.append(swap(part, n, stride, k))
    return sum([part.astype(jnp.float32) for part in received], total[:count])


def dot(a, b):
    return jnp.dot(a, b, preferred_element_type=jnp.float32)


def first_kernel(
    place_ref, placement_ref, hidden_ref, ids_ref, logits_ref, factors_ref, out_ref, *refs
):
    turned_ref, wide_ref, slot_ref = refs[-3:]
    steps, top, rows = ids_ref.shape
    width = hidden_ref.shape[2]
    turned_ref[...] = jnp.zeros_like(turned_ref)
    for s in range(steps):
        logits, ids = logits_ref[s], ids_ref[s]
        scores = jnp.exp(logits - jnp.max(logits, axis=0, keepdims=True))
        gates = scores / jnp.sum(scores, axis=0, keepdims=True)
        expert = lax.broadcasted_iota(jnp.int32, (turned_ref.shape[0], rows), 0)
        dense = jnp.zeros(expert.shape, jnp.float32)
        for k in range(top):
            dense += jnp.where(ids[k : k + 1, :] == expert, gates[k : k + 1, :], 0.0)
        turned_ref[:, s * rows : (s + 1) * rows] = dense
    dense = turned_ref[...].T.astype(jnp.bfloat16)
    for s in range(steps):
        out_ref[s * rows : (s + 1) * rows, :width] = hidden_ref[s]
    out_ref[:, width:] = dense[: steps * rows]

    slots = factors_ref.shape[0]
    out_refs = refs[:-3]
    middle, outer, length, lanes = out_refs[0].shape

    def cut(t, carry):
        start = pl.multiple_of(t * lanes, lanes)
        tile = factors_ref[:, pl.ds(start, lanes)].astype(jnp.float32)
        wide_ref[pl.ds(t, slots, stride=length), :] = tile
        return carry

    lax.fori_loop(0, length, cut, 0, unroll=8)
    for s in range(slots):
        slot_ref[placement_ref[s]] = s
    for core, out_ref in enumerate(out_refs):
        for r in range(middle):
            for q in range(outer):
                slot = slot_ref[place_ref[0] ^ ((q * middle + r) * len(out_refs) + core)]
                block = wide_ref[pl.ds(pl.multiple_of(slot * length, 8), length), :]
                out_ref[r, q] = block.astype(jnp.bfloat16)


def lay_out(place, placement, hidden, route_ids, route_logits, factors, outer, middle, cores):
    steps, rows, width = hidden.shape
    slots, entries = factors.shape
    length = entries // LANES
    padded = -(-slots // LANES) * LANES
    shape = jax.ShapeDtypeStruct((middle, outer, length, LANES), jnp.bfloat16)
    return pl.pallas_call(
        first_kernel,
        out_shape=[jax.ShapeDtypeStruct((steps * rows, width + padded), jnp.bfloat16)]
        + [shape] * cores,
        in_specs=[pl.BlockSpec(memory_space=pltpu.SMEM)] * 2
        + [pl.BlockSpec(memory_space=pltpu.VMEM)] * 4,
        scratch_shapes=[
            pltpu.VMEM((padded, -(-steps * rows // LANES) * LANES), jnp.float32),
            pltpu.VMEM((slots * length, LANES), jnp.float32),
            pltpu.SMEM((slots,), jnp.int32),
        ],
        compiler_params=pltpu.CompilerParams(vmem_limit_bytes=WHOLE_GRANT),
        cost_estimate=LITTLE,
        name="lay_out",
    )(
        place,
        placement,
        hidden,
        jnp.swapaxes(route_ids, 1, 2),
        jnp.swapaxes(route_logits, 1, 2),
        factors,
    )


def relayout_kernel(place_ref, *refs):
    parts, refs = refs[:-7], refs[-7:]
    a_gu_ref, gate_b_ref, up_b_ref, down_a_ref, down_b_ref, flat_ref, wide_ref = refs
    width, units = a_gu_ref.shape[0], gate_b_ref.shape[1]
    rank = gate_b_ref.shape[0]
    near, length, _ = parts[0].shape
    for q, part in enumerate(parts):
        for j in range(near):
            start = pl.multiple_of((place_ref[0] ^ (near * q + j)) * length, 8)
            flat_ref[pl.ds(start, length), :] = part[j].astype(jnp.float32)

    n_wide, n_unit = width // 2, units // 2
    at_ub = 2 * n_wide + n_unit
    at_da = 2 * n_wide + 2 * n_unit
    chunk = 128
    left = lax.broadcasted_iota(jnp.int32, (chunk, LANES), 1) < rank

    def load(start):
        return flat_ref[pl.ds(pl.multiple_of(start, 128), chunk), :]

    def gate_up(i, carry):
        g, u = load(i * chunk), load(n_wide + n_unit + i * chunk)
        at = 2 * i * chunk
        wide_ref[pl.ds(at, chunk, stride=2), :] = jnp.where(left, g, pltpu.roll(u, rank, 1))
        wide_ref[pl.ds(at + 1, chunk, stride=2), :] = jnp.where(left, pltpu.roll(g, rank, 1), u)
        both = wide_ref[pl.ds(pl.multiple_of(at, 128), 2 * chunk), :]
        a_gu_ref[pl.ds(pl.multiple_of(at, 128), 2 * chunk), :] = both.astype(jnp.bfloat16)
        return carry

    lax.fori_loop(0, n_wide // chunk, gate_up, 0, unroll=2)
    for i in range(n_unit // chunk):
        d = load(at_da + i * chunk)
        at = 2 * i * chunk
        wide_ref[pl.ds(at, chunk, stride=2), :] = jnp.where(left, d, 0.0)
        wide_ref[pl.ds(at + 1, chunk, stride=2), :] = jnp.where(left, pltpu.roll(d, rank, 1), 0.0)
        down_a_ref[at : at + 2 * chunk, :] = wide_ref[at : at + 2 * chunk, :].astype(jnp.bfloat16)
    for start, b_ref in (
        (n_wide, gate_b_ref),
        (at_ub, up_b_ref),
        (at_da + n_unit, down_b_ref),
    ):
        tiles = b_ref.shape[1] // LANES
        for j in range(tiles):
            row = flat_ref[pl.ds(start + j, rank, stride=tiles), :]
            b_ref[:, j * LANES : (j + 1) * LANES] = row.astype(jnp.bfloat16)


def relayout_factors(place, parts, width, units, rank, n):
    shapes = [(width, 2 * rank), (rank, units), (rank, units), (units, 2 * rank), (rank, width)]
    length = parts[0].shape[1]
    return pl.pallas_call(
        relayout_kernel,
        out_shape=[jax.ShapeDtypeStruct(shape, jnp.bfloat16) for shape in shapes],
        in_specs=[pl.BlockSpec(memory_space=pltpu.SMEM)]
        + [pl.BlockSpec(memory_space=pltpu.VMEM)] * len(parts),
        scratch_shapes=[
            pltpu.VMEM((n * length, LANES), jnp.float32),
            pltpu.VMEM((width, LANES), jnp.float32),
        ],
        compiler_params=pltpu.CompilerParams(vmem_limit_bytes=GRANT),
        cost_estimate=LITTLE,
        name="relayout_factors",
    )(place, *parts)


def base_kernel(x_ref, w_gate_ref, w_up_ref, gate_ref, up_ref):
    width = w_gate_ref.shape[0]
    gate_ref[...] = dot(x_ref[:, :width], w_gate_ref[...])
    up_ref[...] = dot(x_ref[:, :width], w_up_ref[...])


def base_products(piece, w_gate, w_up):
    out = jax.ShapeDtypeStruct((piece.shape[0], w_gate.shape[1]), jnp.float32)
    return pl.pallas_call(
        base_kernel,
        out_shape=[out, out],
        in_specs=[pl.BlockSpec(memory_space=pltpu.VMEM)] * 3,
        compiler_params=pltpu.CompilerParams(vmem_limit_bytes=EXPERT_GRANT),
        cost_estimate=LITTLE,
        name="base_products",
    )(piece, w_gate, w_up)


def finish_kernel(count, first, rows, place_ref, *refs):
    pieces, refs = refs[:count], refs[count:]
    base, refs = refs[: 2 * count], refs[2 * count :]
    a_gu_ref, gate_b_ref, up_b_ref, down_a_ref, down_b_ref, w_down_ref = refs[:6]
    kept_ref, sent_ref, x_ref, inner_ref = refs[6:]
    width = w_down_ref.shape[1]
    rank = gate_b_ref.shape[0]
    own = kept_ref.shape[0]
    for i, piece in enumerate(pieces):
        x_ref[i * rows : (i + 1) * rows, :] = piece[first : first + rows, :]

    def of_step(refs):
        return jnp.concatenate([ref[first : first + rows, :] for ref in refs])

    low = (adapter_scale * dot(x_ref[:, :width], a_gu_ref[...])).astype(jnp.bfloat16)
    gates = x_ref[:, width:].astype(jnp.float32)
    lane = lax.broadcasted_iota(jnp.int32, gates.shape, 1)
    mine = jnp.sum(jnp.where(lane == place_ref[0], gates, 0.0), axis=1, keepdims=True)
    g = of_step(base[::2]) + dot(low[:, :rank], gate_b_ref[...])
    u = of_step(base[1::2]) + dot(low[:, rank:], up_b_ref[...])
    half = 0.5 * g
    inner_ref[...] = ((half + half * jnp.tanh(half)) * u).astype(jnp.bfloat16)
    low = (adapter_scale * dot(inner_ref[...], down_a_ref[...])).astype(jnp.bfloat16)[:, :rank]
    out = (dot(inner_ref[...], w_down_ref[...]) + dot(low, down_b_ref[...])) * mine
    kept_ref[...] = out[:own]
    sent_ref[...] = out[own:].astype(jnp.bfloat16)


def finish_step(place, pieces, base, first, rows, low_rank, w_down):
    units, width = w_down.shape
    total = rows * len(pieces)
    own = total // 2
    operands = [*pieces, *base, *low_rank, w_down]
    return pl.pallas_call(
        functools.partial(finish_kernel, len(pieces), first, rows),
        out_shape=[
            jax.ShapeDtypeStruct((own, width), jnp.float32),
            jax.ShapeDtypeStruct((own, width), jnp.bfloat16),
        ],
        in_specs=[pl.BlockSpec(memory_space=pltpu.SMEM)]
        + [pl.BlockSpec(memory_space=pltpu.VMEM)] * len(operands),
        scratch_shapes=[
            pltpu.VMEM((total, pieces[0].shape[1]), jnp.bfloat16),
            pltpu.VMEM((total, units), jnp.bfloat16),
        ],
        compiler_params=pltpu.CompilerParams(vmem_limit_bytes=EXPERT_GRANT),
        cost_estimate=MUCH,
        name="finish_step",
    )(place, *operands)


def dense_shards(
    hidden, route_ids, route_logits, placement, factors, w_gate, w_up, down_weight
):
    owners = lax.axis_size("expert")
    experts = placement.shape[0]
    steps, rows, width = hidden.shape
    units = w_gate.shape[2]
    rank = factors.shape[1] * owners // (3 * (width + units))
    outer, middle, cores = split_axis(owners)
    along_outer, along_middle = (middle * cores, outer), (cores, middle)
    place = lax.axis_index("expert").astype(jnp.int32).reshape(1)

    def along(x, stride, size):
        return [x] + [swap(x, owners, stride, k) for k in range(1, size)]

    rows_in, kept, sent = lay_out(
        place, placement, hidden, route_ids, route_logits, factors, outer, middle, cores
    )
    column = [p.reshape(steps, rows, -1) for p in along(rows_in, *along_outer)]
    column = jnp.stack(column, axis=1).reshape(steps * outer * rows, -1)
    blocks = jnp.stack([kept, swap(sent, owners, 1, 1)])
    blocks = [blocks[:, 0], swap(blocks[:, 1], owners, cores, 1)]
    blocks = [jnp.concatenate([block[:, q] for block in blocks]) for q in range(outer)]
    column, blocks = lax.optimization_barrier((column, blocks))
    here = blocks[:1] + [
        swap(block, owners, middle * cores, q) for q, block in enumerate(blocks) if q
    ]
    sheet = along(column, *along_middle)
    others = [swap(column, owners, 1, 1)]
    weights = (w_gate[0], w_up[0])
    base = [base_products(piece, *weights) for piece in (column, others[0])]
    here, sheet[1:], base = lax.optimization_barrier((here, sheet[1:], base))
    for r in range(1, middle):
        others.append(swap(sheet[r], owners, 1, 1))
        base.append(base_products(sheet[r], *weights))
        base.append(base_products(others[r], *weights))
    low_rank = relayout_factors(place, here, width, units, rank, owners)
    pieces = sheet + others
    base = [b for pair in base[::2] + base[1::2] for b in pair]
    span = outer * rows

    summed = []
    for s in range(steps):
        kept, sent = finish_step(place, pieces, base, s * span, span, low_rank, down_weight[0])
        if s == steps - 2:
            pieces, kept = lax.optimization_barrier((pieces, kept))
        total = kept + swap(sent, owners, 1, 1).astype(jnp.float32)
        summed.append(total.reshape(middle, outer, rows, width))
    first = jnp.stack(summed[:-1], axis=1).reshape(-1, width)
    last = jnp.swapaxes(summed[-1], 0, 1).reshape(-1, width)
    first = scatter_along(first, owners, *along_middle)
    last = scatter_along(last, owners, *along_outer)
    first, last = lax.optimization_barrier((first, last))
    first = jnp.swapaxes(first.reshape(steps - 1, outer, rows, width), 0, 1).reshape(-1, width)
    first = scatter_along(first, owners, *along_outer)
    last = scatter_along(last, owners, *along_middle)
    return jnp.concatenate([first, last]).astype(jnp.bfloat16).reshape(hidden.shape)


def row_capacity(rows, top, experts):
    return min(rows, 3 * max(1, rows * top // experts))


def unpack_factors(flat_factors, width, hidden_units, rank_size):
    layouts = [
        (width, rank_size),
        (rank_size, hidden_units),
        (width, rank_size),
        (rank_size, hidden_units),
        (hidden_units, rank_size),
        (rank_size, width),
    ]
    offset = 0
    segments = []
    for leading, trailing in layouts:
        segments.append(
            flat_factors[offset : offset + leading * trailing].reshape(leading, trailing)
        )
        offset = offset + leading * trailing
    return segments


def merge_weight(loaded_weights, factor_a, factor_b):
    adapter_delta = jnp.dot(factor_a, factor_b, preferred_element_type=jnp.float32)
    return (loaded_weights.astype(jnp.float32) + adapter_scale * adapter_delta).astype(jnp.bfloat16)


def apply_expert_block(inputs, merged_gate, merged_up, combined_down_weight):
    gate_part = jnp.dot(inputs, merged_gate, preferred_element_type=jnp.float32)
    up_part = jnp.dot(inputs, merged_up, preferred_element_type=jnp.float32)
    inner = (jax.nn.silu(gate_part) * up_part).astype(jnp.bfloat16)
    return jnp.dot(inner, combined_down_weight, preferred_element_type=jnp.float32).astype(
        jnp.bfloat16
    )


def sparse_shards(hidden, route_ids, route_logits, placement, factors, w_gate, w_up, down_weight):
    owners = lax.axis_size("expert")
    experts = placement.shape[0]
    steps_count, row_count, width = hidden.shape
    top_count = route_ids.shape[2]
    hidden_units = w_gate.shape[2]
    rank_size = factors.shape[1] * owners // (3 * (width + hidden_units))
    capacity = row_capacity(row_count, top_count, experts)
    slot_of = (
        jnp.zeros((experts,), jnp.int32).at[placement].set(jnp.arange(experts, dtype=jnp.int32))
    )
    ordered = jnp.take(factors, slot_of, axis=0)
    received = lax.all_to_all(ordered, "expert", split_axis=0, concat_axis=1, tiled=True)
    segments = unpack_factors(received[0], width, hidden_units, rank_size)
    merged_gate = merge_weight(w_gate[0], segments[0], segments[1])
    merged_up = merge_weight(w_up[0], segments[2], segments[3])
    combined_down_weight = merge_weight(down_weight[0], segments[4], segments[5])

    def layout(step_index):
        ids_flat = route_ids[step_index].reshape(-1)
        onehot = (ids_flat[:, None] == jnp.arange(experts, dtype=jnp.int32)[None, :]).astype(
            jnp.int32
        )
        position = jnp.sum((jnp.cumsum(onehot, axis=0) - 1) * onehot, axis=1)
        target = ids_flat * capacity + position
        placed = (
            jnp.arange(experts * capacity, dtype=jnp.int32)[:, None] == target[None, :]
        ).astype(jnp.bfloat16)
        pair_rows = jnp.repeat(hidden[step_index], top_count, axis=0)
        outgoing = jnp.dot(placed, pair_rows, preferred_element_type=jnp.float32).astype(
            jnp.bfloat16
        )
        outgoing = outgoing.reshape(experts, 1, capacity, width)
        gates = route_gates(route_logits[step_index]).reshape(-1)
        weighted = placed * gates[None, :]
        return (outgoing, weighted)

    layouts_all = [layout(step_index) for step_index in range(steps_count)]
    results = []
    for step_index in range(steps_count):
        outgoing, weighted = layouts_all[step_index]
        arrived = lax.all_to_all(outgoing, "expert", split_axis=0, concat_axis=1, tiled=True)
        outputs = apply_expert_block(
            arrived.reshape(-1, width), merged_gate, merged_up, combined_down_weight
        )
        outputs = outputs.reshape(arrived.shape)
        returned = lax.all_to_all(outputs, "expert", split_axis=1, concat_axis=0, tiled=True)
        flat_back = returned.reshape(experts * capacity, width)
        pair_out = jnp.einsum("cp,cd->pd", weighted, flat_back, preferred_element_type=jnp.float32)
        results.append(
            pair_out.reshape(row_count, top_count, width).sum(axis=1).astype(jnp.bfloat16)
        )
    return jnp.stack(results, axis=0)


def shards(hidden, route_ids, route_logits, placement, factors, w_gate, w_up, down_weight):
    rows, top = route_ids.shape[1:]
    width, units = w_gate.shape[1:]
    owners = lax.axis_size("expert")
    rank = factors.shape[1] * owners // (3 * (width + units))
    dense = row_capacity(rows, top, placement.shape[0]) == rows
    dense = dense and split_axis(owners)[1:] == (2, 2)
    outer = split_axis(owners)[0]
    dense = dense and outer > 1 and outer & (outer - 1) == 0 and split_axis(owners)[1] > 1
    dense = dense and 2 * rank == LANES and width % 256 == 0 and units % 256 == 0
    dense = dense and factors.shape[1] % (8 * LANES) == 0
    return (dense_shards if dense else sparse_shards)(
        hidden, route_ids, route_logits, placement, factors, w_gate, w_up, down_weight
    )


def solution(mesh):
    placed = (
        P(None, ("group", "expert"), None),
        P(None, ("group", "expert"), None),
        P(None, ("group", "expert"), None),
        P(),
        P(None, "expert"),
        P("expert", None, None),
        P("expert", None, None),
        P("expert", None, None),
    )
    return jax.shard_map(
        shards,
        mesh=mesh,
        in_specs=placed,
        out_specs=P(None, ("group", "expert"), None),
        check_vma=False,
    )
```

```python
import functools

import jax
import jax.numpy as jnp
from jax import lax
from jax.experimental import pallas as pl
from jax.experimental.pallas import tpu as pltpu
from jax.sharding import PartitionSpec as P

adapter_scale = 2.0
LANES = 128
GRANT = 16 << 20
EXPERT_GRANT = 30 << 20
WHOLE_GRANT = 60 << 20
MUCH = pl.CostEstimate(flops=1 << 33, bytes_accessed=1, transcendentals=0)
LITTLE = pl.CostEstimate(flops=1, bytes_accessed=1, transcendentals=0)


def route_gates(logits):
    highest = jnp.max(logits, axis=-1, keepdims=True)
    router_scores = jnp.exp(logits - highest)
    return (router_scores / jnp.sum(router_scores, axis=-1, keepdims=True)).astype(jnp.bfloat16)


def split_axis(n):
    cores = 2 if n % 2 == 0 else 1
    chips = n // cores
    middle = 1
    while chips % (2 * middle) == 0 and 4 * middle * middle <= chips:
        middle *= 2
    return chips // middle, middle, cores


def swap(x, n, stride, k):
    return lax.ppermute(x, "expert", [(i, i ^ (k * stride)) for i in range(n)])


def scatter_along(total, n, stride, size):
    count = total.shape[0] // size
    received = []
    for k in range(1, size):
        part = total[k * count : (k + 1) * count].astype(jnp.bfloat16)
        received.append(swap(part, n, stride, k))
    return sum([part.astype(jnp.float32) for part in received], total[:count])


def dot(a, b):
    return jnp.dot(a, b, preferred_element_type=jnp.float32)


def first_kernel(
    place_ref, placement_ref, hidden_ref, ids_ref, logits_ref, factors_ref, out_ref, *refs
):
    turned_ref, wide_ref, slot_ref = refs[-3:]
    steps, top, rows = ids_ref.shape
    width = hidden_ref.shape[2]
    turned_ref[...] = jnp.zeros_like(turned_ref)
    for s in range(steps):
        logits, ids = logits_ref[s], ids_ref[s]
        scores = jnp.exp(logits - jnp.max(logits, axis=0, keepdims=True))
        gates = scores / jnp.sum(scores, axis=0, keepdims=True)
        expert = lax.broadcasted_iota(jnp.int32, (turned_ref.shape[0], rows), 0)
        dense = jnp.zeros(expert.shape, jnp.float32)
        for k in range(top):
            dense += jnp.where(ids[k : k + 1, :] == expert, gates[k : k + 1, :], 0.0)
        turned_ref[:, s * rows : (s + 1) * rows] = dense
    dense = turned_ref[...].T.astype(jnp.bfloat16)
    for s in range(steps):
        out_ref[s * rows : (s + 1) * rows, :width] = hidden_ref[s]
    out_ref[:, width:] = dense[: steps * rows]

    slots = factors_ref.shape[0]
    out_refs = refs[:-3]
    middle, outer, length, lanes = out_refs[0].shape

    def cut(t, carry):
        start = pl.multiple_of(t * lanes, lanes)
        tile = factors_ref[:, pl.ds(start, lanes)].astype(jnp.float32)
        wide_ref[pl.ds(t, slots, stride=length), :] = tile
        return carry

    lax.fori_loop(0, length, cut, 0, unroll=8)
    for s in range(slots):
        slot_ref[placement_ref[s]] = s
    for core, out_ref in enumerate(out_refs):
        for r in range(middle):
            for q in range(outer):
                slot = slot_ref[place_ref[0] ^ ((q * middle + r) * len(out_refs) + core)]
                block = wide_ref[pl.ds(pl.multiple_of(slot * length, 8), length), :]
                out_ref[r, q] = block.astype(jnp.bfloat16)


def lay_out(place, placement, hidden, route_ids, route_logits, factors, outer, middle, cores):
    steps, rows, width = hidden.shape
    slots, entries = factors.shape
    length = entries // LANES
    padded = -(-slots // LANES) * LANES
    shape = jax.ShapeDtypeStruct((middle, outer, length, LANES), jnp.bfloat16)
    return pl.pallas_call(
        first_kernel,
        out_shape=[jax.ShapeDtypeStruct((steps * rows, width + padded), jnp.bfloat16)]
        + [shape] * cores,
        in_specs=[pl.BlockSpec(memory_space=pltpu.SMEM)] * 2
        + [pl.BlockSpec(memory_space=pltpu.VMEM)] * 4,
        scratch_shapes=[
            pltpu.VMEM((padded, -(-steps * rows // LANES) * LANES), jnp.float32),
            pltpu.VMEM((slots * length, LANES), jnp.float32),
            pltpu.SMEM((slots,), jnp.int32),
        ],
        compiler_params=pltpu.CompilerParams(vmem_limit_bytes=WHOLE_GRANT),
        cost_estimate=LITTLE,
        name="lay_out",
    )(
        place,
        placement,
        hidden,
        jnp.swapaxes(route_ids, 1, 2),
        jnp.swapaxes(route_logits, 1, 2),
        factors,
    )


def relayout_kernel(place_ref, *refs):
    parts, refs = refs[:-7], refs[-7:]
    a_gu_ref, gate_b_ref, up_b_ref, down_a_ref, down_b_ref, flat_ref, wide_ref = refs
    width, units = a_gu_ref.shape[0], gate_b_ref.shape[1]
    rank = gate_b_ref.shape[0]
    near, length, _ = parts[0].shape
    for q, part in enumerate(parts):
        for j in range(near):
            start = pl.multiple_of((place_ref[0] ^ (near * q + j)) * length, 8)
            flat_ref[pl.ds(start, length), :] = part[j].astype(jnp.float32)

    n_wide, n_unit = width // 2, units // 2
    at_ub = 2 * n_wide + n_unit
    at_da = 2 * n_wide + 2 * n_unit
    chunk = 128
    left = lax.broadcasted_iota(jnp.int32, (chunk, LANES), 1) < rank

    def load(start):
        return flat_ref[pl.ds(pl.multiple_of(start, 128), chunk), :]

    def gate_up(i, carry):
        g, u = load(i * chunk), load(n_wide + n_unit + i * chunk)
        at = 2 * i * chunk
        wide_ref[pl.ds(at, chunk, stride=2), :] = jnp.where(left, g, pltpu.roll(u, rank, 1))
        wide_ref[pl.ds(at + 1, chunk, stride=2), :] = jnp.where(left, pltpu.roll(g, rank, 1), u)
        both = wide_ref[pl.ds(pl.multiple_of(at, 128), 2 * chunk), :]
        a_gu_ref[pl.ds(pl.multiple_of(at, 128), 2 * chunk), :] = both.astype(jnp.bfloat16)
        return carry

    lax.fori_loop(0, n_wide // chunk, gate_up, 0, unroll=2)
    for i in range(n_unit // chunk):
        d = load(at_da + i * chunk)
        at = 2 * i * chunk
        wide_ref[pl.ds(at, chunk, stride=2), :] = jnp.where(left, d, 0.0)
        wide_ref[pl.ds(at + 1, chunk, stride=2), :] = jnp.where(left, pltpu.roll(d, rank, 1), 0.0)
        down_a_ref[at : at + 2 * chunk, :] = wide_ref[at : at + 2 * chunk, :].astype(jnp.bfloat16)
    for start, b_ref in (
        (n_wide, gate_b_ref),
        (at_ub, up_b_ref),
        (at_da + n_unit, down_b_ref),
    ):
        tiles = b_ref.shape[1] // LANES
        for j in range(tiles):
            row = flat_ref[pl.ds(start + j, rank, stride=tiles), :]
            b_ref[:, j * LANES : (j + 1) * LANES] = row.astype(jnp.bfloat16)


def relayout_factors(place, parts, width, units, rank, n):
    shapes = [(width, 2 * rank), (rank, units), (rank, units), (units, 2 * rank), (rank, width)]
    length = parts[0].shape[1]
    return pl.pallas_call(
        relayout_kernel,
        out_shape=[jax.ShapeDtypeStruct(shape, jnp.bfloat16) for shape in shapes],
        in_specs=[pl.BlockSpec(memory_space=pltpu.SMEM)]
        + [pl.BlockSpec(memory_space=pltpu.VMEM)] * len(parts),
        scratch_shapes=[
            pltpu.VMEM((n * length, LANES), jnp.float32),
            pltpu.VMEM((width, LANES), jnp.float32),
        ],
        compiler_params=pltpu.CompilerParams(vmem_limit_bytes=GRANT),
        cost_estimate=LITTLE,
        name="relayout_factors",
    )(place, *parts)


def base_kernel(x_ref, w_gate_ref, w_up_ref, gate_ref, up_ref):
    width = w_gate_ref.shape[0]
    gate_ref[...] = dot(x_ref[:, :width], w_gate_ref[...])
    up_ref[...] = dot(x_ref[:, :width], w_up_ref[...])


def base_products(piece, w_gate, w_up):
    out = jax.ShapeDtypeStruct((piece.shape[0], w_gate.shape[1]), jnp.float32)
    return pl.pallas_call(
        base_kernel,
        out_shape=[out, out],
        in_specs=[pl.BlockSpec(memory_space=pltpu.VMEM)] * 3,
        compiler_params=pltpu.CompilerParams(vmem_limit_bytes=EXPERT_GRANT),
        cost_estimate=LITTLE,
        name="base_products",
    )(piece, w_gate, w_up)


def finish_kernel(count, first, rows, place_ref, *refs):
    pieces, refs = refs[:count], refs[count:]
    base, refs = refs[: 2 * count], refs[2 * count :]
    a_gu_ref, gate_b_ref, up_b_ref, down_a_ref, down_b_ref, w_down_ref = refs[:6]
    kept_ref, sent_ref, x_ref, inner_ref = refs[6:]
    width = w_down_ref.shape[1]
    rank = gate_b_ref.shape[0]
    own = kept_ref.shape[0]
    for i, piece in enumerate(pieces):
        x_ref[i * rows : (i + 1) * rows, :] = piece[first : first + rows, :]

    def of_step(refs):
        return jnp.concatenate([ref[first : first + rows, :] for ref in refs])

    low = (adapter_scale * dot(x_ref[:, :width], a_gu_ref[...])).astype(jnp.bfloat16)
    gates = x_ref[:, width:].astype(jnp.float32)
    lane = lax.broadcasted_iota(jnp.int32, gates.shape, 1)
    mine = jnp.sum(jnp.where(lane == place_ref[0], gates, 0.0), axis=1, keepdims=True)
    g = of_step(base[::2]) + dot(low[:, :rank], gate_b_ref[...])
    u = of_step(base[1::2]) + dot(low[:, rank:], up_b_ref[...])
    half = 0.5 * g
    inner_ref[...] = ((half + half * jnp.tanh(half)) * u).astype(jnp.bfloat16)
    low = (adapter_scale * dot(inner_ref[...], down_a_ref[...])).astype(jnp.bfloat16)[:, :rank]
    out = (dot(inner_ref[...], w_down_ref[...]) + dot(low, down_b_ref[...])) * mine
    kept_ref[...] = out[:own]
    sent_ref[...] = out[own:].astype(jnp.bfloat16)


def finish_step(place, pieces, base, first, rows, low_rank, w_down):
    units, width = w_down.shape
    total = rows * len(pieces)
    own = total // 2
    operands = [*pieces, *base, *low_rank, w_down]
    return pl.pallas_call(
        functools.partial(finish_kernel, len(pieces), first, rows),
        out_shape=[
            jax.ShapeDtypeStruct((own, width), jnp.float32),
            jax.ShapeDtypeStruct((own, width), jnp.bfloat16),
        ],
        in_specs=[pl.BlockSpec(memory_space=pltpu.SMEM)]
        + [pl.BlockSpec(memory_space=pltpu.VMEM)] * len(operands),
        scratch_shapes=[
            pltpu.VMEM((total, pieces[0].shape[1]), jnp.bfloat16),
            pltpu.VMEM((total, units), jnp.bfloat16),
        ],
        compiler_params=pltpu.CompilerParams(vmem_limit_bytes=EXPERT_GRANT),
        cost_estimate=MUCH,
        name="finish_step",
    )(place, *operands)


def dense_shards(
    hidden, route_ids, route_logits, placement, factors, w_gate, w_up, down_weight
):
    owners = lax.axis_size("expert")
    experts = placement.shape[0]
    steps, rows, width = hidden.shape
    units = w_gate.shape[2]
    rank = factors.shape[1] * owners // (3 * (width + units))
    outer, middle, cores = split_axis(owners)
    along_outer, along_middle = (middle * cores, outer), (cores, middle)
    place = lax.axis_index("expert").astype(jnp.int32).reshape(1)

    def along(x, stride, size):
        return [x] + [swap(x, owners, stride, k) for k in range(1, size)]

    rows_in, kept, sent = lay_out(
        place, placement, hidden, route_ids, route_logits, factors, outer, middle, cores
    )
    column = [p.reshape(steps, rows, -1) for p in along(rows_in, *along_outer)]
    column = jnp.stack(column, axis=1).reshape(steps * outer * rows, -1)
    blocks = jnp.stack([kept, swap(sent, owners, 1, 1)])
    blocks = [blocks[:, 0], swap(blocks[:, 1], owners, cores, 1)]
    blocks = [jnp.concatenate([block[:, q] for block in blocks]) for q in range(outer)]
    column, blocks = lax.optimization_barrier((column, blocks))
    here = blocks[:1] + [
        swap(block, owners, middle * cores, q) for q, block in enumerate(blocks) if q
    ]
    sheet = along(column, *along_middle)
    others = [swap(column, owners, 1, 1)]
    weights = (w_gate[0], w_up[0])
    base = [base_products(piece, *weights) for piece in (column, others[0])]
    here = here[::-1]
    here, sheet[1:], base = lax.optimization_barrier((here, sheet[1:], base))
    here = here[::-1]
    for r in range(1, middle):
        others.append(swap(sheet[r], owners, 1, 1))
        base.append(base_products(sheet[r], *weights))
        base.append(base_products(others[r], *weights))
    low_rank = relayout_factors(place, here, width, units, rank, owners)
    pieces = sheet + others
    base = [b for pair in base[::2] + base[1::2] for b in pair]
    span = outer * rows

    summed = []
    for s in range(steps):
        kept, sent = finish_step(place, pieces, base, s * span, span, low_rank, down_weight[0])
        if s == steps - 2:
            pieces, kept = lax.optimization_barrier((pieces, kept))
        total = kept + swap(sent, owners, 1, 1).astype(jnp.float32)
        summed.append(total.reshape(middle, outer, rows, width))
    first = jnp.stack(summed[:-1], axis=1).reshape(-1, width)
    last = jnp.swapaxes(summed[-1], 0, 1).reshape(-1, width)
    first = scatter_along(first, owners, *along_middle)
    last = scatter_along(last, owners, *along_outer)
    first = jnp.swapaxes(first.reshape(steps - 1, outer, rows, width), 0, 1).reshape(-1, width)
    first = scatter_along(first, owners, *along_outer)
    last = scatter_along(last, owners, *along_middle)
    return jnp.concatenate([first, last]).astype(jnp.bfloat16).reshape(hidden.shape)


def row_capacity(rows, top, experts):
    return min(rows, 3 * max(1, rows * top // experts))


def unpack_factors(flat_factors, width, hidden_units, rank_size):
    layouts = [
        (width, rank_size),
        (rank_size, hidden_units),
        (width, rank_size),
        (rank_size, hidden_units),
        (hidden_units, rank_size),
        (rank_size, width),
    ]
    offset = 0
    segments = []
    for leading, trailing in layouts:
        segments.append(
            flat_factors[offset : offset + leading * trailing].reshape(leading, trailing)
        )
        offset = offset + leading * trailing
    return segments


def merge_weight(loaded_weights, factor_a, factor_b):
    adapter_delta = jnp.dot(factor_a, factor_b, preferred_element_type=jnp.float32)
    return (loaded_weights.astype(jnp.float32) + adapter_scale * adapter_delta).astype(jnp.bfloat16)


def apply_expert_block(inputs, merged_gate, merged_up, combined_down_weight):
    gate_part = jnp.dot(inputs, merged_gate, preferred_element_type=jnp.float32)
    up_part = jnp.dot(inputs, merged_up, preferred_element_type=jnp.float32)
    inner = (jax.nn.silu(gate_part) * up_part).astype(jnp.bfloat16)
    return jnp.dot(inner, combined_down_weight, preferred_element_type=jnp.float32).astype(
        jnp.bfloat16
    )


def sparse_shards(hidden, route_ids, route_logits, placement, factors, w_gate, w_up, down_weight):
    owners = lax.axis_size("expert")
    experts = placement.shape[0]
    steps_count, row_count, width = hidden.shape
    top_count = route_ids.shape[2]
    hidden_units = w_gate.shape[2]
    rank_size = factors.shape[1] * owners // (3 * (width + hidden_units))
    capacity = row_capacity(row_count, top_count, experts)
    slot_of = (
        jnp.zeros((experts,), jnp.int32).at[placement].set(jnp.arange(experts, dtype=jnp.int32))
    )
    ordered = jnp.take(factors, slot_of, axis=0)
    received = lax.all_to_all(ordered, "expert", split_axis=0, concat_axis=1, tiled=True)
    segments = unpack_factors(received[0], width, hidden_units, rank_size)
    merged_gate = merge_weight(w_gate[0], segments[0], segments[1])
    merged_up = merge_weight(w_up[0], segments[2], segments[3])
    combined_down_weight = merge_weight(down_weight[0], segments[4], segments[5])

    def layout(step_index):
        ids_flat = route_ids[step_index].reshape(-1)
        onehot = (ids_flat[:, None] == jnp.arange(experts, dtype=jnp.int32)[None, :]).astype(
            jnp.int32
        )
        position = jnp.sum((jnp.cumsum(onehot, axis=0) - 1) * onehot, axis=1)
        target = ids_flat * capacity + position
        placed = (
            jnp.arange(experts * capacity, dtype=jnp.int32)[:, None] == target[None, :]
        ).astype(jnp.bfloat16)
        pair_rows = jnp.repeat(hidden[step_index], top_count, axis=0)
        outgoing = jnp.dot(placed, pair_rows, preferred_element_type=jnp.float32).astype(
            jnp.bfloat16
        )
        outgoing = outgoing.reshape(experts, 1, capacity, width)
        gates = route_gates(route_logits[step_index]).reshape(-1)
        weighted = placed * gates[None, :]
        return (outgoing, weighted)

    layouts_all = [layout(step_index) for step_index in range(steps_count)]
    results = []
    for step_index in range(steps_count):
        outgoing, weighted = layouts_all[step_index]
        arrived = lax.all_to_all(outgoing, "expert", split_axis=0, concat_axis=1, tiled=True)
        outputs = apply_expert_block(
            arrived.reshape(-1, width), merged_gate, merged_up, combined_down_weight
        )
        outputs = outputs.reshape(arrived.shape)
        returned = lax.all_to_all(outputs, "expert", split_axis=1, concat_axis=0, tiled=True)
        flat_back = returned.reshape(experts * capacity, width)
        pair_out = jnp.einsum("cp,cd->pd", weighted, flat_back, preferred_element_type=jnp.float32)
        results.append(
            pair_out.reshape(row_count, top_count, width).sum(axis=1).astype(jnp.bfloat16)
        )
    return jnp.stack(results, axis=0)


def shards(hidden, route_ids, route_logits, placement, factors, w_gate, w_up, down_weight):
    rows, top = route_ids.shape[1:]
    width, units = w_gate.shape[1:]
    owners = lax.axis_size("expert")
    rank = factors.shape[1] * owners // (3 * (width + units))
    dense = row_capacity(rows, top, placement.shape[0]) == rows
    dense = dense and split_axis(owners)[1:] == (2, 2)
    outer = split_axis(owners)[0]
    dense = dense and outer > 1 and outer & (outer - 1) == 0 and split_axis(owners)[1] > 1
    dense = dense and 2 * rank == LANES and width % 256 == 0 and units % 256 == 0
    dense = dense and factors.shape[1] % (8 * LANES) == 0
    return (dense_shards if dense else sparse_shards)(
        hidden, route_ids, route_logits, placement, factors, w_gate, w_up, down_weight
    )


def solution(mesh):
    placed = (
        P(None, ("group", "expert"), None),
        P(None, ("group", "expert"), None),
        P(None, ("group", "expert"), None),
        P(),
        P(None, "expert"),
        P("expert", None, None),
        P("expert", None, None),
        P("expert", None, None),
    )
    return jax.shard_map(
        shards,
        mesh=mesh,
        in_specs=placed,
        out_specs=P(None, ("group", "expert"), None),
        check_vma=False,
    )
```

```python
import functools

import jax
import jax.numpy as jnp
from jax import lax
from jax.experimental import pallas as pl
from jax.experimental.pallas import tpu as pltpu
from jax.sharding import PartitionSpec as P

adapter_scale = 2.0
LANES = 128
GRANT = 16 << 20
EXPERT_GRANT = 30 << 20
WHOLE_GRANT = 60 << 20
MUCH = pl.CostEstimate(flops=1 << 33, bytes_accessed=1, transcendentals=0)
LITTLE = pl.CostEstimate(flops=1, bytes_accessed=1, transcendentals=0)


def route_gates(logits):
    highest = jnp.max(logits, axis=-1, keepdims=True)
    router_scores = jnp.exp(logits - highest)
    return (router_scores / jnp.sum(router_scores, axis=-1, keepdims=True)).astype(jnp.bfloat16)


def split_axis(n):
    cores = 2 if n % 2 == 0 else 1
    chips = n // cores
    middle = 1
    while chips % (2 * middle) == 0 and 4 * middle * middle <= chips:
        middle *= 2
    return chips // middle, middle, cores


def swap(x, n, stride, k):
    return lax.ppermute(x, "expert", [(i, i ^ (k * stride)) for i in range(n)])


def scatter_along(total, n, stride, size):
    count = total.shape[0] // size
    received = []
    for k in range(1, size):
        part = total[k * count : (k + 1) * count].astype(jnp.bfloat16)
        received.append(swap(part, n, stride, k))
    return sum([part.astype(jnp.float32) for part in received], total[:count])


def dot(a, b):
    return jnp.dot(a, b, preferred_element_type=jnp.float32)


def first_kernel(
    place_ref, placement_ref, hidden_ref, ids_ref, logits_ref, factors_ref, out_ref, *refs
):
    turned_ref, wide_ref, slot_ref = refs[-3:]
    steps, top, rows = ids_ref.shape
    width = hidden_ref.shape[2]
    turned_ref[...] = jnp.zeros_like(turned_ref)
    for s in range(steps):
        logits, ids = logits_ref[s], ids_ref[s]
        scores = jnp.exp(logits - jnp.max(logits, axis=0, keepdims=True))
        gates = scores / jnp.sum(scores, axis=0, keepdims=True)
        expert = lax.broadcasted_iota(jnp.int32, (turned_ref.shape[0], rows), 0)
        dense = jnp.zeros(expert.shape, jnp.float32)
        for k in range(top):
            dense += jnp.where(ids[k : k + 1, :] == expert, gates[k : k + 1, :], 0.0)
        turned_ref[:, s * rows : (s + 1) * rows] = dense
    dense = turned_ref[...].T.astype(jnp.bfloat16)
    for s in range(steps):
        out_ref[s * rows : (s + 1) * rows, :width] = hidden_ref[s]
    out_ref[:, width:] = dense[: steps * rows]

    slots = factors_ref.shape[0]
    out_refs = refs[:-3]
    middle, outer, length, lanes = out_refs[0].shape

    def cut(t, carry):
        start = pl.multiple_of(t * lanes, lanes)
        tile = factors_ref[:, pl.ds(start, lanes)].astype(jnp.float32)
        wide_ref[pl.ds(t, slots, stride=length), :] = tile
        return carry

    lax.fori_loop(0, length, cut, 0, unroll=8)
    for s in range(slots):
        slot_ref[placement_ref[s]] = s
    for core, out_ref in enumerate(out_refs):
        for r in range(middle):
            for q in range(outer):
                slot = slot_ref[place_ref[0] ^ ((q * middle + r) * len(out_refs) + core)]
                block = wide_ref[pl.ds(pl.multiple_of(slot * length, 8), length), :]
                out_ref[r, q] = block.astype(jnp.bfloat16)


def lay_out(place, placement, hidden, route_ids, route_logits, factors, outer, middle, cores):
    steps, rows, width = hidden.shape
    slots, entries = factors.shape
    length = entries // LANES
    padded = -(-slots // LANES) * LANES
    shape = jax.ShapeDtypeStruct((middle, outer, length, LANES), jnp.bfloat16)
    return pl.pallas_call(
        first_kernel,
        out_shape=[jax.ShapeDtypeStruct((steps * rows, width + padded), jnp.bfloat16)]
        + [shape] * cores,
        in_specs=[pl.BlockSpec(memory_space=pltpu.SMEM)] * 2
        + [pl.BlockSpec(memory_space=pltpu.VMEM)] * 4,
        scratch_shapes=[
            pltpu.VMEM((padded, -(-steps * rows // LANES) * LANES), jnp.float32),
            pltpu.VMEM((slots * length, LANES), jnp.float32),
            pltpu.SMEM((slots,), jnp.int32),
        ],
        compiler_params=pltpu.CompilerParams(vmem_limit_bytes=WHOLE_GRANT),
        cost_estimate=LITTLE,
        name="lay_out",
    )(
        place,
        placement,
        hidden,
        jnp.swapaxes(route_ids, 1, 2),
        jnp.swapaxes(route_logits, 1, 2),
        factors,
    )


def relayout_kernel(place_ref, *refs):
    parts, refs = refs[:-7], refs[-7:]
    a_gu_ref, gate_b_ref, up_b_ref, down_a_ref, down_b_ref, flat_ref, wide_ref = refs
    width, units = a_gu_ref.shape[0], gate_b_ref.shape[1]
    rank = gate_b_ref.shape[0]
    near, length, _ = parts[0].shape
    for q, part in enumerate(parts):
        for j in range(near):
            start = pl.multiple_of((place_ref[0] ^ (near * q + j)) * length, 8)
            flat_ref[pl.ds(start, length), :] = part[j].astype(jnp.float32)

    n_wide, n_unit = width // 2, units // 2
    at_ub = 2 * n_wide + n_unit
    at_da = 2 * n_wide + 2 * n_unit
    chunk = 128
    left = lax.broadcasted_iota(jnp.int32, (chunk, LANES), 1) < rank

    def load(start):
        return flat_ref[pl.ds(pl.multiple_of(start, 128), chunk), :]

    def gate_up(i, carry):
        g, u = load(i * chunk), load(n_wide + n_unit + i * chunk)
        at = 2 * i * chunk
        wide_ref[pl.ds(at, chunk, stride=2), :] = jnp.where(left, g, pltpu.roll(u, rank, 1))
        wide_ref[pl.ds(at + 1, chunk, stride=2), :] = jnp.where(left, pltpu.roll(g, rank, 1), u)
        both = wide_ref[pl.ds(pl.multiple_of(at, 128), 2 * chunk), :]
        a_gu_ref[pl.ds(pl.multiple_of(at, 128), 2 * chunk), :] = both.astype(jnp.bfloat16)
        return carry

    lax.fori_loop(0, n_wide // chunk, gate_up, 0, unroll=2)
    for i in range(n_unit // chunk):
        d = load(at_da + i * chunk)
        at = 2 * i * chunk
        wide_ref[pl.ds(at, chunk, stride=2), :] = jnp.where(left, d, 0.0)
        wide_ref[pl.ds(at + 1, chunk, stride=2), :] = jnp.where(left, pltpu.roll(d, rank, 1), 0.0)
        down_a_ref[at : at + 2 * chunk, :] = wide_ref[at : at + 2 * chunk, :].astype(jnp.bfloat16)
    for start, b_ref in (
        (n_wide, gate_b_ref),
        (at_ub, up_b_ref),
        (at_da + n_unit, down_b_ref),
    ):
        tiles = b_ref.shape[1] // LANES
        for j in range(tiles):
            row = flat_ref[pl.ds(start + j, rank, stride=tiles), :]
            b_ref[:, j * LANES : (j + 1) * LANES] = row.astype(jnp.bfloat16)


def relayout_factors(place, parts, width, units, rank, n):
    shapes = [(width, 2 * rank), (rank, units), (rank, units), (units, 2 * rank), (rank, width)]
    length = parts[0].shape[1]
    return pl.pallas_call(
        relayout_kernel,
        out_shape=[jax.ShapeDtypeStruct(shape, jnp.bfloat16) for shape in shapes],
        in_specs=[pl.BlockSpec(memory_space=pltpu.SMEM)]
        + [pl.BlockSpec(memory_space=pltpu.VMEM)] * len(parts),
        scratch_shapes=[
            pltpu.VMEM((n * length, LANES), jnp.float32),
            pltpu.VMEM((width, LANES), jnp.float32),
        ],
        compiler_params=pltpu.CompilerParams(vmem_limit_bytes=GRANT),
        cost_estimate=LITTLE,
        name="relayout_factors",
    )(place, *parts)


def base_kernel(x_ref, w_gate_ref, w_up_ref, gate_ref, up_ref):
    width = w_gate_ref.shape[0]
    gate_ref[...] = dot(x_ref[:, :width], w_gate_ref[...])
    up_ref[...] = dot(x_ref[:, :width], w_up_ref[...])


def base_products(piece, w_gate, w_up):
    out = jax.ShapeDtypeStruct((piece.shape[0], w_gate.shape[1]), jnp.float32)
    return pl.pallas_call(
        base_kernel,
        out_shape=[out, out],
        in_specs=[pl.BlockSpec(memory_space=pltpu.VMEM)] * 3,
        compiler_params=pltpu.CompilerParams(vmem_limit_bytes=EXPERT_GRANT),
        cost_estimate=LITTLE,
        name="base_products",
    )(piece, w_gate, w_up)


def finish_kernel(count, first, rows, place_ref, *refs):
    pieces, refs = refs[:count], refs[count:]
    base, refs = refs[: 2 * count], refs[2 * count :]
    a_gu_ref, gate_b_ref, up_b_ref, down_a_ref, down_b_ref, w_down_ref = refs[:6]
    kept_ref, sent_ref, x_ref, inner_ref = refs[6:]
    width = w_down_ref.shape[1]
    rank = gate_b_ref.shape[0]
    own = kept_ref.shape[0]
    for i, piece in enumerate(pieces):
        x_ref[i * rows : (i + 1) * rows, :] = piece[first : first + rows, :]

    def of_step(refs):
        return jnp.concatenate([ref[first : first + rows, :] for ref in refs])

    low = (adapter_scale * dot(x_ref[:, :width], a_gu_ref[...])).astype(jnp.bfloat16)
    gates = x_ref[:, width:].astype(jnp.float32)
    lane = lax.broadcasted_iota(jnp.int32, gates.shape, 1)
    mine = jnp.sum(jnp.where(lane == place_ref[0], gates, 0.0), axis=1, keepdims=True)
    g = of_step(base[::2]) + dot(low[:, :rank], gate_b_ref[...])
    u = of_step(base[1::2]) + dot(low[:, rank:], up_b_ref[...])
    half = 0.5 * g
    inner_ref[...] = ((half + half * jnp.tanh(half)) * u).astype(jnp.bfloat16)
    low = (adapter_scale * dot(inner_ref[...], down_a_ref[...])).astype(jnp.bfloat16)[:, :rank]
    out = (dot(inner_ref[...], w_down_ref[...]) + dot(low, down_b_ref[...])) * mine
    kept_ref[...] = out[:own]
    sent_ref[...] = out[own:].astype(jnp.bfloat16)


def finish_step(place, pieces, base, first, rows, low_rank, w_down):
    units, width = w_down.shape
    total = rows * len(pieces)
    own = total // 2
    operands = [*pieces, *base, *low_rank, w_down]
    return pl.pallas_call(
        functools.partial(finish_kernel, len(pieces), first, rows),
        out_shape=[
            jax.ShapeDtypeStruct((own, width), jnp.float32),
            jax.ShapeDtypeStruct((own, width), jnp.bfloat16),
        ],
        in_specs=[pl.BlockSpec(memory_space=pltpu.SMEM)]
        + [pl.BlockSpec(memory_space=pltpu.VMEM)] * len(operands),
        scratch_shapes=[
            pltpu.VMEM((total, pieces[0].shape[1]), jnp.bfloat16),
            pltpu.VMEM((total, units), jnp.bfloat16),
        ],
        compiler_params=pltpu.CompilerParams(vmem_limit_bytes=EXPERT_GRANT),
        cost_estimate=MUCH,
        name="finish_step",
    )(place, *operands)


def dense_shards(
    hidden, route_ids, route_logits, placement, factors, w_gate, w_up, down_weight
):
    owners = lax.axis_size("expert")
    experts = placement.shape[0]
    steps, rows, width = hidden.shape
    units = w_gate.shape[2]
    rank = factors.shape[1] * owners // (3 * (width + units))
    outer, middle, cores = split_axis(owners)
    along_outer, along_middle = (middle * cores, outer), (cores, middle)
    place = lax.axis_index("expert").astype(jnp.int32).reshape(1)

    def along(x, stride, size):
        return [x] + [swap(x, owners, stride, k) for k in range(1, size)]

    rows_in, kept, sent = lay_out(
        place, placement, hidden, route_ids, route_logits, factors, outer, middle, cores
    )
    column = [p.reshape(steps, rows, -1) for p in along(rows_in, *along_outer)]
    column = jnp.stack(column, axis=1).reshape(steps * outer * rows, -1)
    blocks = jnp.stack([kept, swap(sent, owners, 1, 1)])
    blocks = [blocks[:, 0], swap(blocks[:, 1], owners, cores, 1)]
    blocks = [jnp.concatenate([block[:, q] for block in blocks]) for q in range(outer)]
    column, blocks = lax.optimization_barrier((column, blocks))
    here = blocks[:1] + [
        swap(block, owners, middle * cores, q) for q, block in enumerate(blocks) if q
    ]
    sheet = along(column, *along_middle)
    others = [swap(column, owners, 1, 1)]
    weights = (w_gate[0], w_up[0])
    base = [base_products(piece, *weights) for piece in (column, others[0])]
    here = here[::-1]
    here, sheet[1:], base = lax.optimization_barrier((here, sheet[1:], base))
    here = here[::-1]
    for r in range(1, middle):
        others.append(swap(sheet[r], owners, 1, 1))
        base.append(base_products(sheet[r], *weights))
        base.append(base_products(others[r], *weights))
    low_rank = relayout_factors(place, here, width, units, rank, owners)
    pieces = sheet + others
    base = [b for pair in base[::2] + base[1::2] for b in pair]
    span = outer * rows

    summed = []
    for s in range(steps):
        kept, sent = finish_step(place, pieces, base, s * span, span, low_rank, down_weight[0])
        if s == steps - 2:
            pieces, kept = lax.optimization_barrier((pieces, kept))
        total = kept + swap(sent, owners, 1, 1).astype(jnp.float32)
        summed.append(total.reshape(middle, outer, rows, width))
    first = jnp.stack(summed[:-1], axis=1).reshape(-1, width)
    last = jnp.swapaxes(summed[-1], 0, 1).reshape(-1, width)
    first = scatter_along(first, owners, *along_middle)
    last = scatter_along(last, owners, *along_outer)
    first, last = lax.optimization_barrier((first, last))
    first = jnp.swapaxes(first.reshape(steps - 1, outer, rows, width), 0, 1).reshape(-1, width)
    first = scatter_along(first, owners, *along_outer)
    last = scatter_along(last, owners, *along_middle)
    return jnp.concatenate([first, last]).astype(jnp.bfloat16).reshape(hidden.shape)


def row_capacity(rows, top, experts):
    return min(rows, 3 * max(1, rows * top // experts))


def unpack_factors(flat_factors, width, hidden_units, rank_size):
    layouts = [
        (width, rank_size),
        (rank_size, hidden_units),
        (width, rank_size),
        (rank_size, hidden_units),
        (hidden_units, rank_size),
        (rank_size, width),
    ]
    offset = 0
    segments = []
    for leading, trailing in layouts:
        segments.append(
            flat_factors[offset : offset + leading * trailing].reshape(leading, trailing)
        )
        offset = offset + leading * trailing
    return segments


def merge_weight(loaded_weights, factor_a, factor_b):
    adapter_delta = jnp.dot(factor_a, factor_b, preferred_element_type=jnp.float32)
    return (loaded_weights.astype(jnp.float32) + adapter_scale * adapter_delta).astype(jnp.bfloat16)


def apply_expert_block(inputs, merged_gate, merged_up, combined_down_weight):
    gate_part = jnp.dot(inputs, merged_gate, preferred_element_type=jnp.float32)
    up_part = jnp.dot(inputs, merged_up, preferred_element_type=jnp.float32)
    inner = (jax.nn.silu(gate_part) * up_part).astype(jnp.bfloat16)
    return jnp.dot(inner, combined_down_weight, preferred_element_type=jnp.float32).astype(
        jnp.bfloat16
    )


def sparse_shards(hidden, route_ids, route_logits, placement, factors, w_gate, w_up, down_weight):
    owners = lax.axis_size("expert")
    experts = placement.shape[0]
    steps_count, row_count, width = hidden.shape
    top_count = route_ids.shape[2]
    hidden_units = w_gate.shape[2]
    rank_size = factors.shape[1] * owners // (3 * (width + hidden_units))
    capacity = row_capacity(row_count, top_count, experts)
    slot_of = (
        jnp.zeros((experts,), jnp.int32).at[placement].set(jnp.arange(experts, dtype=jnp.int32))
    )
    ordered = jnp.take(factors, slot_of, axis=0)
    received = lax.all_to_all(ordered, "expert", split_axis=0, concat_axis=1, tiled=True)
    segments = unpack_factors(received[0], width, hidden_units, rank_size)
    merged_gate = merge_weight(w_gate[0], segments[0], segments[1])
    merged_up = merge_weight(w_up[0], segments[2], segments[3])
    combined_down_weight = merge_weight(down_weight[0], segments[4], segments[5])

    def layout(step_index):
        ids_flat = route_ids[step_index].reshape(-1)
        onehot = (ids_flat[:, None] == jnp.arange(experts, dtype=jnp.int32)[None, :]).astype(
            jnp.int32
        )
        position = jnp.sum((jnp.cumsum(onehot, axis=0) - 1) * onehot, axis=1)
        target = ids_flat * capacity + position
        placed = (
            jnp.arange(experts * capacity, dtype=jnp.int32)[:, None] == target[None, :]
        ).astype(jnp.bfloat16)
        pair_rows = jnp.repeat(hidden[step_index], top_count, axis=0)
        outgoing = jnp.dot(placed, pair_rows, preferred_element_type=jnp.float32).astype(
            jnp.bfloat16
        )
        outgoing = outgoing.reshape(experts, 1, capacity, width)
        gates = route_gates(route_logits[step_index]).reshape(-1)
        weighted = placed * gates[None, :]
        return (outgoing, weighted)

    layouts_all = [layout(step_index) for step_index in range(steps_count)]
    results = []
    for step_index in range(steps_count):
        outgoing, weighted = layouts_all[step_index]
        arrived = lax.all_to_all(outgoing, "expert", split_axis=0, concat_axis=1, tiled=True)
        outputs = apply_expert_block(
            arrived.reshape(-1, width), merged_gate, merged_up, combined_down_weight
        )
        outputs = outputs.reshape(arrived.shape)
        returned = lax.all_to_all(outputs, "expert", split_axis=1, concat_axis=0, tiled=True)
        flat_back = returned.reshape(experts * capacity, width)
        pair_out = jnp.einsum("cp,cd->pd", weighted, flat_back, preferred_element_type=jnp.float32)
        results.append(
            pair_out.reshape(row_count, top_count, width).sum(axis=1).astype(jnp.bfloat16)
        )
    return jnp.stack(results, axis=0)


def shards(hidden, route_ids, route_logits, placement, factors, w_gate, w_up, down_weight):
    rows, top = route_ids.shape[1:]
    width, units = w_gate.shape[1:]
    owners = lax.axis_size("expert")
    rank = factors.shape[1] * owners // (3 * (width + units))
    dense = row_capacity(rows, top, placement.shape[0]) == rows
    dense = dense and split_axis(owners)[1:] == (2, 2)
    outer = split_axis(owners)[0]
    dense = dense and outer > 1 and outer & (outer - 1) == 0 and split_axis(owners)[1] > 1
    dense = dense and 2 * rank == LANES and width % 256 == 0 and units % 256 == 0
    dense = dense and factors.shape[1] % (8 * LANES) == 0
    return (dense_shards if dense else sparse_shards)(
        hidden, route_ids, route_logits, placement, factors, w_gate, w_up, down_weight
    )


def solution(mesh):
    placed = (
        P(None, ("group", "expert"), None),
        P(None, ("group", "expert"), None),
        P(None, ("group", "expert"), None),
        P(),
        P(None, "expert"),
        P("expert", None, None),
        P("expert", None, None),
        P("expert", None, None),
    )
    return jax.shard_map(
        shards,
        mesh=mesh,
        in_specs=placed,
        out_specs=P(None, ("group", "expert"), None),
        check_vma=False,
    )
```

```python
import functools

import jax
import jax.numpy as jnp
from jax import lax
from jax.experimental import pallas as pl
from jax.experimental.pallas import tpu as pltpu
from jax.sharding import PartitionSpec as P

adapter_scale = 2.0
LANES = 128
GRANT = 16 << 20
EXPERT_GRANT = 30 << 20
WHOLE_GRANT = 60 << 20
MUCH = pl.CostEstimate(flops=1 << 33, bytes_accessed=1, transcendentals=0)
LITTLE = pl.CostEstimate(flops=1, bytes_accessed=1, transcendentals=0)


def route_gates(logits):
    highest = jnp.max(logits, axis=-1, keepdims=True)
    router_scores = jnp.exp(logits - highest)
    return (router_scores / jnp.sum(router_scores, axis=-1, keepdims=True)).astype(jnp.bfloat16)


def split_axis(n):
    cores = 2 if n % 2 == 0 else 1
    chips = n // cores
    middle = 1
    while chips % (2 * middle) == 0 and 4 * middle * middle <= chips:
        middle *= 2
    return chips // middle, middle, cores


def swap(x, n, stride, k):
    return lax.ppermute(x, "expert", [(i, i ^ (k * stride)) for i in range(n)])


def scatter_along(total, n, stride, size):
    count = total.shape[0] // size
    received = []
    for k in range(1, size):
        part = total[k * count : (k + 1) * count].astype(jnp.bfloat16)
        received.append(swap(part, n, stride, k))
    return sum([part.astype(jnp.float32) for part in received], total[:count])


def dot(a, b):
    return jnp.dot(a, b, preferred_element_type=jnp.float32)


def first_kernel(
    place_ref, placement_ref, hidden_ref, ids_ref, logits_ref, factors_ref, out_ref, *refs
):
    turned_ref, wide_ref, slot_ref = refs[-3:]
    steps, top, rows = ids_ref.shape
    width = hidden_ref.shape[2]
    turned_ref[...] = jnp.zeros_like(turned_ref)
    for s in range(steps):
        logits, ids = logits_ref[s], ids_ref[s]
        scores = jnp.exp(logits - jnp.max(logits, axis=0, keepdims=True))
        gates = scores / jnp.sum(scores, axis=0, keepdims=True)
        expert = lax.broadcasted_iota(jnp.int32, (turned_ref.shape[0], rows), 0)
        dense = jnp.zeros(expert.shape, jnp.float32)
        for k in range(top):
            dense += jnp.where(ids[k : k + 1, :] == expert, gates[k : k + 1, :], 0.0)
        turned_ref[:, s * rows : (s + 1) * rows] = dense
    dense = turned_ref[...].T.astype(jnp.bfloat16)
    for s in range(steps):
        out_ref[s * rows : (s + 1) * rows, :width] = hidden_ref[s]
    out_ref[:, width:] = dense[: steps * rows]

    slots = factors_ref.shape[0]
    out_refs = refs[:-3]
    middle, outer, length, lanes = out_refs[0].shape

    def cut(t, carry):
        start = pl.multiple_of(t * lanes, lanes)
        tile = factors_ref[:, pl.ds(start, lanes)].astype(jnp.float32)
        wide_ref[pl.ds(t, slots, stride=length), :] = tile
        return carry

    lax.fori_loop(0, length, cut, 0, unroll=24)
    for s in range(slots):
        slot_ref[placement_ref[s]] = s
    for core, out_ref in enumerate(out_refs):
        for r in range(middle):
            for q in range(outer):
                slot = slot_ref[place_ref[0] ^ ((q * middle + r) * len(out_refs) + core)]
                block = wide_ref[pl.ds(pl.multiple_of(slot * length, 8), length), :]
                out_ref[r, q] = block.astype(jnp.bfloat16)


def lay_out(place, placement, hidden, route_ids, route_logits, factors, outer, middle, cores):
    steps, rows, width = hidden.shape
    slots, entries = factors.shape
    length = entries // LANES
    padded = -(-slots // LANES) * LANES
    shape = jax.ShapeDtypeStruct((middle, outer, length, LANES), jnp.bfloat16)
    return pl.pallas_call(
        first_kernel,
        out_shape=[jax.ShapeDtypeStruct((steps * rows, width + padded), jnp.bfloat16)]
        + [shape] * cores,
        in_specs=[pl.BlockSpec(memory_space=pltpu.SMEM)] * 2
        + [pl.BlockSpec(memory_space=pltpu.VMEM)] * 4,
        scratch_shapes=[
            pltpu.VMEM((padded, -(-steps * rows // LANES) * LANES), jnp.float32),
            pltpu.VMEM((slots * length, LANES), jnp.float32),
            pltpu.SMEM((slots,), jnp.int32),
        ],
        compiler_params=pltpu.CompilerParams(vmem_limit_bytes=WHOLE_GRANT),
        cost_estimate=LITTLE,
        name="lay_out",
    )(
        place,
        placement,
        hidden,
        jnp.swapaxes(route_ids, 1, 2),
        jnp.swapaxes(route_logits, 1, 2),
        factors,
    )


def relayout_kernel(place_ref, *refs):
    parts, refs = refs[:-7], refs[-7:]
    a_gu_ref, gate_b_ref, up_b_ref, down_a_ref, down_b_ref, flat_ref, wide_ref = refs
    width, units = a_gu_ref.shape[0], gate_b_ref.shape[1]
    rank = gate_b_ref.shape[0]
    near, length, _ = parts[0].shape
    for q, part in enumerate(parts):
        for j in range(near):
            start = pl.multiple_of((place_ref[0] ^ (near * q + j)) * length, 8)
            flat_ref[pl.ds(start, length), :] = part[j].astype(jnp.float32)

    n_wide, n_unit = width // 2, units // 2
    at_ub = 2 * n_wide + n_unit
    at_da = 2 * n_wide + 2 * n_unit
    chunk = 128
    left = lax.broadcasted_iota(jnp.int32, (chunk, LANES), 1) < rank

    def load(start):
        return flat_ref[pl.ds(pl.multiple_of(start, 128), chunk), :]

    def gate_up(i, carry):
        g, u = load(i * chunk), load(n_wide + n_unit + i * chunk)
        at = 2 * i * chunk
        wide_ref[pl.ds(at, chunk, stride=2), :] = jnp.where(left, g, pltpu.roll(u, rank, 1))
        wide_ref[pl.ds(at + 1, chunk, stride=2), :] = jnp.where(left, pltpu.roll(g, rank, 1), u)
        both = wide_ref[pl.ds(pl.multiple_of(at, 128), 2 * chunk), :]
        a_gu_ref[pl.ds(pl.multiple_of(at, 128), 2 * chunk), :] = both.astype(jnp.bfloat16)
        return carry

    lax.fori_loop(0, n_wide // chunk, gate_up, 0, unroll=2)
    for i in range(n_unit // chunk):
        d = load(at_da + i * chunk)
        at = 2 * i * chunk
        wide_ref[pl.ds(at, chunk, stride=2), :] = jnp.where(left, d, 0.0)
        wide_ref[pl.ds(at + 1, chunk, stride=2), :] = jnp.where(left, pltpu.roll(d, rank, 1), 0.0)
        down_a_ref[at : at + 2 * chunk, :] = wide_ref[at : at + 2 * chunk, :].astype(jnp.bfloat16)
    for start, b_ref in (
        (n_wide, gate_b_ref),
        (at_ub, up_b_ref),
        (at_da + n_unit, down_b_ref),
    ):
        tiles = b_ref.shape[1] // LANES
        for j in range(tiles):
            row = flat_ref[pl.ds(start + j, rank, stride=tiles), :]
            b_ref[:, j * LANES : (j + 1) * LANES] = row.astype(jnp.bfloat16)


def relayout_factors(place, parts, width, units, rank, n):
    shapes = [(width, 2 * rank), (rank, units), (rank, units), (units, 2 * rank), (rank, width)]
    length = parts[0].shape[1]
    return pl.pallas_call(
        relayout_kernel,
        out_shape=[jax.ShapeDtypeStruct(shape, jnp.bfloat16) for shape in shapes],
        in_specs=[pl.BlockSpec(memory_space=pltpu.SMEM)]
        + [pl.BlockSpec(memory_space=pltpu.VMEM)] * len(parts),
        scratch_shapes=[
            pltpu.VMEM((n * length, LANES), jnp.float32),
            pltpu.VMEM((width, LANES), jnp.float32),
        ],
        compiler_params=pltpu.CompilerParams(vmem_limit_bytes=GRANT),
        cost_estimate=LITTLE,
        name="relayout_factors",
    )(place, *parts)


def base_kernel(x_ref, w_gate_ref, w_up_ref, gate_ref, up_ref):
    width = w_gate_ref.shape[0]
    gate_ref[...] = dot(x_ref[:, :width], w_gate_ref[...])
    up_ref[...] = dot(x_ref[:, :width], w_up_ref[...])


def base_products(piece, w_gate, w_up):
    out = jax.ShapeDtypeStruct((piece.shape[0], w_gate.shape[1]), jnp.float32)
    return pl.pallas_call(
        base_kernel,
        out_shape=[out, out],
        in_specs=[pl.BlockSpec(memory_space=pltpu.VMEM)] * 3,
        compiler_params=pltpu.CompilerParams(vmem_limit_bytes=EXPERT_GRANT),
        cost_estimate=LITTLE,
        name="base_products",
    )(piece, w_gate, w_up)


def finish_kernel(count, first, rows, place_ref, *refs):
    pieces, refs = refs[:count], refs[count:]
    base, refs = refs[: 2 * count], refs[2 * count :]
    a_gu_ref, gate_b_ref, up_b_ref, down_a_ref, down_b_ref, w_down_ref = refs[:6]
    kept_ref, sent_ref, x_ref, inner_ref = refs[6:]
    width = w_down_ref.shape[1]
    rank = gate_b_ref.shape[0]
    own = kept_ref.shape[0]
    for i, piece in enumerate(pieces):
        x_ref[i * rows : (i + 1) * rows, :] = piece[first : first + rows, :]

    def of_step(refs):
        return jnp.concatenate([ref[first : first + rows, :] for ref in refs])

    low = (adapter_scale * dot(x_ref[:, :width], a_gu_ref[...])).astype(jnp.bfloat16)
    gates = x_ref[:, width:].astype(jnp.float32)
    lane = lax.broadcasted_iota(jnp.int32, gates.shape, 1)
    mine = jnp.sum(jnp.where(lane == place_ref[0], gates, 0.0), axis=1, keepdims=True)
    g = of_step(base[::2]) + dot(low[:, :rank], gate_b_ref[...])
    u = of_step(base[1::2]) + dot(low[:, rank:], up_b_ref[...])
    half = 0.5 * g
    inner_ref[...] = ((half + half * jnp.tanh(half)) * u).astype(jnp.bfloat16)
    low = (adapter_scale * dot(inner_ref[...], down_a_ref[...])).astype(jnp.bfloat16)[:, :rank]
    out = (dot(inner_ref[...], w_down_ref[...]) + dot(low, down_b_ref[...])) * mine
    kept_ref[...] = out[:own]
    sent_ref[...] = out[own:].astype(jnp.bfloat16)


def finish_step(place, pieces, base, first, rows, low_rank, w_down):
    units, width = w_down.shape
    total = rows * len(pieces)
    own = total // 2
    operands = [*pieces, *base, *low_rank, w_down]
    return pl.pallas_call(
        functools.partial(finish_kernel, len(pieces), first, rows),
        out_shape=[
            jax.ShapeDtypeStruct((own, width), jnp.float32),
            jax.ShapeDtypeStruct((own, width), jnp.bfloat16),
        ],
        in_specs=[pl.BlockSpec(memory_space=pltpu.SMEM)]
        + [pl.BlockSpec(memory_space=pltpu.VMEM)] * len(operands),
        scratch_shapes=[
            pltpu.VMEM((total, pieces[0].shape[1]), jnp.bfloat16),
            pltpu.VMEM((total, units), jnp.bfloat16),
        ],
        compiler_params=pltpu.CompilerParams(vmem_limit_bytes=EXPERT_GRANT),
        cost_estimate=MUCH,
        name="finish_step",
    )(place, *operands)


def dense_shards(
    hidden, route_ids, route_logits, placement, factors, w_gate, w_up, down_weight
):
    owners = lax.axis_size("expert")
    experts = placement.shape[0]
    steps, rows, width = hidden.shape
    units = w_gate.shape[2]
    rank = factors.shape[1] * owners // (3 * (width + units))
    outer, middle, cores = split_axis(owners)
    along_outer, along_middle = (middle * cores, outer), (cores, middle)
    place = lax.axis_index("expert").astype(jnp.int32).reshape(1)

    def along(x, stride, size):
        return [x] + [swap(x, owners, stride, k) for k in range(1, size)]

    rows_in, kept, sent = lay_out(
        place, placement, hidden, route_ids, route_logits, factors, outer, middle, cores
    )
    column = [p.reshape(steps, rows, -1) for p in along(rows_in, *along_outer)]
    column = jnp.stack(column, axis=1).reshape(steps * outer * rows, -1)
    blocks = jnp.stack([kept, swap(sent, owners, 1, 1)])
    blocks = [blocks[:, 0], swap(blocks[:, 1], owners, cores, 1)]
    blocks = [jnp.concatenate([block[:, q] for block in blocks]) for q in range(outer)]
    column, blocks = lax.optimization_barrier((column, blocks))
    here = blocks[:1] + [
        swap(block, owners, middle * cores, q) for q, block in enumerate(blocks) if q
    ]
    sheet = along(column, *along_middle)
    others = [swap(column, owners, 1, 1)]
    weights = (w_gate[0], w_up[0])
    base = [base_products(piece, *weights) for piece in (column, others[0])]
    here = here[::-1]
    here, sheet[1:], base = lax.optimization_barrier((here, sheet[1:], base))
    here = here[::-1]
    for r in range(1, middle):
        others.append(swap(sheet[r], owners, 1, 1))
        base.append(base_products(sheet[r], *weights))
        base.append(base_products(others[r], *weights))
    low_rank = relayout_factors(place, here, width, units, rank, owners)
    pieces = sheet + others
    base = [b for pair in base[::2] + base[1::2] for b in pair]
    span = outer * rows

    summed = []
    for s in range(steps):
        kept, sent = finish_step(place, pieces, base, s * span, span, low_rank, down_weight[0])
        if s == steps - 2:
            pieces, kept = lax.optimization_barrier((pieces, kept))
        total = kept + swap(sent, owners, 1, 1).astype(jnp.float32)
        summed.append(total.reshape(middle, outer, rows, width))
    first = jnp.stack(summed[:-1], axis=1).reshape(-1, width)
    last = jnp.swapaxes(summed[-1], 0, 1).reshape(-1, width)
    first = scatter_along(first, owners, *along_middle)
    last = scatter_along(last, owners, *along_outer)
    first, last = lax.optimization_barrier((first, last))
    first = jnp.swapaxes(first.reshape(steps - 1, outer, rows, width), 0, 1).reshape(-1, width)
    first = scatter_along(first, owners, *along_outer)
    last = scatter_along(last, owners, *along_middle)
    return jnp.concatenate([first, last]).astype(jnp.bfloat16).reshape(hidden.shape)


def row_capacity(rows, top, experts):
    return min(rows, 3 * max(1, rows * top // experts))


def unpack_factors(flat_factors, width, hidden_units, rank_size):
    layouts = [
        (width, rank_size),
        (rank_size, hidden_units),
        (width, rank_size),
        (rank_size, hidden_units),
        (hidden_units, rank_size),
        (rank_size, width),
    ]
    offset = 0
    segments = []
    for leading, trailing in layouts:
        segments.append(
            flat_factors[offset : offset + leading * trailing].reshape(leading, trailing)
        )
        offset = offset + leading * trailing
    return segments


def merge_weight(loaded_weights, factor_a, factor_b):
    adapter_delta = jnp.dot(factor_a, factor_b, preferred_element_type=jnp.float32)
    return (loaded_weights.astype(jnp.float32) + adapter_scale * adapter_delta).astype(jnp.bfloat16)


def apply_expert_block(inputs, merged_gate, merged_up, combined_down_weight):
    gate_part = jnp.dot(inputs, merged_gate, preferred_element_type=jnp.float32)
    up_part = jnp.dot(inputs, merged_up, preferred_element_type=jnp.float32)
    inner = (jax.nn.silu(gate_part) * up_part).astype(jnp.bfloat16)
    return jnp.dot(inner, combined_down_weight, preferred_element_type=jnp.float32).astype(
        jnp.bfloat16
    )


def sparse_shards(hidden, route_ids, route_logits, placement, factors, w_gate, w_up, down_weight):
    owners = lax.axis_size("expert")
    experts = placement.shape[0]
    steps_count, row_count, width = hidden.shape
    top_count = route_ids.shape[2]
    hidden_units = w_gate.shape[2]
    rank_size = factors.shape[1] * owners // (3 * (width + hidden_units))
    capacity = row_capacity(row_count, top_count, experts)
    slot_of = (
        jnp.zeros((experts,), jnp.int32).at[placement].set(jnp.arange(experts, dtype=jnp.int32))
    )
    ordered = jnp.take(factors, slot_of, axis=0)
    received = lax.all_to_all(ordered, "expert", split_axis=0, concat_axis=1, tiled=True)
    segments = unpack_factors(received[0], width, hidden_units, rank_size)
    merged_gate = merge_weight(w_gate[0], segments[0], segments[1])
    merged_up = merge_weight(w_up[0], segments[2], segments[3])
    combined_down_weight = merge_weight(down_weight[0], segments[4], segments[5])

    def layout(step_index):
        ids_flat = route_ids[step_index].reshape(-1)
        onehot = (ids_flat[:, None] == jnp.arange(experts, dtype=jnp.int32)[None, :]).astype(
            jnp.int32
        )
        position = jnp.sum((jnp.cumsum(onehot, axis=0) - 1) * onehot, axis=1)
        target = ids_flat * capacity + position
        placed = (
            jnp.arange(experts * capacity, dtype=jnp.int32)[:, None] == target[None, :]
        ).astype(jnp.bfloat16)
        pair_rows = jnp.repeat(hidden[step_index], top_count, axis=0)
        outgoing = jnp.dot(placed, pair_rows, preferred_element_type=jnp.float32).astype(
            jnp.bfloat16
        )
        outgoing = outgoing.reshape(experts, 1, capacity, width)
        gates = route_gates(route_logits[step_index]).reshape(-1)
        weighted = placed * gates[None, :]
        return (outgoing, weighted)

    layouts_all = [layout(step_index) for step_index in range(steps_count)]
    results = []
    for step_index in range(steps_count):
        outgoing, weighted = layouts_all[step_index]
        arrived = lax.all_to_all(outgoing, "expert", split_axis=0, concat_axis=1, tiled=True)
        outputs = apply_expert_block(
            arrived.reshape(-1, width), merged_gate, merged_up, combined_down_weight
        )
        outputs = outputs.reshape(arrived.shape)
        returned = lax.all_to_all(outputs, "expert", split_axis=1, concat_axis=0, tiled=True)
        flat_back = returned.reshape(experts * capacity, width)
        pair_out = jnp.einsum("cp,cd->pd", weighted, flat_back, preferred_element_type=jnp.float32)
        results.append(
            pair_out.reshape(row_count, top_count, width).sum(axis=1).astype(jnp.bfloat16)
        )
    return jnp.stack(results, axis=0)


def shards(hidden, route_ids, route_logits, placement, factors, w_gate, w_up, down_weight):
    rows, top = route_ids.shape[1:]
    width, units = w_gate.shape[1:]
    owners = lax.axis_size("expert")
    rank = factors.shape[1] * owners // (3 * (width + units))
    dense = row_capacity(rows, top, placement.shape[0]) == rows
    dense = dense and split_axis(owners)[1:] == (2, 2)
    outer = split_axis(owners)[0]
    dense = dense and outer > 1 and outer & (outer - 1) == 0 and split_axis(owners)[1] > 1
    dense = dense and 2 * rank == LANES and width % 256 == 0 and units % 256 == 0
    dense = dense and factors.shape[1] % (8 * LANES) == 0
    return (dense_shards if dense else sparse_shards)(
        hidden, route_ids, route_logits, placement, factors, w_gate, w_up, down_weight
    )


def solution(mesh):
    placed = (
        P(None, ("group", "expert"), None),
        P(None, ("group", "expert"), None),
        P(None, ("group", "expert"), None),
        P(),
        P(None, "expert"),
        P("expert", None, None),
        P("expert", None, None),
        P("expert", None, None),
    )
    return jax.shard_map(
        shards,
        mesh=mesh,
        in_specs=placed,
        out_specs=P(None, ("group", "expert"), None),
        check_vma=False,
    )
```
